32 devices in a mesh: seq: 8 (over z, y), grp: 4 (over x, core).
Axes of the slice: x: 2, y: 2, z: 4, core: 2. Of those that a mesh axis runs over, the one named last changes fastest.
Arguments:
- tokens: bfloat16 [16, 1024, 1024], P('grp', 'seq'), may hold values from -6 to 6
- segment_ids: int32 [16, 1024], P('grp', 'seq'), may hold values from 0 to 3, never falling along the last dimension, each value on 1 to 512 neighbouring positions
- adapter_ids: int32 [16], P('grp'), may hold values from 0 to 7
- input_weight: bfloat16 [1024, 3072], replicated, may hold values from -0.1875 to 0.1875
- conv_weight: float32 [3, 1024], replicated, may hold values from -3.5 to 3.5
- output_weight: bfloat16 [1024, 1024], replicated, may hold values from -0.1875 to 0.1875
- gate_weight: bfloat16 [1024, 4608], replicated, may hold values from -0.1875 to 0.1875
- up_weight: bfloat16 [1024, 4608], replicated, may hold values from -0.1875 to 0.1875
- down_weight: bfloat16 [4608, 1024], replicated, may hold values from -0.09375 to 0.09375
- norm_one: float32 [1024], replicated, may hold values from 0.5 to 1.5
- norm_two: float32 [1024], replicated, may hold values from 0.5 to 1.5
- cotangent: bfloat16 [16, 1024, 1024], P('grp', 'seq'), may hold values from -6 to 6
- adapter_state: float32 [8, 368640], P('grp'), may hold values from -0.18 to 0.18
- first_moment: float32 [8, 368640], P('grp'), as said below
- second_moment: float32 [8, 368640], P('grp'), as said below
- rate: float32 [1], replicated, may hold values from 0.2 to 0.5
- step: int32 [1], replicated, may hold values from 1 to 8
Outputs:
- output: bfloat16 [16, 1024, 1024], P('grp', 'seq')
- input_grad: bfloat16 [16, 1024, 1024], P('grp', 'seq')
- adapter_state_new: float32 [8, 368640], P('grp')
- adapter_table_new: bfloat16 [8, 368640], replicated
The draws below stay inside these ranges and needn't reach their ends.
Inputs may be any that keep to these rules, and one draw needn't show every extreme that they name: `segment_ids`: within a sequence the numbers start at 0 and never fall; each document holds 1 to 512 positions. `first_moment`: real values of either sign. `second_moment`: Positive.
All inputs are finite; a program needn't handle non-finite values.
Results may differ from the reference program's by a relative error of at most 0.01.
The reference program's roundings to bfloat16 on the way count: a program that leaves them out, or rounds other values in their place, can miss the bound.
Values may be sent and summed in bfloat16 or wider, within the bound.
A program may use at most 192 MiB of HBM per device.

```python
import math
import jax
import jax.numpy as jnp
import numpy as np
from jax import lax

D = 1024
FF = 4608
CONV = 3
RANK = 16
ADAPTERS = 8
LENGTH = 1024
SEQS = 16
PACK = 368640
SEG_COUNT = 4
SEG_MOST = 512


def moment_level():
    return 0.1 * math.sqrt(D * LENGTH * SEQS / ADAPTERS)


def draw_first_moment(key, part):
    key = jax.random.fold_in(key, 11)
    normal_values = jax.random.truncated_normal(key, -3.0, 3.0, (ADAPTERS, PACK), jnp.float32)
    return 0.5 * moment_level() * normal_values


def draw_second_moment(key, part):
    key = jax.random.fold_in(key, 23)
    uniform_values = jax.random.uniform(key, (ADAPTERS, PACK), jnp.float32)
    factor = jnp.exp(math.log(2.0) + uniform_values * math.log(4.0))
    level = moment_level()
    return factor * (level * level)


def plant(values, stream_key, smallest, top_value):
    longest = values.shape.index(max(values.shape))
    spots = []
    for shift in (0, 1):
        where = [jax.random.randint(jax.random.fold_in(stream_key, axis), (), 0, length) for axis, length in enumerate(values.shape)]
        where[longest] = (where[longest] + shift) % values.shape[longest]
        spots.append(tuple(where))
    return values.at[spots[0]].set(smallest).at[spots[1]].set(top_value)


def levels(key, shape, shards, low, largest):
    level, own = 1.0, jax.random.fold_in(key, 6)
    for axis_at, shards_of in shards:
        heights = jnp.exp(jax.random.uniform(jax.random.fold_in(own, axis_at), (shards_of,), jnp.float32, low / len(shards), largest / len(shards)))
        level = level * jnp.repeat(heights, shape[axis_at] // shards_of).reshape([-1 if axis == axis_at else 1 for axis in range(len(shape))])
    return level


def length_profile(amount, total, bound, skew):
    weights = [(1 << 20) // math.isqrt(grade ** skew) + 1 for grade in range(2, amount + 1)]
    spare, given = total - bound - (amount - 1), [1] * (amount - 1)
    while spare > 0:
        movable = [i for i in range(amount - 1) if given[i] < bound]
        mass, remaining = sum([weights[i] for i in movable]), spare
        for i in movable:
            addition = min(bound - given[i], max(1, remaining * weights[i] // mass), spare)
            given[i] = given[i] + addition
            spare = spare - addition
    return np.array([bound] + given)


def uneven(own_key, count, total, limit, skew):
    if count == 2:
        one = jax.random.randint(own_key, (), max(1, total - limit), min(limit, total - 1) + 1)
        return jnp.stack([one, total - one])
    lengths = jnp.asarray(length_profile(count, total, limit, skew), jnp.int32)
    twos = (count - 1) // 2
    donor, receiver = lengths[1:1 + 2 * twos:2], lengths[2:2 + 2 * twos:2]
    slack = jnp.minimum(donor - 1, limit - receiver)
    moved = jax.random.randint(jax.random.fold_in(own_key, 1), (twos,), 0, 1 << 20) % (slack + 1)
    lengths = lengths.at[1:1 + 2 * twos:2].set(donor - moved).at[2:2 + 2 * twos:2].set(receiver + moved)
    return lengths[jax.random.permutation(jax.random.fold_in(own_key, 2), count)]


def bell_draw(stream_key, extent, spread, most, cuts=(), dtype=jnp.bfloat16):
    entries = jax.random.normal(stream_key, extent, jnp.float32) * spread
    if len(cuts) > 0:
        entries = levels(stream_key, extent, cuts, -0.22, 0.18) * entries
    return jnp.clip(entries, min=-most, max=most).astype(dtype)


def setup_inputs(seed: int = 0) -> dict:
    key_of = jax.random.split(jax.random.key(seed), 18)
    return {
        "tokens": bell_draw(key_of[0], (SEQS, LENGTH, D), 1.0, 6.0, ((0, 4), (1, 8))),
        "segment_ids": jax.vmap(lambda own: jnp.searchsorted(jnp.cumsum(uneven(own, SEG_COUNT, LENGTH, SEG_MOST, 1)), jnp.arange(LENGTH), side="right"))(jax.random.split(key_of[1], SEQS)).reshape((SEQS, LENGTH)).astype(jnp.int32),
        "adapter_ids": plant(jax.random.randint(key_of[2], (SEQS,), 0, ADAPTERS), jax.random.fold_in(key_of[2], 1), 0, ADAPTERS - 1).astype(jnp.int32),
        "input_weight": bell_draw(key_of[3], (D, 3 * D), D ** -0.5, 0.1875),
        "conv_weight": bell_draw(key_of[4], (CONV, D), 3 ** -0.5, 3.5, (), jnp.float32),
        "output_weight": bell_draw(key_of[5], (D, D), D ** -0.5, 0.1875),
        "gate_weight": bell_draw(key_of[6], (D, FF), D ** -0.5, 0.1875),
        "up_weight": bell_draw(key_of[7], (D, FF), D ** -0.5, 0.1875),
        "down_weight": bell_draw(key_of[8], (FF, D), FF ** -0.5, 0.09375),
        "norm_one": jnp.clip(1.0 + 0.1 * jax.random.normal(key_of[9], (D,), jnp.float32), 0.5, 1.5),
        "norm_two": jnp.clip(1.0 + 0.1 * jax.random.normal(key_of[10], (D,), jnp.float32), 0.5, 1.5),
        "cotangent": bell_draw(key_of[11], (SEQS, LENGTH, D), 1.0, 6.0, ((0, 4), (1, 8))),
        "adapter_state": bell_draw(key_of[12], (ADAPTERS, PACK), 0.03, 0.18, ((0, 4),), jnp.float32),
        "first_moment": draw_first_moment(jax.random.fold_in(key_of[17], 71), 0),
        "second_moment": draw_second_moment(jax.random.fold_in(key_of[17], 71), 0),
        "rate": jnp.clip(jax.random.uniform(key_of[15], (1,), jnp.float32, 0.2, 0.5), 0.2, 0.5),
        "step": jax.random.randint(key_of[16], (1,), 1, 9).astype(jnp.int32),
    }


@jax.custom_vjp
def low(v):
    return lax.optimization_barrier(v.astype(jnp.bfloat16)).astype(jnp.float32)

@jax.custom_vjp
def low_back(v):
    return v

def low_keep(v):
    return (low(v), None)

def low_pass(kept, grad):
    return (grad,)

def back_keep(v):
    return (v, None)

def back_low(kept, grad):
    return (low(grad),)
low.defvjp(low_keep, low_pass)
low_back.defvjp(back_keep, back_low)
EPS = 1e-05
adapter_scale = 2.0
highest = lax.Precision.HIGHEST

def matrix_product(left, right):
    return jnp.dot(left, right, precision=highest, preferred_element_type=jnp.float32)

def unpack(vector):
    shapes = ((D, RANK), (RANK, 3 * D), (D, RANK), (RANK, D), (D, RANK), (RANK, FF), (D, RANK), (RANK, FF), (FF, RANK), (RANK, D))
    pieces = []
    offset = 0
    for height, breadth in shapes:
        flat_piece = lax.slice_in_dim(vector, offset, offset + height * breadth, axis=vector.ndim - 1)
        pieces.append(flat_piece.reshape(vector.shape[:-1] + (height, breadth)))
        offset = offset + height * breadth
    return pieces

def rms_norm(values, norm_gain):
    return values * lax.rsqrt(lax.optimization_barrier(jnp.mean(values * values, axis=-1, keepdims=True)) + EPS) * norm_gain

def project(input_rows, weight_matrix, down_piece, up_piece):
    middle_rows = low(matrix_product(input_rows, down_piece))
    return matrix_product(input_rows, weight_matrix) + adapter_scale * matrix_product(middle_rows, up_piece)

def block_forward(rows_in, adapter, weights, seq_ids):
    input_weight, conv_weight, output_weight, gate_weight, up_weight, down_weight, norm_one, norm_two = weights
    pieces_list = unpack(low(adapter))
    normed = low(rms_norm(rows_in, norm_one))
    projected_rows = low_back(project(normed, input_weight, pieces_list[0], pieces_list[1]))
    gate_b = projected_rows[:, :D]
    gate_c = projected_rows[:, D:2 * D]
    values_x = projected_rows[:, 2 * D:]
    mixed_in = gate_b * values_x
    convolved = conv_weight[2] * mixed_in
    for lag_steps in (1, 2):
        earlier = jnp.concatenate([jnp.zeros((lag_steps, D), jnp.float32), mixed_in[:-lag_steps]], axis=0)
        earlier_ids = jnp.concatenate([jnp.full((lag_steps,), -1, jnp.int32), seq_ids[:-lag_steps]], axis=0)
        same_doc = (earlier_ids == seq_ids).astype(jnp.float32)[:, None]
        convolved = convolved + conv_weight[2 - lag_steps] * same_doc * earlier
    gated_hidden = low(gate_c * convolved)
    branch_output = low_back(project(gated_hidden, output_weight, pieces_list[2], pieces_list[3]))
    hidden_one = rows_in + branch_output
    normed_two = low(rms_norm(hidden_one, norm_two))
    gate_up = low_back(jnp.concatenate([project(normed_two, gate_weight, pieces_list[4], pieces_list[5]), project(normed_two, up_weight, pieces_list[6], pieces_list[7])], axis=1))
    hidden_rows = low(jax.nn.silu(gate_up[:, :FF]) * gate_up[:, FF:])
    feedforward_output = low_back(project(hidden_rows, down_weight, pieces_list[8], pieces_list[9]))
    return hidden_one + feedforward_output

def reference(tokens, segment_ids, adapter_ids, input_weight, conv_weight, output_weight, gate_weight, up_weight, down_weight, norm_one, norm_two, cotangent, adapter_state, first_moment, second_moment, rate, step):
    weights = tuple((weight_matrix.astype(jnp.float32) for weight_matrix in (input_weight, conv_weight, output_weight, gate_weight, up_weight, down_weight, norm_one, norm_two)))

    def one_sequence(totals, input_rows):
        seq_tokens, seq_ids, seq_cot, chosen_index = input_rows
        chosen = adapter_state[chosen_index]

        def forward_fn(rows_in, adapter):
            return block_forward(rows_in, adapter, weights, seq_ids)
        result, pullback = jax.vjp(forward_fn, seq_tokens.astype(jnp.float32), chosen)
        grad_tokens, grad_adapter = pullback(seq_cot.astype(jnp.float32))
        totals = totals.at[chosen_index].add(grad_adapter)
        return (totals, (result.astype(jnp.bfloat16), grad_tokens.astype(jnp.bfloat16)))
    totals, (output, input_grad) = lax.scan(one_sequence, jnp.zeros((ADAPTERS, PACK), jnp.float32), (tokens, segment_ids, cotangent, adapter_ids))
    decay_power = jnp.power(jnp.float32(0.5), step[0].astype(jnp.float32))
    correction = 1.0 - decay_power
    moment_one = 0.5 * first_moment + 0.5 * totals
    moment_two = 0.5 * second_moment + 0.5 * totals * totals
    updated = adapter_state - rate[0] * (moment_one / correction) / (jnp.sqrt(moment_two / correction) + 1e-08)
    return (output, input_grad, updated, updated.astype(jnp.bfloat16))
```

```python
import functools

import jax
import jax.numpy as jnp
from jax import lax
from jax.experimental import pallas as pl
from jax.experimental.pallas import tpu as pltpu
from jax.sharding import PartitionSpec as P

D = 1024
FF = 4608
RANK = 16
EPS = 1e-05
FB = 512
MIB = 2**20

f32 = jnp.float32
bf16 = jnp.bfloat16
MESH = pl.DeviceIdType.MESH

WIRE = RANK * 0 + 23040
PACKROWS = 2880
A_IN, B_IN, A_OUT, B_OUT, A_GATE, B_GATE, A_UP, B_UP, A_DOWN, B_DOWN = (
    0, 1024, 4096, 5120, 6144, 7168, 11776, 12800, 17408, 22016,
)
B_PARTS = ((B_IN, 3 * D), (B_OUT, D), (B_GATE, FF), (B_UP, FF), (B_DOWN, D))
A_PARTS = ((A_IN, D), (A_OUT, D), (A_GATE, D), (A_UP, D), (A_DOWN, FF))
A_CHUNKS = tuple(
    (first + start, min(1024, height - start))
    for first, height in A_PARTS
    for start in range(0, height, 1024)
)


def dot(a, b):
    return jnp.dot(a, b, preferred_element_type=f32)


def dot_nt(a, b):
    return lax.dot_general(a, b, (((1,), (1,)), ((), ())), preferred_element_type=f32)


def dot_tn(a, b):
    return lax.dot_general(a, b, (((0,), (0,)), ((), ())), preferred_element_type=f32)


def shuffle_matrix():
    row = lax.broadcasted_iota(jnp.int32, (1024, 1024), 0)
    col = lax.broadcasted_iota(jnp.int32, (1024, 1024), 1)
    return jnp.where(col == 8 * (row % 128) + row // 128, 1.0, 0.0).astype(bf16)


def table_kernel(na, st_ref, out_ref, lhs_ref):
    for n, (first, count) in enumerate(A_CHUNKS):
        for a in range(na):
            packed = st_ref[pl.ds(na * (first // 8) + a, 128, stride=na), :]
            turned = packed.T.astype(bf16)
            row = (n * na + a) * RANK
            for c in range(8):
                lhs_ref[row : row + RANK, 128 * c : 128 * c + 128] = turned[RANK * c : RANK * c + RANK, :]
    full = dot(lhs_ref[...], shuffle_matrix()).astype(bf16)
    for n, (first, count) in enumerate(A_CHUNKS):
        for a in range(na):
            row = (n * na + a) * RANK
            out_ref[a * RANK : (a + 1) * RANK, first : first + count] = full[row : row + RANK, :count]
    for first, breadth in B_PARTS:
        blocks = breadth // 128
        for a in range(na):
            for c in range(blocks):
                part = st_ref[pl.ds(na * (first // 8 + c) + a, RANK, stride=na * blocks), :]
                out_ref[a * RANK : (a + 1) * RANK, first + 128 * c : first + 128 * c + 128] = part.astype(bf16)


def build_table(state_native, na):
    return pl.pallas_call(
        functools.partial(table_kernel, na),
        out_shape=jax.ShapeDtypeStruct((na * RANK, WIRE), bf16),
        scratch_shapes=[pltpu.VMEM((len(A_CHUNKS) * na * RANK, 1024), bf16)],
        compiler_params=pltpu.CompilerParams(vmem_limit_bytes=40 * MIB),
    )(state_native)


def adam_kernel(na, scal_ref, gw_ref, st_ref, m_ref, v_ref, new_ref, tab_ref, lhs_ref, gn_ref):
    for n, (first, count) in enumerate(A_CHUNKS):
        for a in range(na):
            row = (n * na + a) * RANK
            lhs_ref[row : row + RANK, :] = gw_ref[a * RANK : (a + 1) * RANK, first : first + 1024].astype(bf16)
    full = dot_nt(lhs_ref[...], shuffle_matrix())
    for n, (first, count) in enumerate(A_CHUNKS):
        for a in range(na):
            row = (n * na + a) * RANK
            turned = jnp.concatenate(
                [full[row : row + RANK, 128 * c : 128 * c + 128] for c in range(8)], axis=0
            )
            gn_ref[pl.ds(na * (first // 8) + a, count // 8, stride=na), :] = turned.T[: count // 8]
    for first, breadth in B_PARTS:
        blocks = breadth // 128
        for a in range(na):
            for c in range(blocks):
                gn_ref[pl.ds(na * (first // 8 + c) + a, RANK, stride=na * blocks), :] = gw_ref[
                    a * RANK : (a + 1) * RANK, first + 128 * c : first + 128 * c + 128
                ].astype(f32)
    rate = scal_ref[0]
    inv = scal_ref[1]
    grad = gn_ref[...]
    one = 0.5 * m_ref[...] + 0.5 * grad
    two = 0.5 * v_ref[...] + 0.5 * grad * grad
    new = st_ref[...] - rate * (one * inv) / (jnp.sqrt(two * inv) + 1e-08)
    new_ref[...] = new
    tab_ref[...] = new.astype(bf16)


def adam(scal, gw, st, m, v, na):
    rows = na * PACKROWS
    vm = pl.BlockSpec(memory_space=pltpu.VMEM)
    return pl.pallas_call(
        functools.partial(adam_kernel, na),
        in_specs=[pl.BlockSpec(memory_space=pltpu.SMEM)] + [vm] * 4,
        out_shape=(jax.ShapeDtypeStruct((rows, 128), f32), jax.ShapeDtypeStruct((rows, 128), bf16)),
        scratch_shapes=[
            pltpu.VMEM((len(A_CHUNKS) * na * RANK, 1024), bf16),
            pltpu.VMEM((rows, 128), f32),
        ],
        compiler_params=pltpu.CompilerParams(vmem_limit_bytes=56 * MIB),
    )(scal, gw, st, m, v)


def greet(seq, count):
    barrier = pltpu.get_barrier_semaphore()

    @pl.when(seq > 0)
    def _():
        pl.semaphore_signal(barrier, inc=1, device_id={"seq": seq - 1}, device_id_type=MESH)

    @pl.when(seq < count - 1)
    def _():
        pl.semaphore_signal(barrier, inc=1, device_id={"seq": seq + 1}, device_id_type=MESH)

    before = (seq + count - 1) // count
    after = (2 * count - 2 - seq) // count
    pl.semaphore_wait(barrier, before + after)


def row_mask(mask_ref, seqs, length):
    return jnp.concatenate(
        [jnp.broadcast_to(mask_ref[s : s + 1, :], (length, 128)) for s in range(seqs)], axis=0
    )


def norm(values, gain):
    inverse = lax.rsqrt(jnp.mean(values * values, axis=-1, keepdims=True) + EPS)
    return values * inverse * gain, inverse


def pre_kernel(
    seqs, length, count,
    tok_ref, ids_ref, mask_ref, tb_ref, wi_ref, cw_ref, wo_ref, n1_ref, n2_ref, cot_ref,
    u1_ref, mi_ref, b_ref, c_ref, x_ref, conv_ref, same_ref, gated_ref, mo_ref, h1_ref, u2_ref, mg_ref, mu_ref, gd_ref,
    ext_ref, out_ref, in_ref, send_sem, recv_sem,
):
    seq = lax.axis_index("seq")
    greet(seq, count)
    mask = row_mask(mask_ref, seqs, length)
    twice = 2.0 * mask
    tokens = tok_ref[...].astype(f32)
    u1 = norm(tokens, n1_ref[...])[0].astype(bf16)
    u1_ref[...] = u1
    mid = (dot_nt(u1, tb_ref[:, A_IN : A_IN + D]).astype(bf16).astype(f32) * twice).astype(bf16)
    mi_ref[...] = mid
    for third, to_ref in ((0, b_ref), (2, x_ref)):
        for k in range(2):
            col = third * D + 512 * k
            to_ref[:, 512 * k : 512 * k + 512] = dot(u1, wi_ref[:, col : col + 512]) + dot(
                mid, tb_ref[:, B_IN + col : B_IN + col + 512]
            )
    width = D + 128
    for s in range(seqs):
        rows = pl.ds(s * length, length)
        ext_ref[s, 0:8, :] = jnp.zeros((8, width), f32)
        ext_ref[s, 8:, :D] = b_ref[rows, :] * x_ref[rows, :]
        ext_ref[s, 8:, D:] = jnp.broadcast_to(ids_ref[s : s + 1, :], (length, 128)).T
        out_ref[2 * s : 2 * s + 2, :] = ext_ref[s, length + 6 : length + 8, :]
    along = pltpu.make_async_remote_copy(
        src_ref=out_ref, dst_ref=in_ref, send_sem=send_sem, recv_sem=recv_sem,
        device_id={"seq": seq + 1}, device_id_type=MESH,
    )

    @pl.when(seq < count - 1)
    def _():
        along.start()

    for k in range(2):
        col = D + 512 * k
        c_ref[:, 512 * k : 512 * k + 512] = dot(u1, wi_ref[:, col : col + 512]) + dot(
            mid, tb_ref[:, B_IN + col : B_IN + col + 512]
        )
    gd_ref[...] = (dot_nt(cot_ref[...], tb_ref[:, B_DOWN : B_DOWN + D]) * twice).astype(bf16)

    @pl.when(seq < count - 1)
    def _():
        along.wait_send()

    @pl.when(seq > 0)
    def _():
        along.wait_recv()
        for s in range(seqs):
            ext_ref[s, 6:8, :] = in_ref[2 * s : 2 * s + 2, :]

    for s in range(seqs):
        rows = pl.ds(s * length, length)
        now_ids = ext_ref[s, 8:, D:]
        same1 = jnp.where(ext_ref[s, pl.ds(7, length), D:] == now_ids, 1.0, 0.0)
        same2 = jnp.where(ext_ref[s, pl.ds(6, length), D:] == now_ids, 1.0, 0.0)
        same_ref[0, rows, :] = same1
        same_ref[1, rows, :] = same2
        conv = (
            cw_ref[2:3, :] * ext_ref[s, 8:, :D]
            + cw_ref[1:2, :] * same1[:, :1] * ext_ref[s, pl.ds(7, length), :D]
            + cw_ref[0:1, :] * same2[:, :1] * ext_ref[s, pl.ds(6, length), :D]
        )
        conv_ref[rows, :] = conv
        gated_ref[rows, :] = (c_ref[rows, :] * conv).astype(bf16)
    gated = gated_ref[...]
    mid_out = (dot_nt(gated, tb_ref[:, A_OUT : A_OUT + D]).astype(bf16).astype(f32) * twice).astype(bf16)
    mo_ref[...] = mid_out
    for k in range(2):
        cols = slice(512 * k, 512 * k + 512)
        h1_ref[:, cols] = (
            tok_ref[:, cols].astype(f32)
            + dot(gated, wo_ref[:, cols])
            + dot(mid_out, tb_ref[:, B_OUT + 512 * k : B_OUT + 512 * k + 512])
        )
    u2 = norm(h1_ref[...], n2_ref[...])[0].astype(bf16)
    u2_ref[...] = u2
    mg_ref[...] = (dot_nt(u2, tb_ref[:, A_GATE : A_GATE + D]).astype(bf16).astype(f32) * twice).astype(bf16)
    mu_ref[...] = (dot_nt(u2, tb_ref[:, A_UP : A_UP + D]).astype(bf16).astype(f32) * twice).astype(bf16)


def pre(seqs, length, count, *args):
    rows = seqs * length
    sd = jax.ShapeDtypeStruct
    width = D + 128
    vm = pl.BlockSpec(memory_space=pltpu.VMEM)
    wide = sd((rows, D), f32)
    half = sd((rows, D), bf16)
    thin = sd((rows, 128), bf16)
    return pl.pallas_call(
        functools.partial(pre_kernel, seqs, length, count),
        in_specs=[vm] * 10,
        out_specs=[vm] * 14,
        out_shape=[half, thin, wide, wide, wide, wide, sd((2, rows, 128), f32), half, thin, wide, half, thin, thin, thin],
        scratch_shapes=[
            pltpu.VMEM((seqs, length + 8, width), f32),
            pltpu.VMEM((2 * seqs, width), f32),
            pltpu.VMEM((2 * seqs, width), f32),
            pltpu.SemaphoreType.DMA,
            pltpu.SemaphoreType.DMA,
        ],
        compiler_params=pltpu.CompilerParams(vmem_limit_bytes=60 * MIB, collective_id=0, has_side_effects=True),
    )(*args)


def ffn_kernel(
    seqs, length,
    u_ref, cot_ref, mg_ref, mu_ref, gd_ref, mask_ref, h1_ref, wg_ref, wu_ref, wd_ref, bg_ref, bu_ref, ad_ref, ag_ref, au_ref, bd_ref,
    out_ref, gn_ref, dbg_ref, dbu_ref, dad_ref, dag_ref, dau_ref, dbd_ref,
    acc_ref, dmid_ref, gmg_ref, gmu_ref,
):
    j = pl.program_id(0)

    @pl.when(j == 0)
    def _():
        for ref in (acc_ref, gn_ref, dmid_ref, gmg_ref, gmu_ref):
            ref[...] = jnp.zeros_like(ref)

    u = u_ref[...]
    gate = dot(u, wg_ref[...]) + dot(mg_ref[...], bg_ref[...])
    up = dot(u, wu_ref[...]) + dot(mu_ref[...], bu_ref[...])
    back = dot_nt(cot_ref[...], wd_ref[...]) + dot(gd_ref[...], ad_ref[...])
    sig = jax.nn.sigmoid(gate)
    silu = gate * sig
    hidden = (silu * up).astype(bf16)
    grad_gate = (back * up * sig * (1.0 + gate * (1.0 - sig))).astype(bf16)
    grad_up = (back * silu).astype(bf16)
    acc_ref[...] += dot(hidden, wd_ref[...])
    gn_ref[...] += dot_nt(grad_gate, wg_ref[...]) + dot_nt(grad_up, wu_ref[...])
    dmid_ref[...] += dot_nt(hidden, ad_ref[...])
    gmg_ref[...] += dot_nt(grad_gate, bg_ref[...])
    gmu_ref[...] += dot_nt(grad_up, bu_ref[...])
    dbg_ref[...] = dot_tn(mg_ref[...], grad_gate).astype(bf16)
    dbu_ref[...] = dot_tn(mu_ref[...], grad_up).astype(bf16)
    dad_ref[...] = dot_tn(gd_ref[...], hidden).astype(bf16)

    @pl.when(j == pl.num_programs(0) - 1)
    def _():
        twice = 2.0 * row_mask(mask_ref, seqs, length)
        dmid = (dmid_ref[...].astype(bf16).astype(f32) * twice).astype(bf16)
        out_ref[...] = (h1_ref[...] + acc_ref[...] + dot(dmid, bd_ref[...])).astype(bf16)
        dbd_ref[...] = dot_tn(dmid, cot_ref[...]).astype(bf16)
        gm_gate = (gmg_ref[...] * twice).astype(bf16)
        gm_up = (gmu_ref[...] * twice).astype(bf16)
        gn_ref[...] += dot(gm_gate, ag_ref[...]) + dot(gm_up, au_ref[...])
        dag_ref[...] = dot_tn(gm_gate, u_ref[...]).astype(bf16)
        dau_ref[...] = dot_tn(gm_up, u_ref[...]).astype(bf16)


def ffn(seqs, length, u2, cot, mg, mu, gd, mask, h1, wg, wu, wd, table):
    rows = seqs * length
    sd = jax.ShapeDtypeStruct
    whole = lambda s: pl.BlockSpec(s, lambda j: (0, 0))
    col = lambda h: pl.BlockSpec((h, FB), lambda j: (0, j))
    tab = lambda first: pl.BlockSpec((128, FB), lambda j: (0, first // FB + j))
    fixed = lambda first: pl.BlockSpec((128, D), lambda j: (0, 0))
    cut = lambda first: lax.slice_in_dim(table, first, first + D, axis=1)
    return pl.pallas_call(
        functools.partial(ffn_kernel, seqs, length),
        grid=(FF // FB,),
        in_specs=[whole((rows, D)), whole((rows, D)), whole((rows, 128)), whole((rows, 128)), whole((rows, 128)),
                  whole(mask.shape), whole((rows, D)),
                  col(D), col(D), pl.BlockSpec((FB, D), lambda j: (j, 0)),
                  tab(B_GATE), tab(B_UP), tab(A_DOWN), whole((128, D)), whole((128, D)), whole((128, D))],
        out_specs=[whole((rows, D)), whole((rows, D)), col(128), col(128), col(128),
                   whole((128, D)), whole((128, D)), whole((128, D))],
        out_shape=[sd((rows, D), bf16), sd((rows, D), f32)] + [sd((128, FF), bf16)] * 3 + [sd((128, D), bf16)] * 3,
        scratch_shapes=[pltpu.VMEM((rows, D), f32)] + [pltpu.VMEM((rows, 128), f32)] * 3,
        compiler_params=pltpu.CompilerParams(vmem_limit_bytes=60 * MIB),
    )(u2, cot, mg, mu, gd, mask, h1, wg, wu, wd, table, table, table, cut(A_GATE), cut(A_UP), cut(B_DOWN))


def post_kernel(
    seqs, length, count,
    tok_ref, cot_ref, mask_ref, h1_ref, gn_ref, gated_ref, mo_ref, b_ref, c_ref, x_ref, conv_ref, same_ref, u1_ref, mi_ref,
    tb_ref, wi_ref, cw_ref, wo_ref, n1_ref, n2_ref,
    ig_ref, dai_ref, dbi_ref, dao_ref, dbo_ref,
    gh_ref, gb_ref, gg_ref, gc_ref, gp_ref, one_ref, two_ref, out_ref, in_ref, send_sem, recv_sem,
):
    seq = lax.axis_index("seq")
    greet(seq, count)
    twice = 2.0 * row_mask(mask_ref, seqs, length)
    h1 = h1_ref[...]
    inv2 = norm(h1, n2_ref[...])[1]
    e2 = gn_ref[...] * n2_ref[...]
    gh = cot_ref[...].astype(f32) + inv2 * e2 - h1 * (inv2 * inv2 * inv2 * jnp.mean(h1 * e2, axis=-1, keepdims=True))
    gh_ref[...] = gh
    gb = gh.astype(bf16)
    gb_ref[...] = gb
    gm_out = (dot_nt(gb, tb_ref[:, B_OUT : B_OUT + D]) * twice).astype(bf16)
    for k in range(2):
        cols = slice(512 * k, 512 * k + 512)
        gg_ref[:, cols] = dot_nt(gb, wo_ref[cols, :]) + dot(gm_out, tb_ref[:, A_OUT + 512 * k : A_OUT + 512 * k + 512])
    for s in range(seqs):
        rows = pl.ds(s * length, length)
        gg = gg_ref[rows, :]
        gp_ref[rows, D : 2 * D] = (gg * conv_ref[rows, :]).astype(bf16)
        gconv = gg * c_ref[rows, :]
        gc_ref[rows, :] = gconv
        one_ref[s, 0:length, :] = cw_ref[1:2, :] * same_ref[0, rows, 0:1] * gconv
        two_ref[s, 0:length, :] = cw_ref[0:1, :] * same_ref[1, rows, 0:1] * gconv
        one_ref[s, length:, :] = jnp.zeros((8, D), f32)
        two_ref[s, length:, :] = jnp.zeros((8, D), f32)
        out_ref[2 * s : 2 * s + 1, :] = two_ref[s, 0:1, :]
        out_ref[2 * s + 1 : 2 * s + 2, :] = two_ref[s, 1:2, :] + one_ref[s, 0:1, :]
    along = pltpu.make_async_remote_copy(
        src_ref=out_ref, dst_ref=in_ref, send_sem=send_sem, recv_sem=recv_sem,
        device_id={"seq": seq - 1}, device_id_type=MESH,
    )

    @pl.when(seq > 0)
    def _():
        along.start()

    dbo_ref[...] = dot_tn(mo_ref[...], gb).astype(bf16)
    dao_ref[...] = dot_tn(gm_out, gated_ref[...]).astype(bf16)

    @pl.when(seq > 0)
    def _():
        along.wait_send()

    @pl.when(seq < count - 1)
    def _():
        along.wait_recv()
        for s in range(seqs):
            two_ref[s, length : length + 2, :] = in_ref[2 * s : 2 * s + 2, :]

    for s in range(seqs):
        rows = pl.ds(s * length, length)
        gmix = (
            cw_ref[2:3, :] * gc_ref[rows, :]
            + one_ref[s, pl.ds(1, length), :]
            + two_ref[s, pl.ds(2, length), :]
        )
        gp_ref[rows, 0:D] = (gmix * x_ref[rows, :]).astype(bf16)
        gp_ref[rows, 2 * D :] = (gmix * b_ref[rows, :]).astype(bf16)
    gm_in = (dot_nt(gp_ref[...], tb_ref[:, B_IN : B_IN + 3 * D]) * twice).astype(bf16)
    for k in range(2):
        cols = slice(512 * k, 512 * k + 512)
        gg_ref[:, cols] = dot_nt(gp_ref[...], wi_ref[cols, :]) + dot(gm_in, tb_ref[:, A_IN + 512 * k : A_IN + 512 * k + 512])
    for k in range(6):
        cols = slice(512 * k, 512 * k + 512)
        dbi_ref[:, cols] = dot_tn(mi_ref[...], gp_ref[:, cols]).astype(bf16)
    dai_ref[...] = dot_tn(gm_in, u1_ref[...]).astype(bf16)
    tokens = tok_ref[...].astype(f32)
    inv1 = norm(tokens, n1_ref[...])[1]
    e1 = gg_ref[...] * n1_ref[...]
    ig_ref[...] = (
        gh_ref[...] + inv1 * e1 - tokens * (inv1 * inv1 * inv1 * jnp.mean(tokens * e1, axis=-1, keepdims=True))
    ).astype(bf16)


def post(seqs, length, count, *args):
    rows = seqs * length
    sd = jax.ShapeDtypeStruct
    vm = pl.BlockSpec(memory_space=pltpu.VMEM)
    return pl.pallas_call(
        functools.partial(post_kernel, seqs, length, count),
        in_specs=[vm] * 20,
        out_specs=[vm] * 5,
        out_shape=[sd((rows, D), bf16), sd((128, D), bf16), sd((128, 3 * D), bf16), sd((128, D), bf16), sd((128, D), bf16)],
        scratch_shapes=[
            pltpu.VMEM((rows, D), f32),
            pltpu.VMEM((rows, D), bf16),
            pltpu.VMEM((rows, D), f32),
            pltpu.VMEM((rows, D), f32),
            pltpu.VMEM((rows, 3 * D), bf16),
            pltpu.VMEM((seqs, length + 8, D), f32),
            pltpu.VMEM((seqs, length + 8, D), f32),
            pltpu.VMEM((2 * seqs, D), f32),
            pltpu.VMEM((2 * seqs, D), f32),
            pltpu.SemaphoreType.DMA,
            pltpu.SemaphoreType.DMA,
        ],
        compiler_params=pltpu.CompilerParams(vmem_limit_bytes=62 * MIB, collective_id=1, has_side_effects=True),
    )(*args)


def per_device(
    tokens, segment_ids, adapter_ids, input_weight, conv_weight, output_weight, gate_weight, up_weight, down_weight,
    norm_one, norm_two, cotangent, adapter_state, first_moment, second_moment, rate, step,
):
    seqs, length, _ = tokens.shape
    na = adapter_state.shape[0]
    groups = lax.axis_size("grp")
    count = lax.axis_size("seq")
    native = lambda x: x.reshape(na, PACKROWS, 128).swapaxes(0, 1).reshape(na * PACKROWS, 128)
    st, m, v = native(adapter_state), native(first_moment), native(second_moment)
    own = build_table(st, na)
    table = lax.all_gather(own, "grp", axis=0, tiled=True)
    adapters = na * groups
    mask = (adapter_ids[:, None] == jnp.arange(adapters * RANK, dtype=jnp.int32)[None, :] // RANK).astype(f32)
    ids = segment_ids.astype(f32)
    rows = seqs * length
    tok2, cot2 = tokens.reshape(rows, D), cotangent.reshape(rows, D)
    n1, n2 = norm_one.reshape(1, D), norm_two.reshape(1, D)
    u1, mi, b, c, x, conv, same, gated, mo, h1, u2, mg, mu, gd = pre(
        seqs, length, count, tok2, ids, mask, table, input_weight, conv_weight, output_weight, n1, n2, cot2
    )
    out, gn, dbg, dbu, dad, dag, dau, dbd = ffn(
        seqs, length, u2, cot2, mg, mu, gd, mask, h1, gate_weight, up_weight, down_weight, table
    )
    ig, dai, dbi, dao, dbo = post(
        seqs, length, count, tok2, cot2, mask, h1, gn, gated, mo, b, c, x, conv, same, u1, mi,
        table, input_weight, conv_weight, output_weight, n1, n2,
    )
    grads = jnp.concatenate([dai, dbi, dao, dbo, dag, dbg, dau, dbu, dad, dbd], axis=1).astype(f32)
    owned = lax.psum(lax.psum_scatter(grads, "grp", scatter_dimension=0, tiled=True), "seq")
    correction = 1.0 - jnp.power(jnp.float32(0.5), step[0].astype(f32))
    scal = jnp.stack([rate[0], 1.0 / correction])
    new, tab = adam(scal, owned, st, m, v, na)
    every = lax.all_gather(tab, "grp", axis=0, tiled=False)
    every = every.reshape(groups, PACKROWS, na, 128).transpose(0, 2, 1, 3).reshape(adapters, PACKROWS * 128)
    new = new.reshape(PACKROWS, na, 128).swapaxes(0, 1).reshape(na, PACKROWS * 128)
    return out.reshape(tokens.shape), ig.reshape(tokens.shape), new, every


def solution(mesh):
    rows = P("grp", "seq", None)
    own = P("grp", None)
    return jax.shard_map(
        per_device,
        mesh=mesh,
        in_specs=(rows, P("grp", "seq"), P("grp")) + (P(),) * 8 + (rows, own, own, own, P(), P()),
        out_specs=(rows, rows, own, P()),
        check_vma=False,
    )
```

```python
import functools

import jax
import jax.numpy as jnp
from jax import lax
from jax.experimental import pallas as pl
from jax.experimental.pallas import tpu as pltpu
from jax.sharding import PartitionSpec as P

D = 1024
FF = 4608
RANK = 16
EPS = 1e-05
FB = 512
MIB = 2**20

f32 = jnp.float32
bf16 = jnp.bfloat16
MESH = pl.DeviceIdType.MESH

WIRE = RANK * 0 + 23040
PACKROWS = 2880
A_IN, B_IN, A_OUT, B_OUT, A_GATE, B_GATE, A_UP, B_UP, A_DOWN, B_DOWN = (
    0, 1024, 4096, 5120, 6144, 7168, 11776, 12800, 17408, 22016,
)
B_PARTS = ((B_IN, 3 * D), (B_OUT, D), (B_GATE, FF), (B_UP, FF), (B_DOWN, D))
A_PARTS = ((A_IN, D), (A_OUT, D), (A_GATE, D), (A_UP, D), (A_DOWN, FF))
A_CHUNKS = tuple(
    (first + start, min(1024, height - start))
    for first, height in A_PARTS
    for start in range(0, height, 1024)
)


def dot(a, b):
    return jnp.dot(a, b, preferred_element_type=f32)


def dot_nt(a, b):
    return lax.dot_general(a, b, (((1,), (1,)), ((), ())), preferred_element_type=f32)


def dot_tn(a, b):
    return lax.dot_general(a, b, (((0,), (0,)), ((), ())), preferred_element_type=f32)


def shuffle_matrix():
    row = lax.broadcasted_iota(jnp.int32, (1024, 1024), 0)
    col = lax.broadcasted_iota(jnp.int32, (1024, 1024), 1)
    return jnp.where(col == 8 * (row % 128) + row // 128, 1.0, 0.0).astype(bf16)


def table_kernel(na, st_ref, out_ref, lhs_ref):
    for n, (first, count) in enumerate(A_CHUNKS):
        for a in range(na):
            packed = st_ref[pl.ds(na * (first // 8) + a, 128, stride=na), :]
            turned = packed.T.astype(bf16)
            row = (n * na + a) * RANK
            for c in range(8):
                lhs_ref[row : row + RANK, 128 * c : 128 * c + 128] = turned[RANK * c : RANK * c + RANK, :]
    full = dot(lhs_ref[...], shuffle_matrix()).astype(bf16)
    for n, (first, count) in enumerate(A_CHUNKS):
        for a in range(na):
            row = (n * na + a) * RANK
            out_ref[a * RANK : (a + 1) * RANK, first : first + count] = full[row : row + RANK, :count]
    for first, breadth in B_PARTS:
        blocks = breadth // 128
        for a in range(na):
            for c in range(blocks):
                part = st_ref[pl.ds(na * (first // 8 + c) + a, RANK, stride=na * blocks), :]
                out_ref[a * RANK : (a + 1) * RANK, first + 128 * c : first + 128 * c + 128] = part.astype(bf16)


def build_table(state_native, na):
    return pl.pallas_call(
        functools.partial(table_kernel, na),
        out_shape=jax.ShapeDtypeStruct((na * RANK, WIRE), bf16),
        scratch_shapes=[pltpu.VMEM((len(A_CHUNKS) * na * RANK, 1024), bf16)],
        compiler_params=pltpu.CompilerParams(vmem_limit_bytes=40 * MIB),
    )(state_native)


def adam_kernel(na, scal_ref, gw_ref, st_ref, m_ref, v_ref, new_ref, tab_ref, lhs_ref, gn_ref):
    for n, (first, count) in enumerate(A_CHUNKS):
        for a in range(na):
            row = (n * na + a) * RANK
            lhs_ref[row : row + RANK, :] = gw_ref[a * RANK : (a + 1) * RANK, first : first + 1024].astype(bf16)
    full = dot_nt(lhs_ref[...], shuffle_matrix())
    for n, (first, count) in enumerate(A_CHUNKS):
        for a in range(na):
            row = (n * na + a) * RANK
            turned = jnp.concatenate(
                [full[row : row + RANK, 128 * c : 128 * c + 128] for c in range(8)], axis=0
            )
            gn_ref[pl.ds(na * (first // 8) + a, count // 8, stride=na), :] = turned.T[: count // 8]
    for first, breadth in B_PARTS:
        blocks = breadth // 128
        for a in range(na):
            for c in range(blocks):
                gn_ref[pl.ds(na * (first // 8 + c) + a, RANK, stride=na * blocks), :] = gw_ref[
                    a * RANK : (a + 1) * RANK, first + 128 * c : first + 128 * c + 128
                ].astype(f32)
    rate = scal_ref[0]
    inv = scal_ref[1]
    grad = gn_ref[...]
    one = 0.5 * m_ref[...] + 0.5 * grad
    two = 0.5 * v_ref[...] + 0.5 * grad * grad
    new = st_ref[...] - rate * (one * inv) / (jnp.sqrt(two * inv) + 1e-08)
    new_ref[...] = new
    tab_ref[...] = new.astype(bf16)


def adam(scal, gw, st, m, v, na):
    rows = na * PACKROWS
    vm = pl.BlockSpec(memory_space=pltpu.VMEM)
    return pl.pallas_call(
        functools.partial(adam_kernel, na),
        in_specs=[pl.BlockSpec(memory_space=pltpu.SMEM)] + [vm] * 4,
        out_shape=(jax.ShapeDtypeStruct((rows, 128), f32), jax.ShapeDtypeStruct((rows, 128), bf16)),
        scratch_shapes=[
            pltpu.VMEM((len(A_CHUNKS) * na * RANK, 1024), bf16),
            pltpu.VMEM((rows, 128), f32),
        ],
        compiler_params=pltpu.CompilerParams(vmem_limit_bytes=56 * MIB),
    )(scal, gw, st, m, v)


def greet(seq, count):
    barrier = pltpu.get_barrier_semaphore()

    @pl.when(seq > 0)
    def _():
        pl.semaphore_signal(barrier, inc=1, device_id={"seq": seq - 1}, device_id_type=MESH)

    @pl.when(seq < count - 1)
    def _():
        pl.semaphore_signal(barrier, inc=1, device_id={"seq": seq + 1}, device_id_type=MESH)

    before = (seq + count - 1) // count
    after = (2 * count - 2 - seq) // count
    pl.semaphore_wait(barrier, before + after)


def row_mask(mask_ref, seqs, length):
    return jnp.concatenate(
        [jnp.broadcast_to(mask_ref[s : s + 1, :], (length, 128)) for s in range(seqs)], axis=0
    )


def norm(values, gain):
    inverse = lax.rsqrt(jnp.mean(values * values, axis=-1, keepdims=True) + EPS)
    return values * inverse * gain, inverse


def pre_kernel(
    seqs, length, count,
    tok_ref, ids_ref, mask_ref, tb_ref, wi_ref, cw_ref, wo_ref, n1_ref, n2_ref, cot_ref,
    u1_ref, mi_ref, b_ref, c_ref, x_ref, conv_ref, same_ref, gated_ref, mo_ref, h1_ref, u2_ref, mg_ref, mu_ref, gd_ref,
    ext_ref, out_ref, in_ref, send_sem, recv_sem,
):
    seq = lax.axis_index("seq")
    greet(seq, count)
    mask = row_mask(mask_ref, seqs, length)
    twice = 2.0 * mask
    tokens = tok_ref[...].astype(f32)
    u1 = norm(tokens, n1_ref[...])[0].astype(bf16)
    u1_ref[...] = u1
    mid = (dot_nt(u1, tb_ref[:, A_IN : A_IN + D]).astype(bf16).astype(f32) * twice).astype(bf16)
    mi_ref[...] = mid
    for third, to_ref in ((0, b_ref), (2, x_ref)):
        for k in range(2):
            col = third * D + 512 * k
            to_ref[:, 512 * k : 512 * k + 512] = dot(u1, wi_ref[:, col : col + 512]) + dot(
                mid, tb_ref[:, B_IN + col : B_IN + col + 512]
            )
    width = D + 128
    for s in range(seqs):
        rows = pl.ds(s * length, length)
        ext_ref[s, 0:8, :] = jnp.zeros((8, width), f32)
        ext_ref[s, 8:, :D] = b_ref[rows, :] * x_ref[rows, :]
        ext_ref[s, 8:, D:] = jnp.broadcast_to(ids_ref[s : s + 1, :], (length, 128)).T
        out_ref[2 * s : 2 * s + 2, :] = ext_ref[s, length + 6 : length + 8, :]
    along = pltpu.make_async_remote_copy(
        src_ref=out_ref, dst_ref=in_ref, send_sem=send_sem, recv_sem=recv_sem,
        device_id={"seq": seq + 1}, device_id_type=MESH,
    )

    @pl.when(seq < count - 1)
    def _():
        along.start()

    for k in range(2):
        col = D + 512 * k
        c_ref[:, 512 * k : 512 * k + 512] = dot(u1, wi_ref[:, col : col + 512]) + dot(
            mid, tb_ref[:, B_IN + col : B_IN + col + 512]
        )
    gd_ref[...] = (dot_nt(cot_ref[...], tb_ref[:, B_DOWN : B_DOWN + D]) * twice).astype(bf16)

    @pl.when(seq < count - 1)
    def _():
        along.wait_send()

    @pl.when(seq > 0)
    def _():
        along.wait_recv()
        for s in range(seqs):
            ext_ref[s, 6:8, :] = in_ref[2 * s : 2 * s + 2, :]

    for s in range(seqs):
        rows = pl.ds(s * length, length)
        now_ids = ext_ref[s, 8:, D:]
        same1 = jnp.where(ext_ref[s, pl.ds(7, length), D:] == now_ids, 1.0, 0.0)
        same2 = jnp.where(ext_ref[s, pl.ds(6, length), D:] == now_ids, 1.0, 0.0)
        same_ref[0, rows, :] = same1
        same_ref[1, rows, :] = same2
        conv = (
            cw_ref[2:3, :] * ext_ref[s, 8:, :D]
            + cw_ref[1:2, :] * same1[:, :1] * ext_ref[s, pl.ds(7, length), :D]
            + cw_ref[0:1, :] * same2[:, :1] * ext_ref[s, pl.ds(6, length), :D]
        )
        conv_ref[rows, :] = conv
        gated_ref[rows, :] = (c_ref[rows, :] * conv).astype(bf16)
    gated = gated_ref[...]
    mid_out = (dot_nt(gated, tb_ref[:, A_OUT : A_OUT + D]).astype(bf16).astype(f32) * twice).astype(bf16)
    mo_ref[...] = mid_out
    for k in range(2):
        cols = slice(512 * k, 512 * k + 512)
        h1_ref[:, cols] = (
            tok_ref[:, cols].astype(f32)
            + dot(gated, wo_ref[:, cols])
            + dot(mid_out, tb_ref[:, B_OUT + 512 * k : B_OUT + 512 * k + 512])
        )
    u2 = norm(h1_ref[...], n2_ref[...])[0].astype(bf16)
    u2_ref[...] = u2
    mg_ref[...] = (dot_nt(u2, tb_ref[:, A_GATE : A_GATE + D]).astype(bf16).astype(f32) * twice).astype(bf16)
    mu_ref[...] = (dot_nt(u2, tb_ref[:, A_UP : A_UP + D]).astype(bf16).astype(f32) * twice).astype(bf16)


def pre(seqs, length, count, *args):
    rows = seqs * length
    sd = jax.ShapeDtypeStruct
    width = D + 128
    vm = pl.BlockSpec(memory_space=pltpu.VMEM)
    wide = sd((rows, D), f32)
    half = sd((rows, D), bf16)
    thin = sd((rows, 128), bf16)
    return pl.pallas_call(
        functools.partial(pre_kernel, seqs, length, count),
        in_specs=[vm] * 10,
        out_specs=[vm] * 14,
        out_shape=[half, thin, wide, wide, wide, wide, sd((2, rows, 128), f32), half, thin, wide, half, thin, thin, thin],
        scratch_shapes=[
            pltpu.VMEM((seqs, length + 8, width), f32),
            pltpu.VMEM((2 * seqs, width), f32),
            pltpu.VMEM((2 * seqs, width), f32),
            pltpu.SemaphoreType.DMA,
            pltpu.SemaphoreType.DMA,
        ],
        compiler_params=pltpu.CompilerParams(vmem_limit_bytes=60 * MIB, collective_id=0, has_side_effects=True),
    )(*args)


def ffn_kernel(
    seqs, length,
    u_ref, cot_ref, mg_ref, mu_ref, gd_ref, mask_ref, h1_ref, wg_ref, wu_ref, wd_ref, bg_ref, bu_ref, ad_ref, ag_ref, au_ref, bd_ref,
    out_ref, gn_ref, dbg_ref, dbu_ref, dad_ref, dag_ref, dau_ref, dbd_ref,
    acc_ref, dmid_ref, gmg_ref, gmu_ref,
):
    j = pl.program_id(0)

    @pl.when(j == 0)
    def _():
        for ref in (acc_ref, gn_ref, dmid_ref, gmg_ref, gmu_ref):
            ref[...] = jnp.zeros_like(ref)

    u = u_ref[...]
    gate = dot(u, wg_ref[...]) + dot(mg_ref[...], bg_ref[...])
    up = dot(u, wu_ref[...]) + dot(mu_ref[...], bu_ref[...])
    back = dot_nt(cot_ref[...], wd_ref[...]) + dot(gd_ref[...], ad_ref[...])
    sig = jax.nn.sigmoid(gate)
    silu = gate * sig
    hidden = (silu * up).astype(bf16)
    grad_gate = (back * up * sig * (1.0 + gate * (1.0 - sig))).astype(bf16)
    grad_up = (back * silu).astype(bf16)
    acc_ref[...] += dot(hidden, wd_ref[...])
    gn_ref[...] += dot_nt(grad_gate, wg_ref[...]) + dot_nt(grad_up, wu_ref[...])
    dmid_ref[...] += dot_nt(hidden, ad_ref[...])
    gmg_ref[...] += dot_nt(grad_gate, bg_ref[...])
    gmu_ref[...] += dot_nt(grad_up, bu_ref[...])
    dbg_ref[...] = dot_tn(mg_ref[...], grad_gate).astype(bf16)
    dbu_ref[...] = dot_tn(mu_ref[...], grad_up).astype(bf16)
    dad_ref[...] = dot_tn(gd_ref[...], hidden).astype(bf16)

    @pl.when(j == pl.num_programs(0) - 1)
    def _():
        twice = 2.0 * row_mask(mask_ref, seqs, length)
        dmid = (dmid_ref[...].astype(bf16).astype(f32) * twice).astype(bf16)
        out_ref[...] = (h1_ref[...] + acc_ref[...] + dot(dmid, bd_ref[...])).astype(bf16)
        dbd_ref[...] = dot_tn(dmid, cot_ref[...]).astype(bf16)
        gm_gate = (gmg_ref[...] * twice).astype(bf16)
        gm_up = (gmu_ref[...] * twice).astype(bf16)
        gn_ref[...] += dot(gm_gate, ag_ref[...]) + dot(gm_up, au_ref[...])
        dag_ref[...] = dot_tn(gm_gate, u_ref[...]).astype(bf16)
        dau_ref[...] = dot_tn(gm_up, u_ref[...]).astype(bf16)


def ffn(seqs, length, u2, cot, mg, mu, gd, mask, h1, wg, wu, wd, table):
    rows = seqs * length
    sd = jax.ShapeDtypeStruct
    whole = lambda s: pl.BlockSpec(s, lambda j: (0, 0))
    col = lambda h: pl.BlockSpec((h, FB), lambda j: (0, j))
    tab = lambda first: pl.BlockSpec((128, FB), lambda j: (0, first // FB + j))
    fixed = lambda first: pl.BlockSpec((128, D), lambda j: (0, 0))
    cut = lambda first: lax.slice_in_dim(table, first, first + D, axis=1)
    return pl.pallas_call(
        functools.partial(ffn_kernel, seqs, length),
        grid=(FF // FB,),
        in_specs=[whole((rows, D)), whole((rows, D)), whole((rows, 128)), whole((rows, 128)), whole((rows, 128)),
                  whole(mask.shape), whole((rows, D)),
                  col(D), col(D), pl.BlockSpec((FB, D), lambda j: (j, 0)),
                  tab(B_GATE), tab(B_UP), tab(A_DOWN), whole((128, D)), whole((128, D)), whole((128, D))],
        out_specs=[whole((rows, D)), whole((rows, D)), col(128), col(128), col(128),
                   whole((128, D)), whole((128, D)), whole((128, D))],
        out_shape=[sd((rows, D), bf16), sd((rows, D), f32)] + [sd((128, FF), bf16)] * 3 + [sd((128, D), bf16)] * 3,
        scratch_shapes=[pltpu.VMEM((rows, D), f32)] + [pltpu.VMEM((rows, 128), f32)] * 3,
        compiler_params=pltpu.CompilerParams(vmem_limit_bytes=60 * MIB),
    )(u2, cot, mg, mu, gd, mask, h1, wg, wu, wd, table, table, table, cut(A_GATE), cut(A_UP), cut(B_DOWN))


def post_kernel(
    seqs, length, count,
    tok_ref, cot_ref, mask_ref, h1_ref, gn_ref, gated_ref, mo_ref, b_ref, c_ref, x_ref, conv_ref, same_ref, u1_ref, mi_ref,
    tb_ref, wi_ref, cw_ref, wo_ref, n1_ref, n2_ref,
    ig_ref, dai_ref, dbi_ref, dao_ref, dbo_ref,
    gh_ref, gb_ref, gg_ref, gc_ref, gp_ref, one_ref, two_ref, out_ref, in_ref, send_sem, recv_sem,
):
    seq = lax.axis_index("seq")
    greet(seq, count)
    twice = 2.0 * row_mask(mask_ref, seqs, length)
    h1 = h1_ref[...]
    inv2 = norm(h1, n2_ref[...])[1]
    e2 = gn_ref[...] * n2_ref[...]
    gh = cot_ref[...].astype(f32) + inv2 * e2 - h1 * (inv2 * inv2 * inv2 * jnp.mean(h1 * e2, axis=-1, keepdims=True))
    gh_ref[...] = gh
    gb = gh.astype(bf16)
    gb_ref[...] = gb
    gm_out = (dot_nt(gb, tb_ref[:, B_OUT : B_OUT + D]) * twice).astype(bf16)
    for k in range(2):
        cols = slice(512 * k, 512 * k + 512)
        gg_ref[:, cols] = dot_nt(gb, wo_ref[cols, :]) + dot(gm_out, tb_ref[:, A_OUT + 512 * k : A_OUT + 512 * k + 512])
    for s in range(seqs):
        rows = pl.ds(s * length, length)
        gg = gg_ref[rows, :]
        gp_ref[rows, D : 2 * D] = (gg * conv_ref[rows, :]).astype(bf16)
        gconv = gg * c_ref[rows, :]
        gc_ref[rows, :] = gconv
        one_ref[s, 0:length, :] = cw_ref[1:2, :] * same_ref[0, rows, 0:1] * gconv
        two_ref[s, 0:length, :] = cw_ref[0:1, :] * same_ref[1, rows, 0:1] * gconv
        one_ref[s, length:, :] = jnp.zeros((8, D), f32)
        two_ref[s, length:, :] = jnp.zeros((8, D), f32)
        out_ref[2 * s : 2 * s + 1, :] = two_ref[s, 0:1, :]
        out_ref[2 * s + 1 : 2 * s + 2, :] = two_ref[s, 1:2, :] + one_ref[s, 0:1, :]
    along = pltpu.make_async_remote_copy(
        src_ref=out_ref, dst_ref=in_ref, send_sem=send_sem, recv_sem=recv_sem,
        device_id={"seq": seq - 1}, device_id_type=MESH,
    )

    @pl.when(seq > 0)
    def _():
        along.start()

    dbo_ref[...] = dot_tn(mo_ref[...], gb).astype(bf16)
    dao_ref[...] = dot_tn(gm_out, gated_ref[...]).astype(bf16)

    @pl.when(seq > 0)
    def _():
        along.wait_send()

    @pl.when(seq < count - 1)
    def _():
        along.wait_recv()
        for s in range(seqs):
            two_ref[s, length : length + 2, :] = in_ref[2 * s : 2 * s + 2, :]

    for s in range(seqs):
        rows = pl.ds(s * length, length)
        gmix = (
            cw_ref[2:3, :] * gc_ref[rows, :]
            + one_ref[s, pl.ds(1, length), :]
            + two_ref[s, pl.ds(2, length), :]
        )
        gp_ref[rows, 0:D] = (gmix * x_ref[rows, :]).astype(bf16)
        gp_ref[rows, 2 * D :] = (gmix * b_ref[rows, :]).astype(bf16)
    gm_in = (dot_nt(gp_ref[...], tb_ref[:, B_IN : B_IN + 3 * D]) * twice).astype(bf16)
    for k in range(2):
        cols = slice(512 * k, 512 * k + 512)
        gg_ref[:, cols] = dot_nt(gp_ref[...], wi_ref[cols, :]) + dot(gm_in, tb_ref[:, A_IN + 512 * k : A_IN + 512 * k + 512])
    for k in range(6):
        cols = slice(512 * k, 512 * k + 512)
        dbi_ref[:, cols] = dot_tn(mi_ref[...], gp_ref[:, cols]).astype(bf16)
    dai_ref[...] = dot_tn(gm_in, u1_ref[...]).astype(bf16)
    tokens = tok_ref[...].astype(f32)
    inv1 = norm(tokens, n1_ref[...])[1]
    e1 = gg_ref[...] * n1_ref[...]
    ig_ref[...] = (
        gh_ref[...] + inv1 * e1 - tokens * (inv1 * inv1 * inv1 * jnp.mean(tokens * e1, axis=-1, keepdims=True))
    ).astype(bf16)


def post(seqs, length, count, *args):
    rows = seqs * length
    sd = jax.ShapeDtypeStruct
    vm = pl.BlockSpec(memory_space=pltpu.VMEM)
    return pl.pallas_call(
        functools.partial(post_kernel, seqs, length, count),
        in_specs=[vm] * 20,
        out_specs=[vm] * 5,
        out_shape=[sd((rows, D), bf16), sd((128, D), bf16), sd((128, 3 * D), bf16), sd((128, D), bf16), sd((128, D), bf16)],
        scratch_shapes=[
            pltpu.VMEM((rows, D), f32),
            pltpu.VMEM((rows, D), bf16),
            pltpu.VMEM((rows, D), f32),
            pltpu.VMEM((rows, D), f32),
            pltpu.VMEM((rows, 3 * D), bf16),
            pltpu.VMEM((seqs, length + 8, D), f32),
            pltpu.VMEM((seqs, length + 8, D), f32),
            pltpu.VMEM((2 * seqs, D), f32),
            pltpu.VMEM((2 * seqs, D), f32),
            pltpu.SemaphoreType.DMA,
            pltpu.SemaphoreType.DMA,
        ],
        compiler_params=pltpu.CompilerParams(vmem_limit_bytes=62 * MIB, collective_id=1, has_side_effects=True),
    )(*args)


def general_device(
    tokens, segment_ids, adapter_ids, input_weight, conv_weight, output_weight, gate_weight, up_weight, down_weight,
    norm_one, norm_two, cotangent, adapter_state, first_moment, second_moment, rate, step,
):
    seqs, length, _ = tokens.shape
    na = adapter_state.shape[0]
    groups = lax.axis_size("grp")
    count = lax.axis_size("seq")
    native = lambda x: x.reshape(na, PACKROWS, 128).swapaxes(0, 1).reshape(na * PACKROWS, 128)
    st, m, v = native(adapter_state), native(first_moment), native(second_moment)
    own = build_table(st, na)
    table = lax.all_gather(own, "grp", axis=0, tiled=True)
    adapters = na * groups
    mask = (adapter_ids[:, None] == jnp.arange(adapters * RANK, dtype=jnp.int32)[None, :] // RANK).astype(f32)
    ids = segment_ids.astype(f32)
    rows = seqs * length
    tok2, cot2 = tokens.reshape(rows, D), cotangent.reshape(rows, D)
    n1, n2 = norm_one.reshape(1, D), norm_two.reshape(1, D)
    u1, mi, b, c, x, conv, same, gated, mo, h1, u2, mg, mu, gd = pre(
        seqs, length, count, tok2, ids, mask, table, input_weight, conv_weight, output_weight, n1, n2, cot2
    )
    out, gn, dbg, dbu, dad, dag, dau, dbd = ffn(
        seqs, length, u2, cot2, mg, mu, gd, mask, h1, gate_weight, up_weight, down_weight, table
    )
    ig, dai, dbi, dao, dbo = post(
        seqs, length, count, tok2, cot2, mask, h1, gn, gated, mo, b, c, x, conv, same, u1, mi,
        table, input_weight, conv_weight, output_weight, n1, n2,
    )
    grads = jnp.concatenate([dai, dbi, dao, dbo, dag, dbg, dau, dbu, dad, dbd], axis=1).astype(f32)
    owned = lax.psum(lax.psum_scatter(grads, "grp", scatter_dimension=0, tiled=True), "seq")
    correction = 1.0 - jnp.power(jnp.float32(0.5), step[0].astype(f32))
    scal = jnp.stack([rate[0], 1.0 / correction])
    new, tab = adam(scal, owned, st, m, v, na)
    every = lax.all_gather(tab, "grp", axis=0, tiled=False)
    every = every.reshape(groups, PACKROWS, na, 128).transpose(1, 0, 2, 3).reshape(PACKROWS, adapters, 128)
    every = every.swapaxes(0, 1).reshape(adapters, PACKROWS * 128)
    new = new.reshape(PACKROWS, na, 128).swapaxes(0, 1).reshape(na, PACKROWS * 128)
    return out.reshape(tokens.shape), ig.reshape(tokens.shape), new, every


W_A_IN, W_B_B, W_B_X, W_B_C, W_A_OUT, W_B_OUT, W_A_GATE, W_A_UP, W_B_DOWN, W_FFN = (1024 * n for n in range(10))
W_ENDS = W_A_GATE
BLOCKS = FF // FB
W_BLOCK = 3 * FB
FFN_COLS = WIRE - W_ENDS
SPREAD_BLOCKS = 2


def wire(first, n):
    if first == B_IN:
        return (W_B_B, W_B_C, W_B_X)[n // D] + n % D
    for place, matrix in enumerate((B_GATE, B_UP, A_DOWN)):
        if first == matrix:
            return W_FFN + n // FB * W_BLOCK + place * FB + n % FB
    return {A_IN: W_A_IN, A_OUT: W_A_OUT, B_OUT: W_B_OUT, A_GATE: W_A_GATE, A_UP: W_A_UP, B_DOWN: W_B_DOWN}[first] + n


def a_pieces(first, count):
    for matrix, height in A_PARTS:
        if matrix <= first < matrix + height:
            return [(k, wire(matrix, first - matrix + k), FB) for k in range(0, count, FB)]


class Place:
    def __init__(self):
        seq, grp = lax.axis_index("seq"), lax.axis_index("grp")
        self.seq, self.grp = seq, grp
        self.c, self.x, self.y, self.z = grp % 2, grp // 2, seq % 2, seq // 2
        self.core = grp + 1 - 2 * self.c
        self.gx = (grp + 2) % 4
        self.sy = seq + 1 - 2 * self.y
        self.sz = seq + 2 - 4 * (self.z % 2)

    def along_z(self, d):
        return (self.seq + 2 * d) % 8


def announce(seq, count, devices, both=True):
    barrier = pltpu.get_barrier_semaphore()
    if both:

        @pl.when(seq > 0)
        def _():
            pl.semaphore_signal(barrier, inc=1, device_id={"seq": seq - 1}, device_id_type=MESH)

        @pl.when(seq < count - 1)
        def _():
            pl.semaphore_signal(barrier, inc=1, device_id={"seq": seq + 1}, device_id_type=MESH)

    for device in devices:
        pl.semaphore_signal(barrier, inc=1, device_id=device, device_id_type=MESH)
    ends = (seq + count - 1) // count + (2 * count - 2 - seq) // count if both else 0
    return lambda: pl.semaphore_wait(barrier, ends + len(devices))


class Spread:
    KINDS = ("core", "x", "y", "z", "dy", "dz", "cx", "cy", "cz", "cd")

    def __init__(self, at, own, slot, pieces, step, send_sems, recv_sems):
        self.at, self.own, self.slot, self.pieces, self.step = at, own, slot, pieces, step
        self.send_sems, self.recv_sems = send_sems, recv_sems

    def copy(self, kind, p):
        at = self.at
        first, size = self.pieces[p]
        quarter = size // 4
        half = -(-quarter // (2 * self.step)) * self.step
        part = lambda q: pl.multiple_of(first + q * quarter, self.step)
        q = at.seq % 4
        qy, qz, qd = q + 1 - 2 * (q % 2), (q + 2) % 4, 3 - q
        core, y, z = {"grp": at.core}, {"seq": at.sy}, {"seq": at.sz}
        if kind == "core":
            src, dst, device = self.own(first, size), self.slot(at.grp, first, size), core
        elif kind == "x":
            src, dst, device = self.own(part(q), quarter), self.slot(at.grp, part(q), quarter), {"grp": at.gx}
        else:
            start, count, device = {
                "y": (part(q), quarter, y),
                "z": (part(q), quarter, z),
                "dy": (part(qz), half, y),
                "dz": (pl.multiple_of(part(qy) + half, self.step), quarter - half, z),
                "cx": (part(q), quarter, core),
                "cy": (part(qy), quarter, core),
                "cz": (part(qz), quarter, core),
                "cd": (part(qd), quarter, core),
            }[kind]
            src = dst = self.slot(at.gx, start, count)
        n = len(self.KINDS) * p + self.KINDS.index(kind)
        return pltpu.make_async_remote_copy(
            src_ref=src, dst_ref=dst, send_sem=self.send_sems.at[n], recv_sem=self.recv_sems.at[n],
            device_id=device, device_id_type=MESH,
        )

    def leg(self, number, p):
        waits, starts = (
            ((), ("x", "core")),
            (("x",), ("y", "z", "cx")),
            (("y",), ("dz", "cy")),
            (("z",), ("dy", "cz")),
            (("dy", "dz"), ("cd",)),
            (("core", "cx", "cy", "cz", "cd"), ()),
        )[number]
        for kind in waits:
            self.copy(kind, p).wait_recv()
        for kind in starts:
            self.copy(kind, p).start()

    def sent(self, p):
        for kind in self.KINDS:
            self.copy(kind, p).wait_send()


def fill_shuffle(perm_ref):
    diff = lax.broadcasted_iota(jnp.int32, (128, 1024), 1) - 8 * lax.broadcasted_iota(jnp.int32, (128, 1024), 0)
    for c in range(8):
        perm_ref[128 * c : 128 * c + 128, :] = jnp.where(diff == c, 1.0, 0.0).astype(bf16)


def build_own(na, grp, st_ref, tb_ref, lhs_ref, perm_ref):
    own = lambda a: pl.ds(pl.multiple_of((grp * na + a) * RANK, RANK), RANK)
    fill_shuffle(perm_ref)
    for n, (first, count) in enumerate(A_CHUNKS):
        for a in range(na):
            packed = st_ref[pl.ds(na * (first // 8) + a, 128, stride=na), :]
            turned = packed.T.astype(bf16)
            row = (n * na + a) * RANK
            for c in range(8):
                lhs_ref[row : row + RANK, 128 * c : 128 * c + 128] = turned[RANK * c : RANK * c + RANK, :]
    full = dot(lhs_ref[...], perm_ref[...]).astype(bf16)
    for n, (first, count) in enumerate(A_CHUNKS):
        for a in range(na):
            row = (n * na + a) * RANK
            for k, col, size in a_pieces(first, count):
                tb_ref[own(a), col : col + size] = full[row : row + RANK, k : k + size]
    for first, breadth in B_PARTS:
        blocks = breadth // 128
        for a in range(na):
            for c in range(blocks):
                part = st_ref[pl.ds(na * (first // 8 + c) + a, RANK, stride=na * blocks), :]
                col = wire(first, 128 * c)
                tb_ref[own(a), col : col + 128] = part.astype(bf16)


SPREAD_PIECES = ((0, 4096), (W_A_OUT, 5120), (W_FFN, SPREAD_BLOCKS * W_BLOCK))


def start_kernel(
    seqs, length, count, na,
    st_ref, tok_ref, ids_ref, mask_ref, wi_hbm, cw_ref, wo_hbm, n1_ref, n2_ref,
    tb_hbm, u1_hbm, mi_ref, b_hbm, c_hbm, x_hbm, conv_hbm, same_hbm, gated_hbm, mo_ref, h1_hbm, u2_hbm, mg_ref, mu_ref,
    tb_ref, lhs_ref, perm_ref, wi_ref, wo_ref, u1_ref, b_ref, c_ref, x_ref, conv_ref, same_ref, gated_ref, h1_ref, u2_ref,
    ext_ref, out_ref, in_ref, halo_sems, load_sems, store_sems, send_sems, recv_sems,
):
    at = Place()
    seq, grp = at.seq, at.grp
    load_in = pltpu.make_async_copy(wi_hbm, wi_ref, load_sems.at[0])
    load_out = pltpu.make_async_copy(wo_hbm, wo_ref, load_sems.at[1])
    load_in.start()
    load_out.start()
    met = announce(seq, count, ({"grp": at.core}, {"grp": at.gx}, {"seq": at.sz}))
    build_own(na, grp, st_ref, tb_ref, lhs_ref, perm_ref)
    height = na * RANK
    block = lambda owner, first, size: tb_ref.at[
        pl.ds(pl.multiple_of(owner * height, height), height), pl.ds(first, size)
    ]
    spread = Spread(at, functools.partial(block, grp), block, SPREAD_PIECES, 128, send_sems, recv_sems)
    leg = spread.leg

    def keep(n, src, dst):
        return pltpu.make_async_copy(src, dst, store_sems.at[n])

    met()
    leg(0, 0)
    twice = 2.0 * row_mask(mask_ref, seqs, length)
    tokens = tok_ref[...].astype(f32)
    u1 = norm(tokens, n1_ref[...])[0].astype(bf16)
    u1_ref[...] = u1
    keep(0, u1_ref, u1_hbm).start()
    load_in.wait()
    for k in range(2):
        b_ref[:, 512 * k : 512 * k + 512] = dot(u1, wi_ref[:, 512 * k : 512 * k + 512])
    leg(1, 0)
    for p in range(1, len(SPREAD_PIECES)):
        leg(0, p)
    for k in range(2):
        x_ref[:, 512 * k : 512 * k + 512] = dot(u1, wi_ref[:, 2 * D + 512 * k : 2 * D + 512 * k + 512])
    leg(1, 1)
    leg(2, 0)
    leg(3, 0)
    for k in range(2):
        c_ref[:, 512 * k : 512 * k + 512] = dot(u1, wi_ref[:, D + 512 * k : D + 512 * k + 512])
    leg(1, 2)
    leg(4, 0)
    leg(5, 0)
    mid = (dot_nt(u1, tb_ref[:, W_A_IN : W_A_IN + D]).astype(bf16).astype(f32) * twice).astype(bf16)
    mi_ref[...] = mid
    for first, to_ref in ((W_B_B, b_ref), (W_B_X, x_ref)):
        for k in range(2):
            col = first + 512 * k
            to_ref[:, 512 * k : 512 * k + 512] += dot(mid, tb_ref[:, col : col + 512])
    leg(2, 1)
    leg(3, 1)
    keep(1, b_ref, b_hbm).start()
    keep(2, x_ref, x_hbm).start()
    width = D + 128
    for s in range(seqs):
        rows = pl.ds(s * length, length)
        ext_ref[s, 0:8, :] = jnp.zeros((8, width), f32)
        ext_ref[s, 8:, :D] = b_ref[rows, :] * x_ref[rows, :]
        ext_ref[s, 8:, D:] = jnp.broadcast_to(ids_ref[s : s + 1, :], (length, 128)).T
        out_ref[2 * s : 2 * s + 2, :] = ext_ref[s, length + 6 : length + 8, :]
    along = pltpu.make_async_remote_copy(
        src_ref=out_ref, dst_ref=in_ref, send_sem=halo_sems.at[0], recv_sem=halo_sems.at[1],
        device_id={"seq": seq + 1}, device_id_type=MESH,
    )

    @pl.when(seq < count - 1)
    def _():
        along.start()

    for k in range(2):
        col = W_B_C + 512 * k
        c_ref[:, 512 * k : 512 * k + 512] += dot(mid, tb_ref[:, col : col + 512])
    keep(3, c_ref, c_hbm).start()
    leg(2, 2)
    leg(3, 2)

    @pl.when(seq < count - 1)
    def _():
        along.wait_send()

    @pl.when(seq > 0)
    def _():
        along.wait_recv()
        for s in range(seqs):
            ext_ref[s, 6:8, :] = in_ref[2 * s : 2 * s + 2, :]

    for s in range(seqs):
        rows = pl.ds(s * length, length)
        now_ids = ext_ref[s, 8:, D:]
        same1 = jnp.where(ext_ref[s, pl.ds(7, length), D:] == now_ids, 1.0, 0.0)
        same2 = jnp.where(ext_ref[s, pl.ds(6, length), D:] == now_ids, 1.0, 0.0)
        same_ref[0, rows, :] = same1
        same_ref[1, rows, :] = same2
        conv = (
            cw_ref[2:3, :] * ext_ref[s, 8:, :D]
            + cw_ref[1:2, :] * same1[:, :1] * ext_ref[s, pl.ds(7, length), :D]
            + cw_ref[0:1, :] * same2[:, :1] * ext_ref[s, pl.ds(6, length), :D]
        )
        conv_ref[rows, :] = conv
        gated_ref[rows, :] = (c_ref[rows, :] * conv).astype(bf16)
    keep(4, conv_ref, conv_hbm).start()
    keep(5, same_ref, same_hbm).start()
    leg(4, 1)
    leg(4, 2)
    keep(6, gated_ref, gated_hbm).start()
    gated = gated_ref[...]
    load_out.wait()
    for k in range(2):
        cols = slice(512 * k, 512 * k + 512)
        h1_ref[:, cols] = tok_ref[:, cols].astype(f32) + dot(gated, wo_ref[:, cols])
    leg(5, 1)
    mid_out = (dot_nt(gated, tb_ref[:, W_A_OUT : W_A_OUT + D]).astype(bf16).astype(f32) * twice).astype(bf16)
    mo_ref[...] = mid_out
    for k in range(2):
        cols = slice(512 * k, 512 * k + 512)
        h1_ref[:, cols] += dot(mid_out, tb_ref[:, W_B_OUT + 512 * k : W_B_OUT + 512 * k + 512])
    keep(7, h1_ref, h1_hbm).start()
    u2 = norm(h1_ref[...], n2_ref[...])[0].astype(bf16)
    u2_ref[...] = u2
    keep(8, u2_ref, u2_hbm).start()
    keep(9, tb_ref.at[:, :W_FFN], tb_hbm.at[:, :W_FFN]).start()
    mg_ref[...] = (dot_nt(u2, tb_ref[:, W_A_GATE : W_A_GATE + D]).astype(bf16).astype(f32) * twice).astype(bf16)
    mu_ref[...] = (dot_nt(u2, tb_ref[:, W_A_UP : W_A_UP + D]).astype(bf16).astype(f32) * twice).astype(bf16)
    leg(5, 2)
    keep(10, tb_ref.at[:, W_FFN:], tb_hbm.at[:, W_FFN:]).start()
    for p in range(len(SPREAD_PIECES)):
        spread.sent(p)
    for n, (src, dst) in enumerate((
        (u1_ref, u1_hbm), (b_ref, b_hbm), (x_ref, x_hbm), (c_ref, c_hbm), (conv_ref, conv_hbm), (same_ref, same_hbm),
        (gated_ref, gated_hbm), (h1_ref, h1_hbm), (u2_ref, u2_hbm),
        (tb_ref.at[:, :W_FFN], tb_hbm.at[:, :W_FFN]), (tb_ref.at[:, W_FFN:], tb_hbm.at[:, W_FFN:]),
    )):
        keep(n, src, dst).wait()


def start(seqs, length, count, na, *args):
    rows = seqs * length
    sd = jax.ShapeDtypeStruct
    width = D + 128
    vm = pl.BlockSpec(memory_space=pltpu.VMEM)
    hbm = pl.BlockSpec(memory_space=pl.ANY)
    table = sd((128, WIRE), bf16)
    wide = sd((rows, D), f32)
    half = sd((rows, D), bf16)
    thin = sd((rows, 128), bf16)
    same = sd((2, rows, 128), f32)
    scratch = lambda x: pltpu.VMEM(x.shape, x.dtype)
    return pl.pallas_call(
        functools.partial(start_kernel, seqs, length, count, na),
        in_specs=[vm, vm, vm, vm, hbm, vm, hbm, vm, vm],
        out_specs=[hbm, hbm, vm, hbm, hbm, hbm, hbm, hbm, hbm, vm, hbm, hbm, vm, vm],
        out_shape=[table, half, thin, wide, wide, wide, wide, same, half, thin, wide, half, thin, thin],
        scratch_shapes=[
            scratch(table),
            pltpu.VMEM((len(A_CHUNKS) * na * RANK, 1024), bf16),
            pltpu.VMEM((1024, 1024), bf16),
            pltpu.VMEM((D, 3 * D), bf16),
            pltpu.VMEM((D, D), bf16),
            scratch(half), scratch(wide), scratch(wide), scratch(wide), scratch(wide), scratch(same), scratch(half),
            scratch(wide), scratch(half),
            pltpu.VMEM((seqs, length + 8, width), f32),
            pltpu.VMEM((2 * seqs, width), f32),
            pltpu.VMEM((2 * seqs, width), f32),
            pltpu.SemaphoreType.DMA((2,)),
            pltpu.SemaphoreType.DMA((2,)),
            pltpu.SemaphoreType.DMA((11,)),
            pltpu.SemaphoreType.DMA((len(Spread.KINDS) * len(SPREAD_PIECES),)),
            pltpu.SemaphoreType.DMA((len(Spread.KINDS) * len(SPREAD_PIECES),)),
        ],
        compiler_params=pltpu.CompilerParams(vmem_limit_bytes=60 * MIB, collective_id=2, has_side_effects=True),
    )(*args)


class Sums:
    CORE, X, Y, Z, BACK_Z, BACK_Y = range(6)
    COPIES = 10

    def __init__(self, at, g_ref, cr_ref, xr_ref, yr_ref, zr_ref, sum_ref, send_sems, recv_sems):
        self.at, self.g, self.cr, self.xr, self.yr, self.zr, self.sum = at, g_ref, cr_ref, xr_ref, yr_ref, zr_ref, sum_ref
        self.send_sems, self.recv_sems = send_sems, recv_sems

    def unit(self, z, start, size):
        rows = pl.ds(pl.multiple_of(RANK * (z // 2), RANK), RANK)
        quarter = size // 4
        return rows, pl.ds(pl.multiple_of(start + self.at.y * (size // 2) + (z % 2) * quarter, 128), quarter)

    def half(self, y, start, size):
        return pl.ds(pl.multiple_of(start + y * (size // 2), 128), size // 2)

    def slot(self, start, size, share):
        return pl.ds(pl.multiple_of(start // share, 128), size // share)

    def copies(self, stage, group):
        index, start, size = group
        at = self.at
        cols = pl.ds(start, size)
        if stage == self.CORE:
            parts = [(self.g.at[:, 1 - at.c, :, cols], self.cr.at[:, :, cols], {"grp": at.core})]
        elif stage == self.X:
            parts = [(self.g.at[1 - at.x, at.c, :, cols], self.xr.at[:, cols], {"grp": at.gx})]
        elif stage == self.Y:
            away = self.half(1 - at.y, start, size)
            parts = [(self.g.at[at.x, at.c, :, away], self.yr.at[:, self.slot(start, size, 2)], {"seq": at.sy})]
        elif stage == self.BACK_Y:
            part = self.sum.at[:, self.half(at.y, start, size)]
            parts = [(part, part, {"seq": at.sy})]
        else:
            parts = []
            for d in range(1, 4):
                if stage == self.Z:
                    rows, span = self.unit((at.z + d) % 4, start, size)
                    parts.append((
                        self.g.at[at.x, at.c, rows, span], self.zr.at[d - 1, :, self.slot(start, size, 4)],
                        {"seq": at.along_z(d)},
                    ))
                else:
                    rows, span = self.unit(at.z, start, size)
                    part = self.sum.at[rows, span]
                    parts.append((part, part, {"seq": at.along_z(d)}))
        first = self.COPIES * index + {self.CORE: 0, self.X: 1, self.Y: 2, self.Z: 3, self.BACK_Z: 6, self.BACK_Y: 9}[stage]
        return [
            pltpu.make_async_remote_copy(
                src_ref=src, dst_ref=dst, send_sem=self.send_sems.at[first + n], recv_sem=self.recv_sems.at[first + n],
                device_id=device, device_id_type=MESH,
            )
            for n, (src, dst, device) in enumerate(parts)
        ]

    def send(self, stage, group):
        for copy in self.copies(stage, group):
            copy.start()

    def take(self, stage, group):
        for copy in self.copies(stage, group):
            copy.wait()
        _, start, size = group
        at = self.at
        cols = pl.ds(start, size)
        wide = lambda value: value.astype(f32)
        if stage == self.CORE:
            for x in range(2):
                self.g[x, at.c, :, cols] = (wide(self.g[x, at.c, :, cols]) + wide(self.cr[x, :, cols])).astype(bf16)
        elif stage == self.X:
            self.g[at.x, at.c, :, cols] = (wide(self.g[at.x, at.c, :, cols]) + wide(self.xr[:, cols])).astype(bf16)
        elif stage == self.Y:
            mine = self.half(at.y, start, size)
            came = self.yr[:, self.slot(start, size, 2)]
            self.g[at.x, at.c, :, mine] = (wide(self.g[at.x, at.c, :, mine]) + wide(came)).astype(bf16)
        elif stage == self.Z:
            rows, span = self.unit(at.z, start, size)
            total = wide(self.g[at.x, at.c, rows, span])
            for d in range(3):
                total = total + wide(self.zr[d, :, self.slot(start, size, 4)])
            self.sum[rows, span] = total.astype(bf16)


def sums_scratch(cols):
    return [
        pltpu.VMEM((2, 2, 32, cols), bf16),
        pltpu.VMEM((2, 32, cols), bf16),
        pltpu.VMEM((32, cols), bf16),
        pltpu.VMEM((32, cols // 2), bf16),
        pltpu.VMEM((3, 16, cols // 4), bf16),
        pltpu.VMEM((32, cols), bf16),
    ]


def put_grad(g_ref, cols, value):
    for x in range(2):
        for c in range(2):
            first = 64 * x + 32 * c
            g_ref[x, c, :, cols] = value[first : first + 32, :].astype(bf16)


ENDS_COLS = W_FFN - W_ENDS


def ffn_group(j):
    start = ENDS_COLS + j * W_BLOCK
    return j, start if isinstance(j, int) else pl.multiple_of(start, 128), W_BLOCK


def middle_kernel(
    seqs, length,
    u_ref, cot_ref, mg_ref, mu_ref, mask_ref, h1_hbm, wg_hbm, wu_hbm, wd_hbm, tb_hbm,
    out_ref, gn_ref, g_hbm, sum_hbm,
    tb_ref, wg_ref, wu_ref, wd_ref, h1_ref, acc_ref, dmid_ref, gmg_ref, gmu_ref, gd_ref,
    g_ref, cr_ref, xr_ref, yr_ref, zr_ref, sum_ref,
    load_sems, weight_sems, tab_send, tab_recv, send_sems, recv_sems,
):
    at = Place()
    along = [{"seq": at.along_z(d)} for d in range(1, 4)]
    met = announce(at.seq, 8, [{"grp": at.core}, {"grp": at.gx}, {"seq": at.sy}] + along, both=False)

    def fetch(j, slot):
        cols = pl.ds(j * FB if isinstance(j, int) else pl.multiple_of(j * FB, FB), FB)
        return [
            pltpu.make_async_copy(wg_hbm.at[:, cols], wg_ref.at[slot], weight_sems.at[slot, 0]),
            pltpu.make_async_copy(wu_hbm.at[:, cols], wu_ref.at[slot], weight_sems.at[slot, 1]),
            pltpu.make_async_copy(wd_hbm.at[cols, :], wd_ref.at[slot], weight_sems.at[slot, 2]),
        ]

    for copy in fetch(0, 0):
        copy.start()
    here = ENDS_COLS + SPREAD_BLOCKS * W_BLOCK
    rows32 = lambda owner: pl.ds(pl.multiple_of(owner * 32, 32), 32)
    loads = [
        pltpu.make_async_copy(tb_hbm.at[:, W_ENDS : W_ENDS + here], tb_ref.at[:, :here], load_sems.at[0]),
        pltpu.make_async_copy(
            tb_hbm.at[rows32(at.grp), W_ENDS + here :], tb_ref.at[rows32(at.grp), here:], load_sems.at[1]
        ),
        pltpu.make_async_copy(h1_hbm, h1_ref, load_sems.at[2]),
    ]
    for copy in loads:
        copy.start()

    def table_copy(kind, j):
        _, start, size = ffn_group(j)
        owner, device = {
            "core": (at.grp, {"grp": at.core}), "x": (at.grp, {"grp": at.gx}), "far": (at.gx, {"grp": at.core})
        }[kind]
        part = tb_ref.at[rows32(owner), pl.ds(start, size)]
        n = 3 * j + ("core", "x", "far").index(kind)
        return pltpu.make_async_remote_copy(
            src_ref=part, dst_ref=part, send_sem=tab_send.at[n], recv_sem=tab_recv.at[n], device_id=device, device_id_type=MESH
        )

    sums = Sums(at, g_ref, cr_ref, xr_ref, yr_ref, zr_ref, sum_ref, send_sems, recv_sems)
    twice = 2.0 * row_mask(mask_ref, seqs, length)
    for ref in (acc_ref, gn_ref, dmid_ref, gmg_ref, gmu_ref):
        ref[...] = jnp.zeros_like(ref)
    loads[0].wait()
    a_gate, a_up, b_down = (tb_ref.at[:, first - W_ENDS : first - W_ENDS + D] for first in (W_A_GATE, W_A_UP, W_B_DOWN))
    gd_ref[...] = (dot_nt(cot_ref[...], b_down[...]) * twice).astype(bf16)
    loads[1].wait()
    met()

    def when(first, j, last, run):
        @pl.when((j >= first) & (j <= last))
        def _():
            run()

    def block(j, carry):
        slot = j % 2
        for copy in fetch(j, slot):
            copy.wait()

        def more():
            for copy in fetch(j + 1, 1 - slot):
                copy.start()

        when(0, j, BLOCKS - 2, more)
        lead = SPREAD_BLOCKS

        def leave():
            table_copy("x", j + lead).start()
            table_copy("core", j + lead).start()

        def go_on():
            table_copy("x", j + lead - 1).wait()
            table_copy("far", j + lead - 1).start()

        def there():
            table_copy("core", j).wait()
            table_copy("far", j).wait()

        when(0, j, BLOCKS - 1 - lead, leave)
        when(1, j, BLOCKS - lead, go_on)
        when(lead, j, BLOCKS - 1, there)
        for stage in range(6):

            def advance(stage=stage):
                if stage > 0:
                    sums.take(stage - 1, ffn_group(j - 1 - stage))
                sums.send(stage, ffn_group(j - 1 - stage))

            when(1 + stage, j, BLOCKS - 1, advance)

        def finished():
            sums.take(5, ffn_group(j - 7))

        when(7, j, BLOCKS - 1, finished)

        base = ENDS_COLS + j * W_BLOCK
        part = lambda place: pl.ds(pl.multiple_of(base + place * FB, 128), FB)
        tab_gate, tab_up, tab_down = (tb_ref.at[:, part(place)] for place in range(3))
        u = u_ref[...]
        gate = dot(u, wg_ref[slot]) + dot(mg_ref[...], tab_gate[...])
        up = dot(u, wu_ref[slot]) + dot(mu_ref[...], tab_up[...])
        back = dot_nt(cot_ref[...], wd_ref[slot]) + dot(gd_ref[...], tab_down[...])
        sig = jax.nn.sigmoid(gate)
        silu = gate * sig
        hidden = (silu * up).astype(bf16)
        grad_gate = (back * up * sig * (1.0 + gate * (1.0 - sig))).astype(bf16)
        grad_up = (back * silu).astype(bf16)
        acc_ref[...] += dot(hidden, wd_ref[slot])
        gn_ref[...] += dot_nt(grad_gate, wg_ref[slot]) + dot_nt(grad_up, wu_ref[slot])
        dmid_ref[...] += dot_nt(hidden, tab_down[...])
        gmg_ref[...] += dot_nt(grad_gate, tab_gate[...])
        gmu_ref[...] += dot_nt(grad_up, tab_up[...])
        put_grad(g_ref, part(0), dot_tn(mg_ref[...], grad_gate))
        put_grad(g_ref, part(1), dot_tn(mu_ref[...], grad_up))
        put_grad(g_ref, part(2), dot_tn(gd_ref[...], hidden))
        return carry

    lax.fori_loop(0, BLOCKS, block, 0)
    dmid = (dmid_ref[...].astype(bf16).astype(f32) * twice).astype(bf16)
    loads[2].wait()
    for k in range(2):
        cols = slice(512 * k, 512 * k + 512)
        out_ref[:, cols] = (h1_ref[:, cols] + acc_ref[:, cols] + dot(dmid, b_down[:, cols])).astype(bf16)
    put_grad(g_ref, slice(2 * D, 3 * D), dot_tn(dmid, cot_ref[...]))
    gm_gate = (gmg_ref[...] * twice).astype(bf16)
    gm_up = (gmu_ref[...] * twice).astype(bf16)
    for k in range(2):
        cols = slice(512 * k, 512 * k + 512)
        gn_ref[:, cols] += dot(gm_gate, a_gate[:, cols]) + dot(gm_up, a_up[:, cols])
    put_grad(g_ref, slice(0, D), dot_tn(gm_gate, u_ref[...]))
    put_grad(g_ref, slice(D, 2 * D), dot_tn(gm_up, u_ref[...]))
    for stage in range(6):
        sums.take(stage, ffn_group(BLOCKS - 2 - stage))
    stores = [
        pltpu.make_async_copy(g_ref, g_hbm, load_sems.at[0]),
        pltpu.make_async_copy(sum_ref, sum_hbm, load_sems.at[1]),
    ]
    for copy in stores:
        copy.start()
    for copy in stores:
        copy.wait()


def middle(seqs, length, *args):
    rows = seqs * length
    sd = jax.ShapeDtypeStruct
    vm = pl.BlockSpec(memory_space=pltpu.VMEM)
    hbm = pl.BlockSpec(memory_space=pl.ANY)
    return pl.pallas_call(
        functools.partial(middle_kernel, seqs, length),
        in_specs=[vm] * 5 + [hbm] * 5,
        out_specs=[vm, vm, hbm, hbm],
        out_shape=[
            sd((rows, D), bf16), sd((rows, D), f32), sd((2, 2, 32, FFN_COLS), bf16), sd((32, FFN_COLS), bf16),
        ],
        scratch_shapes=[
            pltpu.VMEM((128, FFN_COLS), bf16),
            pltpu.VMEM((2, D, FB), bf16),
            pltpu.VMEM((2, D, FB), bf16),
            pltpu.VMEM((2, FB, D), bf16),
            pltpu.VMEM((rows, D), f32),
            pltpu.VMEM((rows, D), f32),
            pltpu.VMEM((rows, 128), f32),
            pltpu.VMEM((rows, 128), f32),
            pltpu.VMEM((rows, 128), f32),
            pltpu.VMEM((rows, 128), bf16),
            *sums_scratch(FFN_COLS),
            pltpu.SemaphoreType.DMA((3,)),
            pltpu.SemaphoreType.DMA((2, 3)),
            pltpu.SemaphoreType.DMA((3 * BLOCKS,)),
            pltpu.SemaphoreType.DMA((3 * BLOCKS,)),
            pltpu.SemaphoreType.DMA((Sums.COPIES * BLOCKS,)),
            pltpu.SemaphoreType.DMA((Sums.COPIES * BLOCKS,)),
        ],
        compiler_params=pltpu.CompilerParams(vmem_limit_bytes=60 * MIB, collective_id=3, has_side_effects=True),
    )(*args)


UPDATES = (
    (B_GATE - D, D + FF), (B_UP - D, D + FF), (A_DOWN, FF + D), (A_OUT, 2 * D), (A_IN, 4 * D),
)
MOST = 2 * (D + FF) // 8
NATIVE = tuple((2 * first // 8, 2 * count // 8) for first, count in UPDATES)


def update_grad(na, part, sum_ref, lhs_ref, perm_ref, gn_ref):
    first, count = UPDATES[part]
    begin = na * first // 8
    inside = lambda start: first <= start < first + count
    chunks = [chunk for chunk in A_CHUNKS if inside(chunk[0])]
    for n, (start, size) in enumerate(chunks):
        for a in range(na):
            row = (n * na + a) * RANK
            if size < 1024:
                lhs_ref[row : row + RANK, size:] = jnp.zeros((RANK, 1024 - size), bf16)
            for k, col, breadth in a_pieces(start, size):
                lhs_ref[row : row + RANK, k : k + breadth] = sum_ref[a * RANK : (a + 1) * RANK, col : col + breadth]
    height = len(chunks) * na * RANK
    full = dot_nt(lhs_ref[:height, :], perm_ref[...])
    for n, (start, size) in enumerate(chunks):
        for a in range(na):
            row = (n * na + a) * RANK
            turned = jnp.concatenate([full[row : row + RANK, 128 * c : 128 * c + 128] for c in range(8)], axis=0)
            gn_ref[pl.ds(na * (start // 8) + a - begin, size // 8, stride=na), :] = turned.T[: size // 8]
    for start, breadth in B_PARTS:
        if inside(start):
            blocks = breadth // 128
            for a in range(na):
                for c in range(blocks):
                    col = wire(start, 128 * c)
                    gn_ref[pl.ds(na * (start // 8 + c) + a - begin, RANK, stride=na * blocks), :] = sum_ref[
                        a * RANK : (a + 1) * RANK, col : col + 128
                    ].astype(f32)


def finish_kernel(
    seqs, length, count, na,
    scal_ref, mask_ref, mo_ref, mi_ref, cw_ref, n1_ref, n2_ref,
    tok_hbm, cot_hbm, h1_hbm, gn_hbm, gated_hbm, b_hbm, c_hbm, x_hbm, conv_hbm, same_hbm, u1_hbm,
    tb_hbm, wi_hbm, wo_hbm, g_hbm, part_hbm, st_hbm, m_hbm, v_hbm,
    ig_ref, new_hbm, all_hbm,
    tok_ref, cot_ref, h1_ref, gn_ref, gated_ref, b_ref, c_ref, x_ref, conv_ref, same_ref, u1_ref,
    tb_ref, wi_ref, wo_ref,
    gh_ref, gb_ref, gg_ref, gp_ref, out_ref, in_ref,
    g_ref, cr_ref, xr_ref, yr_ref, zr_ref, sum_ref,
    lhs_ref, perm_ref, old_ref, grad_ref, new_ref, tab_ref,
    halo_sems, load_sems, old_sems, new_sems, own_sems, spread_send, spread_recv, send_sems, recv_sems,
):
    at = Place()
    seq = at.seq
    met = announce(seq, count, [{"grp": at.core}, {"grp": at.gx}] + [{"seq": at.along_z(d)} for d in range(1, 4)])
    ends = slice(W_ENDS, WIRE)
    pairs = {
        "h1": (h1_hbm, h1_ref), "gn": (gn_hbm, gn_ref), "cot": (cot_hbm, cot_ref),
        "g": (g_hbm, g_ref.at[:, :, :, ends]),
        "tb": (tb_hbm.at[:, :W_ENDS], tb_ref), "wo": (wo_hbm, wo_ref),
        "c": (c_hbm, c_ref), "conv": (conv_hbm, conv_ref), "same": (same_hbm, same_ref.at[:, :, :length, :]),
        "gated": (gated_hbm, gated_ref), "x": (x_hbm, x_ref), "b": (b_hbm, b_ref), "wi": (wi_hbm, wi_ref),
        "u1": (u1_hbm, u1_ref), "tok": (tok_hbm, tok_ref),
    }
    sums = Sums(at, g_ref, cr_ref, xr_ref, yr_ref, zr_ref, sum_ref, send_sems, recv_sems)
    every_row = slice(None)
    for n, (rows, cols, shifted) in enumerate((
        (every_row, pl.ds(W_FFN, 3 * W_BLOCK), pl.ds(ENDS_COLS, 3 * W_BLOCK)),
        (every_row, *(sums.half(at.y, base + 3 * W_BLOCK, W_BLOCK) for base in (W_FFN, ENDS_COLS))),
        (sums.unit(at.z, W_FFN, W_BLOCK)[0], *(sums.unit(at.z, base + 4 * W_BLOCK, W_BLOCK)[1] for base in (W_FFN, ENDS_COLS))),
    )):
        pairs["sum" + str(n)] = (part_hbm.at[rows, shifted], sum_ref.at[rows, cols])
    names = list(pairs)

    def load(*which):
        return [pltpu.make_async_copy(*pairs[name], load_sems.at[names.index(name)]) for name in which]

    def begin(*which):
        for copy in load(*which):
            copy.start()

    def ready(*which):
        for copy in load(*which):
            copy.wait()

    def old(part, slot):
        first, size = NATIVE[part]
        return [
            pltpu.make_async_copy(ref.at[first : first + size], old_ref.at[slot, n, :size], old_sems.at[slot, n])
            for n, ref in enumerate((st_hbm, m_hbm, v_hbm))
        ]

    begin("h1", "gn", "cot", "g", "sum0", "sum1", "sum2", "tb", "wo", "c", "conv", "same")
    groups = {j: (j, W_FFN + j * W_BLOCK, W_BLOCK) for j in range(3, BLOCKS)}
    groups["ends"] = (0, W_ENDS, W_FFN - W_ENDS)
    groups["out"] = (1, W_B_C, W_ENDS - W_B_C)
    groups["in"] = (2, 0, W_B_C)
    following = {BLOCKS - 1 - stage: stage for stage in range(6)}
    following["ends"] = 0

    def step():
        for name in list(following):
            stage = following[name]
            if stage > 0 and (isinstance(name, str) or stage > BLOCKS - 1 - name):
                sums.take(stage - 1, groups[name])
            if stage < 6:
                sums.send(stage, groups[name])
                following[name] = stage + 1
            else:
                del following[name]

    own = lambda first, size: tab_ref.at[pl.ds(first, size), :]
    slot_of = lambda owner, first, size: all_hbm.at[owner, pl.ds(first, size), :]
    spread = Spread(at, own, slot_of, NATIVE, 16, spread_send, spread_recv)
    going = {}

    def pass_on():
        for part in list(going):
            spread.leg(going[part], part)
            going[part] += 1
            if going[part] > 5:
                del going[part]

    rate, inv = scal_ref[0], scal_ref[1]

    def new_copy(part):
        first, size = NATIVE[part]
        return pltpu.make_async_copy(new_ref.at[part % 2, :size], new_hbm.at[first : first + size], new_sems.at[part % 2])

    def own_copy(part):
        first, size = NATIVE[part]
        return pltpu.make_async_copy(
            tab_ref.at[first : first + size], all_hbm.at[at.grp, first : first + size], own_sems.at[part]
        )

    def update(part):
        first, size = NATIVE[part]
        slot = part % 2
        update_grad(na, part, sum_ref, lhs_ref, perm_ref, grad_ref)
        for copy in old(part, slot):
            copy.wait()
        if part >= 2:
            new_copy(part - 2).wait()
        grad = grad_ref[:size]
        one = 0.5 * old_ref[slot, 1, :size] + 0.5 * grad
        two = 0.5 * old_ref[slot, 2, :size] + 0.5 * grad * grad
        new = old_ref[slot, 0, :size] - rate * (one * inv) / (jnp.sqrt(two * inv) + 1e-08)
        new_ref[slot, :size] = new
        tab_ref[first : first + size] = new.astype(bf16)
        new_copy(part).start()
        own_copy(part).start()
        if part + 2 < len(NATIVE):
            for copy in old(part + 2, slot):
                copy.start()
        going[part] = 0

    twice = 2.0 * row_mask(mask_ref, seqs, length)
    ready("h1", "gn", "cot")
    h1 = h1_ref[...]
    inv2 = norm(h1, n2_ref[...])[1]
    e2 = gn_ref[...] * n2_ref[...]
    gh = cot_ref[...].astype(f32) + inv2 * e2 - h1 * (inv2 * inv2 * inv2 * jnp.mean(h1 * e2, axis=-1, keepdims=True))
    gh_ref[...] = gh
    gb_ref[...] = gh.astype(bf16)
    begin("gated", "x", "b", "wi", "u1", "tok")
    for part in range(2):
        for copy in old(part, part):
            copy.start()
    ready("g", "sum0", "sum1", "sum2")
    met()
    step()
    ready("tb", "wo")
    gb = gb_ref[...]
    gm_out = (dot_nt(gb, tb_ref[:, W_B_OUT : W_B_OUT + D]) * twice).astype(bf16)
    for k in range(2):
        cols = slice(512 * k, 512 * k + 512)
        part = dot_nt(gb, wo_ref[cols, :]) + dot(gm_out, tb_ref[:, W_A_OUT + 512 * k : W_A_OUT + 512 * k + 512])
        for s in range(seqs):
            gg_ref[s, :length, cols] = part[s * length : (s + 1) * length, :]
    step()
    ready("c", "conv", "same")
    for s in range(seqs):
        rows = pl.ds(s * length, length)
        gg = gg_ref[s, :length, :]
        gp_ref[rows, D : 2 * D] = (gg * conv_ref[rows, :]).astype(bf16)
        gg_ref[s, :length, :] = gg * c_ref[rows, :]
        gg_ref[s, length:, :] = jnp.zeros((8, D), f32)
        for k in range(2):
            same_ref[k, s, length:, :] = jnp.zeros((8, 128), f32)
        out_ref[2 * s : 2 * s + 1, :] = cw_ref[0:1, :] * same_ref[1, s, 0:1, 0:1] * gg_ref[s, 0:1, :]
        out_ref[2 * s + 1 : 2 * s + 2, :] = (
            cw_ref[0:1, :] * same_ref[1, s, 1:2, 0:1] * gg_ref[s, 1:2, :]
            + cw_ref[1:2, :] * same_ref[0, s, 0:1, 0:1] * gg_ref[s, 0:1, :]
        )
    along = pltpu.make_async_remote_copy(
        src_ref=out_ref, dst_ref=in_ref, send_sem=halo_sems.at[0], recv_sem=halo_sems.at[1],
        device_id={"seq": seq - 1}, device_id_type=MESH,
    )

    @pl.when(seq > 0)
    def _():
        along.start()

    ready("gated")
    put_grad(g_ref, slice(W_A_OUT, W_A_OUT + D), dot_tn(gm_out, gated_ref[...]))
    put_grad(g_ref, slice(W_B_OUT, W_B_OUT + D), dot_tn(mo_ref[...], gb))
    put_grad(g_ref, slice(W_B_C, W_B_C + D), dot_tn(mi_ref[...], gp_ref[:, D : 2 * D]))
    following["out"] = 0
    step()

    @pl.when(seq > 0)
    def _():
        along.wait_send()

    @pl.when(seq < count - 1)
    def _():
        along.wait_recv()

    ready("x", "b")
    for s in range(seqs):
        rows = pl.ds(s * length, length)
        one, two = pl.ds(1, length), pl.ds(2, length)
        gmix = (
            cw_ref[2:3, :] * gg_ref[s, :length, :]
            + cw_ref[1:2, :] * same_ref[0, s, one, 0:1] * gg_ref[s, one, :]
            + cw_ref[0:1, :] * same_ref[1, s, two, 0:1] * gg_ref[s, two, :]
        )
        gg_ref[s, :length, :] = gmix

    @pl.when(seq < count - 1)
    def _():
        for s in range(seqs):
            gg_ref[s, length - 2 : length, :] += in_ref[2 * s : 2 * s + 2, :]

    for s in range(seqs):
        rows = pl.ds(s * length, length)
        gmix = gg_ref[s, :length, :]
        gp_ref[rows, 0:D] = (gmix * x_ref[rows, :]).astype(bf16)
        gp_ref[rows, 2 * D :] = (gmix * b_ref[rows, :]).astype(bf16)
    step()
    gm_in = dot_nt(gp_ref[:, :D], tb_ref[:, W_B_B : W_B_B + D])
    gm_in += dot_nt(gp_ref[:, D : 2 * D], tb_ref[:, W_B_C : W_B_C + D])
    gm_in += dot_nt(gp_ref[:, 2 * D :], tb_ref[:, W_B_X : W_B_X + D])
    gm_in = (gm_in * twice).astype(bf16)
    ready("u1")
    put_grad(g_ref, slice(W_B_B, W_B_B + D), dot_tn(mi_ref[...], gp_ref[:, :D]))
    put_grad(g_ref, slice(W_B_X, W_B_X + D), dot_tn(mi_ref[...], gp_ref[:, 2 * D :]))
    put_grad(g_ref, slice(W_A_IN, W_A_IN + D), dot_tn(gm_in, u1_ref[...]))
    following["in"] = 0
    step()
    fill_shuffle(perm_ref)
    ready("wi")
    for k in range(4):
        cols = slice(256 * k, 256 * k + 256)
        gn_ref[:, cols] = dot_nt(gp_ref[...], wi_ref[cols, :]) + dot(gm_in, tb_ref[:, W_A_IN + 256 * k : W_A_IN + 256 * k + 256])
        if k % 2 == 1:
            step()
    ready("tok")
    tokens = tok_ref[...].astype(f32)
    inv1 = norm(tokens, n1_ref[...])[1]
    e1 = gn_ref[...] * n1_ref[...]
    ig_ref[...] = (
        gh_ref[...] + inv1 * e1 - tokens * (inv1 * inv1 * inv1 * jnp.mean(tokens * e1, axis=-1, keepdims=True))
    ).astype(bf16)
    for part in range(3):
        while any(not isinstance(name, str) or name == "ends" for name in following):
            step()
        update(part)
        pass_on()
        step()
    while following:
        step()
        pass_on()
    for part in range(3, len(NATIVE)):
        update(part)
        pass_on()
    while going:
        pass_on()
    for part in range(len(NATIVE)):
        spread.sent(part)
        own_copy(part).wait()
    for part in range(len(NATIVE) - 2, len(NATIVE)):
        new_copy(part).wait()


def finish(seqs, length, count, na, *args):
    rows = seqs * length
    sd = jax.ShapeDtypeStruct
    vm = pl.BlockSpec(memory_space=pltpu.VMEM)
    hbm = pl.BlockSpec(memory_space=pl.ANY)
    wide = pltpu.VMEM((rows, D), f32)
    half = pltpu.VMEM((rows, D), bf16)
    parts = len(NATIVE)
    return pl.pallas_call(
        functools.partial(finish_kernel, seqs, length, count, na),
        in_specs=[pl.BlockSpec(memory_space=pltpu.SMEM)] + [vm] * 6 + [hbm] * 19,
        out_specs=[vm, hbm, hbm],
        out_shape=[sd((rows, D), bf16), sd((na * PACKROWS, 128), f32), sd((4, na * PACKROWS, 128), bf16)],
        scratch_shapes=[
            half, half, wide, wide, half, wide, wide, wide, wide, pltpu.VMEM((2, seqs, length + 8, 128), f32), half,
            pltpu.VMEM((128, W_ENDS), bf16), pltpu.VMEM((D, 3 * D), bf16), pltpu.VMEM((D, D), bf16),
            wide, half, pltpu.VMEM((seqs, length + 8, D), f32), pltpu.VMEM((rows, 3 * D), bf16),
            pltpu.VMEM((2 * seqs, D), f32), pltpu.VMEM((2 * seqs, D), f32),
            *sums_scratch(WIRE),
            pltpu.VMEM((5 * na * RANK, 1024), bf16), pltpu.VMEM((1024, 1024), bf16),
            pltpu.VMEM((2, 3, MOST, 128), f32), pltpu.VMEM((MOST, 128), f32), pltpu.VMEM((2, MOST, 128), f32),
            pltpu.VMEM((na * PACKROWS, 128), bf16),
            pltpu.SemaphoreType.DMA((2,)),
            pltpu.SemaphoreType.DMA((18,)),
            pltpu.SemaphoreType.DMA((2, 3)),
            pltpu.SemaphoreType.DMA((2,)),
            pltpu.SemaphoreType.DMA((parts,)),
            pltpu.SemaphoreType.DMA((len(Spread.KINDS) * parts,)),
            pltpu.SemaphoreType.DMA((len(Spread.KINDS) * parts,)),
            pltpu.SemaphoreType.DMA((Sums.COPIES * BLOCKS,)),
            pltpu.SemaphoreType.DMA((Sums.COPIES * BLOCKS,)),
        ],
        compiler_params=pltpu.CompilerParams(vmem_limit_bytes=63 * MIB, collective_id=4, has_side_effects=True),
    )(*args)


def lay_kernel(all_hbm, to_ref, all_ref, load_sems, store_sems):
    cuts = 4
    share = PACKROWS // cuts
    parts = [(k, g, pl.ds(k * share, share)) for k in range(cuts) for g in range(4)]
    loads = [pltpu.make_async_copy(all_hbm.at[g, rows], all_ref.at[g, rows], load_sems.at[k, g]) for k, g, rows in parts]
    stores = [pltpu.make_async_copy(all_ref.at[g, rows], to_ref.at[rows, g], store_sems.at[k, g]) for k, g, rows in parts]
    for copy in loads:
        copy.start()
    for came, goes in zip(loads, stores):
        came.wait()
        goes.start()
    for copy in stores:
        copy.wait()


def lay_out(every, na):
    hbm = pl.BlockSpec(memory_space=pl.ANY)
    return pl.pallas_call(
        lay_kernel,
        in_specs=[hbm],
        out_specs=hbm,
        out_shape=jax.ShapeDtypeStruct((PACKROWS, 4, na, 128), bf16),
        scratch_shapes=[
            pltpu.VMEM((4, PACKROWS, na, 128), bf16),
            pltpu.SemaphoreType.DMA((4, 4)),
            pltpu.SemaphoreType.DMA((4, 4)),
        ],
        compiler_params=pltpu.CompilerParams(vmem_limit_bytes=60 * MIB),
    )(every.reshape(4, PACKROWS, na, 128))


def fast_device(
    tokens, segment_ids, adapter_ids, input_weight, conv_weight, output_weight, gate_weight, up_weight, down_weight,
    norm_one, norm_two, cotangent, adapter_state, first_moment, second_moment, rate, step,
):
    seqs, length, _ = tokens.shape
    na = adapter_state.shape[0]
    groups, count = lax.axis_size("grp"), lax.axis_size("seq")
    native = lambda x: x.reshape(na, PACKROWS, 128).swapaxes(0, 1).reshape(na * PACKROWS, 128)
    st, m, v = native(adapter_state), native(first_moment), native(second_moment)
    adapters = na * groups
    mask = (adapter_ids[:, None] == jnp.arange(adapters * RANK, dtype=jnp.int32)[None, :] // RANK).astype(f32)
    ids = segment_ids.astype(f32)
    rows = seqs * length
    tok2, cot2 = tokens.reshape(rows, D), cotangent.reshape(rows, D)
    n1, n2 = norm_one.reshape(1, D), norm_two.reshape(1, D)
    table, u1, mi, b, c, x, conv, same, gated, mo, h1, u2, mg, mu = start(
        seqs, length, count, na, st, tok2, ids, mask, input_weight, conv_weight, output_weight, n1, n2
    )
    out, gn, grads, sums = middle(
        seqs, length, u2, cot2, mg, mu, mask, h1, gate_weight, up_weight, down_weight, table
    )
    correction = 1.0 - jnp.power(jnp.float32(0.5), step[0].astype(f32))
    scal = jnp.stack([rate[0], 1.0 / correction])
    ig, new, every = finish(
        seqs, length, count, na, scal, mask, mo, mi, conv_weight, n1, n2,
        tok2, cot2, h1, gn, gated, b, c, x, conv, same.reshape(2, seqs, length, 128), u1,
        table, input_weight, output_weight, grads, sums, st, m, v,
    )
    every = lay_out(every, na).reshape(PACKROWS, adapters, 128).swapaxes(0, 1).reshape(adapters, PACKROWS * 128)
    new = new.reshape(PACKROWS, na, 128).swapaxes(0, 1).reshape(na, PACKROWS * 128)
    return out.reshape(tokens.shape), ig.reshape(tokens.shape), new, every


def solution(mesh):
    rows = P("grp", "seq", None)
    own = P("grp", None)
    return jax.shard_map(
        fast_device if tuple(mesh.shape[axis] for axis in ("seq", "grp")) == (8, 4) else general_device,
        mesh=mesh,
        in_specs=(rows, P("grp", "seq"), P("grp")) + (P(),) * 8 + (rows, own, own, own, P(), P()),
        out_specs=(rows, rows, own, P()),
        check_vma=False,
    )
```

```python
import functools

import jax
import jax.numpy as jnp
from jax import lax
from jax.experimental import pallas as pl
from jax.experimental.pallas import tpu as pltpu
from jax.sharding import PartitionSpec as P

D = 1024
FF = 4608
RANK = 16
EPS = 1e-05
FB = 512
MIB = 2**20

f32 = jnp.float32
bf16 = jnp.bfloat16
MESH = pl.DeviceIdType.MESH

WIRE = RANK * 0 + 23040
PACKROWS = 2880
A_IN, B_IN, A_OUT, B_OUT, A_GATE, B_GATE, A_UP, B_UP, A_DOWN, B_DOWN = (
    0, 1024, 4096, 5120, 6144, 7168, 11776, 12800, 17408, 22016,
)
B_PARTS = ((B_IN, 3 * D), (B_OUT, D), (B_GATE, FF), (B_UP, FF), (B_DOWN, D))
A_PARTS = ((A_IN, D), (A_OUT, D), (A_GATE, D), (A_UP, D), (A_DOWN, FF))
A_CHUNKS = tuple(
    (first + start, min(1024, height - start))
    for first, height in A_PARTS
    for start in range(0, height, 1024)
)


def dot(a, b):
    return jnp.dot(a, b, preferred_element_type=f32)


def dot_nt(a, b):
    return lax.dot_general(a, b, (((1,), (1,)), ((), ())), preferred_element_type=f32)


def dot_tn(a, b):
    return lax.dot_general(a, b, (((0,), (0,)), ((), ())), preferred_element_type=f32)


def shuffle_matrix():
    row = lax.broadcasted_iota(jnp.int32, (1024, 1024), 0)
    col = lax.broadcasted_iota(jnp.int32, (1024, 1024), 1)
    return jnp.where(col == 8 * (row % 128) + row // 128, 1.0, 0.0).astype(bf16)


def table_kernel(na, st_ref, out_ref, lhs_ref):
    for n, (first, count) in enumerate(A_CHUNKS):
        for a in range(na):
            packed = st_ref[pl.ds(na * (first // 8) + a, 128, stride=na), :]
            turned = packed.T.astype(bf16)
            row = (n * na + a) * RANK
            for c in range(8):
                lhs_ref[row : row + RANK, 128 * c : 128 * c + 128] = turned[RANK * c : RANK * c + RANK, :]
    full = dot(lhs_ref[...], shuffle_matrix()).astype(bf16)
    for n, (first, count) in enumerate(A_CHUNKS):
        for a in range(na):
            row = (n * na + a) * RANK
            out_ref[a * RANK : (a + 1) * RANK, first : first + count] = full[row : row + RANK, :count]
    for first, breadth in B_PARTS:
        blocks = breadth // 128
        for a in range(na):
            for c in range(blocks):
                part = st_ref[pl.ds(na * (first // 8 + c) + a, RANK, stride=na * blocks), :]
                out_ref[a * RANK : (a + 1) * RANK, first + 128 * c : first + 128 * c + 128] = part.astype(bf16)


def build_table(state_native, na):
    return pl.pallas_call(
        functools.partial(table_kernel, na),
        out_shape=jax.ShapeDtypeStruct((na * RANK, WIRE), bf16),
        scratch_shapes=[pltpu.VMEM((len(A_CHUNKS) * na * RANK, 1024), bf16)],
        compiler_params=pltpu.CompilerParams(vmem_limit_bytes=40 * MIB),
    )(state_native)


def adam_kernel(na, scal_ref, gw_ref, st_ref, m_ref, v_ref, new_ref, tab_ref, lhs_ref, gn_ref):
    for n, (first, count) in enumerate(A_CHUNKS):
        for a in range(na):
            row = (n * na + a) * RANK
            lhs_ref[row : row + RANK, :] = gw_ref[a * RANK : (a + 1) * RANK, first : first + 1024].astype(bf16)
    full = dot_nt(lhs_ref[...], shuffle_matrix())
    for n, (first, count) in enumerate(A_CHUNKS):
        for a in range(na):
            row = (n * na + a) * RANK
            turned = jnp.concatenate(
                [full[row : row + RANK, 128 * c : 128 * c + 128] for c in range(8)], axis=0
            )
            gn_ref[pl.ds(na * (first // 8) + a, count // 8, stride=na), :] = turned.T[: count // 8]
    for first, breadth in B_PARTS:
        blocks = breadth // 128
        for a in range(na):
            for c in range(blocks):
                gn_ref[pl.ds(na * (first // 8 + c) + a, RANK, stride=na * blocks), :] = gw_ref[
                    a * RANK : (a + 1) * RANK, first + 128 * c : first + 128 * c + 128
                ].astype(f32)
    rate = scal_ref[0]
    inv = scal_ref[1]
    grad = gn_ref[...]
    one = 0.5 * m_ref[...] + 0.5 * grad
    two = 0.5 * v_ref[...] + 0.5 * grad * grad
    new = st_ref[...] - rate * (one * inv) / (jnp.sqrt(two * inv) + 1e-08)
    new_ref[...] = new
    tab_ref[...] = new.astype(bf16)


def adam(scal, gw, st, m, v, na):
    rows = na * PACKROWS
    vm = pl.BlockSpec(memory_space=pltpu.VMEM)
    return pl.pallas_call(
        functools.partial(adam_kernel, na),
        in_specs=[pl.BlockSpec(memory_space=pltpu.SMEM)] + [vm] * 4,
        out_shape=(jax.ShapeDtypeStruct((rows, 128), f32), jax.ShapeDtypeStruct((rows, 128), bf16)),
        scratch_shapes=[
            pltpu.VMEM((len(A_CHUNKS) * na * RANK, 1024), bf16),
            pltpu.VMEM((rows, 128), f32),
        ],
        compiler_params=pltpu.CompilerParams(vmem_limit_bytes=56 * MIB),
    )(scal, gw, st, m, v)


def greet(seq, count):
    barrier = pltpu.get_barrier_semaphore()

    @pl.when(seq > 0)
    def _():
        pl.semaphore_signal(barrier, inc=1, device_id={"seq": seq - 1}, device_id_type=MESH)

    @pl.when(seq < count - 1)
    def _():
        pl.semaphore_signal(barrier, inc=1, device_id={"seq": seq + 1}, device_id_type=MESH)

    before = (seq + count - 1) // count
    after = (2 * count - 2 - seq) // count
    pl.semaphore_wait(barrier, before + after)


def row_mask(mask_ref, seqs, length):
    return jnp.concatenate(
        [jnp.broadcast_to(mask_ref[s : s + 1, :], (length, 128)) for s in range(seqs)], axis=0
    )


def norm(values, gain):
    inverse = lax.rsqrt(jnp.mean(values * values, axis=-1, keepdims=True) + EPS)
    return values * inverse * gain, inverse


def pre_kernel(
    seqs, length, count,
    tok_ref, ids_ref, mask_ref, tb_ref, wi_ref, cw_ref, wo_ref, n1_ref, n2_ref, cot_ref,
    u1_ref, mi_ref, b_ref, c_ref, x_ref, conv_ref, same_ref, gated_ref, mo_ref, h1_ref, u2_ref, mg_ref, mu_ref, gd_ref,
    ext_ref, out_ref, in_ref, send_sem, recv_sem,
):
    seq = lax.axis_index("seq")
    greet(seq, count)
    mask = row_mask(mask_ref, seqs, length)
    twice = 2.0 * mask
    tokens = tok_ref[...].astype(f32)
    u1 = norm(tokens, n1_ref[...])[0].astype(bf16)
    u1_ref[...] = u1
    mid = (dot_nt(u1, tb_ref[:, A_IN : A_IN + D]).astype(bf16).astype(f32) * twice).astype(bf16)
    mi_ref[...] = mid
    for third, to_ref in ((0, b_ref), (2, x_ref)):
        for k in range(2):
            col = third * D + 512 * k
            to_ref[:, 512 * k : 512 * k + 512] = dot(u1, wi_ref[:, col : col + 512]) + dot(
                mid, tb_ref[:, B_IN + col : B_IN + col + 512]
            )
    width = D + 128
    for s in range(seqs):
        rows = pl.ds(s * length, length)
        ext_ref[s, 0:8, :] = jnp.zeros((8, width), f32)
        ext_ref[s, 8:, :D] = b_ref[rows, :] * x_ref[rows, :]
        ext_ref[s, 8:, D:] = jnp.broadcast_to(ids_ref[s : s + 1, :], (length, 128)).T
        out_ref[2 * s : 2 * s + 2, :] = ext_ref[s, length + 6 : length + 8, :]
    along = pltpu.make_async_remote_copy(
        src_ref=out_ref, dst_ref=in_ref, send_sem=send_sem, recv_sem=recv_sem,
        device_id={"seq": seq + 1}, device_id_type=MESH,
    )

    @pl.when(seq < count - 1)
    def _():
        along.start()

    for k in range(2):
        col = D + 512 * k
        c_ref[:, 512 * k : 512 * k + 512] = dot(u1, wi_ref[:, col : col + 512]) + dot(
            mid, tb_ref[:, B_IN + col : B_IN + col + 512]
        )
    gd_ref[...] = (dot_nt(cot_ref[...], tb_ref[:, B_DOWN : B_DOWN + D]) * twice).astype(bf16)

    @pl.when(seq < count - 1)
    def _():
        along.wait_send()

    @pl.when(seq > 0)
    def _():
        along.wait_recv()
        for s in range(seqs):
            ext_ref[s, 6:8, :] = in_ref[2 * s : 2 * s + 2, :]

    for s in range(seqs):
        rows = pl.ds(s * length, length)
        now_ids = ext_ref[s, 8:, D:]
        same1 = jnp.where(ext_ref[s, pl.ds(7, length), D:] == now_ids, 1.0, 0.0)
        same2 = jnp.where(ext_ref[s, pl.ds(6, length), D:] == now_ids, 1.0, 0.0)
        same_ref[0, rows, :] = same1
        same_ref[1, rows, :] = same2
        conv = (
            cw_ref[2:3, :] * ext_ref[s, 8:, :D]
            + cw_ref[1:2, :] * same1[:, :1] * ext_ref[s, pl.ds(7, length), :D]
            + cw_ref[0:1, :] * same2[:, :1] * ext_ref[s, pl.ds(6, length), :D]
        )
        conv_ref[rows, :] = conv
        gated_ref[rows, :] = (c_ref[rows, :] * conv).astype(bf16)
    gated = gated_ref[...]
    mid_out = (dot_nt(gated, tb_ref[:, A_OUT : A_OUT + D]).astype(bf16).astype(f32) * twice).astype(bf16)
    mo_ref[...] = mid_out
    for k in range(2):
        cols = slice(512 * k, 512 * k + 512)
        h1_ref[:, cols] = (
            tok_ref[:, cols].astype(f32)
            + dot(gated, wo_ref[:, cols])
            + dot(mid_out, tb_ref[:, B_OUT + 512 * k : B_OUT + 512 * k + 512])
        )
    u2 = norm(h1_ref[...], n2_ref[...])[0].astype(bf16)
    u2_ref[...] = u2
    mg_ref[...] = (dot_nt(u2, tb_ref[:, A_GATE : A_GATE + D]).astype(bf16).astype(f32) * twice).astype(bf16)
    mu_ref[...] = (dot_nt(u2, tb_ref[:, A_UP : A_UP + D]).astype(bf16).astype(f32) * twice).astype(bf16)


def pre(seqs, length, count, *args):
    rows = seqs * length
    sd = jax.ShapeDtypeStruct
    width = D + 128
    vm = pl.BlockSpec(memory_space=pltpu.VMEM)
    wide = sd((rows, D), f32)
    half = sd((rows, D), bf16)
    thin = sd((rows, 128), bf16)
    return pl.pallas_call(
        functools.partial(pre_kernel, seqs, length, count),
        in_specs=[vm] * 10,
        out_specs=[vm] * 14,
        out_shape=[half, thin, wide, wide, wide, wide, sd((2, rows, 128), f32), half, thin, wide, half, thin, thin, thin],
        scratch_shapes=[
            pltpu.VMEM((seqs, length + 8, width), f32),
            pltpu.VMEM((2 * seqs, width), f32),
            pltpu.VMEM((2 * seqs, width), f32),
            pltpu.SemaphoreType.DMA,
            pltpu.SemaphoreType.DMA,
        ],
        compiler_params=pltpu.CompilerParams(vmem_limit_bytes=60 * MIB, collective_id=0, has_side_effects=True),
    )(*args)


def ffn_kernel(
    seqs, length,
    u_ref, cot_ref, mg_ref, mu_ref, gd_ref, mask_ref, h1_ref, wg_ref, wu_ref, wd_ref, bg_ref, bu_ref, ad_ref, ag_ref, au_ref, bd_ref,
    out_ref, gn_ref, dbg_ref, dbu_ref, dad_ref, dag_ref, dau_ref, dbd_ref,
    acc_ref, dmid_ref, gmg_ref, gmu_ref,
):
    j = pl.program_id(0)

    @pl.when(j == 0)
    def _():
        for ref in (acc_ref, gn_ref, dmid_ref, gmg_ref, gmu_ref):
            ref[...] = jnp.zeros_like(ref)

    u = u_ref[...]
    gate = dot(u, wg_ref[...]) + dot(mg_ref[...], bg_ref[...])
    up = dot(u, wu_ref[...]) + dot(mu_ref[...], bu_ref[...])
    back = dot_nt(cot_ref[...], wd_ref[...]) + dot(gd_ref[...], ad_ref[...])
    sig = jax.nn.sigmoid(gate)
    silu = gate * sig
    hidden = (silu * up).astype(bf16)
    grad_gate = (back * up * sig * (1.0 + gate * (1.0 - sig))).astype(bf16)
    grad_up = (back * silu).astype(bf16)
    acc_ref[...] += dot(hidden, wd_ref[...])
    gn_ref[...] += dot_nt(grad_gate, wg_ref[...]) + dot_nt(grad_up, wu_ref[...])
    dmid_ref[...] += dot_nt(hidden, ad_ref[...])
    gmg_ref[...] += dot_nt(grad_gate, bg_ref[...])
    gmu_ref[...] += dot_nt(grad_up, bu_ref[...])
    dbg_ref[...] = dot_tn(mg_ref[...], grad_gate).astype(bf16)
    dbu_ref[...] = dot_tn(mu_ref[...], grad_up).astype(bf16)
    dad_ref[...] = dot_tn(gd_ref[...], hidden).astype(bf16)

    @pl.when(j == pl.num_programs(0) - 1)
    def _():
        twice = 2.0 * row_mask(mask_ref, seqs, length)
        dmid = (dmid_ref[...].astype(bf16).astype(f32) * twice).astype(bf16)
        out_ref[...] = (h1_ref[...] + acc_ref[...] + dot(dmid, bd_ref[...])).astype(bf16)
        dbd_ref[...] = dot_tn(dmid, cot_ref[...]).astype(bf16)
        gm_gate = (gmg_ref[...] * twice).astype(bf16)
        gm_up = (gmu_ref[...] * twice).astype(bf16)
        gn_ref[...] += dot(gm_gate, ag_ref[...]) + dot(gm_up, au_ref[...])
        dag_ref[...] = dot_tn(gm_gate, u_ref[...]).astype(bf16)
        dau_ref[...] = dot_tn(gm_up, u_ref[...]).astype(bf16)


def ffn(seqs, length, u2, cot, mg, mu, gd, mask, h1, wg, wu, wd, table):
    rows = seqs * length
    sd = jax.ShapeDtypeStruct
    whole = lambda s: pl.BlockSpec(s, lambda j: (0, 0))
    col = lambda h: pl.BlockSpec((h, FB), lambda j: (0, j))
    tab = lambda first: pl.BlockSpec((128, FB), lambda j: (0, first // FB + j))
    fixed = lambda first: pl.BlockSpec((128, D), lambda j: (0, 0))
    cut = lambda first: lax.slice_in_dim(table, first, first + D, axis=1)
    return pl.pallas_call(
        functools.partial(ffn_kernel, seqs, length),
        grid=(FF // FB,),
        in_specs=[whole((rows, D)), whole((rows, D)), whole((rows, 128)), whole((rows, 128)), whole((rows, 128)),
                  whole(mask.shape), whole((rows, D)),
                  col(D), col(D), pl.BlockSpec((FB, D), lambda j: (j, 0)),
                  tab(B_GATE), tab(B_UP), tab(A_DOWN), whole((128, D)), whole((128, D)), whole((128, D))],
        out_specs=[whole((rows, D)), whole((rows, D)), col(128), col(128), col(128),
                   whole((128, D)), whole((128, D)), whole((128, D))],
        out_shape=[sd((rows, D), bf16), sd((rows, D), f32)] + [sd((128, FF), bf16)] * 3 + [sd((128, D), bf16)] * 3,
        scratch_shapes=[pltpu.VMEM((rows, D), f32)] + [pltpu.VMEM((rows, 128), f32)] * 3,
        compiler_params=pltpu.CompilerParams(vmem_limit_bytes=60 * MIB),
    )(u2, cot, mg, mu, gd, mask, h1, wg, wu, wd, table, table, table, cut(A_GATE), cut(A_UP), cut(B_DOWN))


def post_kernel(
    seqs, length, count,
    tok_ref, cot_ref, mask_ref, h1_ref, gn_ref, gated_ref, mo_ref, b_ref, c_ref, x_ref, conv_ref, same_ref, u1_ref, mi_ref,
    tb_ref, wi_ref, cw_ref, wo_ref, n1_ref, n2_ref,
    ig_ref, dai_ref, dbi_ref, dao_ref, dbo_ref,
    gh_ref, gb_ref, gg_ref, gc_ref, gp_ref, one_ref, two_ref, out_ref, in_ref, send_sem, recv_sem,
):
    seq = lax.axis_index("seq")
    greet(seq, count)
    twice = 2.0 * row_mask(mask_ref, seqs, length)
    h1 = h1_ref[...]
    inv2 = norm(h1, n2_ref[...])[1]
    e2 = gn_ref[...] * n2_ref[...]
    gh = cot_ref[...].astype(f32) + inv2 * e2 - h1 * (inv2 * inv2 * inv2 * jnp.mean(h1 * e2, axis=-1, keepdims=True))
    gh_ref[...] = gh
    gb = gh.astype(bf16)
    gb_ref[...] = gb
    gm_out = (dot_nt(gb, tb_ref[:, B_OUT : B_OUT + D]) * twice).astype(bf16)
    for k in range(2):
        cols = slice(512 * k, 512 * k + 512)
        gg_ref[:, cols] = dot_nt(gb, wo_ref[cols, :]) + dot(gm_out, tb_ref[:, A_OUT + 512 * k : A_OUT + 512 * k + 512])
    for s in range(seqs):
        rows = pl.ds(s * length, length)
        gg = gg_ref[rows, :]
        gp_ref[rows, D : 2 * D] = (gg * conv_ref[rows, :]).astype(bf16)
        gconv = gg * c_ref[rows, :]
        gc_ref[rows, :] = gconv
        one_ref[s, 0:length, :] = cw_ref[1:2, :] * same_ref[0, rows, 0:1] * gconv
        two_ref[s, 0:length, :] = cw_ref[0:1, :] * same_ref[1, rows, 0:1] * gconv
        one_ref[s, length:, :] = jnp.zeros((8, D), f32)
        two_ref[s, length:, :] = jnp.zeros((8, D), f32)
        out_ref[2 * s : 2 * s + 1, :] = two_ref[s, 0:1, :]
        out_ref[2 * s + 1 : 2 * s + 2, :] = two_ref[s, 1:2, :] + one_ref[s, 0:1, :]
    along = pltpu.make_async_remote_copy(
        src_ref=out_ref, dst_ref=in_ref, send_sem=send_sem, recv_sem=recv_sem,
        device_id={"seq": seq - 1}, device_id_type=MESH,
    )

    @pl.when(seq > 0)
    def _():
        along.start()

    dbo_ref[...] = dot_tn(mo_ref[...], gb).astype(bf16)
    dao_ref[...] = dot_tn(gm_out, gated_ref[...]).astype(bf16)

    @pl.when(seq > 0)
    def _():
        along.wait_send()

    @pl.when(seq < count - 1)
    def _():
        along.wait_recv()
        for s in range(seqs):
            two_ref[s, length : length + 2, :] = in_ref[2 * s : 2 * s + 2, :]

    for s in range(seqs):
        rows = pl.ds(s * length, length)
        gmix = (
            cw_ref[2:3, :] * gc_ref[rows, :]
            + one_ref[s, pl.ds(1, length), :]
            + two_ref[s, pl.ds(2, length), :]
        )
        gp_ref[rows, 0:D] = (gmix * x_ref[rows, :]).astype(bf16)
        gp_ref[rows, 2 * D :] = (gmix * b_ref[rows, :]).astype(bf16)
    gm_in = (dot_nt(gp_ref[...], tb_ref[:, B_IN : B_IN + 3 * D]) * twice).astype(bf16)
    for k in range(2):
        cols = slice(512 * k, 512 * k + 512)
        gg_ref[:, cols] = dot_nt(gp_ref[...], wi_ref[cols, :]) + dot(gm_in, tb_ref[:, A_IN + 512 * k : A_IN + 512 * k + 512])
    for k in range(6):
        cols = slice(512 * k, 512 * k + 512)
        dbi_ref[:, cols] = dot_tn(mi_ref[...], gp_ref[:, cols]).astype(bf16)
    dai_ref[...] = dot_tn(gm_in, u1_ref[...]).astype(bf16)
    tokens = tok_ref[...].astype(f32)
    inv1 = norm(tokens, n1_ref[...])[1]
    e1 = gg_ref[...] * n1_ref[...]
    ig_ref[...] = (
        gh_ref[...] + inv1 * e1 - tokens * (inv1 * inv1 * inv1 * jnp.mean(tokens * e1, axis=-1, keepdims=True))
    ).astype(bf16)


def post(seqs, length, count, *args):
    rows = seqs * length
    sd = jax.ShapeDtypeStruct
    vm = pl.BlockSpec(memory_space=pltpu.VMEM)
    return pl.pallas_call(
        functools.partial(post_kernel, seqs, length, count),
        in_specs=[vm] * 20,
        out_specs=[vm] * 5,
        out_shape=[sd((rows, D), bf16), sd((128, D), bf16), sd((128, 3 * D), bf16), sd((128, D), bf16), sd((128, D), bf16)],
        scratch_shapes=[
            pltpu.VMEM((rows, D), f32),
            pltpu.VMEM((rows, D), bf16),
            pltpu.VMEM((rows, D), f32),
            pltpu.VMEM((rows, D), f32),
            pltpu.VMEM((rows, 3 * D), bf16),
            pltpu.VMEM((seqs, length + 8, D), f32),
            pltpu.VMEM((seqs, length + 8, D), f32),
            pltpu.VMEM((2 * seqs, D), f32),
            pltpu.VMEM((2 * seqs, D), f32),
            pltpu.SemaphoreType.DMA,
            pltpu.SemaphoreType.DMA,
        ],
        compiler_params=pltpu.CompilerParams(vmem_limit_bytes=62 * MIB, collective_id=1, has_side_effects=True),
    )(*args)


def general_device(
    tokens, segment_ids, adapter_ids, input_weight, conv_weight, output_weight, gate_weight, up_weight, down_weight,
    norm_one, norm_two, cotangent, adapter_state, first_moment, second_moment, rate, step,
):
    seqs, length, _ = tokens.shape
    na = adapter_state.shape[0]
    groups = lax.axis_size("grp")
    count = lax.axis_size("seq")
    native = lambda x: x.reshape(na, PACKROWS, 128).swapaxes(0, 1).reshape(na * PACKROWS, 128)
    st, m, v = native(adapter_state), native(first_moment), native(second_moment)
    own = build_table(st, na)
    table = lax.all_gather(own, "grp", axis=0, tiled=True)
    adapters = na * groups
    mask = (adapter_ids[:, None] == jnp.arange(adapters * RANK, dtype=jnp.int32)[None, :] // RANK).astype(f32)
    ids = segment_ids.astype(f32)
    rows = seqs * length
    tok2, cot2 = tokens.reshape(rows, D), cotangent.reshape(rows, D)
    n1, n2 = norm_one.reshape(1, D), norm_two.reshape(1, D)
    u1, mi, b, c, x, conv, same, gated, mo, h1, u2, mg, mu, gd = pre(
        seqs, length, count, tok2, ids, mask, table, input_weight, conv_weight, output_weight, n1, n2, cot2
    )
    out, gn, dbg, dbu, dad, dag, dau, dbd = ffn(
        seqs, length, u2, cot2, mg, mu, gd, mask, h1, gate_weight, up_weight, down_weight, table
    )
    ig, dai, dbi, dao, dbo = post(
        seqs, length, count, tok2, cot2, mask, h1, gn, gated, mo, b, c, x, conv, same, u1, mi,
        table, input_weight, conv_weight, output_weight, n1, n2,
    )
    grads = jnp.concatenate([dai, dbi, dao, dbo, dag, dbg, dau, dbu, dad, dbd], axis=1).astype(f32)
    owned = lax.psum(lax.psum_scatter(grads, "grp", scatter_dimension=0, tiled=True), "seq")
    correction = 1.0 - jnp.power(jnp.float32(0.5), step[0].astype(f32))
    scal = jnp.stack([rate[0], 1.0 / correction])
    new, tab = adam(scal, owned, st, m, v, na)
    every = lax.all_gather(tab, "grp", axis=0, tiled=False)
    every = every.reshape(groups, PACKROWS, na, 128).transpose(1, 0, 2, 3).reshape(PACKROWS, adapters, 128)
    every = every.swapaxes(0, 1).reshape(adapters, PACKROWS * 128)
    new = new.reshape(PACKROWS, na, 128).swapaxes(0, 1).reshape(na, PACKROWS * 128)
    return out.reshape(tokens.shape), ig.reshape(tokens.shape), new, every


W_A_IN, W_B_B, W_B_X, W_B_C, W_A_OUT, W_B_OUT, W_A_GATE, W_A_UP, W_B_DOWN, W_FFN = (1024 * n for n in range(10))
W_ENDS = W_A_GATE
BLOCKS = FF // FB
W_BLOCK = 3 * FB
FFN_COLS = WIRE - W_ENDS
SPREAD_BLOCKS = 2


def wire(first, n):
    if first == B_IN:
        return (W_B_B, W_B_C, W_B_X)[n // D] + n % D
    for place, matrix in enumerate((B_GATE, B_UP, A_DOWN)):
        if first == matrix:
            return W_FFN + n // FB * W_BLOCK + place * FB + n % FB
    return {A_IN: W_A_IN, A_OUT: W_A_OUT, B_OUT: W_B_OUT, A_GATE: W_A_GATE, A_UP: W_A_UP, B_DOWN: W_B_DOWN}[first] + n


def a_pieces(first, count):
    for matrix, height in A_PARTS:
        if matrix <= first < matrix + height:
            return [(k, wire(matrix, first - matrix + k), FB) for k in range(0, count, FB)]


class Place:
    def __init__(self):
        seq, grp = lax.axis_index("seq"), lax.axis_index("grp")
        self.seq, self.grp = seq, grp
        self.c, self.x, self.y, self.z = grp % 2, grp // 2, seq % 2, seq // 2
        self.core = grp + 1 - 2 * self.c
        self.gx = (grp + 2) % 4
        self.sy = seq + 1 - 2 * self.y
        self.sz = seq + 2 - 4 * (self.z % 2)

    def along_z(self, d):
        return (self.seq + 2 * d) % 8


def announce(seq, count, devices, both=True):
    barrier = pltpu.get_barrier_semaphore()
    if both:

        @pl.when(seq > 0)
        def _():
            pl.semaphore_signal(barrier, inc=1, device_id={"seq": seq - 1}, device_id_type=MESH)

        @pl.when(seq < count - 1)
        def _():
            pl.semaphore_signal(barrier, inc=1, device_id={"seq": seq + 1}, device_id_type=MESH)

    for device in devices:
        pl.semaphore_signal(barrier, inc=1, device_id=device, device_id_type=MESH)
    ends = (seq + count - 1) // count + (2 * count - 2 - seq) // count if both else 0
    return lambda: pl.semaphore_wait(barrier, ends + len(devices))


class Spread:
    KINDS = ("core", "x", "y", "z", "dy", "dz", "cx", "cy", "cz", "cd")

    def __init__(self, at, own, slot, pieces, step, send_sems, recv_sems):
        self.at, self.own, self.slot, self.pieces, self.step = at, own, slot, pieces, step
        self.send_sems, self.recv_sems = send_sems, recv_sems

    def copy(self, kind, p):
        at = self.at
        first, size = self.pieces[p]
        quarter = size // 4
        half = -(-quarter // (2 * self.step)) * self.step
        part = lambda q: pl.multiple_of(first + q * quarter, self.step)
        q = at.seq % 4
        qy, qz, qd = q + 1 - 2 * (q % 2), (q + 2) % 4, 3 - q
        core, y, z = {"grp": at.core}, {"seq": at.sy}, {"seq": at.sz}
        if kind == "core":
            src, dst, device = self.own(first, size), self.slot(at.grp, first, size), core
        elif kind == "x":
            src, dst, device = self.own(part(q), quarter), self.slot(at.grp, part(q), quarter), {"grp": at.gx}
        else:
            start, count, device = {
                "y": (part(q), quarter, y),
                "z": (part(q), quarter, z),
                "dy": (part(qz), half, y),
                "dz": (pl.multiple_of(part(qy) + half, self.step), quarter - half, z),
                "cx": (part(q), quarter, core),
                "cy": (part(qy), quarter, core),
                "cz": (part(qz), quarter, core),
                "cd": (part(qd), quarter, core),
            }[kind]
            src = dst = self.slot(at.gx, start, count)
        n = len(self.KINDS) * p + self.KINDS.index(kind)
        return pltpu.make_async_remote_copy(
            src_ref=src, dst_ref=dst, send_sem=self.send_sems.at[n], recv_sem=self.recv_sems.at[n],
            device_id=device, device_id_type=MESH,
        )

    def leg(self, number, p):
        waits, starts = (
            ((), ("x", "core")),
            (("x",), ("y", "z", "cx")),
            (("y",), ("dz", "cy")),
            (("z",), ("dy", "cz")),
            (("dy", "dz"), ("cd",)),
            (("core", "cx", "cy", "cz", "cd"), ()),
        )[number]
        for kind in waits:
            self.copy(kind, p).wait_recv()
        for kind in starts:
            self.copy(kind, p).start()

    def sent(self, p):
        for kind in self.KINDS:
            self.copy(kind, p).wait_send()


def adapter_mask(adapter_ref, seqs, length):
    column = lax.broadcasted_iota(jnp.int32, (length, 128), 1) // RANK
    return jnp.concatenate([jnp.where(column == adapter_ref[s], 1.0, 0.0) for s in range(seqs)], axis=0)


def fill_shuffle(perm_ref):
    diff = lax.broadcasted_iota(jnp.int32, (128, 1024), 1) - 8 * lax.broadcasted_iota(jnp.int32, (128, 1024), 0)
    for c in range(8):
        perm_ref[128 * c : 128 * c + 128, :] = jnp.where(diff == c, 1.0, 0.0).astype(bf16)


def build_own(na, grp, st_ref, tb_ref, lhs_ref, perm_ref):
    own = lambda a: pl.ds(pl.multiple_of((grp * na + a) * RANK, RANK), RANK)
    fill_shuffle(perm_ref)
    for n, (first, count) in enumerate(A_CHUNKS):
        for a in range(na):
            packed = st_ref[pl.ds(na * (first // 8) + a, 128, stride=na), :]
            turned = packed.T.astype(bf16)
            row = (n * na + a) * RANK
            for c in range(8):
                lhs_ref[row : row + RANK, 128 * c : 128 * c + 128] = turned[RANK * c : RANK * c + RANK, :]
    full = dot(lhs_ref[...], perm_ref[...]).astype(bf16)
    for n, (first, count) in enumerate(A_CHUNKS):
        for a in range(na):
            row = (n * na + a) * RANK
            for k, col, size in a_pieces(first, count):
                tb_ref[own(a), col : col + size] = full[row : row + RANK, k : k + size]
    for first, breadth in B_PARTS:
        blocks = breadth // 128
        for a in range(na):
            for c in range(blocks):
                part = st_ref[pl.ds(na * (first // 8 + c) + a, RANK, stride=na * blocks), :]
                col = wire(first, 128 * c)
                tb_ref[own(a), col : col + 128] = part.astype(bf16)


SPREAD_PIECES = ((0, 4096), (W_A_OUT, 5120), (W_FFN, SPREAD_BLOCKS * W_BLOCK))


def start_kernel(
    seqs, length, count, na,
    adapter_ref, st_ref, tok_ref, ids_ref, wi_hbm, cw_ref, wo_hbm, n1_ref, n2_ref,
    tb_hbm, u1_hbm, mi_ref, b_hbm, c_hbm, x_hbm, conv_hbm, same_hbm, gated_hbm, mo_ref, h1_hbm, u2_hbm, mg_ref, mu_ref,
    tb_ref, lhs_ref, perm_ref, wi_ref, wo_ref, u1_ref, b_ref, c_ref, x_ref, conv_ref, same_ref, gated_ref, h1_ref, u2_ref,
    ext_ref, out_ref, in_ref, halo_sems, load_sems, store_sems, send_sems, recv_sems,
):
    at = Place()
    seq, grp = at.seq, at.grp
    load_in = pltpu.make_async_copy(wi_hbm, wi_ref, load_sems.at[0])
    load_out = pltpu.make_async_copy(wo_hbm, wo_ref, load_sems.at[1])
    load_in.start()
    load_out.start()
    met = announce(seq, count, ({"grp": at.core}, {"grp": at.gx}, {"seq": at.sz}))
    build_own(na, grp, st_ref, tb_ref, lhs_ref, perm_ref)
    height = na * RANK
    block = lambda owner, first, size: tb_ref.at[
        pl.ds(pl.multiple_of(owner * height, height), height), pl.ds(first, size)
    ]
    spread = Spread(at, functools.partial(block, grp), block, SPREAD_PIECES, 128, send_sems, recv_sems)
    leg = spread.leg

    def keep(n, src, dst):
        return pltpu.make_async_copy(src, dst, store_sems.at[n])

    met()
    leg(0, 0)
    twice = 2.0 * adapter_mask(adapter_ref, seqs, length)
    tokens = tok_ref[...].astype(f32)
    u1 = norm(tokens, n1_ref[...])[0].astype(bf16)
    u1_ref[...] = u1
    keep(0, u1_ref, u1_hbm).start()
    load_in.wait()
    for k in range(2):
        b_ref[:, 512 * k : 512 * k + 512] = dot(u1, wi_ref[:, 512 * k : 512 * k + 512])
    leg(1, 0)
    for p in range(1, len(SPREAD_PIECES)):
        leg(0, p)
    for k in range(2):
        x_ref[:, 512 * k : 512 * k + 512] = dot(u1, wi_ref[:, 2 * D + 512 * k : 2 * D + 512 * k + 512])
    leg(1, 1)
    leg(2, 0)
    leg(3, 0)
    for k in range(2):
        c_ref[:, 512 * k : 512 * k + 512] = dot(u1, wi_ref[:, D + 512 * k : D + 512 * k + 512])
    leg(1, 2)
    leg(4, 0)
    leg(5, 0)
    mid = (dot_nt(u1, tb_ref[:, W_A_IN : W_A_IN + D]).astype(bf16).astype(f32) * twice).astype(bf16)
    mi_ref[...] = mid
    for first, to_ref in ((W_B_B, b_ref), (W_B_X, x_ref)):
        for k in range(2):
            col = first + 512 * k
            to_ref[:, 512 * k : 512 * k + 512] += dot(mid, tb_ref[:, col : col + 512])
    leg(2, 1)
    leg(3, 1)
    keep(1, b_ref, b_hbm).start()
    keep(2, x_ref, x_hbm).start()
    width = D + 128
    for s in range(seqs):
        rows = pl.ds(s * length, length)
        ext_ref[s, 0:8, :] = jnp.zeros((8, width), f32)
        ext_ref[s, 8:, :D] = b_ref[rows, :] * x_ref[rows, :]
        ext_ref[s, 8:, D:] = jnp.broadcast_to(ids_ref[s : s + 1, :].astype(f32), (length, 128)).T
        out_ref[2 * s : 2 * s + 2, :] = ext_ref[s, length + 6 : length + 8, :]
    along = pltpu.make_async_remote_copy(
        src_ref=out_ref, dst_ref=in_ref, send_sem=halo_sems.at[0], recv_sem=halo_sems.at[1],
        device_id={"seq": seq + 1}, device_id_type=MESH,
    )

    @pl.when(seq < count - 1)
    def _():
        along.start()

    for k in range(2):
        col = W_B_C + 512 * k
        c_ref[:, 512 * k : 512 * k + 512] += dot(mid, tb_ref[:, col : col + 512])
    keep(3, c_ref, c_hbm).start()
    leg(2, 2)
    leg(3, 2)

    @pl.when(seq < count - 1)
    def _():
        along.wait_send()

    @pl.when(seq > 0)
    def _():
        along.wait_recv()
        for s in range(seqs):
            ext_ref[s, 6:8, :] = in_ref[2 * s : 2 * s + 2, :]

    for s in range(seqs):
        rows = pl.ds(s * length, length)
        now_ids = ext_ref[s, 8:, D:]
        same1 = jnp.where(ext_ref[s, pl.ds(7, length), D:] == now_ids, 1.0, 0.0)
        same2 = jnp.where(ext_ref[s, pl.ds(6, length), D:] == now_ids, 1.0, 0.0)
        same_ref[0, rows, :] = same1
        same_ref[1, rows, :] = same2
        conv = (
            cw_ref[2:3, :] * ext_ref[s, 8:, :D]
            + cw_ref[1:2, :] * same1[:, :1] * ext_ref[s, pl.ds(7, length), :D]
            + cw_ref[0:1, :] * same2[:, :1] * ext_ref[s, pl.ds(6, length), :D]
        )
        conv_ref[rows, :] = conv
        gated_ref[rows, :] = (c_ref[rows, :] * conv).astype(bf16)
    keep(4, conv_ref, conv_hbm).start()
    keep(5, same_ref, same_hbm).start()
    leg(4, 1)
    leg(4, 2)
    keep(6, gated_ref, gated_hbm).start()
    gated = gated_ref[...]
    load_out.wait()
    for k in range(2):
        cols = slice(512 * k, 512 * k + 512)
        h1_ref[:, cols] = tok_ref[:, cols].astype(f32) + dot(gated, wo_ref[:, cols])
    leg(5, 1)
    mid_out = (dot_nt(gated, tb_ref[:, W_A_OUT : W_A_OUT + D]).astype(bf16).astype(f32) * twice).astype(bf16)
    mo_ref[...] = mid_out
    for k in range(2):
        cols = slice(512 * k, 512 * k + 512)
        h1_ref[:, cols] += dot(mid_out, tb_ref[:, W_B_OUT + 512 * k : W_B_OUT + 512 * k + 512])
    keep(7, h1_ref, h1_hbm).start()
    u2 = norm(h1_ref[...], n2_ref[...])[0].astype(bf16)
    u2_ref[...] = u2
    keep(8, u2_ref, u2_hbm).start()
    keep(9, tb_ref.at[:, :W_FFN], tb_hbm.at[:, :W_FFN]).start()
    mg_ref[...] = (dot_nt(u2, tb_ref[:, W_A_GATE : W_A_GATE + D]).astype(bf16).astype(f32) * twice).astype(bf16)
    mu_ref[...] = (dot_nt(u2, tb_ref[:, W_A_UP : W_A_UP + D]).astype(bf16).astype(f32) * twice).astype(bf16)
    leg(5, 2)
    keep(10, tb_ref.at[:, W_FFN:], tb_hbm.at[:, W_FFN:]).start()
    for p in range(len(SPREAD_PIECES)):
        spread.sent(p)
    for n, (src, dst) in enumerate((
        (u1_ref, u1_hbm), (b_ref, b_hbm), (x_ref, x_hbm), (c_ref, c_hbm), (conv_ref, conv_hbm), (same_ref, same_hbm),
        (gated_ref, gated_hbm), (h1_ref, h1_hbm), (u2_ref, u2_hbm),
        (tb_ref.at[:, :W_FFN], tb_hbm.at[:, :W_FFN]), (tb_ref.at[:, W_FFN:], tb_hbm.at[:, W_FFN:]),
    )):
        keep(n, src, dst).wait()


def start(seqs, length, count, na, *args):
    rows = seqs * length
    sd = jax.ShapeDtypeStruct
    width = D + 128
    vm = pl.BlockSpec(memory_space=pltpu.VMEM)
    hbm = pl.BlockSpec(memory_space=pl.ANY)
    table = sd((128, WIRE), bf16)
    wide = sd((rows, D), f32)
    half = sd((rows, D), bf16)
    thin = sd((rows, 128), bf16)
    same = sd((2, rows, 128), f32)
    scratch = lambda x: pltpu.VMEM(x.shape, x.dtype)
    return pl.pallas_call(
        functools.partial(start_kernel, seqs, length, count, na),
        in_specs=[pl.BlockSpec(memory_space=pltpu.SMEM), vm, vm, vm, hbm, vm, hbm, vm, vm],
        out_specs=[hbm, hbm, vm, hbm, hbm, hbm, hbm, hbm, hbm, vm, hbm, hbm, vm, vm],
        out_shape=[table, half, thin, wide, wide, wide, wide, same, half, thin, wide, half, thin, thin],
        scratch_shapes=[
            scratch(table),
            pltpu.VMEM((len(A_CHUNKS) * na * RANK, 1024), bf16),
            pltpu.VMEM((1024, 1024), bf16),
            pltpu.VMEM((D, 3 * D), bf16),
            pltpu.VMEM((D, D), bf16),
            scratch(half), scratch(wide), scratch(wide), scratch(wide), scratch(wide), scratch(same), scratch(half),
            scratch(wide), scratch(half),
            pltpu.VMEM((seqs, length + 8, width), f32),
            pltpu.VMEM((2 * seqs, width), f32),
            pltpu.VMEM((2 * seqs, width), f32),
            pltpu.SemaphoreType.DMA((2,)),
            pltpu.SemaphoreType.DMA((2,)),
            pltpu.SemaphoreType.DMA((11,)),
            pltpu.SemaphoreType.DMA((len(Spread.KINDS) * len(SPREAD_PIECES),)),
            pltpu.SemaphoreType.DMA((len(Spread.KINDS) * len(SPREAD_PIECES),)),
        ],
        compiler_params=pltpu.CompilerParams(vmem_limit_bytes=60 * MIB, collective_id=2, has_side_effects=True),
    )(*args)


class Sums:
    CORE, X, Y, Z, BACK_Z, BACK_Y = range(6)
    COPIES = 10

    def __init__(self, at, g_ref, cr_ref, xr_ref, yr_ref, zr_ref, sum_ref, send_sems, recv_sems):
        self.at, self.g, self.cr, self.xr, self.yr, self.zr, self.sum = at, g_ref, cr_ref, xr_ref, yr_ref, zr_ref, sum_ref
        self.send_sems, self.recv_sems = send_sems, recv_sems

    def unit(self, z, start, size):
        rows = pl.ds(pl.multiple_of(RANK * (z // 2), RANK), RANK)
        quarter = size // 4
        return rows, pl.ds(pl.multiple_of(start + self.at.y * (size // 2) + (z % 2) * quarter, 128), quarter)

    def half(self, y, start, size):
        return pl.ds(pl.multiple_of(start + y * (size // 2), 128), size // 2)

    def slot(self, start, size, share):
        return pl.ds(pl.multiple_of(start // share, 128), size // share)

    def copies(self, stage, group):
        index, start, size = group
        at = self.at
        cols = pl.ds(start, size)
        if stage == self.CORE:
            parts = [(self.g.at[:, 1 - at.c, :, cols], self.cr.at[:, :, cols], {"grp": at.core})]
        elif stage == self.X:
            parts = [(self.g.at[1 - at.x, at.c, :, cols], self.xr.at[:, cols], {"grp": at.gx})]
        elif stage == self.Y:
            away = self.half(1 - at.y, start, size)
            parts = [(self.g.at[at.x, at.c, :, away], self.yr.at[:, self.slot(start, size, 2)], {"seq": at.sy})]
        elif stage == self.BACK_Y:
            part = self.sum.at[:, self.half(at.y, start, size)]
            parts = [(part, part, {"seq": at.sy})]
        else:
            parts = []
            for d in range(1, 4):
                if stage == self.Z:
                    rows, span = self.unit((at.z + d) % 4, start, size)
                    parts.append((
                        self.g.at[at.x, at.c, rows, span], self.zr.at[d - 1, :, self.slot(start, size, 4)],
                        {"seq": at.along_z(d)},
                    ))
                else:
                    rows, span = self.unit(at.z, start, size)
                    part = self.sum.at[rows, span]
                    parts.append((part, part, {"seq": at.along_z(d)}))
        first = self.COPIES * index + {self.CORE: 0, self.X: 1, self.Y: 2, self.Z: 3, self.BACK_Z: 6, self.BACK_Y: 9}[stage]
        return [
            pltpu.make_async_remote_copy(
                src_ref=src, dst_ref=dst, send_sem=self.send_sems.at[first + n], recv_sem=self.recv_sems.at[first + n],
                device_id=device, device_id_type=MESH,
            )
            for n, (src, dst, device) in enumerate(parts)
        ]

    def send(self, stage, group):
        for copy in self.copies(stage, group):
            copy.start()

    def take(self, stage, group):
        for copy in self.copies(stage, group):
            copy.wait()
        _, start, size = group
        at = self.at
        cols = pl.ds(start, size)
        wide = lambda value: value.astype(f32)
        if stage == self.CORE:
            for x in range(2):
                self.g[x, at.c, :, cols] = (wide(self.g[x, at.c, :, cols]) + wide(self.cr[x, :, cols])).astype(bf16)
        elif stage == self.X:
            self.g[at.x, at.c, :, cols] = (wide(self.g[at.x, at.c, :, cols]) + wide(self.xr[:, cols])).astype(bf16)
        elif stage == self.Y:
            mine = self.half(at.y, start, size)
            came = self.yr[:, self.slot(start, size, 2)]
            self.g[at.x, at.c, :, mine] = (wide(self.g[at.x, at.c, :, mine]) + wide(came)).astype(bf16)
        elif stage == self.Z:
            rows, span = self.unit(at.z, start, size)
            total = wide(self.g[at.x, at.c, rows, span])
            for d in range(3):
                total = total + wide(self.zr[d, :, self.slot(start, size, 4)])
            self.sum[rows, span] = total.astype(bf16)


def sums_scratch(cols):
    return [
        pltpu.VMEM((2, 2, 32, cols), bf16),
        pltpu.VMEM((2, 32, cols), bf16),
        pltpu.VMEM((32, cols), bf16),
        pltpu.VMEM((32, cols // 2), bf16),
        pltpu.VMEM((3, 16, cols // 4), bf16),
        pltpu.VMEM((32, cols), bf16),
    ]


def put_grad(g_ref, cols, value):
    for x in range(2):
        for c in range(2):
            first = 64 * x + 32 * c
            g_ref[x, c, :, cols] = value[first : first + 32, :].astype(bf16)


UPDATES = (
    (B_GATE, FF), (B_UP, FF), (A_DOWN, FF), (A_GATE, D), (A_UP, D), (B_DOWN, D), (A_OUT, 2 * D), (A_IN, 4 * D),
)
MOST = 2 * FF // 8
NATIVE = tuple((2 * first // 8, 2 * count // 8) for first, count in UPDATES)


def update_grad(na, part, sum_ref, lhs_ref, perm_ref, gn_ref):
    first, count = UPDATES[part]
    begin = na * first // 8
    inside = lambda start: first <= start < first + count
    chunks = [chunk for chunk in A_CHUNKS if inside(chunk[0])]
    for n, (start, size) in enumerate(chunks):
        for a in range(na):
            row = (n * na + a) * RANK
            if size < 1024:
                lhs_ref[row : row + RANK, size:] = jnp.zeros((RANK, 1024 - size), bf16)
            for k, col, breadth in a_pieces(start, size):
                lhs_ref[row : row + RANK, k : k + breadth] = sum_ref[a * RANK : (a + 1) * RANK, col : col + breadth]
    if chunks:
        height = len(chunks) * na * RANK
        full = dot_nt(lhs_ref[:height, :], perm_ref[...])
    for n, (start, size) in enumerate(chunks):
        for a in range(na):
            row = (n * na + a) * RANK
            turned = jnp.concatenate([full[row : row + RANK, 128 * c : 128 * c + 128] for c in range(8)], axis=0)
            gn_ref[pl.ds(na * (start // 8) + a - begin, size // 8, stride=na), :] = turned.T[: size // 8]
    for start, breadth in B_PARTS:
        if inside(start):
            blocks = breadth // 128
            for a in range(na):
                for c in range(blocks):
                    col = wire(start, 128 * c)
                    gn_ref[pl.ds(na * (start // 8 + c) + a - begin, RANK, stride=na * blocks), :] = sum_ref[
                        a * RANK : (a + 1) * RANK, col : col + 128
                    ].astype(f32)


def group_of(j):
    start = W_FFN + j * W_BLOCK
    return j, start if isinstance(j, int) else pl.multiple_of(start, 128), W_BLOCK


GROUPS = {
    "ends": (BLOCKS, W_ENDS, W_FFN - W_ENDS),
    "out": (BLOCKS + 1, W_B_C, W_ENDS - W_B_C),
    "in": (BLOCKS + 2, 0, W_B_C),
}
GROUPS.update({j: group_of(j) for j in range(BLOCKS)})


def rest_kernel(
    seqs, length, count, na,
    adapter_ref, rate_ref, step_ref, u_ref, cot_ref, mg_ref, mu_ref, mo_ref, mi_ref, cw_ref, n1_ref, n2_ref,
    h1_hbm, wg_hbm, wu_hbm, wd_hbm, tb_hbm,
    tok_hbm, gated_hbm, b_hbm, c_hbm, x_hbm, conv_hbm, same_hbm, u1_hbm, wi_hbm, wo_hbm, st_hbm, m_hbm, v_hbm,
    out_ref, ig_ref, new_hbm, all_hbm, hid_hbm,
    tb_ref, h1_ref, gn_ref, gh_ref, gb_ref, dmid_ref, gmg_ref, gmu_ref, gd_ref,
    edge_out_ref, edge_in_ref, g_ref, cr_ref, xr_ref, yr_ref, zr_ref, sum_ref, tab_ref,
    load_sems, weight_sems, hid_sems, tab_send, tab_recv, send_sems, recv_sems,
    halo_sems, old_sems, new_sems, own_sems, spread_send, spread_recv,
):
    rows_all = seqs * length
    at = Place()
    seq = at.seq
    met = announce(seq, count, [{"grp": at.core}, {"grp": at.gx}] + [{"seq": at.along_z(d)} for d in range(1, 4)])
    sums = Sums(at, g_ref, cr_ref, xr_ref, yr_ref, zr_ref, sum_ref, send_sems, recv_sems)
    here = W_FFN + SPREAD_BLOCKS * W_BLOCK
    rows32 = lambda owner: pl.ds(pl.multiple_of(owner * 32, 32), 32)
    loads = [
        pltpu.make_async_copy(tb_hbm.at[:, :here], tb_ref.at[:, :here], load_sems.at[0]),
        pltpu.make_async_copy(tb_hbm.at[rows32(at.grp), here:], tb_ref.at[rows32(at.grp), here:], load_sems.at[1]),
        pltpu.make_async_copy(h1_hbm, h1_ref, load_sems.at[2]),
    ]
    twice = 2.0 * adapter_mask(adapter_ref, seqs, length)

    def table_copy(kind, j):
        _, start, size = group_of(j)
        owner, device = {
            "core": (at.grp, {"grp": at.core}), "x": (at.grp, {"grp": at.gx}), "far": (at.gx, {"grp": at.core})
        }[kind]
        part = tb_ref.at[rows32(owner), pl.ds(start, size)]
        n = 3 * j + ("core", "x", "far").index(kind)
        return pltpu.make_async_remote_copy(
            src_ref=part, dst_ref=part, send_sem=tab_send.at[n], recv_sem=tab_recv.at[n], device_id=device, device_id_type=MESH
        )

    def when(first, j, last, run):
        @pl.when((j >= first) & (j <= last))
        def _():
            run()

    def feed_forward(wg_ref, wu_ref, wd_ref, hid_ref):
        def fetch(j, slot):
            cols = pl.ds(j * FB if isinstance(j, int) else pl.multiple_of(j * FB, FB), FB)
            return [
                pltpu.make_async_copy(wg_hbm.at[:, cols], wg_ref.at[slot], weight_sems.at[slot, 0]),
                pltpu.make_async_copy(wu_hbm.at[:, cols], wu_ref.at[slot], weight_sems.at[slot, 1]),
                pltpu.make_async_copy(wd_hbm.at[cols, :], wd_ref.at[slot], weight_sems.at[slot, 2]),
            ]

        def keep(j, slot):
            cols = pl.ds(j * FB if isinstance(j, int) else pl.multiple_of(j * FB, FB), FB)
            return pltpu.make_async_copy(hid_ref.at[slot], hid_hbm.at[:, cols], hid_sems.at[slot])

        loads[0].start()
        for copy in fetch(0, 0):
            copy.start()
        loads[1].start()
        loads[2].start()
        for ref in (gn_ref, dmid_ref, gmg_ref, gmu_ref):
            ref[...] = jnp.zeros_like(ref)
        loads[0].wait()
        gd_ref[...] = (dot_nt(cot_ref[...], tb_ref[:, W_B_DOWN : W_B_DOWN + D]) * twice).astype(bf16)
        loads[1].wait()
        met()

        def block(j, carry):
            slot = j % 2
            for copy in fetch(j, slot):
                copy.wait()

            def more():
                for copy in fetch(j + 1, 1 - slot):
                    copy.start()

            when(0, j, BLOCKS - 2, more)
            when(2, j, BLOCKS - 1, lambda: keep(j - 2, slot).wait())
            lead = SPREAD_BLOCKS

            def leave():
                table_copy("x", j + lead).start()
                table_copy("core", j + lead).start()

            def go_on():
                table_copy("x", j + lead - 1).wait()
                table_copy("far", j + lead - 1).start()

            def there():
                table_copy("core", j).wait()
                table_copy("far", j).wait()

            when(0, j, BLOCKS - 1 - lead, leave)
            when(1, j, BLOCKS - lead, go_on)
            when(lead, j, BLOCKS - 1, there)
            for stage in range(6):

                def advance(stage=stage):
                    if stage > 0:
                        sums.take(stage - 1, group_of(j - 1 - stage))
                    sums.send(stage, group_of(j - 1 - stage))

                when(1 + stage, j, BLOCKS - 1, advance)
            when(7, j, BLOCKS - 1, lambda: sums.take(5, group_of(j - 7)))

            base = W_FFN + j * W_BLOCK
            part = lambda place: pl.ds(pl.multiple_of(base + place * FB, 128), FB)
            tab_gate, tab_up, tab_down = (tb_ref.at[:, part(place)] for place in range(3))
            u = u_ref[...]
            gate = dot(u, wg_ref[slot]) + dot(mg_ref[...], tab_gate[...])
            up = dot(u, wu_ref[slot]) + dot(mu_ref[...], tab_up[...])
            back = dot_nt(cot_ref[...], wd_ref[slot]) + dot(gd_ref[...], tab_down[...])
            sig = jax.nn.sigmoid(gate)
            silu = gate * sig
            hidden = (silu * up).astype(bf16)
            hid_ref[slot] = hidden
            keep(j, slot).start()
            grad_gate = (back * up * sig * (1.0 + gate * (1.0 - sig))).astype(bf16)
            grad_up = (back * silu).astype(bf16)
            gn_ref[...] += dot_nt(grad_gate, wg_ref[slot]) + dot_nt(grad_up, wu_ref[slot])
            dmid_ref[...] += dot_nt(hidden, tab_down[...])
            gmg_ref[...] += dot_nt(grad_gate, tab_gate[...])
            gmu_ref[...] += dot_nt(grad_up, tab_up[...])
            put_grad(g_ref, part(0), dot_tn(mg_ref[...], grad_gate))
            put_grad(g_ref, part(1), dot_tn(mu_ref[...], grad_up))
            put_grad(g_ref, part(2), dot_tn(gd_ref[...], hidden))
            return carry

        lax.fori_loop(0, BLOCKS, block, 0)
        for j in range(BLOCKS - 2, BLOCKS):
            keep(j, j % 2).wait()

    pl.run_scoped(
        feed_forward,
        pltpu.VMEM((2, D, FB), bf16), pltpu.VMEM((2, D, FB), bf16), pltpu.VMEM((2, FB, D), bf16),
        pltpu.VMEM((2, rows_all, FB), bf16),
    )

    sent = {BLOCKS - 2 - stage: stage for stage in range(6)}

    def advance(*names):
        for name in names:
            stage = sent.get(name, -1)
            if stage >= 0:
                sums.take(stage, GROUPS[name])
            if stage < 5:
                sums.send(stage + 1, GROUPS[name])
            sent[name] = stage + 1

    dmid = (dmid_ref[...].astype(bf16).astype(f32) * twice).astype(bf16)

    def backward(gated_ref, one_ref, two_ref, same_ref, u1_ref, tok_ref, wi_ref, wo_ref, gg_ref, gp_ref):
        pairs = (
            (wo_hbm, wo_ref), (c_hbm, one_ref), (conv_hbm, two_ref), (same_hbm, same_ref.at[:, :, :length, :]),
            (gated_hbm, gated_ref), (wi_hbm, wi_ref), (u1_hbm, u1_ref), (tok_hbm, tok_ref), (x_hbm, one_ref), (b_hbm, two_ref),
        )
        copies = [pltpu.make_async_copy(*pair, load_sems.at[3 + n]) for n, pair in enumerate(pairs)]
        get_wo, get_c, get_conv, get_same, get_gated, get_wi, get_u1, get_tok, get_x, get_b = copies
        for copy in (get_wo, get_c, get_conv, get_same):
            copy.start()
        advance(8, 7, 6, 5, 4, 3, 2)
        gm_gate = (gmg_ref[...] * twice).astype(bf16)
        gm_up = (gmu_ref[...] * twice).astype(bf16)
        put_grad(g_ref, slice(W_A_GATE, W_A_GATE + D), dot_tn(gm_gate, u_ref[...]))
        put_grad(g_ref, slice(W_A_UP, W_A_UP + D), dot_tn(gm_up, u_ref[...]))
        put_grad(g_ref, slice(W_B_DOWN, W_B_DOWN + D), dot_tn(dmid, cot_ref[...]))
        advance("ends", 3)
        for k in range(2):
            cols = slice(512 * k, 512 * k + 512)
            gn_ref[:, cols] += dot(gm_gate, tb_ref[:, W_A_GATE + 512 * k : W_A_GATE + 512 * k + 512]) + dot(
                gm_up, tb_ref[:, W_A_UP + 512 * k : W_A_UP + 512 * k + 512]
            )
        loads[2].wait()
        for s in range(seqs):
            rows = pl.ds(s * length, length)
            h1 = h1_ref[rows, :]
            inv2 = norm(h1, n2_ref[...])[1]
            e2 = gn_ref[rows, :] * n2_ref[...]
            gh = cot_ref[rows, :].astype(f32) + inv2 * e2
            gh = gh - h1 * (inv2 * inv2 * inv2 * jnp.mean(h1 * e2, axis=-1, keepdims=True))
            gh_ref[rows, :] = gh
            gb_ref[rows, :] = gh.astype(bf16)
        for copy in (get_gated, get_wi, get_u1, get_tok):
            copy.start()
        advance(8, 7, 6, 5, 4)
        advance("ends")
        get_wo.wait()
        gb = gb_ref[...]
        gm_out = (dot_nt(gb, tb_ref[:, W_B_OUT : W_B_OUT + D]) * twice).astype(bf16)
        for k in range(2):
            cols = slice(512 * k, 512 * k + 512)
            part = dot_nt(gb, wo_ref[cols, :]) + dot(gm_out, tb_ref[:, W_A_OUT + 512 * k : W_A_OUT + 512 * k + 512])
            for s in range(seqs):
                gg_ref[s, :length, cols] = part[s * length : (s + 1) * length, :]
        advance(8, 7, 6, 5, 4)
        for copy in (get_c, get_conv, get_same):
            copy.wait()
        for s in range(seqs):
            rows = pl.ds(s * length, length)
            gg = gg_ref[s, :length, :]
            gp_ref[rows, D : 2 * D] = (gg * two_ref[rows, :]).astype(bf16)
            gg_ref[s, :length, :] = gg * one_ref[rows, :]
            gg_ref[s, length:, :] = jnp.zeros((8, D), f32)
            for k in range(2):
                same_ref[k, s, length:, :] = jnp.zeros((8, 128), f32)
            edge_out_ref[2 * s : 2 * s + 1, :] = cw_ref[0:1, :] * same_ref[1, s, 0:1, 0:1] * gg_ref[s, 0:1, :]
            edge_out_ref[2 * s + 1 : 2 * s + 2, :] = (
                cw_ref[0:1, :] * same_ref[1, s, 1:2, 0:1] * gg_ref[s, 1:2, :]
                + cw_ref[1:2, :] * same_ref[0, s, 0:1, 0:1] * gg_ref[s, 0:1, :]
            )
        get_x.start()
        get_b.start()
        along = pltpu.make_async_remote_copy(
            src_ref=edge_out_ref, dst_ref=edge_in_ref, send_sem=halo_sems.at[0], recv_sem=halo_sems.at[1],
            device_id={"seq": seq - 1}, device_id_type=MESH,
        )

        @pl.when(seq > 0)
        def _():
            along.start()

        get_gated.wait()
        put_grad(g_ref, slice(W_A_OUT, W_A_OUT + D), dot_tn(gm_out, gated_ref[...]))
        put_grad(g_ref, slice(W_B_OUT, W_B_OUT + D), dot_tn(mo_ref[...], gb))
        put_grad(g_ref, slice(W_B_C, W_B_C + D), dot_tn(mi_ref[...], gp_ref[:, D : 2 * D]))
        advance("out", 8, 7, 6, 5)

        @pl.when(seq > 0)
        def _():
            along.wait_send()

        @pl.when(seq < count - 1)
        def _():
            along.wait_recv()

        get_x.wait()
        get_b.wait()
        for s in range(seqs):
            one, two = pl.ds(1, length), pl.ds(2, length)
            gg_ref[s, :length, :] = (
                cw_ref[2:3, :] * gg_ref[s, :length, :]
                + cw_ref[1:2, :] * same_ref[0, s, one, 0:1] * gg_ref[s, one, :]
                + cw_ref[0:1, :] * same_ref[1, s, two, 0:1] * gg_ref[s, two, :]
            )

        @pl.when(seq < count - 1)
        def _():
            for s in range(seqs):
                gg_ref[s, length - 2 : length, :] += edge_in_ref[2 * s : 2 * s + 2, :]

        for s in range(seqs):
            rows = pl.ds(s * length, length)
            gmix = gg_ref[s, :length, :]
            gp_ref[rows, 0:D] = (gmix * one_ref[rows, :]).astype(bf16)
            gp_ref[rows, 2 * D :] = (gmix * two_ref[rows, :]).astype(bf16)
        advance("ends", "out", 8, 7, 6)
        gm_in = dot_nt(gp_ref[:, :D], tb_ref[:, W_B_B : W_B_B + D])
        gm_in += dot_nt(gp_ref[:, D : 2 * D], tb_ref[:, W_B_C : W_B_C + D])
        gm_in += dot_nt(gp_ref[:, 2 * D :], tb_ref[:, W_B_X : W_B_X + D])
        gm_in = (gm_in * twice).astype(bf16)
        get_u1.wait()
        put_grad(g_ref, slice(W_B_B, W_B_B + D), dot_tn(mi_ref[...], gp_ref[:, :D]))
        put_grad(g_ref, slice(W_B_X, W_B_X + D), dot_tn(mi_ref[...], gp_ref[:, 2 * D :]))
        put_grad(g_ref, slice(W_A_IN, W_A_IN + D), dot_tn(gm_in, u1_ref[...]))
        advance("in", "ends", 8, 7)
        get_wi.wait()
        for k in range(4):
            cols = slice(256 * k, 256 * k + 256)
            gn_ref[:, cols] = dot_nt(gp_ref[...], wi_ref[cols, :]) + dot(
                gm_in, tb_ref[:, W_A_IN + 256 * k : W_A_IN + 256 * k + 256]
            )
            if k == 1:
                advance("in", "out")
        get_tok.wait()
        for s in range(seqs):
            rows = pl.ds(s * length, length)
            tokens = tok_ref[rows, :].astype(f32)
            inv1 = norm(tokens, n1_ref[...])[1]
            e1 = gn_ref[rows, :] * n1_ref[...]
            ig = gh_ref[rows, :] + inv1 * e1
            ig_ref[rows, :] = (
                ig - tokens * (inv1 * inv1 * inv1 * jnp.mean(tokens * e1, axis=-1, keepdims=True))
            ).astype(bf16)

    wide = pltpu.VMEM((rows_all, D), f32)
    half = pltpu.VMEM((rows_all, D), bf16)
    pl.run_scoped(
        backward,
        half, wide, wide, pltpu.VMEM((2, seqs, length + 8, 128), f32), half, half,
        pltpu.VMEM((D, 3 * D), bf16), pltpu.VMEM((D, D), bf16), pltpu.VMEM((seqs, length + 8, D), f32),
        pltpu.VMEM((rows_all, 3 * D), bf16),
    )

    def updates(lhs_ref, perm_ref, old_ref, grad_ref, new_ref, wd_ref, hid_ref):
        own = lambda first, size: tab_ref.at[pl.ds(first, size), :]
        slot_of = lambda owner, first, size: all_hbm.at[owner, pl.ds(first, size), :]
        spread = Spread(at, own, slot_of, NATIVE, 16, spread_send, spread_recv)
        order = (0, 1, 2, 3, 4, 5, 6, 7)
        going = {}

        def pass_on(*parts):
            for part in parts:
                spread.leg(going[part], part)
                going[part] += 1

        power = jnp.float32(1.0)
        for bit in range(8):
            power = power * jnp.where((step_ref[0] >> bit) % 2 == 1, jnp.float32(0.5 ** (2**bit)), jnp.float32(1.0))
        rate = rate_ref[0]
        correction = 1.0 - jnp.full((8, 128), power, f32)
        inv = (1.0 / correction)[0:1, :]

        def old(part):
            first, size = NATIVE[part]
            slot = part % 2
            return [
                pltpu.make_async_copy(ref.at[first : first + size], old_ref.at[slot, n, :size], old_sems.at[slot, n])
                for n, ref in enumerate((st_hbm, m_hbm, v_hbm))
            ]

        def new_copy(part):
            first, size = NATIVE[part]
            return pltpu.make_async_copy(new_ref.at[part % 2, :size], new_hbm.at[first : first + size], new_sems.at[part % 2])

        def own_copy(part):
            first, size = NATIVE[part]
            return pltpu.make_async_copy(
                tab_ref.at[first : first + size], all_hbm.at[at.grp, first : first + size], own_sems.at[part]
            )

        def update(part):
            first, size = NATIVE[part]
            slot = part % 2
            update_grad(na, part, sum_ref, lhs_ref, perm_ref, grad_ref)
            for copy in old(part):
                copy.wait()
            if part >= 2:
                new_copy(part - 2).wait()
            grad = grad_ref[:size]
            one = 0.5 * old_ref[slot, 1, :size] + 0.5 * grad
            two = 0.5 * old_ref[slot, 2, :size] + 0.5 * grad * grad
            new = old_ref[slot, 0, :size] - rate * (one * inv) / (jnp.sqrt(two * inv) + 1e-08)
            new_ref[slot, :size] = new
            tab_ref[first : first + size] = new.astype(bf16)
            new_copy(part).start()
            own_copy(part).start()
            if part + 2 < len(NATIVE):
                for copy in old(part + 2):
                    copy.start()
            going[part] = 0
            pass_on(part)

        def fetch(j):
            slot = j % 2
            return [
                pltpu.make_async_copy(wd_hbm.at[j * FB : (j + 1) * FB, :], wd_ref.at[slot], weight_sems.at[slot, 0]),
                pltpu.make_async_copy(hid_hbm.at[:, j * FB : (j + 1) * FB], hid_ref.at[slot], weight_sems.at[slot, 1]),
            ]

        def outputs(*blocks):
            for j in blocks:
                for copy in fetch(j):
                    copy.wait()
                h1_ref[...] += dot(hid_ref[j % 2], wd_ref[j % 2])
                if j + 2 < BLOCKS:
                    for copy in fetch(j + 2):
                        copy.start()

        for part in range(2):
            for copy in old(part):
                copy.start()
        for j in range(2):
            for copy in fetch(j):
                copy.start()
        fill_shuffle(perm_ref)
        for k in range(2):
            cols = slice(512 * k, 512 * k + 512)
            h1_ref[:, cols] += dot(dmid, tb_ref[:, W_B_DOWN + 512 * k : W_B_DOWN + 512 * k + 512])
        advance("ends", "out", 8)
        update(0)
        advance("in")
        update(1)
        advance("ends")
        pass_on(0)
        outputs(0)
        update(2)
        advance("in", "out")
        pass_on(0, 1)
        outputs(1, 2)
        advance("ends")
        update(3)
        pass_on(0, 1, 2)
        update(4)
        advance("in", "out")
        update(5)
        pass_on(0, 1, 2, 3)
        outputs(3, 4)
        pass_on(0, 1, 2, 3, 4, 5)
        advance("out")
        update(6)
        advance("in")
        pass_on(1, 2, 3, 4, 5)
        outputs(5, 6)
        pass_on(2, 3, 4, 5, 6)
        outputs(7, 8)
        advance("in")
        update(7)
        while any(leg < 6 for leg in going.values()):
            pass_on(*[part for part in order if going[part] < 6])
        out_ref[...] = h1_ref[...].astype(bf16)
        for part in range(len(NATIVE)):
            spread.sent(part)
            own_copy(part).wait()
        for part in range(len(NATIVE) - 2, len(NATIVE)):
            new_copy(part).wait()

    pl.run_scoped(
        updates,
        pltpu.VMEM((5 * na * RANK, 1024), bf16), pltpu.VMEM((1024, 1024), bf16),
        pltpu.VMEM((2, 3, MOST, 128), f32), pltpu.VMEM((MOST, 128), f32), pltpu.VMEM((2, MOST, 128), f32),
        pltpu.VMEM((2, FB, D), bf16), pltpu.VMEM((2, rows_all, FB), bf16),
    )


def rest(seqs, length, count, na, *args):
    rows = seqs * length
    sd = jax.ShapeDtypeStruct
    sm = pl.BlockSpec(memory_space=pltpu.SMEM)
    vm = pl.BlockSpec(memory_space=pltpu.VMEM)
    hbm = pl.BlockSpec(memory_space=pl.ANY)
    wide = pltpu.VMEM((rows, D), f32)
    thin = pltpu.VMEM((rows, 128), f32)
    parts = len(NATIVE)
    dma = lambda *shape: pltpu.SemaphoreType.DMA(shape)
    return pl.pallas_call(
        functools.partial(rest_kernel, seqs, length, count, na),
        in_specs=[sm] * 3 + [vm] * 9 + [hbm] * 18,
        out_specs=[vm, vm, hbm, hbm, hbm],
        out_shape=[
            sd((rows, D), bf16), sd((rows, D), bf16), sd((na * PACKROWS, 128), f32), sd((4, na * PACKROWS, 128), bf16),
            sd((rows, FF), bf16),
        ],
        scratch_shapes=[
            pltpu.VMEM((128, WIRE), bf16), wide, wide, wide, pltpu.VMEM((rows, D), bf16), thin, thin, thin,
            pltpu.VMEM((rows, 128), bf16),
            pltpu.VMEM((2 * seqs, D), f32), pltpu.VMEM((2 * seqs, D), f32),
            *sums_scratch(WIRE),
            pltpu.VMEM((na * PACKROWS, 128), bf16),
            dma(13), dma(2, 3), dma(2), dma(3 * BLOCKS), dma(3 * BLOCKS),
            dma(Sums.COPIES * len(GROUPS)), dma(Sums.COPIES * len(GROUPS)),
            dma(2), dma(2, 3), dma(2), dma(parts), dma(len(Spread.KINDS) * parts), dma(len(Spread.KINDS) * parts),
        ],
        compiler_params=pltpu.CompilerParams(vmem_limit_bytes=63 * MIB, collective_id=3, has_side_effects=True),
    )(*args)


def lay_kernel(all_hbm, to_ref, all_ref, load_sems, store_sems):
    cuts = 4
    share = PACKROWS // cuts
    parts = [(k, g, pl.ds(k * share, share)) for k in range(cuts) for g in range(4)]
    loads = [pltpu.make_async_copy(all_hbm.at[g, rows], all_ref.at[g, rows], load_sems.at[k, g]) for k, g, rows in parts]
    stores = [pltpu.make_async_copy(all_ref.at[g, rows], to_ref.at[rows, g], store_sems.at[k, g]) for k, g, rows in parts]
    for copy in loads:
        copy.start()
    for came, goes in zip(loads, stores):
        came.wait()
        goes.start()
    for copy in stores:
        copy.wait()


def lay_out(every, na):
    hbm = pl.BlockSpec(memory_space=pl.ANY)
    return pl.pallas_call(
        lay_kernel,
        in_specs=[hbm],
        out_specs=hbm,
        out_shape=jax.ShapeDtypeStruct((PACKROWS, 4, na, 128), bf16),
        scratch_shapes=[
            pltpu.VMEM((4, PACKROWS, na, 128), bf16),
            pltpu.SemaphoreType.DMA((4, 4)),
            pltpu.SemaphoreType.DMA((4, 4)),
        ],
        compiler_params=pltpu.CompilerParams(vmem_limit_bytes=60 * MIB),
    )(every.reshape(4, PACKROWS, na, 128))


def fast_device(
    tokens, segment_ids, adapter_ids, input_weight, conv_weight, output_weight, gate_weight, up_weight, down_weight,
    norm_one, norm_two, cotangent, adapter_state, first_moment, second_moment, rate, step,
):
    seqs, length, _ = tokens.shape
    na = adapter_state.shape[0]
    adapters, count = na * lax.axis_size("grp"), lax.axis_size("seq")
    native = lambda x: x.reshape(na, PACKROWS, 128).swapaxes(0, 1).reshape(na * PACKROWS, 128)
    st, m, v = native(adapter_state), native(first_moment), native(second_moment)
    rows = seqs * length
    tok2, cot2 = tokens.reshape(rows, D), cotangent.reshape(rows, D)
    n1, n2 = norm_one.reshape(1, D), norm_two.reshape(1, D)
    table, u1, mi, b, c, x, conv, same, gated, mo, h1, u2, mg, mu = start(
        seqs, length, count, na, adapter_ids, st, tok2, segment_ids, input_weight, conv_weight, output_weight, n1, n2
    )
    out, ig, new, every, _ = rest(
        seqs, length, count, na, adapter_ids, rate, step, u2, cot2, mg, mu, mo, mi, conv_weight, n1, n2,
        h1, gate_weight, up_weight, down_weight, table,
        tok2, gated, b, c, x, conv, same.reshape(2, seqs, length, 128), u1, input_weight, output_weight, st, m, v,
    )
    every = lay_out(every, na).reshape(PACKROWS, adapters, 128).swapaxes(0, 1).reshape(adapters, PACKROWS * 128)
    new = new.reshape(PACKROWS, na, 128).swapaxes(0, 1).reshape(na, PACKROWS * 128)
    return out.reshape(tokens.shape), ig.reshape(tokens.shape), new, every


def solution(mesh):
    rows = P("grp", "seq", None)
    own = P("grp", None)
    return jax.shard_map(
        fast_device if tuple(mesh.shape[axis] for axis in ("seq", "grp")) == (8, 4) else general_device,
        mesh=mesh,
        in_specs=(rows, P("grp", "seq"), P("grp")) + (P(),) * 8 + (rows, own, own, own, P(), P()),
        out_specs=(rows, rows, own, P()),
        check_vma=False,
    )
```

```python
import functools

import jax
import jax.numpy as jnp
from jax import lax
from jax.experimental import pallas as pl
from jax.experimental.pallas import tpu as pltpu
from jax.sharding import PartitionSpec as P

D = 1024
FF = 4608
RANK = 16
EPS = 1e-05
FB = 512
MIB = 2**20

f32 = jnp.float32
bf16 = jnp.bfloat16
MESH = pl.DeviceIdType.MESH

WIRE = RANK * 0 + 23040
PACKROWS = 2880
A_IN, B_IN, A_OUT, B_OUT, A_GATE, B_GATE, A_UP, B_UP, A_DOWN, B_DOWN = (
    0, 1024, 4096, 5120, 6144, 7168, 11776, 12800, 17408, 22016,
)
B_PARTS = ((B_IN, 3 * D), (B_OUT, D), (B_GATE, FF), (B_UP, FF), (B_DOWN, D))
A_PARTS = ((A_IN, D), (A_OUT, D), (A_GATE, D), (A_UP, D), (A_DOWN, FF))
A_CHUNKS = tuple(
    (first + start, min(1024, height - start))
    for first, height in A_PARTS
    for start in range(0, height, 1024)
)


def dot(a, b):
    return jnp.dot(a, b, preferred_element_type=f32)


def dot_nt(a, b):
    return lax.dot_general(a, b, (((1,), (1,)), ((), ())), preferred_element_type=f32)


def dot_tn(a, b):
    return lax.dot_general(a, b, (((0,), (0,)), ((), ())), preferred_element_type=f32)


def shuffle_matrix():
    row = lax.broadcasted_iota(jnp.int32, (1024, 1024), 0)
    col = lax.broadcasted_iota(jnp.int32, (1024, 1024), 1)
    return jnp.where(col == 8 * (row % 128) + row // 128, 1.0, 0.0).astype(bf16)


def table_kernel(na, st_ref, out_ref, lhs_ref):
    for n, (first, count) in enumerate(A_CHUNKS):
        for a in range(na):
            packed = st_ref[pl.ds(na * (first // 8) + a, 128, stride=na), :]
            turned = packed.T.astype(bf16)
            row = (n * na + a) * RANK
            for c in range(8):
                lhs_ref[row : row + RANK, 128 * c : 128 * c + 128] = turned[RANK * c : RANK * c + RANK, :]
    full = dot(lhs_ref[...], shuffle_matrix()).astype(bf16)
    for n, (first, count) in enumerate(A_CHUNKS):
        for a in range(na):
            row = (n * na + a) * RANK
            out_ref[a * RANK : (a + 1) * RANK, first : first + count] = full[row : row + RANK, :count]
    for first, breadth in B_PARTS:
        blocks = breadth // 128
        for a in range(na):
            for c in range(blocks):
                part = st_ref[pl.ds(na * (first // 8 + c) + a, RANK, stride=na * blocks), :]
                out_ref[a * RANK : (a + 1) * RANK, first + 128 * c : first + 128 * c + 128] = part.astype(bf16)


def build_table(state_native, na):
    return pl.pallas_call(
        functools.partial(table_kernel, na),
        out_shape=jax.ShapeDtypeStruct((na * RANK, WIRE), bf16),
        scratch_shapes=[pltpu.VMEM((len(A_CHUNKS) * na * RANK, 1024), bf16)],
        compiler_params=pltpu.CompilerParams(vmem_limit_bytes=40 * MIB),
    )(state_native)


def adam_kernel(na, scal_ref, gw_ref, st_ref, m_ref, v_ref, new_ref, tab_ref, lhs_ref, gn_ref):
    for n, (first, count) in enumerate(A_CHUNKS):
        for a in range(na):
            row = (n * na + a) * RANK
            lhs_ref[row : row + RANK, :] = gw_ref[a * RANK : (a + 1) * RANK, first : first + 1024].astype(bf16)
    full = dot_nt(lhs_ref[...], shuffle_matrix())
    for n, (first, count) in enumerate(A_CHUNKS):
        for a in range(na):
            row = (n * na + a) * RANK
            turned = jnp.concatenate(
                [full[row : row + RANK, 128 * c : 128 * c + 128] for c in range(8)], axis=0
            )
            gn_ref[pl.ds(na * (first // 8) + a, count // 8, stride=na), :] = turned.T[: count // 8]
    for first, breadth in B_PARTS:
        blocks = breadth // 128
        for a in range(na):
            for c in range(blocks):
                gn_ref[pl.ds(na * (first // 8 + c) + a, RANK, stride=na * blocks), :] = gw_ref[
                    a * RANK : (a + 1) * RANK, first + 128 * c : first + 128 * c + 128
                ].astype(f32)
    rate = scal_ref[0]
    inv = scal_ref[1]
    grad = gn_ref[...]
    one = 0.5 * m_ref[...] + 0.5 * grad
    two = 0.5 * v_ref[...] + 0.5 * grad * grad
    new = st_ref[...] - rate * (one * inv) / (jnp.sqrt(two * inv) + 1e-08)
    new_ref[...] = new
    tab_ref[...] = new.astype(bf16)


def adam(scal, gw, st, m, v, na):
    rows = na * PACKROWS
    vm = pl.BlockSpec(memory_space=pltpu.VMEM)
    return pl.pallas_call(
        functools.partial(adam_kernel, na),
        in_specs=[pl.BlockSpec(memory_space=pltpu.SMEM)] + [vm] * 4,
        out_shape=(jax.ShapeDtypeStruct((rows, 128), f32), jax.ShapeDtypeStruct((rows, 128), bf16)),
        scratch_shapes=[
            pltpu.VMEM((len(A_CHUNKS) * na * RANK, 1024), bf16),
            pltpu.VMEM((rows, 128), f32),
        ],
        compiler_params=pltpu.CompilerParams(vmem_limit_bytes=56 * MIB),
    )(scal, gw, st, m, v)


def greet(seq, count):
    barrier = pltpu.get_barrier_semaphore()

    @pl.when(seq > 0)
    def _():
        pl.semaphore_signal(barrier, inc=1, device_id={"seq": seq - 1}, device_id_type=MESH)

    @pl.when(seq < count - 1)
    def _():
        pl.semaphore_signal(barrier, inc=1, device_id={"seq": seq + 1}, device_id_type=MESH)

    before = (seq + count - 1) // count
    after = (2 * count - 2 - seq) // count
    pl.semaphore_wait(barrier, before + after)


def row_mask(mask_ref, seqs, length):
    return jnp.concatenate(
        [jnp.broadcast_to(mask_ref[s : s + 1, :], (length, 128)) for s in range(seqs)], axis=0
    )


def norm(values, gain):
    inverse = lax.rsqrt(jnp.mean(values * values, axis=-1, keepdims=True) + EPS)
    return values * inverse * gain, inverse


def pre_kernel(
    seqs, length, count,
    tok_ref, ids_ref, mask_ref, tb_ref, wi_ref, cw_ref, wo_ref, n1_ref, n2_ref, cot_ref,
    u1_ref, mi_ref, b_ref, c_ref, x_ref, conv_ref, same_ref, gated_ref, mo_ref, h1_ref, u2_ref, mg_ref, mu_ref, gd_ref,
    ext_ref, out_ref, in_ref, send_sem, recv_sem,
):
    seq = lax.axis_index("seq")
    greet(seq, count)
    mask = row_mask(mask_ref, seqs, length)
    twice = 2.0 * mask
    tokens = tok_ref[...].astype(f32)
    u1 = norm(tokens, n1_ref[...])[0].astype(bf16)
    u1_ref[...] = u1
    mid = (dot_nt(u1, tb_ref[:, A_IN : A_IN + D]).astype(bf16).astype(f32) * twice).astype(bf16)
    mi_ref[...] = mid
    for third, to_ref in ((0, b_ref), (2, x_ref)):
        for k in range(2):
            col = third * D + 512 * k
            to_ref[:, 512 * k : 512 * k + 512] = dot(u1, wi_ref[:, col : col + 512]) + dot(
                mid, tb_ref[:, B_IN + col : B_IN + col + 512]
            )
    width = D + 128
    for s in range(seqs):
        rows = pl.ds(s * length, length)
        ext_ref[s, 0:8, :] = jnp.zeros((8, width), f32)
        ext_ref[s, 8:, :D] = b_ref[rows, :] * x_ref[rows, :]
        ext_ref[s, 8:, D:] = jnp.broadcast_to(ids_ref[s : s + 1, :], (length, 128)).T
        out_ref[2 * s : 2 * s + 2, :] = ext_ref[s, length + 6 : length + 8, :]
    along = pltpu.make_async_remote_copy(
        src_ref=out_ref, dst_ref=in_ref, send_sem=send_sem, recv_sem=recv_sem,
        device_id={"seq": seq + 1}, device_id_type=MESH,
    )

    @pl.when(seq < count - 1)
    def _():
        along.start()

    for k in range(2):
        col = D + 512 * k
        c_ref[:, 512 * k : 512 * k + 512] = dot(u1, wi_ref[:, col : col + 512]) + dot(
            mid, tb_ref[:, B_IN + col : B_IN + col + 512]
        )
    gd_ref[...] = (dot_nt(cot_ref[...], tb_ref[:, B_DOWN : B_DOWN + D]) * twice).astype(bf16)

    @pl.when(seq < count - 1)
    def _():
        along.wait_send()

    @pl.when(seq > 0)
    def _():
        along.wait_recv()
        for s in range(seqs):
            ext_ref[s, 6:8, :] = in_ref[2 * s : 2 * s + 2, :]

    for s in range(seqs):
        rows = pl.ds(s * length, length)
        now_ids = ext_ref[s, 8:, D:]
        same1 = jnp.where(ext_ref[s, pl.ds(7, length), D:] == now_ids, 1.0, 0.0)
        same2 = jnp.where(ext_ref[s, pl.ds(6, length), D:] == now_ids, 1.0, 0.0)
        same_ref[0, rows, :] = same1
        same_ref[1, rows, :] = same2
        conv = (
            cw_ref[2:3, :] * ext_ref[s, 8:, :D]
            + cw_ref[1:2, :] * same1[:, :1] * ext_ref[s, pl.ds(7, length), :D]
            + cw_ref[0:1, :] * same2[:, :1] * ext_ref[s, pl.ds(6, length), :D]
        )
        conv_ref[rows, :] = conv
        gated_ref[rows, :] = (c_ref[rows, :] * conv).astype(bf16)
    gated = gated_ref[...]
    mid_out = (dot_nt(gated, tb_ref[:, A_OUT : A_OUT + D]).astype(bf16).astype(f32) * twice).astype(bf16)
    mo_ref[...] = mid_out
    for k in range(2):
        cols = slice(512 * k, 512 * k + 512)
        h1_ref[:, cols] = (
            tok_ref[:, cols].astype(f32)
            + dot(gated, wo_ref[:, cols])
            + dot(mid_out, tb_ref[:, B_OUT + 512 * k : B_OUT + 512 * k + 512])
        )
    u2 = norm(h1_ref[...], n2_ref[...])[0].astype(bf16)
    u2_ref[...] = u2
    mg_ref[...] = (dot_nt(u2, tb_ref[:, A_GATE : A_GATE + D]).astype(bf16).astype(f32) * twice).astype(bf16)
    mu_ref[...] = (dot_nt(u2, tb_ref[:, A_UP : A_UP + D]).astype(bf16).astype(f32) * twice).astype(bf16)


def pre(seqs, length, count, *args):
    rows = seqs * length
    sd = jax.ShapeDtypeStruct
    width = D + 128
    vm = pl.BlockSpec(memory_space=pltpu.VMEM)
    wide = sd((rows, D), f32)
    half = sd((rows, D), bf16)
    thin = sd((rows, 128), bf16)
    return pl.pallas_call(
        functools.partial(pre_kernel, seqs, length, count),
        in_specs=[vm] * 10,
        out_specs=[vm] * 14,
        out_shape=[half, thin, wide, wide, wide, wide, sd((2, rows, 128), f32), half, thin, wide, half, thin, thin, thin],
        scratch_shapes=[
            pltpu.VMEM((seqs, length + 8, width), f32),
            pltpu.VMEM((2 * seqs, width), f32),
            pltpu.VMEM((2 * seqs, width), f32),
            pltpu.SemaphoreType.DMA,
            pltpu.SemaphoreType.DMA,
        ],
        compiler_params=pltpu.CompilerParams(vmem_limit_bytes=60 * MIB, collective_id=0, has_side_effects=True),
    )(*args)


def ffn_kernel(
    seqs, length,
    u_ref, cot_ref, mg_ref, mu_ref, gd_ref, mask_ref, h1_ref, wg_ref, wu_ref, wd_ref, bg_ref, bu_ref, ad_ref, ag_ref, au_ref, bd_ref,
    out_ref, gn_ref, dbg_ref, dbu_ref, dad_ref, dag_ref, dau_ref, dbd_ref,
    acc_ref, dmid_ref, gmg_ref, gmu_ref,
):
    j = pl.program_id(0)

    @pl.when(j == 0)
    def _():
        for ref in (acc_ref, gn_ref, dmid_ref, gmg_ref, gmu_ref):
            ref[...] = jnp.zeros_like(ref)

    u = u_ref[...]
    gate = dot(u, wg_ref[...]) + dot(mg_ref[...], bg_ref[...])
    up = dot(u, wu_ref[...]) + dot(mu_ref[...], bu_ref[...])
    back = dot_nt(cot_ref[...], wd_ref[...]) + dot(gd_ref[...], ad_ref[...])
    sig = jax.nn.sigmoid(gate)
    silu = gate * sig
    hidden = (silu * up).astype(bf16)
    grad_gate = (back * up * sig * (1.0 + gate * (1.0 - sig))).astype(bf16)
    grad_up = (back * silu).astype(bf16)
    acc_ref[...] += dot(hidden, wd_ref[...])
    gn_ref[...] += dot_nt(grad_gate, wg_ref[...]) + dot_nt(grad_up, wu_ref[...])
    dmid_ref[...] += dot_nt(hidden, ad_ref[...])
    gmg_ref[...] += dot_nt(grad_gate, bg_ref[...])
    gmu_ref[...] += dot_nt(grad_up, bu_ref[...])
    dbg_ref[...] = dot_tn(mg_ref[...], grad_gate).astype(bf16)
    dbu_ref[...] = dot_tn(mu_ref[...], grad_up).astype(bf16)
    dad_ref[...] = dot_tn(gd_ref[...], hidden).astype(bf16)

    @pl.when(j == pl.num_programs(0) - 1)
    def _():
        twice = 2.0 * row_mask(mask_ref, seqs, length)
        dmid = (dmid_ref[...].astype(bf16).astype(f32) * twice).astype(bf16)
        out_ref[...] = (h1_ref[...] + acc_ref[...] + dot(dmid, bd_ref[...])).astype(bf16)
        dbd_ref[...] = dot_tn(dmid, cot_ref[...]).astype(bf16)
        gm_gate = (gmg_ref[...] * twice).astype(bf16)
        gm_up = (gmu_ref[...] * twice).astype(bf16)
        gn_ref[...] += dot(gm_gate, ag_ref[...]) + dot(gm_up, au_ref[...])
        dag_ref[...] = dot_tn(gm_gate, u_ref[...]).astype(bf16)
        dau_ref[...] = dot_tn(gm_up, u_ref[...]).astype(bf16)


def ffn(seqs, length, u2, cot, mg, mu, gd, mask, h1, wg, wu, wd, table):
    rows = seqs * length
    sd = jax.ShapeDtypeStruct
    whole = lambda s: pl.BlockSpec(s, lambda j: (0, 0))
    col = lambda h: pl.BlockSpec((h, FB), lambda j: (0, j))
    tab = lambda first: pl.BlockSpec((128, FB), lambda j: (0, first // FB + j))
    fixed = lambda first: pl.BlockSpec((128, D), lambda j: (0, 0))
    cut = lambda first: lax.slice_in_dim(table, first, first + D, axis=1)
    return pl.pallas_call(
        functools.partial(ffn_kernel, seqs, length),
        grid=(FF // FB,),
        in_specs=[whole((rows, D)), whole((rows, D)), whole((rows, 128)), whole((rows, 128)), whole((rows, 128)),
                  whole(mask.shape), whole((rows, D)),
                  col(D), col(D), pl.BlockSpec((FB, D), lambda j: (j, 0)),
                  tab(B_GATE), tab(B_UP), tab(A_DOWN), whole((128, D)), whole((128, D)), whole((128, D))],
        out_specs=[whole((rows, D)), whole((rows, D)), col(128), col(128), col(128),
                   whole((128, D)), whole((128, D)), whole((128, D))],
        out_shape=[sd((rows, D), bf16), sd((rows, D), f32)] + [sd((128, FF), bf16)] * 3 + [sd((128, D), bf16)] * 3,
        scratch_shapes=[pltpu.VMEM((rows, D), f32)] + [pltpu.VMEM((rows, 128), f32)] * 3,
        compiler_params=pltpu.CompilerParams(vmem_limit_bytes=60 * MIB),
    )(u2, cot, mg, mu, gd, mask, h1, wg, wu, wd, table, table, table, cut(A_GATE), cut(A_UP), cut(B_DOWN))


def post_kernel(
    seqs, length, count,
    tok_ref, cot_ref, mask_ref, h1_ref, gn_ref, gated_ref, mo_ref, b_ref, c_ref, x_ref, conv_ref, same_ref, u1_ref, mi_ref,
    tb_ref, wi_ref, cw_ref, wo_ref, n1_ref, n2_ref,
    ig_ref, dai_ref, dbi_ref, dao_ref, dbo_ref,
    gh_ref, gb_ref, gg_ref, gc_ref, gp_ref, one_ref, two_ref, out_ref, in_ref, send_sem, recv_sem,
):
    seq = lax.axis_index("seq")
    greet(seq, count)
    twice = 2.0 * row_mask(mask_ref, seqs, length)
    h1 = h1_ref[...]
    inv2 = norm(h1, n2_ref[...])[1]
    e2 = gn_ref[...] * n2_ref[...]
    gh = cot_ref[...].astype(f32) + inv2 * e2 - h1 * (inv2 * inv2 * inv2 * jnp.mean(h1 * e2, axis=-1, keepdims=True))
    gh_ref[...] = gh
    gb = gh.astype(bf16)
    gb_ref[...] = gb
    gm_out = (dot_nt(gb, tb_ref[:, B_OUT : B_OUT + D]) * twice).astype(bf16)
    for k in range(2):
        cols = slice(512 * k, 512 * k + 512)
        gg_ref[:, cols] = dot_nt(gb, wo_ref[cols, :]) + dot(gm_out, tb_ref[:, A_OUT + 512 * k : A_OUT + 512 * k + 512])
    for s in range(seqs):
        rows = pl.ds(s * length, length)
        gg = gg_ref[rows, :]
        gp_ref[rows, D : 2 * D] = (gg * conv_ref[rows, :]).astype(bf16)
        gconv = gg * c_ref[rows, :]
        gc_ref[rows, :] = gconv
        one_ref[s, 0:length, :] = cw_ref[1:2, :] * same_ref[0, rows, 0:1] * gconv
        two_ref[s, 0:length, :] = cw_ref[0:1, :] * same_ref[1, rows, 0:1] * gconv
        one_ref[s, length:, :] = jnp.zeros((8, D), f32)
        two_ref[s, length:, :] = jnp.zeros((8, D), f32)
        out_ref[2 * s : 2 * s + 1, :] = two_ref[s, 0:1, :]
        out_ref[2 * s + 1 : 2 * s + 2, :] = two_ref[s, 1:2, :] + one_ref[s, 0:1, :]
    along = pltpu.make_async_remote_copy(
        src_ref=out_ref, dst_ref=in_ref, send_sem=send_sem, recv_sem=recv_sem,
        device_id={"seq": seq - 1}, device_id_type=MESH,
    )

    @pl.when(seq > 0)
    def _():
        along.start()

    dbo_ref[...] = dot_tn(mo_ref[...], gb).astype(bf16)
    dao_ref[...] = dot_tn(gm_out, gated_ref[...]).astype(bf16)

    @pl.when(seq > 0)
    def _():
        along.wait_send()

    @pl.when(seq < count - 1)
    def _():
        along.wait_recv()
        for s in range(seqs):
            two_ref[s, length : length + 2, :] = in_ref[2 * s : 2 * s + 2, :]

    for s in range(seqs):
        rows = pl.ds(s * length, length)
        gmix = (
            cw_ref[2:3, :] * gc_ref[rows, :]
            + one_ref[s, pl.ds(1, length), :]
            + two_ref[s, pl.ds(2, length), :]
        )
        gp_ref[rows, 0:D] = (gmix * x_ref[rows, :]).astype(bf16)
        gp_ref[rows, 2 * D :] = (gmix * b_ref[rows, :]).astype(bf16)
    gm_in = (dot_nt(gp_ref[...], tb_ref[:, B_IN : B_IN + 3 * D]) * twice).astype(bf16)
    for k in range(2):
        cols = slice(512 * k, 512 * k + 512)
        gg_ref[:, cols] = dot_nt(gp_ref[...], wi_ref[cols, :]) + dot(gm_in, tb_ref[:, A_IN + 512 * k : A_IN + 512 * k + 512])
    for k in range(6):
        cols = slice(512 * k, 512 * k + 512)
        dbi_ref[:, cols] = dot_tn(mi_ref[...], gp_ref[:, cols]).astype(bf16)
    dai_ref[...] = dot_tn(gm_in, u1_ref[...]).astype(bf16)
    tokens = tok_ref[...].astype(f32)
    inv1 = norm(tokens, n1_ref[...])[1]
    e1 = gg_ref[...] * n1_ref[...]
    ig_ref[...] = (
        gh_ref[...] + inv1 * e1 - tokens * (inv1 * inv1 * inv1 * jnp.mean(tokens * e1, axis=-1, keepdims=True))
    ).astype(bf16)


def post(seqs, length, count, *args):
    rows = seqs * length
    sd = jax.ShapeDtypeStruct
    vm = pl.BlockSpec(memory_space=pltpu.VMEM)
    return pl.pallas_call(
        functools.partial(post_kernel, seqs, length, count),
        in_specs=[vm] * 20,
        out_specs=[vm] * 5,
        out_shape=[sd((rows, D), bf16), sd((128, D), bf16), sd((128, 3 * D), bf16), sd((128, D), bf16), sd((128, D), bf16)],
        scratch_shapes=[
            pltpu.VMEM((rows, D), f32),
            pltpu.VMEM((rows, D), bf16),
            pltpu.VMEM((rows, D), f32),
            pltpu.VMEM((rows, D), f32),
            pltpu.VMEM((rows, 3 * D), bf16),
            pltpu.VMEM((seqs, length + 8, D), f32),
            pltpu.VMEM((seqs, length + 8, D), f32),
            pltpu.VMEM((2 * seqs, D), f32),
            pltpu.VMEM((2 * seqs, D), f32),
            pltpu.SemaphoreType.DMA,
            pltpu.SemaphoreType.DMA,
        ],
        compiler_params=pltpu.CompilerParams(vmem_limit_bytes=62 * MIB, collective_id=1, has_side_effects=True),
    )(*args)


def general_device(
    tokens, segment_ids, adapter_ids, input_weight, conv_weight, output_weight, gate_weight, up_weight, down_weight,
    norm_one, norm_two, cotangent, adapter_state, first_moment, second_moment, rate, step,
):
    seqs, length, _ = tokens.shape
    na = adapter_state.shape[0]
    groups = lax.axis_size("grp")
    count = lax.axis_size("seq")
    native = lambda x: x.reshape(na, PACKROWS, 128).swapaxes(0, 1).reshape(na * PACKROWS, 128)
    st, m, v = native(adapter_state), native(first_moment), native(second_moment)
    own = build_table(st, na)
    table = lax.all_gather(own, "grp", axis=0, tiled=True)
    adapters = na * groups
    mask = (adapter_ids[:, None] == jnp.arange(adapters * RANK, dtype=jnp.int32)[None, :] // RANK).astype(f32)
    ids = segment_ids.astype(f32)
    rows = seqs * length
    tok2, cot2 = tokens.reshape(rows, D), cotangent.reshape(rows, D)
    n1, n2 = norm_one.reshape(1, D), norm_two.reshape(1, D)
    u1, mi, b, c, x, conv, same, gated, mo, h1, u2, mg, mu, gd = pre(
        seqs, length, count, tok2, ids, mask, table, input_weight, conv_weight, output_weight, n1, n2, cot2
    )
    out, gn, dbg, dbu, dad, dag, dau, dbd = ffn(
        seqs, length, u2, cot2, mg, mu, gd, mask, h1, gate_weight, up_weight, down_weight, table
    )
    ig, dai, dbi, dao, dbo = post(
        seqs, length, count, tok2, cot2, mask, h1, gn, gated, mo, b, c, x, conv, same, u1, mi,
        table, input_weight, conv_weight, output_weight, n1, n2,
    )
    grads = jnp.concatenate([dai, dbi, dao, dbo, dag, dbg, dau, dbu, dad, dbd], axis=1).astype(f32)
    owned = lax.psum(lax.psum_scatter(grads, "grp", scatter_dimension=0, tiled=True), "seq")
    correction = 1.0 - jnp.power(jnp.float32(0.5), step[0].astype(f32))
    scal = jnp.stack([rate[0], 1.0 / correction])
    new, tab = adam(scal, owned, st, m, v, na)
    every = lax.all_gather(tab, "grp", axis=0, tiled=False)
    every = every.reshape(groups, PACKROWS, na, 128).transpose(1, 0, 2, 3).reshape(PACKROWS, adapters, 128)
    every = every.swapaxes(0, 1).reshape(adapters, PACKROWS * 128)
    new = new.reshape(PACKROWS, na, 128).swapaxes(0, 1).reshape(na, PACKROWS * 128)
    return out.reshape(tokens.shape), ig.reshape(tokens.shape), new, every


W_A_IN, W_B_B, W_B_X, W_B_C, W_A_OUT, W_B_OUT, W_A_GATE, W_A_UP, W_B_DOWN, W_FFN = (1024 * n for n in range(10))
W_ENDS = W_A_GATE
BLOCKS = FF // FB
W_BLOCK = 3 * FB
FFN_COLS = WIRE - W_ENDS
SPREAD_BLOCKS = 2


def wire(first, n):
    if first == B_IN:
        return (W_B_B, W_B_C, W_B_X)[n // D] + n % D
    for place, matrix in enumerate((B_GATE, B_UP, A_DOWN)):
        if first == matrix:
            return W_FFN + n // FB * W_BLOCK + place * FB + n % FB
    return {A_IN: W_A_IN, A_OUT: W_A_OUT, B_OUT: W_B_OUT, A_GATE: W_A_GATE, A_UP: W_A_UP, B_DOWN: W_B_DOWN}[first] + n


def a_pieces(first, count):
    for matrix, height in A_PARTS:
        if matrix <= first < matrix + height:
            return [(k, wire(matrix, first - matrix + k), FB) for k in range(0, count, FB)]


class Place:
    def __init__(self):
        seq, grp = lax.axis_index("seq"), lax.axis_index("grp")
        self.seq, self.grp = seq, grp
        self.c, self.x, self.y, self.z = grp % 2, grp // 2, seq % 2, seq // 2
        self.core = grp + 1 - 2 * self.c
        self.gx = (grp + 2) % 4
        self.sy = seq + 1 - 2 * self.y
        self.sz = seq + 2 - 4 * (self.z % 2)

    def along_z(self, d):
        return (self.seq + 2 * d) % 8


def announce(seq, count, devices, both=True):
    barrier = pltpu.get_barrier_semaphore()
    if both:

        @pl.when(seq > 0)
        def _():
            pl.semaphore_signal(barrier, inc=1, device_id={"seq": seq - 1}, device_id_type=MESH)

        @pl.when(seq < count - 1)
        def _():
            pl.semaphore_signal(barrier, inc=1, device_id={"seq": seq + 1}, device_id_type=MESH)

    for device in devices:
        pl.semaphore_signal(barrier, inc=1, device_id=device, device_id_type=MESH)
    ends = (seq + count - 1) // count + (2 * count - 2 - seq) // count if both else 0
    return lambda: pl.semaphore_wait(barrier, ends + len(devices))


class Spread:
    WAYS = {
        "X": (((), ("x", "core")), (("x",), ("cx",)), (("core", "cx"), ())),
        "Y": (((), ("x", "core")), (("x",), ("y", "cx")), (("y",), ("cy",)), (("core", "cx", "cy"), ())),
        "Z": (((), ("x", "core")), (("x",), ("z", "cx")), (("z",), ("cz",)), (("core", "cx", "cz"), ())),
        "S": (
            ((), ("x", "core")), (("x",), ("y", "z", "cx")), (("y",), ("dz", "cy")), (("z",), ("dy", "cz")), (("dy", "dz"), ("cd",)),
            (("core", "cx", "cy", "cz", "cd"), ()),
        ),
    }
    KINDS = ("core", "x", "y", "z", "dy", "dz", "cx", "cy", "cz", "cd")

    def __init__(self, at, own, slot, pieces, ways, step, send_sems, recv_sems):
        self.at, self.own, self.slot, self.pieces, self.ways, self.step = at, own, slot, pieces, ways, step
        self.send_sems, self.recv_sems = send_sems, recv_sems

    def copy(self, kind, p):
        at, way = self.at, self.ways[p]
        first, size = self.pieces[p]
        share = size // {"X": 1, "Y": 2, "Z": 2, "S": 4}[way]
        part = lambda q: pl.multiple_of(first + q * share, self.step) if way != "X" else first
        q = {"X": 0, "Y": at.y, "Z": at.z % 2, "S": at.seq % 4}[way]
        if way == "S":
            qy, qz, qd = q + 1 - 2 * (q % 2), (q + 2) % 4, 3 - q
        else:
            qy = qz = qd = 1 - q
        half = -(-share // (2 * self.step)) * self.step
        core, y, z = {"grp": at.core}, {"seq": at.sy}, {"seq": at.sz}
        if kind == "core":
            src, dst, device = self.own(first, size), self.slot(at.grp, first, size), core
        elif kind == "x":
            src, dst, device = self.own(part(q), share), self.slot(at.grp, part(q), share), {"grp": at.gx}
        else:
            start, count, device = {
                "y": (part(q), share, y),
                "z": (part(q), share, z),
                "dy": (part(qz), half, y),
                "dz": (part(qy) + half, share - half, z),
                "cx": (part(q), share, core),
                "cy": (part(qy), share, core),
                "cz": (part(qz), share, core),
                "cd": (part(qd), share, core),
            }[kind]
            if kind == "dz":
                start = pl.multiple_of(start, self.step)
            src = dst = self.slot(at.gx, start, count)
        n = len(self.KINDS) * p + self.KINDS.index(kind)
        return pltpu.make_async_remote_copy(
            src_ref=src, dst_ref=dst, send_sem=self.send_sems.at[n], recv_sem=self.recv_sems.at[n],
            device_id=device, device_id_type=MESH,
        )

    def steps(self, p):
        return len(self.WAYS[self.ways[p]])

    def leg(self, number, p):
        waits, starts = self.WAYS[self.ways[p]][number]
        for kind in waits:
            self.copy(kind, p).wait_recv()
        for kind in starts:
            self.copy(kind, p).start()

    def sent(self, p):
        for _, starts in self.WAYS[self.ways[p]]:
            for kind in starts:
                self.copy(kind, p).wait_send()


def adapter_mask(adapter_ref, seqs, length):
    column = lax.broadcasted_iota(jnp.int32, (length, 128), 1) // RANK
    return jnp.concatenate([jnp.where(column == adapter_ref[s], 1.0, 0.0) for s in range(seqs)], axis=0)


def fill_shuffle(perm_ref):
    diff = lax.broadcasted_iota(jnp.int32, (128, 1024), 1) - 8 * lax.broadcasted_iota(jnp.int32, (128, 1024), 0)
    for c in range(8):
        perm_ref[128 * c : 128 * c + 128, :] = jnp.where(diff == c, 1.0, 0.0).astype(bf16)


def build_own(na, grp, st_ref, tb_ref, lhs_ref, perm_ref):
    own = lambda a: pl.ds(pl.multiple_of((grp * na + a) * RANK, RANK), RANK)
    fill_shuffle(perm_ref)
    for n, (first, count) in enumerate(A_CHUNKS):
        for a in range(na):
            packed = st_ref[pl.ds(na * (first // 8) + a, 128, stride=na), :]
            turned = packed.T.astype(bf16)
            row = (n * na + a) * RANK
            for c in range(8):
                lhs_ref[row : row + RANK, 128 * c : 128 * c + 128] = turned[RANK * c : RANK * c + RANK, :]
    full = dot(lhs_ref[...], perm_ref[...]).astype(bf16)
    for n, (first, count) in enumerate(A_CHUNKS):
        for a in range(na):
            row = (n * na + a) * RANK
            for k, col, size in a_pieces(first, count):
                tb_ref[own(a), col : col + size] = full[row : row + RANK, k : k + size]
    for first, breadth in B_PARTS:
        blocks = breadth // 128
        for a in range(na):
            for c in range(blocks):
                part = st_ref[pl.ds(na * (first // 8 + c) + a, RANK, stride=na * blocks), :]
                col = wire(first, 128 * c)
                tb_ref[own(a), col : col + 128] = part.astype(bf16)


SPREAD_PIECES = ((0, 4096), (W_A_OUT, 5120), (W_FFN, SPREAD_BLOCKS * W_BLOCK))


def start_kernel(
    seqs, length, count, na,
    adapter_ref, st_ref, tok_ref, ids_ref, wi_hbm, cw_ref, wo_hbm, n1_ref, n2_ref,
    tb_hbm, u1_hbm, mi_ref, b_hbm, c_hbm, x_hbm, conv_hbm, same_hbm, gated_hbm, mo_ref, h1_hbm, u2_hbm, mg_ref, mu_ref,
    tb_ref, lhs_ref, perm_ref, wi_ref, wo_ref, u1_ref, b_ref, c_ref, x_ref, conv_ref, same_ref, gated_ref, h1_ref, u2_ref,
    ext_ref, out_ref, in_ref, halo_sems, load_sems, store_sems, send_sems, recv_sems,
):
    at = Place()
    seq, grp = at.seq, at.grp
    load_in = pltpu.make_async_copy(wi_hbm, wi_ref, load_sems.at[0])
    load_out = pltpu.make_async_copy(wo_hbm, wo_ref, load_sems.at[1])
    load_in.start()
    load_out.start()
    met = announce(seq, count, ({"grp": at.core}, {"grp": at.gx}, {"seq": at.sz}))
    build_own(na, grp, st_ref, tb_ref, lhs_ref, perm_ref)
    height = na * RANK
    block = lambda owner, first, size: tb_ref.at[
        pl.ds(pl.multiple_of(owner * height, height), height), pl.ds(first, size)
    ]
    spread = Spread(at, functools.partial(block, grp), block, SPREAD_PIECES, "SSS", 128, send_sems, recv_sems)
    leg = spread.leg

    def keep(n, src, dst):
        return pltpu.make_async_copy(src, dst, store_sems.at[n])

    met()
    leg(0, 0)
    twice = 2.0 * adapter_mask(adapter_ref, seqs, length)
    tokens = tok_ref[...].astype(f32)
    u1 = norm(tokens, n1_ref[...])[0].astype(bf16)
    u1_ref[...] = u1
    keep(0, u1_ref, u1_hbm).start()
    load_in.wait()
    for k in range(2):
        b_ref[:, 512 * k : 512 * k + 512] = dot(u1, wi_ref[:, 512 * k : 512 * k + 512])
    leg(1, 0)
    for p in range(1, len(SPREAD_PIECES)):
        leg(0, p)
    for k in range(2):
        x_ref[:, 512 * k : 512 * k + 512] = dot(u1, wi_ref[:, 2 * D + 512 * k : 2 * D + 512 * k + 512])
    leg(1, 1)
    leg(2, 0)
    leg(3, 0)
    for k in range(2):
        c_ref[:, 512 * k : 512 * k + 512] = dot(u1, wi_ref[:, D + 512 * k : D + 512 * k + 512])
    leg(1, 2)
    leg(4, 0)
    leg(5, 0)
    mid = (dot_nt(u1, tb_ref[:, W_A_IN : W_A_IN + D]).astype(bf16).astype(f32) * twice).astype(bf16)
    mi_ref[...] = mid
    for first, to_ref in ((W_B_B, b_ref), (W_B_X, x_ref)):
        for k in range(2):
            col = first + 512 * k
            to_ref[:, 512 * k : 512 * k + 512] += dot(mid, tb_ref[:, col : col + 512])
    leg(2, 1)
    leg(3, 1)
    keep(1, b_ref, b_hbm).start()
    keep(2, x_ref, x_hbm).start()
    width = D + 128
    for s in range(seqs):
        rows = pl.ds(s * length, length)
        ext_ref[s, 0:8, :] = jnp.zeros((8, width), f32)
        ext_ref[s, 8:, :D] = b_ref[rows, :] * x_ref[rows, :]
        ext_ref[s, 8:, D:] = jnp.broadcast_to(ids_ref[s : s + 1, :].astype(f32), (length, 128)).T
        out_ref[2 * s : 2 * s + 2, :] = ext_ref[s, length + 6 : length + 8, :]
    along = pltpu.make_async_remote_copy(
        src_ref=out_ref, dst_ref=in_ref, send_sem=halo_sems.at[0], recv_sem=halo_sems.at[1],
        device_id={"seq": seq + 1}, device_id_type=MESH,
    )

    @pl.when(seq < count - 1)
    def _():
        along.start()

    for k in range(2):
        col = W_B_C + 512 * k
        c_ref[:, 512 * k : 512 * k + 512] += dot(mid, tb_ref[:, col : col + 512])
    keep(3, c_ref, c_hbm).start()
    leg(2, 2)
    leg(3, 2)

    @pl.when(seq < count - 1)
    def _():
        along.wait_send()

    @pl.when(seq > 0)
    def _():
        along.wait_recv()
        for s in range(seqs):
            ext_ref[s, 6:8, :] = in_ref[2 * s : 2 * s + 2, :]

    for s in range(seqs):
        rows = pl.ds(s * length, length)
        now_ids = ext_ref[s, 8:, D:]
        same1 = jnp.where(ext_ref[s, pl.ds(7, length), D:] == now_ids, 1.0, 0.0)
        same2 = jnp.where(ext_ref[s, pl.ds(6, length), D:] == now_ids, 1.0, 0.0)
        same_ref[0, rows, :] = same1
        same_ref[1, rows, :] = same2
        conv = (
            cw_ref[2:3, :] * ext_ref[s, 8:, :D]
            + cw_ref[1:2, :] * same1[:, :1] * ext_ref[s, pl.ds(7, length), :D]
            + cw_ref[0:1, :] * same2[:, :1] * ext_ref[s, pl.ds(6, length), :D]
        )
        conv_ref[rows, :] = conv
        gated_ref[rows, :] = (c_ref[rows, :] * conv).astype(bf16)
    keep(4, conv_ref, conv_hbm).start()
    keep(5, same_ref, same_hbm).start()
    leg(4, 1)
    leg(4, 2)
    keep(6, gated_ref, gated_hbm).start()
    gated = gated_ref[...]
    load_out.wait()
    for k in range(2):
        cols = slice(512 * k, 512 * k + 512)
        h1_ref[:, cols] = tok_ref[:, cols].astype(f32) + dot(gated, wo_ref[:, cols])
    leg(5, 1)
    mid_out = (dot_nt(gated, tb_ref[:, W_A_OUT : W_A_OUT + D]).astype(bf16).astype(f32) * twice).astype(bf16)
    mo_ref[...] = mid_out
    for k in range(2):
        cols = slice(512 * k, 512 * k + 512)
        h1_ref[:, cols] += dot(mid_out, tb_ref[:, W_B_OUT + 512 * k : W_B_OUT + 512 * k + 512])
    keep(7, h1_ref, h1_hbm).start()
    u2 = norm(h1_ref[...], n2_ref[...])[0].astype(bf16)
    u2_ref[...] = u2
    keep(8, u2_ref, u2_hbm).start()
    keep(9, tb_ref.at[:, :W_FFN], tb_hbm.at[:, :W_FFN]).start()
    mg_ref[...] = (dot_nt(u2, tb_ref[:, W_A_GATE : W_A_GATE + D]).astype(bf16).astype(f32) * twice).astype(bf16)
    mu_ref[...] = (dot_nt(u2, tb_ref[:, W_A_UP : W_A_UP + D]).astype(bf16).astype(f32) * twice).astype(bf16)
    leg(5, 2)
    keep(10, tb_ref.at[:, W_FFN:], tb_hbm.at[:, W_FFN:]).start()
    for p in range(len(SPREAD_PIECES)):
        spread.sent(p)
    for n, (src, dst) in enumerate((
        (u1_ref, u1_hbm), (b_ref, b_hbm), (x_ref, x_hbm), (c_ref, c_hbm), (conv_ref, conv_hbm), (same_ref, same_hbm),
        (gated_ref, gated_hbm), (h1_ref, h1_hbm), (u2_ref, u2_hbm),
        (tb_ref.at[:, :W_FFN], tb_hbm.at[:, :W_FFN]), (tb_ref.at[:, W_FFN:], tb_hbm.at[:, W_FFN:]),
    )):
        keep(n, src, dst).wait()


def start(seqs, length, count, na, *args):
    rows = seqs * length
    sd = jax.ShapeDtypeStruct
    width = D + 128
    vm = pl.BlockSpec(memory_space=pltpu.VMEM)
    hbm = pl.BlockSpec(memory_space=pl.ANY)
    table = sd((128, WIRE), bf16)
    wide = sd((rows, D), f32)
    half = sd((rows, D), bf16)
    thin = sd((rows, 128), bf16)
    same = sd((2, rows, 128), f32)
    scratch = lambda x: pltpu.VMEM(x.shape, x.dtype)
    return pl.pallas_call(
        functools.partial(start_kernel, seqs, length, count, na),
        in_specs=[pl.BlockSpec(memory_space=pltpu.SMEM), vm, vm, vm, hbm, vm, hbm, vm, vm],
        out_specs=[hbm, hbm, vm, hbm, hbm, hbm, hbm, hbm, hbm, vm, hbm, hbm, vm, vm],
        out_shape=[table, half, thin, wide, wide, wide, wide, same, half, thin, wide, half, thin, thin],
        scratch_shapes=[
            scratch(table),
            pltpu.VMEM((len(A_CHUNKS) * na * RANK, 1024), bf16),
            pltpu.VMEM((1024, 1024), bf16),
            pltpu.VMEM((D, 3 * D), bf16),
            pltpu.VMEM((D, D), bf16),
            scratch(half), scratch(wide), scratch(wide), scratch(wide), scratch(wide), scratch(same), scratch(half),
            scratch(wide), scratch(half),
            pltpu.VMEM((seqs, length + 8, width), f32),
            pltpu.VMEM((2 * seqs, width), f32),
            pltpu.VMEM((2 * seqs, width), f32),
            pltpu.SemaphoreType.DMA((2,)),
            pltpu.SemaphoreType.DMA((2,)),
            pltpu.SemaphoreType.DMA((11,)),
            pltpu.SemaphoreType.DMA((len(Spread.KINDS) * len(SPREAD_PIECES),)),
            pltpu.SemaphoreType.DMA((len(Spread.KINDS) * len(SPREAD_PIECES),)),
        ],
        compiler_params=pltpu.CompilerParams(vmem_limit_bytes=60 * MIB, collective_id=2, has_side_effects=True),
    )(*args)


class Sums:
    CORE, X, Y, Z, BACK_Z, BACK_Y = range(6)
    COPIES = 10

    def __init__(self, at, g_ref, cr_ref, xr_ref, yr_ref, zr_ref, sum_ref, send_sems, recv_sems):
        self.at, self.g, self.cr, self.xr, self.yr, self.zr, self.sum = at, g_ref, cr_ref, xr_ref, yr_ref, zr_ref, sum_ref
        self.send_sems, self.recv_sems = send_sems, recv_sems

    def unit(self, z, start, size):
        rows = pl.ds(pl.multiple_of(RANK * (z // 2), RANK), RANK)
        quarter = size // 4
        return rows, pl.ds(pl.multiple_of(start + self.at.y * (size // 2) + (z % 2) * quarter, 128), quarter)

    def half(self, y, start, size):
        return pl.ds(pl.multiple_of(start + y * (size // 2), 128), size // 2)

    def slot(self, start, size, share):
        return pl.ds(pl.multiple_of(start // share, 128), size // share)

    def copies(self, stage, group):
        index, start, size = group
        at = self.at
        cols = pl.ds(start, size)
        if stage == self.CORE:
            parts = [(self.g.at[:, 1 - at.c, :, cols], self.cr.at[:, :, cols], {"grp": at.core})]
        elif stage == self.X:
            parts = [(self.g.at[1 - at.x, at.c, :, cols], self.xr.at[:, cols], {"grp": at.gx})]
        elif stage == self.Y:
            away = self.half(1 - at.y, start, size)
            parts = [(self.g.at[at.x, at.c, :, away], self.yr.at[:, self.slot(start, size, 2)], {"seq": at.sy})]
        elif stage == self.BACK_Y:
            part = self.sum.at[:, self.half(at.y, start, size)]
            parts = [(part, part, {"seq": at.sy})]
        else:
            parts = []
            for d in range(1, 4):
                if stage == self.Z:
                    rows, span = self.unit((at.z + d) % 4, start, size)
                    parts.append((
                        self.g.at[at.x, at.c, rows, span], self.zr.at[d - 1, :, self.slot(start, size, 4)],
                        {"seq": at.along_z(d)},
                    ))
                else:
                    rows, span = self.unit(at.z, start, size)
                    part = self.sum.at[rows, span]
                    parts.append((part, part, {"seq": at.along_z(d)}))
        first = self.COPIES * index + {self.CORE: 0, self.X: 1, self.Y: 2, self.Z: 3, self.BACK_Z: 6, self.BACK_Y: 9}[stage]
        return [
            pltpu.make_async_remote_copy(
                src_ref=src, dst_ref=dst, send_sem=self.send_sems.at[first + n], recv_sem=self.recv_sems.at[first + n],
                device_id=device, device_id_type=MESH,
            )
            for n, (src, dst, device) in enumerate(parts)
        ]

    def send(self, stage, group):
        for copy in self.copies(stage, group):
            copy.start()

    def take(self, stage, group):
        for copy in self.copies(stage, group):
            copy.wait()
        _, start, size = group
        at = self.at
        cols = pl.ds(start, size)
        wide = lambda value: value.astype(f32)
        if stage == self.CORE:
            for x in range(2):
                self.g[x, at.c, :, cols] = (wide(self.g[x, at.c, :, cols]) + wide(self.cr[x, :, cols])).astype(bf16)
        elif stage == self.X:
            self.g[at.x, at.c, :, cols] = (wide(self.g[at.x, at.c, :, cols]) + wide(self.xr[:, cols])).astype(bf16)
        elif stage == self.Y:
            mine = self.half(at.y, start, size)
            came = self.yr[:, self.slot(start, size, 2)]
            self.g[at.x, at.c, :, mine] = (wide(self.g[at.x, at.c, :, mine]) + wide(came)).astype(bf16)
        elif stage == self.Z:
            rows, span = self.unit(at.z, start, size)
            total = wide(self.g[at.x, at.c, rows, span])
            for d in range(3):
                total = total + wide(self.zr[d, :, self.slot(start, size, 4)])
            self.sum[rows, span] = total.astype(bf16)


def sums_scratch(cols):
    return [
        pltpu.VMEM((2, 2, 32, cols), bf16),
        pltpu.VMEM((2, 32, cols), bf16),
        pltpu.VMEM((32, cols), bf16),
        pltpu.VMEM((32, cols // 2), bf16),
        pltpu.VMEM((3, 16, cols // 4), bf16),
        pltpu.VMEM((32, cols), bf16),
    ]


def put_grad(g_ref, cols, value):
    for x in range(2):
        for c in range(2):
            first = 64 * x + 32 * c
            g_ref[x, c, :, cols] = value[first : first + 32, :].astype(bf16)


UPDATES = (
    (B_GATE, FF), (B_UP, FF), (A_DOWN, FF), (A_GATE, D), (A_UP, D), (B_DOWN, D), (A_OUT, 2 * D), (B_IN, 3 * D),
    (A_IN, D),
)
MOST = 2 * FF // 8
NATIVE = tuple((2 * first // 8, 2 * count // 8) for first, count in UPDATES)


def update_grad(na, part, sum_ref, lhs_ref, perm_ref, gn_ref):
    first, count = UPDATES[part]
    begin = na * first // 8
    inside = lambda start: first <= start < first + count
    chunks = [chunk for chunk in A_CHUNKS if inside(chunk[0])]
    for n, (start, size) in enumerate(chunks):
        for a in range(na):
            row = (n * na + a) * RANK
            if size < 1024:
                lhs_ref[row : row + RANK, size:] = jnp.zeros((RANK, 1024 - size), bf16)
            for k, col, breadth in a_pieces(start, size):
                lhs_ref[row : row + RANK, k : k + breadth] = sum_ref[a * RANK : (a + 1) * RANK, col : col + breadth]
    if chunks:
        height = len(chunks) * na * RANK
        full = dot_nt(lhs_ref[:height, :], perm_ref[...])
    for n, (start, size) in enumerate(chunks):
        for a in range(na):
            row = (n * na + a) * RANK
            turned = jnp.concatenate([full[row : row + RANK, 128 * c : 128 * c + 128] for c in range(8)], axis=0)
            gn_ref[pl.ds(na * (start // 8) + a - begin, size // 8, stride=na), :] = turned.T[: size // 8]
    for start, breadth in B_PARTS:
        if inside(start):
            blocks = breadth // 128
            for a in range(na):
                for c in range(blocks):
                    col = wire(start, 128 * c)
                    gn_ref[pl.ds(na * (start // 8 + c) + a - begin, RANK, stride=na * blocks), :] = sum_ref[
                        a * RANK : (a + 1) * RANK, col : col + 128
                    ].astype(f32)


def group_of(j):
    start = W_FFN + j * W_BLOCK
    return j, start if isinstance(j, int) else pl.multiple_of(start, 128), W_BLOCK


GROUPS = {
    "ends": (BLOCKS, W_ENDS, W_FFN - W_ENDS),
    "out": (BLOCKS + 1, W_B_C, W_ENDS - W_B_C),
    "in1": (BLOCKS + 2, W_B_B, W_B_C - W_B_B),
    "in2": (BLOCKS + 3, W_A_IN, W_B_B),
}
GROUPS.update({j: group_of(j) for j in range(BLOCKS)})


WAYS = "ZZYXXXYXX"
BACKWARD_ORDER = (
    (8, 7, 6, 5, 4, 3, 2, 8), 0, ("ends", 6, 7, 3, 5), 1, ("ends", 4, 8, 7, 6, 5), 2, (4, 8), 3, ("ends", 7, 5, 6), 4,
    ("out", 8), 5, ("out", "ends", 7, 6, 8), 6, ("in1",), 7, ("in1", "in2", 7, 8), 8, ("in2", "out", "ends"), 9,
    ("in1", "in2"), 10,
)
TAIL_ORDER = (
    ("sum", "out"), ("update", 0), ("sum", "in1"), ("sum", "in2"), ("sum", "ends"), ("update", 1), ("update", 2),
    ("out", 0), ("sum", "out"), ("sum", "ends"), ("update", 3), ("sum", "in1"), ("update", 4), ("sum", "in2"),
    ("update", 5), ("pass", 0), ("out", 1), ("pass", 1), ("out", 2), ("sum", "out"), ("out", 3), ("sum", "in1"),
    ("out", 4), ("sum", "in2"), ("pass", 2), ("out", 5), ("sum", "out"), ("update", 6), ("pass", 3), ("sum", "in1"),
    ("update", 7), ("sum", "in2"), ("update", 8), ("pass", 0), ("pass", 3), ("pass", 4), ("pass", 5), ("out", 6),
    ("pass", 0), ("pass", 1), ("pass", 4), ("pass", 2), ("pass", 5), ("pass", 6), ("out", 7), ("pass", 1), ("pass", 2),
    ("out", 8), ("pass", 7), ("pass", 6), ("pass", 8), ("pass", 7), ("pass", 6), ("pass", 8),
)


def rest_kernel(
    seqs, length, count, na,
    adapter_ref, rate_ref, step_ref, u_ref, cot_ref, mg_ref, mu_ref, mo_ref, mi_ref, cw_ref, n1_ref, n2_ref,
    h1_hbm, wg_hbm, wu_hbm, wd_hbm, tb_hbm,
    tok_hbm, gated_hbm, b_hbm, c_hbm, x_hbm, conv_hbm, same_hbm, u1_hbm, wi_hbm, wo_hbm, st_hbm, m_hbm, v_hbm,
    out_ref, ig_ref, new_hbm, all_hbm, hid_hbm,
    tb_ref, h1_ref, gn_ref, gh_ref, gb_ref, dmid_ref, gmg_ref, gmu_ref, gd_ref,
    edge_out_ref, edge_in_ref, g_ref, cr_ref, xr_ref, yr_ref, zr_ref, sum_ref, tab_ref,
    load_sems, weight_sems, hid_sems, tab_send, tab_recv, send_sems, recv_sems,
    halo_sems, old_sems, new_sems, own_sems, spread_send, spread_recv,
):
    rows_all = seqs * length
    at = Place()
    seq = at.seq
    met = announce(seq, count, [{"grp": at.core}, {"grp": at.gx}] + [{"seq": at.along_z(d)} for d in range(1, 4)])
    sums = Sums(at, g_ref, cr_ref, xr_ref, yr_ref, zr_ref, sum_ref, send_sems, recv_sems)
    here = W_FFN + SPREAD_BLOCKS * W_BLOCK
    rows32 = lambda owner: pl.ds(pl.multiple_of(owner * 32, 32), 32)
    loads = [
        pltpu.make_async_copy(tb_hbm.at[:, :here], tb_ref.at[:, :here], load_sems.at[0]),
        pltpu.make_async_copy(tb_hbm.at[rows32(at.grp), here:], tb_ref.at[rows32(at.grp), here:], load_sems.at[1]),
        pltpu.make_async_copy(h1_hbm, h1_ref, load_sems.at[2]),
    ]
    twice = 2.0 * adapter_mask(adapter_ref, seqs, length)

    def table_copy(kind, j):
        _, start, size = group_of(j)
        owner, device = {
            "core": (at.grp, {"grp": at.core}), "x": (at.grp, {"grp": at.gx}), "far": (at.gx, {"grp": at.core})
        }[kind]
        part = tb_ref.at[rows32(owner), pl.ds(start, size)]
        n = 3 * j + ("core", "x", "far").index(kind)
        return pltpu.make_async_remote_copy(
            src_ref=part, dst_ref=part, send_sem=tab_send.at[n], recv_sem=tab_recv.at[n], device_id=device, device_id_type=MESH
        )

    def when(first, j, last, run):
        @pl.when((j >= first) & (j <= last))
        def _():
            run()

    def feed_forward(wg_ref, wu_ref, wd_ref, hid_ref):
        def fetch(j, slot):
            cols = pl.ds(j * FB if isinstance(j, int) else pl.multiple_of(j * FB, FB), FB)
            return [
                pltpu.make_async_copy(wg_hbm.at[:, cols], wg_ref.at[slot], weight_sems.at[slot, 0]),
                pltpu.make_async_copy(wu_hbm.at[:, cols], wu_ref.at[slot], weight_sems.at[slot, 1]),
                pltpu.make_async_copy(wd_hbm.at[cols, :], wd_ref.at[slot], weight_sems.at[slot, 2]),
            ]

        def keep(j, slot):
            cols = pl.ds(j * FB if isinstance(j, int) else pl.multiple_of(j * FB, FB), FB)
            return pltpu.make_async_copy(hid_ref.at[slot], hid_hbm.at[:, cols], hid_sems.at[slot])

        loads[0].start()
        for copy in fetch(0, 0):
            copy.start()
        loads[1].start()
        loads[2].start()
        for ref in (gn_ref, dmid_ref, gmg_ref, gmu_ref):
            ref[...] = jnp.zeros_like(ref)
        loads[0].wait()
        gd_ref[...] = (dot_nt(cot_ref[...], tb_ref[:, W_B_DOWN : W_B_DOWN + D]) * twice).astype(bf16)
        loads[1].wait()
        met()

        def block(j, carry):
            slot = j % 2
            for copy in fetch(j, slot):
                copy.wait()

            def more():
                for copy in fetch(j + 1, 1 - slot):
                    copy.start()

            when(0, j, BLOCKS - 2, more)
            when(2, j, BLOCKS - 1, lambda: keep(j - 2, slot).wait())
            lead = SPREAD_BLOCKS

            def leave():
                table_copy("x", j + lead).start()
                table_copy("core", j + lead).start()

            def go_on():
                table_copy("x", j + lead - 1).wait()
                table_copy("far", j + lead - 1).start()

            def there():
                table_copy("core", j).wait()
                table_copy("far", j).wait()

            when(0, j, BLOCKS - 1 - lead, leave)
            when(1, j, BLOCKS - lead, go_on)
            when(lead, j, BLOCKS - 1, there)
            for stage in range(6):

                def advance(stage=stage):
                    if stage > 0:
                        sums.take(stage - 1, group_of(j - 1 - stage))
                    sums.send(stage, group_of(j - 1 - stage))

                when(1 + stage, j, BLOCKS - 1, advance)
            when(7, j, BLOCKS - 1, lambda: sums.take(5, group_of(j - 7)))

            base = W_FFN + j * W_BLOCK
            part = lambda place: pl.ds(pl.multiple_of(base + place * FB, 128), FB)
            tab_gate, tab_up, tab_down = (tb_ref.at[:, part(place)] for place in range(3))
            u = u_ref[...]
            gate = dot(u, wg_ref[slot]) + dot(mg_ref[...], tab_gate[...])
            up = dot(u, wu_ref[slot]) + dot(mu_ref[...], tab_up[...])
            back = dot_nt(cot_ref[...], wd_ref[slot]) + dot(gd_ref[...], tab_down[...])
            sig = jax.nn.sigmoid(gate)
            silu = gate * sig
            hidden = (silu * up).astype(bf16)
            hid_ref[slot] = hidden
            keep(j, slot).start()
            grad_gate = (back * up * sig * (1.0 + gate * (1.0 - sig))).astype(bf16)
            grad_up = (back * silu).astype(bf16)
            gn_ref[...] += dot_nt(grad_gate, wg_ref[slot]) + dot_nt(grad_up, wu_ref[slot])
            dmid_ref[...] += dot_nt(hidden, tab_down[...])
            gmg_ref[...] += dot_nt(grad_gate, tab_gate[...])
            gmu_ref[...] += dot_nt(grad_up, tab_up[...])
            put_grad(g_ref, part(0), dot_tn(mg_ref[...], grad_gate))
            put_grad(g_ref, part(1), dot_tn(mu_ref[...], grad_up))
            put_grad(g_ref, part(2), dot_tn(gd_ref[...], hidden))
            return carry

        lax.fori_loop(0, BLOCKS, block, 0)
        for j in range(BLOCKS - 2, BLOCKS):
            keep(j, j % 2).wait()

    pl.run_scoped(
        feed_forward,
        pltpu.VMEM((2, D, FB), bf16), pltpu.VMEM((2, D, FB), bf16), pltpu.VMEM((2, FB, D), bf16),
        pltpu.VMEM((2, rows_all, FB), bf16),
    )

    sent = {BLOCKS - 2 - stage: stage for stage in range(6)}

    def advance(*names):
        for name in names:
            stage = sent.get(name, -1)
            if stage >= 0:
                sums.take(stage, GROUPS[name])
            if stage < 5:
                sums.send(stage + 1, GROUPS[name])
            sent[name] = stage + 1

    dmid = (dmid_ref[...].astype(bf16).astype(f32) * twice).astype(bf16)

    def backward(gated_ref, one_ref, two_ref, same_ref, u1_ref, tok_ref, wi_ref, wo_ref, gg_ref, gp_ref):
        pairs = (
            (wo_hbm, wo_ref), (c_hbm, one_ref), (conv_hbm, two_ref), (same_hbm, same_ref.at[:, :, :length, :]),
            (gated_hbm, gated_ref), (wi_hbm, wi_ref), (u1_hbm, u1_ref), (tok_hbm, tok_ref), (x_hbm, one_ref), (b_hbm, two_ref),
        )
        copies = [pltpu.make_async_copy(*pair, load_sems.at[3 + n]) for n, pair in enumerate(pairs)]
        get_wo, get_c, get_conv, get_same, get_gated, get_wi, get_u1, get_tok, get_x, get_b = copies
        for copy in (get_wo, get_c, get_conv, get_same):
            copy.start()
        held = {}

        def part0():
            held["gm_gate"] = (gmg_ref[...] * twice).astype(bf16)
            held["gm_up"] = (gmu_ref[...] * twice).astype(bf16)
            put_grad(g_ref, slice(W_A_GATE, W_A_GATE + D), dot_tn(held["gm_gate"], u_ref[...]))
            put_grad(g_ref, slice(W_A_UP, W_A_UP + D), dot_tn(held["gm_up"], u_ref[...]))
            put_grad(g_ref, slice(W_B_DOWN, W_B_DOWN + D), dot_tn(dmid, cot_ref[...]))

        def part1():
            for k in range(2):
                cols = slice(512 * k, 512 * k + 512)
                gn_ref[:, cols] += dot(held["gm_gate"], tb_ref[:, W_A_GATE + 512 * k : W_A_GATE + 512 * k + 512]) + dot(
                    held["gm_up"], tb_ref[:, W_A_UP + 512 * k : W_A_UP + 512 * k + 512]
                )
            loads[2].wait()
            for s in range(seqs):
                rows = pl.ds(s * length, length)
                h1 = h1_ref[rows, :]
                inv2 = norm(h1, n2_ref[...])[1]
                e2 = gn_ref[rows, :] * n2_ref[...]
                gh = cot_ref[rows, :].astype(f32) + inv2 * e2
                gh = gh - h1 * (inv2 * inv2 * inv2 * jnp.mean(h1 * e2, axis=-1, keepdims=True))
                gh_ref[rows, :] = gh
                gb_ref[rows, :] = gh.astype(bf16)
            for copy in (get_gated, get_wi, get_u1, get_tok):
                copy.start()

        def part2():
            get_wo.wait()
            held["gb"] = gb_ref[...]
            held["gm_out"] = (dot_nt(held["gb"], tb_ref[:, W_B_OUT : W_B_OUT + D]) * twice).astype(bf16)
            for k in range(2):
                cols = slice(512 * k, 512 * k + 512)
                part = dot_nt(held["gb"], wo_ref[cols, :]) + dot(held["gm_out"], tb_ref[:, W_A_OUT + 512 * k : W_A_OUT + 512 * k + 512])
                for s in range(seqs):
                    gg_ref[s, :length, cols] = part[s * length : (s + 1) * length, :]

        def part3():
            for copy in (get_c, get_conv, get_same):
                copy.wait()
            for s in range(seqs):
                rows = pl.ds(s * length, length)
                gg = gg_ref[s, :length, :]
                gp_ref[rows, D : 2 * D] = (gg * two_ref[rows, :]).astype(bf16)
                gg_ref[s, :length, :] = gg * one_ref[rows, :]
                gg_ref[s, length:, :] = jnp.zeros((8, D), f32)
                for k in range(2):
                    same_ref[k, s, length:, :] = jnp.zeros((8, 128), f32)
                edge_out_ref[2 * s : 2 * s + 1, :] = cw_ref[0:1, :] * same_ref[1, s, 0:1, 0:1] * gg_ref[s, 0:1, :]
                edge_out_ref[2 * s + 1 : 2 * s + 2, :] = (
                    cw_ref[0:1, :] * same_ref[1, s, 1:2, 0:1] * gg_ref[s, 1:2, :]
                    + cw_ref[1:2, :] * same_ref[0, s, 0:1, 0:1] * gg_ref[s, 0:1, :]
                )
            get_x.start()
            get_b.start()
            held["along"] = pltpu.make_async_remote_copy(
                src_ref=edge_out_ref, dst_ref=edge_in_ref, send_sem=halo_sems.at[0], recv_sem=halo_sems.at[1],
                device_id={"seq": seq - 1}, device_id_type=MESH,
            )

            @pl.when(seq > 0)
            def _():
                held["along"].start()

        def part4():
            get_gated.wait()
            put_grad(g_ref, slice(W_A_OUT, W_A_OUT + D), dot_tn(held["gm_out"], gated_ref[...]))
            put_grad(g_ref, slice(W_B_OUT, W_B_OUT + D), dot_tn(mo_ref[...], held["gb"]))
            put_grad(g_ref, slice(W_B_C, W_B_C + D), dot_tn(mi_ref[...], gp_ref[:, D : 2 * D]))

        def part5():

            @pl.when(seq > 0)
            def _():
                held["along"].wait_send()

            @pl.when(seq < count - 1)
            def _():
                held["along"].wait_recv()

            get_x.wait()
            get_b.wait()
            for s in range(seqs):
                one, two = pl.ds(1, length), pl.ds(2, length)
                gg_ref[s, :length, :] = (
                    cw_ref[2:3, :] * gg_ref[s, :length, :]
                    + cw_ref[1:2, :] * same_ref[0, s, one, 0:1] * gg_ref[s, one, :]
                    + cw_ref[0:1, :] * same_ref[1, s, two, 0:1] * gg_ref[s, two, :]
                )

            @pl.when(seq < count - 1)
            def _():
                for s in range(seqs):
                    gg_ref[s, length - 2 : length, :] += edge_in_ref[2 * s : 2 * s + 2, :]

            for s in range(seqs):
                rows = pl.ds(s * length, length)
                gmix = gg_ref[s, :length, :]
                gp_ref[rows, 0:D] = (gmix * one_ref[rows, :]).astype(bf16)
                gp_ref[rows, 2 * D :] = (gmix * two_ref[rows, :]).astype(bf16)

        def part6():
            put_grad(g_ref, slice(W_B_B, W_B_B + D), dot_tn(mi_ref[...], gp_ref[:, :D]))
            put_grad(g_ref, slice(W_B_X, W_B_X + D), dot_tn(mi_ref[...], gp_ref[:, 2 * D :]))

        def part7():
            gm_part = dot_nt(gp_ref[:, :D], tb_ref[:, W_B_B : W_B_B + D])
            gm_part += dot_nt(gp_ref[:, D : 2 * D], tb_ref[:, W_B_C : W_B_C + D])
            gm_part += dot_nt(gp_ref[:, 2 * D :], tb_ref[:, W_B_X : W_B_X + D])
            held["gm_in"] = (gm_part * twice).astype(bf16)
            get_u1.wait()
            put_grad(g_ref, slice(W_A_IN, W_A_IN + D), dot_tn(held["gm_in"], u1_ref[...]))

        def part8():
            get_wi.wait()
            for k in range(2):
                cols = slice(256 * k, 256 * k + 256)
                gn_ref[:, cols] = dot_nt(gp_ref[...], wi_ref[cols, :]) + dot(
                    held["gm_in"], tb_ref[:, W_A_IN + 256 * k : W_A_IN + 256 * k + 256]
                )

        def part9():
            for k in range(2, 4):
                cols = slice(256 * k, 256 * k + 256)
                gn_ref[:, cols] = dot_nt(gp_ref[...], wi_ref[cols, :]) + dot(
                    held["gm_in"], tb_ref[:, W_A_IN + 256 * k : W_A_IN + 256 * k + 256]
                )

        def part10():
            get_tok.wait()
            for s in range(seqs):
                rows = pl.ds(s * length, length)
                tokens = tok_ref[rows, :].astype(f32)
                inv1 = norm(tokens, n1_ref[...])[1]
                e1 = gn_ref[rows, :] * n1_ref[...]
                ig = gh_ref[rows, :] + inv1 * e1
                ig_ref[rows, :] = (
                    ig - tokens * (inv1 * inv1 * inv1 * jnp.mean(tokens * e1, axis=-1, keepdims=True))
                ).astype(bf16)

        parts = (part0, part1, part2, part3, part4, part5, part6, part7, part8, part9, part10)
        for what in BACKWARD_ORDER:
            if isinstance(what, tuple):
                advance(*what)
            else:
                parts[what]()

    wide = pltpu.VMEM((rows_all, D), f32)
    half = pltpu.VMEM((rows_all, D), bf16)
    pl.run_scoped(
        backward,
        half, wide, wide, pltpu.VMEM((2, seqs, length + 8, 128), f32), half, half,
        pltpu.VMEM((D, 3 * D), bf16), pltpu.VMEM((D, D), bf16), pltpu.VMEM((seqs, length + 8, D), f32),
        pltpu.VMEM((rows_all, 3 * D), bf16),
    )

    def updates(lhs_ref, perm_ref, old_ref, grad_ref, new_ref, wd_ref, hid_ref):
        own = lambda first, size: tab_ref.at[pl.ds(first, size), :]
        slot_of = lambda owner, first, size: all_hbm.at[owner, pl.ds(first, size), :]
        spread = Spread(at, own, slot_of, NATIVE, WAYS, 16, spread_send, spread_recv)
        going = {}

        def pass_on(*parts):
            for part in parts:
                spread.leg(going[part], part)
                going[part] += 1

        power = jnp.float32(1.0)
        for bit in range(8):
            power = power * jnp.where((step_ref[0] >> bit) % 2 == 1, jnp.float32(0.5 ** (2**bit)), jnp.float32(1.0))
        rate = rate_ref[0]
        correction = 1.0 - jnp.full((8, 128), power, f32)
        inv = (1.0 / correction)[0:1, :]

        def old(part):
            first, size = NATIVE[part]
            slot = part % 2
            return [
                pltpu.make_async_copy(ref.at[first : first + size], old_ref.at[slot, n, :size], old_sems.at[slot, n])
                for n, ref in enumerate((st_hbm, m_hbm, v_hbm))
            ]

        def new_copy(part):
            first, size = NATIVE[part]
            return pltpu.make_async_copy(new_ref.at[part % 2, :size], new_hbm.at[first : first + size], new_sems.at[part % 2])

        def own_copy(part):
            first, size = NATIVE[part]
            return pltpu.make_async_copy(
                tab_ref.at[first : first + size], all_hbm.at[at.grp, first : first + size], own_sems.at[part]
            )

        def update(part):
            first, size = NATIVE[part]
            slot = part % 2
            update_grad(na, part, sum_ref, lhs_ref, perm_ref, grad_ref)
            for copy in old(part):
                copy.wait()
            if part >= 2:
                new_copy(part - 2).wait()
            grad = grad_ref[:size]
            one = 0.5 * old_ref[slot, 1, :size] + 0.5 * grad
            two = 0.5 * old_ref[slot, 2, :size] + 0.5 * grad * grad
            new = old_ref[slot, 0, :size] - rate * (one * inv) / (jnp.sqrt(two * inv) + 1e-08)
            new_ref[slot, :size] = new
            tab_ref[first : first + size] = new.astype(bf16)
            new_copy(part).start()
            own_copy(part).start()
            if part + 2 < len(NATIVE):
                for copy in old(part + 2):
                    copy.start()
            going[part] = 0
            pass_on(part)

        def fetch(j):
            slot = j % 2
            return [
                pltpu.make_async_copy(wd_hbm.at[j * FB : (j + 1) * FB, :], wd_ref.at[slot], weight_sems.at[slot, 0]),
                pltpu.make_async_copy(hid_hbm.at[:, j * FB : (j + 1) * FB], hid_ref.at[slot], weight_sems.at[slot, 1]),
            ]

        def outputs(*blocks):
            for j in blocks:
                for copy in fetch(j):
                    copy.wait()
                h1_ref[...] += dot(hid_ref[j % 2], wd_ref[j % 2])
                if j + 2 < BLOCKS:
                    for copy in fetch(j + 2):
                        copy.start()

        for part in range(2):
            for copy in old(part):
                copy.start()
        for j in range(2):
            for copy in fetch(j):
                copy.start()
        fill_shuffle(perm_ref)
        for k in range(2):
            cols = slice(512 * k, 512 * k + 512)
            h1_ref[:, cols] += dot(dmid, tb_ref[:, W_B_DOWN + 512 * k : W_B_DOWN + 512 * k + 512])
        for what, *which in TAIL_ORDER:
            {"sum": advance, "update": update, "pass": pass_on, "out": outputs}[what](*which)
        out_ref[...] = h1_ref[...].astype(bf16)
        for part in range(len(NATIVE)):
            spread.sent(part)
            own_copy(part).wait()
        for part in range(len(NATIVE) - 2, len(NATIVE)):
            new_copy(part).wait()

    pl.run_scoped(
        updates,
        pltpu.VMEM((5 * na * RANK, 1024), bf16), pltpu.VMEM((1024, 1024), bf16),
        pltpu.VMEM((2, 3, MOST, 128), f32), pltpu.VMEM((MOST, 128), f32), pltpu.VMEM((2, MOST, 128), f32),
        pltpu.VMEM((2, FB, D), bf16), pltpu.VMEM((2, rows_all, FB), bf16),
    )


def rest(seqs, length, count, na, *args):
    rows = seqs * length
    sd = jax.ShapeDtypeStruct
    sm = pl.BlockSpec(memory_space=pltpu.SMEM)
    vm = pl.BlockSpec(memory_space=pltpu.VMEM)
    hbm = pl.BlockSpec(memory_space=pl.ANY)
    wide = pltpu.VMEM((rows, D), f32)
    thin = pltpu.VMEM((rows, 128), f32)
    parts = len(NATIVE)
    dma = lambda *shape: pltpu.SemaphoreType.DMA(shape)
    return pl.pallas_call(
        functools.partial(rest_kernel, seqs, length, count, na),
        in_specs=[sm] * 3 + [vm] * 9 + [hbm] * 18,
        out_specs=[vm, vm, hbm, hbm, hbm],
        out_shape=[
            sd((rows, D), bf16), sd((rows, D), bf16), sd((na * PACKROWS, 128), f32), sd((4, na * PACKROWS, 128), bf16),
            sd((rows, FF), bf16),
        ],
        scratch_shapes=[
            pltpu.VMEM((128, WIRE), bf16), wide, wide, wide, pltpu.VMEM((rows, D), bf16), thin, thin, thin,
            pltpu.VMEM((rows, 128), bf16),
            pltpu.VMEM((2 * seqs, D), f32), pltpu.VMEM((2 * seqs, D), f32),
            *sums_scratch(WIRE),
            pltpu.VMEM((na * PACKROWS, 128), bf16),
            dma(13), dma(2, 3), dma(2), dma(3 * BLOCKS), dma(3 * BLOCKS),
            dma(Sums.COPIES * len(GROUPS)), dma(Sums.COPIES * len(GROUPS)),
            dma(2), dma(2, 3), dma(2), dma(parts), dma(len(Spread.KINDS) * parts), dma(len(Spread.KINDS) * parts),
        ],
        compiler_params=pltpu.CompilerParams(vmem_limit_bytes=63 * MIB, collective_id=3, has_side_effects=True),
    )(*args)


def lay_kernel(all_hbm, to_ref, all_ref, load_sems, store_sems):
    cuts = 4
    share = PACKROWS // cuts
    parts = [(k, g, pl.ds(k * share, share)) for k in range(cuts) for g in range(4)]
    loads = [pltpu.make_async_copy(all_hbm.at[g, rows], all_ref.at[g, rows], load_sems.at[k, g]) for k, g, rows in parts]
    stores = [pltpu.make_async_copy(all_ref.at[g, rows], to_ref.at[rows, g], store_sems.at[k, g]) for k, g, rows in parts]
    for copy in loads:
        copy.start()
    for came, goes in zip(loads, stores):
        came.wait()
        goes.start()
    for copy in stores:
        copy.wait()


def lay_out(every, na):
    hbm = pl.BlockSpec(memory_space=pl.ANY)
    return pl.pallas_call(
        lay_kernel,
        in_specs=[hbm],
        out_specs=hbm,
        out_shape=jax.ShapeDtypeStruct((PACKROWS, 4, na, 128), bf16),
        scratch_shapes=[
            pltpu.VMEM((4, PACKROWS, na, 128), bf16),
            pltpu.SemaphoreType.DMA((4, 4)),
            pltpu.SemaphoreType.DMA((4, 4)),
        ],
        compiler_params=pltpu.CompilerParams(vmem_limit_bytes=60 * MIB),
    )(every.reshape(4, PACKROWS, na, 128))


def fast_device(
    tokens, segment_ids, adapter_ids, input_weight, conv_weight, output_weight, gate_weight, up_weight, down_weight,
    norm_one, norm_two, cotangent, adapter_state, first_moment, second_moment, rate, step,
):
    seqs, length, _ = tokens.shape
    na = adapter_state.shape[0]
    adapters, count = na * lax.axis_size("grp"), lax.axis_size("seq")
    native = lambda x: x.reshape(na, PACKROWS, 128).swapaxes(0, 1).reshape(na * PACKROWS, 128)
    st, m, v = native(adapter_state), native(first_moment), native(second_moment)
    rows = seqs * length
    tok2, cot2 = tokens.reshape(rows, D), cotangent.reshape(rows, D)
    n1, n2 = norm_one.reshape(1, D), norm_two.reshape(1, D)
    table, u1, mi, b, c, x, conv, same, gated, mo, h1, u2, mg, mu = start(
        seqs, length, count, na, adapter_ids, st, tok2, segment_ids, input_weight, conv_weight, output_weight, n1, n2
    )
    out, ig, new, every, _ = rest(
        seqs, length, count, na, adapter_ids, rate, step, u2, cot2, mg, mu, mo, mi, conv_weight, n1, n2,
        h1, gate_weight, up_weight, down_weight, table,
        tok2, gated, b, c, x, conv, same.reshape(2, seqs, length, 128), u1, input_weight, output_weight, st, m, v,
    )
    every = lay_out(every, na).reshape(PACKROWS, adapters, 128).swapaxes(0, 1).reshape(adapters, PACKROWS * 128)
    new = new.reshape(PACKROWS, na, 128).swapaxes(0, 1).reshape(na, PACKROWS * 128)
    return out.reshape(tokens.shape), ig.reshape(tokens.shape), new, every


def solution(mesh):
    rows = P("grp", "seq", None)
    own = P("grp", None)
    return jax.shard_map(
        fast_device if tuple(mesh.shape[axis] for axis in ("seq", "grp")) == (8, 4) else general_device,
        mesh=mesh,
        in_specs=(rows, P("grp", "seq"), P("grp")) + (P(),) * 8 + (rows, own, own, own, P(), P()),
        out_specs=(rows, rows, own, P()),
        check_vma=False,
    )
```

```python
import functools

import jax
import jax.numpy as jnp
from jax import lax
from jax.experimental import pallas as pl
from jax.experimental.pallas import tpu as pltpu
from jax.sharding import PartitionSpec as P

D = 1024
FF = 4608
RANK = 16
EPS = 1e-05
FB = 512
MIB = 2**20

f32 = jnp.float32
bf16 = jnp.bfloat16
MESH = pl.DeviceIdType.MESH

WIRE = RANK * 0 + 23040
PACKROWS = 2880
A_IN, B_IN, A_OUT, B_OUT, A_GATE, B_GATE, A_UP, B_UP, A_DOWN, B_DOWN = (
    0, 1024, 4096, 5120, 6144, 7168, 11776, 12800, 17408, 22016,
)
B_PARTS = ((B_IN, 3 * D), (B_OUT, D), (B_GATE, FF), (B_UP, FF), (B_DOWN, D))
A_PARTS = ((A_IN, D), (A_OUT, D), (A_GATE, D), (A_UP, D), (A_DOWN, FF))
A_CHUNKS = tuple(
    (first + start, min(1024, height - start))
    for first, height in A_PARTS
    for start in range(0, height, 1024)
)


def dot(a, b):
    return jnp.dot(a, b, preferred_element_type=f32)


def dot_nt(a, b):
    return lax.dot_general(a, b, (((1,), (1,)), ((), ())), preferred_element_type=f32)


def dot_tn(a, b):
    return lax.dot_general(a, b, (((0,), (0,)), ((), ())), preferred_element_type=f32)


def shuffle_matrix():
    row = lax.broadcasted_iota(jnp.int32, (1024, 1024), 0)
    col = lax.broadcasted_iota(jnp.int32, (1024, 1024), 1)
    return jnp.where(col == 8 * (row % 128) + row // 128, 1.0, 0.0).astype(bf16)


def table_kernel(na, st_ref, out_ref, lhs_ref):
    for n, (first, count) in enumerate(A_CHUNKS):
        for a in range(na):
            packed = st_ref[pl.ds(na * (first // 8) + a, 128, stride=na), :]
            turned = packed.T.astype(bf16)
            row = (n * na + a) * RANK
            for c in range(8):
                lhs_ref[row : row + RANK, 128 * c : 128 * c + 128] = turned[RANK * c : RANK * c + RANK, :]
    full = dot(lhs_ref[...], shuffle_matrix()).astype(bf16)
    for n, (first, count) in enumerate(A_CHUNKS):
        for a in range(na):
            row = (n * na + a) * RANK
            out_ref[a * RANK : (a + 1) * RANK, first : first + count] = full[row : row + RANK, :count]
    for first, breadth in B_PARTS:
        blocks = breadth // 128
        for a in range(na):
            for c in range(blocks):
                part = st_ref[pl.ds(na * (first // 8 + c) + a, RANK, stride=na * blocks), :]
                out_ref[a * RANK : (a + 1) * RANK, first + 128 * c : first + 128 * c + 128] = part.astype(bf16)


def build_table(state_native, na):
    return pl.pallas_call(
        functools.partial(table_kernel, na),
        out_shape=jax.ShapeDtypeStruct((na * RANK, WIRE), bf16),
        scratch_shapes=[pltpu.VMEM((len(A_CHUNKS) * na * RANK, 1024), bf16)],
        compiler_params=pltpu.CompilerParams(vmem_limit_bytes=40 * MIB),
    )(state_native)


def adam_kernel(na, scal_ref, gw_ref, st_ref, m_ref, v_ref, new_ref, tab_ref, lhs_ref, gn_ref):
    for n, (first, count) in enumerate(A_CHUNKS):
        for a in range(na):
            row = (n * na + a) * RANK
            lhs_ref[row : row + RANK, :] = gw_ref[a * RANK : (a + 1) * RANK, first : first + 1024].astype(bf16)
    full = dot_nt(lhs_ref[...], shuffle_matrix())
    for n, (first, count) in enumerate(A_CHUNKS):
        for a in range(na):
            row = (n * na + a) * RANK
            turned = jnp.concatenate(
                [full[row : row + RANK, 128 * c : 128 * c + 128] for c in range(8)], axis=0
            )
            gn_ref[pl.ds(na * (first // 8) + a, count // 8, stride=na), :] = turned.T[: count // 8]
    for first, breadth in B_PARTS:
        blocks = breadth // 128
        for a in range(na):
            for c in range(blocks):
                gn_ref[pl.ds(na * (first // 8 + c) + a, RANK, stride=na * blocks), :] = gw_ref[
                    a * RANK : (a + 1) * RANK, first + 128 * c : first + 128 * c + 128
                ].astype(f32)
    rate = scal_ref[0]
    inv = scal_ref[1]
    grad = gn_ref[...]
    one = 0.5 * m_ref[...] + 0.5 * grad
    two = 0.5 * v_ref[...] + 0.5 * grad * grad
    new = st_ref[...] - rate * (one * inv) / (jnp.sqrt(two * inv) + 1e-08)
    new_ref[...] = new
    tab_ref[...] = new.astype(bf16)


def adam(scal, gw, st, m, v, na):
    rows = na * PACKROWS
    vm = pl.BlockSpec(memory_space=pltpu.VMEM)
    return pl.pallas_call(
        functools.partial(adam_kernel, na),
        in_specs=[pl.BlockSpec(memory_space=pltpu.SMEM)] + [vm] * 4,
        out_shape=(jax.ShapeDtypeStruct((rows, 128), f32), jax.ShapeDtypeStruct((rows, 128), bf16)),
        scratch_shapes=[
            pltpu.VMEM((len(A_CHUNKS) * na * RANK, 1024), bf16),
            pltpu.VMEM((rows, 128), f32),
        ],
        compiler_params=pltpu.CompilerParams(vmem_limit_bytes=56 * MIB),
    )(scal, gw, st, m, v)


def greet(seq, count):
    barrier = pltpu.get_barrier_semaphore()

    @pl.when(seq > 0)
    def _():
        pl.semaphore_signal(barrier, inc=1, device_id={"seq": seq - 1}, device_id_type=MESH)

    @pl.when(seq < count - 1)
    def _():
        pl.semaphore_signal(barrier, inc=1, device_id={"seq": seq + 1}, device_id_type=MESH)

    before = (seq + count - 1) // count
    after = (2 * count - 2 - seq) // count
    pl.semaphore_wait(barrier, before + after)


def row_mask(mask_ref, seqs, length):
    return jnp.concatenate(
        [jnp.broadcast_to(mask_ref[s : s + 1, :], (length, 128)) for s in range(seqs)], axis=0
    )


def norm(values, gain):
    inverse = lax.rsqrt(jnp.mean(values * values, axis=-1, keepdims=True) + EPS)
    return values * inverse * gain, inverse


def pre_kernel(
    seqs, length, count,
    tok_ref, ids_ref, mask_ref, tb_ref, wi_ref, cw_ref, wo_ref, n1_ref, n2_ref, cot_ref,
    u1_ref, mi_ref, b_ref, c_ref, x_ref, conv_ref, same_ref, gated_ref, mo_ref, h1_ref, u2_ref, mg_ref, mu_ref, gd_ref,
    ext_ref, out_ref, in_ref, send_sem, recv_sem,
):
    seq = lax.axis_index("seq")
    greet(seq, count)
    mask = row_mask(mask_ref, seqs, length)
    twice = 2.0 * mask
    tokens = tok_ref[...].astype(f32)
    u1 = norm(tokens, n1_ref[...])[0].astype(bf16)
    u1_ref[...] = u1
    mid = (dot_nt(u1, tb_ref[:, A_IN : A_IN + D]).astype(bf16).astype(f32) * twice).astype(bf16)
    mi_ref[...] = mid
    for third, to_ref in ((0, b_ref), (2, x_ref)):
        for k in range(2):
            col = third * D + 512 * k
            to_ref[:, 512 * k : 512 * k + 512] = dot(u1, wi_ref[:, col : col + 512]) + dot(
                mid, tb_ref[:, B_IN + col : B_IN + col + 512]
            )
    width = D + 128
    for s in range(seqs):
        rows = pl.ds(s * length, length)
        ext_ref[s, 0:8, :] = jnp.zeros((8, width), f32)
        ext_ref[s, 8:, :D] = b_ref[rows, :] * x_ref[rows, :]
        ext_ref[s, 8:, D:] = jnp.broadcast_to(ids_ref[s : s + 1, :], (length, 128)).T
        out_ref[2 * s : 2 * s + 2, :] = ext_ref[s, length + 6 : length + 8, :]
    along = pltpu.make_async_remote_copy(
        src_ref=out_ref, dst_ref=in_ref, send_sem=send_sem, recv_sem=recv_sem,
        device_id={"seq": seq + 1}, device_id_type=MESH,
    )

    @pl.when(seq < count - 1)
    def _():
        along.start()

    for k in range(2):
        col = D + 512 * k
        c_ref[:, 512 * k : 512 * k + 512] = dot(u1, wi_ref[:, col : col + 512]) + dot(
            mid, tb_ref[:, B_IN + col : B_IN + col + 512]
        )
    gd_ref[...] = (dot_nt(cot_ref[...], tb_ref[:, B_DOWN : B_DOWN + D]) * twice).astype(bf16)

    @pl.when(seq < count - 1)
    def _():
        along.wait_send()

    @pl.when(seq > 0)
    def _():
        along.wait_recv()
        for s in range(seqs):
            ext_ref[s, 6:8, :] = in_ref[2 * s : 2 * s + 2, :]

    for s in range(seqs):
        rows = pl.ds(s * length, length)
        now_ids = ext_ref[s, 8:, D:]
        same1 = jnp.where(ext_ref[s, pl.ds(7, length), D:] == now_ids, 1.0, 0.0)
        same2 = jnp.where(ext_ref[s, pl.ds(6, length), D:] == now_ids, 1.0, 0.0)
        same_ref[0, rows, :] = same1
        same_ref[1, rows, :] = same2
        conv = (
            cw_ref[2:3, :] * ext_ref[s, 8:, :D]
            + cw_ref[1:2, :] * same1[:, :1] * ext_ref[s, pl.ds(7, length), :D]
            + cw_ref[0:1, :] * same2[:, :1] * ext_ref[s, pl.ds(6, length), :D]
        )
        conv_ref[rows, :] = conv
        gated_ref[rows, :] = (c_ref[rows, :] * conv).astype(bf16)
    gated = gated_ref[...]
    mid_out = (dot_nt(gated, tb_ref[:, A_OUT : A_OUT + D]).astype(bf16).astype(f32) * twice).astype(bf16)
    mo_ref[...] = mid_out
    for k in range(2):
        cols = slice(512 * k, 512 * k + 512)
        h1_ref[:, cols] = (
            tok_ref[:, cols].astype(f32)
            + dot(gated, wo_ref[:, cols])
            + dot(mid_out, tb_ref[:, B_OUT + 512 * k : B_OUT + 512 * k + 512])
        )
    u2 = norm(h1_ref[...], n2_ref[...])[0].astype(bf16)
    u2_ref[...] = u2
    mg_ref[...] = (dot_nt(u2, tb_ref[:, A_GATE : A_GATE + D]).astype(bf16).astype(f32) * twice).astype(bf16)
    mu_ref[...] = (dot_nt(u2, tb_ref[:, A_UP : A_UP + D]).astype(bf16).astype(f32) * twice).astype(bf16)


def pre(seqs, length, count, *args):
    rows = seqs * length
    sd = jax.ShapeDtypeStruct
    width = D + 128
    vm = pl.BlockSpec(memory_space=pltpu.VMEM)
    wide = sd((rows, D), f32)
    half = sd((rows, D), bf16)
    thin = sd((rows, 128), bf16)
    return pl.pallas_call(
        functools.partial(pre_kernel, seqs, length, count),
        in_specs=[vm] * 10,
        out_specs=[vm] * 14,
        out_shape=[half, thin, wide, wide, wide, wide, sd((2, rows, 128), f32), half, thin, wide, half, thin, thin, thin],
        scratch_shapes=[
            pltpu.VMEM((seqs, length + 8, width), f32),
            pltpu.VMEM((2 * seqs, width), f32),
            pltpu.VMEM((2 * seqs, width), f32),
            pltpu.SemaphoreType.DMA,
            pltpu.SemaphoreType.DMA,
        ],
        compiler_params=pltpu.CompilerParams(vmem_limit_bytes=60 * MIB, collective_id=0, has_side_effects=True),
    )(*args)


def ffn_kernel(
    seqs, length,
    u_ref, cot_ref, mg_ref, mu_ref, gd_ref, mask_ref, h1_ref, wg_ref, wu_ref, wd_ref, bg_ref, bu_ref, ad_ref, ag_ref, au_ref, bd_ref,
    out_ref, gn_ref, dbg_ref, dbu_ref, dad_ref, dag_ref, dau_ref, dbd_ref,
    acc_ref, dmid_ref, gmg_ref, gmu_ref,
):
    j = pl.program_id(0)

    @pl.when(j == 0)
    def _():
        for ref in (acc_ref, gn_ref, dmid_ref, gmg_ref, gmu_ref):
            ref[...] = jnp.zeros_like(ref)

    u = u_ref[...]
    gate = dot(u, wg_ref[...]) + dot(mg_ref[...], bg_ref[...])
    up = dot(u, wu_ref[...]) + dot(mu_ref[...], bu_ref[...])
    back = dot_nt(cot_ref[...], wd_ref[...]) + dot(gd_ref[...], ad_ref[...])
    sig = jax.nn.sigmoid(gate)
    silu = gate * sig
    hidden = (silu * up).astype(bf16)
    grad_gate = (back * up * sig * (1.0 + gate * (1.0 - sig))).astype(bf16)
    grad_up = (back * silu).astype(bf16)
    acc_ref[...] += dot(hidden, wd_ref[...])
    gn_ref[...] += dot_nt(grad_gate, wg_ref[...]) + dot_nt(grad_up, wu_ref[...])
    dmid_ref[...] += dot_nt(hidden, ad_ref[...])
    gmg_ref[...] += dot_nt(grad_gate, bg_ref[...])
    gmu_ref[...] += dot_nt(grad_up, bu_ref[...])
    dbg_ref[...] = dot_tn(mg_ref[...], grad_gate).astype(bf16)
    dbu_ref[...] = dot_tn(mu_ref[...], grad_up).astype(bf16)
    dad_ref[...] = dot_tn(gd_ref[...], hidden).astype(bf16)

    @pl.when(j == pl.num_programs(0) - 1)
    def _():
        twice = 2.0 * row_mask(mask_ref, seqs, length)
        dmid = (dmid_ref[...].astype(bf16).astype(f32) * twice).astype(bf16)
        out_ref[...] = (h1_ref[...] + acc_ref[...] + dot(dmid, bd_ref[...])).astype(bf16)
        dbd_ref[...] = dot_tn(dmid, cot_ref[...]).astype(bf16)
        gm_gate = (gmg_ref[...] * twice).astype(bf16)
        gm_up = (gmu_ref[...] * twice).astype(bf16)
        gn_ref[...] += dot(gm_gate, ag_ref[...]) + dot(gm_up, au_ref[...])
        dag_ref[...] = dot_tn(gm_gate, u_ref[...]).astype(bf16)
        dau_ref[...] = dot_tn(gm_up, u_ref[...]).astype(bf16)


def ffn(seqs, length, u2, cot, mg, mu, gd, mask, h1, wg, wu, wd, table):
    rows = seqs * length
    sd = jax.ShapeDtypeStruct
    whole = lambda s: pl.BlockSpec(s, lambda j: (0, 0))
    col = lambda h: pl.BlockSpec((h, FB), lambda j: (0, j))
    tab = lambda first: pl.BlockSpec((128, FB), lambda j: (0, first // FB + j))
    fixed = lambda first: pl.BlockSpec((128, D), lambda j: (0, 0))
    cut = lambda first: lax.slice_in_dim(table, first, first + D, axis=1)
    return pl.pallas_call(
        functools.partial(ffn_kernel, seqs, length),
        grid=(FF // FB,),
        in_specs=[whole((rows, D)), whole((rows, D)), whole((rows, 128)), whole((rows, 128)), whole((rows, 128)),
                  whole(mask.shape), whole((rows, D)),
                  col(D), col(D), pl.BlockSpec((FB, D), lambda j: (j, 0)),
                  tab(B_GATE), tab(B_UP), tab(A_DOWN), whole((128, D)), whole((128, D)), whole((128, D))],
        out_specs=[whole((rows, D)), whole((rows, D)), col(128), col(128), col(128),
                   whole((128, D)), whole((128, D)), whole((128, D))],
        out_shape=[sd((rows, D), bf16), sd((rows, D), f32)] + [sd((128, FF), bf16)] * 3 + [sd((128, D), bf16)] * 3,
        scratch_shapes=[pltpu.VMEM((rows, D), f32)] + [pltpu.VMEM((rows, 128), f32)] * 3,
        compiler_params=pltpu.CompilerParams(vmem_limit_bytes=60 * MIB),
    )(u2, cot, mg, mu, gd, mask, h1, wg, wu, wd, table, table, table, cut(A_GATE), cut(A_UP), cut(B_DOWN))


def post_kernel(
    seqs, length, count,
    tok_ref, cot_ref, mask_ref, h1_ref, gn_ref, gated_ref, mo_ref, b_ref, c_ref, x_ref, conv_ref, same_ref, u1_ref, mi_ref,
    tb_ref, wi_ref, cw_ref, wo_ref, n1_ref, n2_ref,
    ig_ref, dai_ref, dbi_ref, dao_ref, dbo_ref,
    gh_ref, gb_ref, gg_ref, gc_ref, gp_ref, one_ref, two_ref, out_ref, in_ref, send_sem, recv_sem,
):
    seq = lax.axis_index("seq")
    greet(seq, count)
    twice = 2.0 * row_mask(mask_ref, seqs, length)
    h1 = h1_ref[...]
    inv2 = norm(h1, n2_ref[...])[1]
    e2 = gn_ref[...] * n2_ref[...]
    gh = cot_ref[...].astype(f32) + inv2 * e2 - h1 * (inv2 * inv2 * inv2 * jnp.mean(h1 * e2, axis=-1, keepdims=True))
    gh_ref[...] = gh
    gb = gh.astype(bf16)
    gb_ref[...] = gb
    gm_out = (dot_nt(gb, tb_ref[:, B_OUT : B_OUT + D]) * twice).astype(bf16)
    for k in range(2):
        cols = slice(512 * k, 512 * k + 512)
        gg_ref[:, cols] = dot_nt(gb, wo_ref[cols, :]) + dot(gm_out, tb_ref[:, A_OUT + 512 * k : A_OUT + 512 * k + 512])
    for s in range(seqs):
        rows = pl.ds(s * length, length)
        gg = gg_ref[rows, :]
        gp_ref[rows, D : 2 * D] = (gg * conv_ref[rows, :]).astype(bf16)
        gconv = gg * c_ref[rows, :]
        gc_ref[rows, :] = gconv
        one_ref[s, 0:length, :] = cw_ref[1:2, :] * same_ref[0, rows, 0:1] * gconv
        two_ref[s, 0:length, :] = cw_ref[0:1, :] * same_ref[1, rows, 0:1] * gconv
        one_ref[s, length:, :] = jnp.zeros((8, D), f32)
        two_ref[s, length:, :] = jnp.zeros((8, D), f32)
        out_ref[2 * s : 2 * s + 1, :] = two_ref[s, 0:1, :]
        out_ref[2 * s + 1 : 2 * s + 2, :] = two_ref[s, 1:2, :] + one_ref[s, 0:1, :]
    along = pltpu.make_async_remote_copy(
        src_ref=out_ref, dst_ref=in_ref, send_sem=send_sem, recv_sem=recv_sem,
        device_id={"seq": seq - 1}, device_id_type=MESH,
    )

    @pl.when(seq > 0)
    def _():
        along.start()

    dbo_ref[...] = dot_tn(mo_ref[...], gb).astype(bf16)
    dao_ref[...] = dot_tn(gm_out, gated_ref[...]).astype(bf16)

    @pl.when(seq > 0)
    def _():
        along.wait_send()

    @pl.when(seq < count - 1)
    def _():
        along.wait_recv()
        for s in range(seqs):
            two_ref[s, length : length + 2, :] = in_ref[2 * s : 2 * s + 2, :]

    for s in range(seqs):
        rows = pl.ds(s * length, length)
        gmix = (
            cw_ref[2:3, :] * gc_ref[rows, :]
            + one_ref[s, pl.ds(1, length), :]
            + two_ref[s, pl.ds(2, length), :]
        )
        gp_ref[rows, 0:D] = (gmix * x_ref[rows, :]).astype(bf16)
        gp_ref[rows, 2 * D :] = (gmix * b_ref[rows, :]).astype(bf16)
    gm_in = (dot_nt(gp_ref[...], tb_ref[:, B_IN : B_IN + 3 * D]) * twice).astype(bf16)
    for k in range(2):
        cols = slice(512 * k, 512 * k + 512)
        gg_ref[:, cols] = dot_nt(gp_ref[...], wi_ref[cols, :]) + dot(gm_in, tb_ref[:, A_IN + 512 * k : A_IN + 512 * k + 512])
    for k in range(6):
        cols = slice(512 * k, 512 * k + 512)
        dbi_ref[:, cols] = dot_tn(mi_ref[...], gp_ref[:, cols]).astype(bf16)
    dai_ref[...] = dot_tn(gm_in, u1_ref[...]).astype(bf16)
    tokens = tok_ref[...].astype(f32)
    inv1 = norm(tokens, n1_ref[...])[1]
    e1 = gg_ref[...] * n1_ref[...]
    ig_ref[...] = (
        gh_ref[...] + inv1 * e1 - tokens * (inv1 * inv1 * inv1 * jnp.mean(tokens * e1, axis=-1, keepdims=True))
    ).astype(bf16)


def post(seqs, length, count, *args):
    rows = seqs * length
    sd = jax.ShapeDtypeStruct
    vm = pl.BlockSpec(memory_space=pltpu.VMEM)
    return pl.pallas_call(
        functools.partial(post_kernel, seqs, length, count),
        in_specs=[vm] * 20,
        out_specs=[vm] * 5,
        out_shape=[sd((rows, D), bf16), sd((128, D), bf16), sd((128, 3 * D), bf16), sd((128, D), bf16), sd((128, D), bf16)],
        scratch_shapes=[
            pltpu.VMEM((rows, D), f32),
            pltpu.VMEM((rows, D), bf16),
            pltpu.VMEM((rows, D), f32),
            pltpu.VMEM((rows, D), f32),
            pltpu.VMEM((rows, 3 * D), bf16),
            pltpu.VMEM((seqs, length + 8, D), f32),
            pltpu.VMEM((seqs, length + 8, D), f32),
            pltpu.VMEM((2 * seqs, D), f32),
            pltpu.VMEM((2 * seqs, D), f32),
            pltpu.SemaphoreType.DMA,
            pltpu.SemaphoreType.DMA,
        ],
        compiler_params=pltpu.CompilerParams(vmem_limit_bytes=62 * MIB, collective_id=1, has_side_effects=True),
    )(*args)


def general_device(
    tokens, segment_ids, adapter_ids, input_weight, conv_weight, output_weight, gate_weight, up_weight, down_weight,
    norm_one, norm_two, cotangent, adapter_state, first_moment, second_moment, rate, step,
):
    seqs, length, _ = tokens.shape
    na = adapter_state.shape[0]
    groups = lax.axis_size("grp")
    count = lax.axis_size("seq")
    native = lambda x: x.reshape(na, PACKROWS, 128).swapaxes(0, 1).reshape(na * PACKROWS, 128)
    st, m, v = native(adapter_state), native(first_moment), native(second_moment)
    own = build_table(st, na)
    table = lax.all_gather(own, "grp", axis=0, tiled=True)
    adapters = na * groups
    mask = (adapter_ids[:, None] == jnp.arange(adapters * RANK, dtype=jnp.int32)[None, :] // RANK).astype(f32)
    ids = segment_ids.astype(f32)
    rows = seqs * length
    tok2, cot2 = tokens.reshape(rows, D), cotangent.reshape(rows, D)
    n1, n2 = norm_one.reshape(1, D), norm_two.reshape(1, D)
    u1, mi, b, c, x, conv, same, gated, mo, h1, u2, mg, mu, gd = pre(
        seqs, length, count, tok2, ids, mask, table, input_weight, conv_weight, output_weight, n1, n2, cot2
    )
    out, gn, dbg, dbu, dad, dag, dau, dbd = ffn(
        seqs, length, u2, cot2, mg, mu, gd, mask, h1, gate_weight, up_weight, down_weight, table
    )
    ig, dai, dbi, dao, dbo = post(
        seqs, length, count, tok2, cot2, mask, h1, gn, gated, mo, b, c, x, conv, same, u1, mi,
        table, input_weight, conv_weight, output_weight, n1, n2,
    )
    grads = jnp.concatenate([dai, dbi, dao, dbo, dag, dbg, dau, dbu, dad, dbd], axis=1).astype(f32)
    owned = lax.psum(lax.psum_scatter(grads, "grp", scatter_dimension=0, tiled=True), "seq")
    correction = 1.0 - jnp.power(jnp.float32(0.5), step[0].astype(f32))
    scal = jnp.stack([rate[0], 1.0 / correction])
    new, tab = adam(scal, owned, st, m, v, na)
    every = lax.all_gather(tab, "grp", axis=0, tiled=False)
    every = every.reshape(groups, PACKROWS, na, 128).transpose(1, 0, 2, 3).reshape(PACKROWS, adapters, 128)
    every = every.swapaxes(0, 1).reshape(adapters, PACKROWS * 128)
    new = new.reshape(PACKROWS, na, 128).swapaxes(0, 1).reshape(na, PACKROWS * 128)
    return out.reshape(tokens.shape), ig.reshape(tokens.shape), new, every


W_A_IN, W_B_B, W_B_X, W_B_C, W_A_OUT, W_B_OUT, W_A_GATE, W_A_UP, W_B_DOWN, W_FFN = (1024 * n for n in range(10))
W_ENDS = W_A_GATE
BLOCKS = FF // FB
W_BLOCK = 3 * FB
FFN_COLS = WIRE - W_ENDS
SPREAD_BLOCKS = 2


def wire(first, n):
    if first == B_IN:
        return (W_B_B, W_B_C, W_B_X)[n // D] + n % D
    for place, matrix in enumerate((B_GATE, B_UP, A_DOWN)):
        if first == matrix:
            return W_FFN + n // FB * W_BLOCK + place * FB + n % FB
    return {A_IN: W_A_IN, A_OUT: W_A_OUT, B_OUT: W_B_OUT, A_GATE: W_A_GATE, A_UP: W_A_UP, B_DOWN: W_B_DOWN}[first] + n


def a_pieces(first, count):
    for matrix, height in A_PARTS:
        if matrix <= first < matrix + height:
            return [(k, wire(matrix, first - matrix + k), FB) for k in range(0, count, FB)]


class Place:
    def __init__(self):
        seq, grp = lax.axis_index("seq"), lax.axis_index("grp")
        self.seq, self.grp = seq, grp
        self.c, self.x, self.y, self.z = grp % 2, grp // 2, seq % 2, seq // 2
        self.core = grp + 1 - 2 * self.c
        self.gx = (grp + 2) % 4
        self.sy = seq + 1 - 2 * self.y
        self.sz = seq + 2 - 4 * (self.z % 2)

    def along_z(self, d):
        return (self.seq + 2 * d) % 8


def announce(seq, count, devices, both=True):
    barrier = pltpu.get_barrier_semaphore()
    if both:

        @pl.when(seq > 0)
        def _():
            pl.semaphore_signal(barrier, inc=1, device_id={"seq": seq - 1}, device_id_type=MESH)

        @pl.when(seq < count - 1)
        def _():
            pl.semaphore_signal(barrier, inc=1, device_id={"seq": seq + 1}, device_id_type=MESH)

    for device in devices:
        pl.semaphore_signal(barrier, inc=1, device_id=device, device_id_type=MESH)
    ends = (seq + count - 1) // count + (2 * count - 2 - seq) // count if both else 0
    return lambda: pl.semaphore_wait(barrier, ends + len(devices))


class Spread:
    WAYS = {
        "X": (((), ("x", "core")), (("x",), ("cx",)), (("core", "cx"), ())),
        "Y": (((), ("x", "core")), (("x",), ("y", "cx")), (("y",), ("cy",)), (("core", "cx", "cy"), ())),
        "Z": (((), ("x", "core")), (("x",), ("z", "cx")), (("z",), ("cz",)), (("core", "cx", "cz"), ())),
        "S": (
            ((), ("x", "core")), (("x",), ("y", "z", "cx")), (("y",), ("dz", "cy")), (("z",), ("dy", "cz")), (("dy", "dz"), ("cd",)),
            (("core", "cx", "cy", "cz", "cd"), ()),
        ),
    }
    KINDS = ("core", "x", "y", "z", "dy", "dz", "cx", "cy", "cz", "cd")

    def __init__(self, at, own, slot, pieces, ways, step, send_sems, recv_sems):
        self.at, self.own, self.slot, self.pieces, self.ways, self.step = at, own, slot, pieces, ways, step
        self.send_sems, self.recv_sems = send_sems, recv_sems

    def copy(self, kind, p):
        at, way = self.at, self.ways[p]
        first, size = self.pieces[p]
        share = size // {"X": 1, "Y": 2, "Z": 2, "S": 4}[way]
        part = lambda q: pl.multiple_of(first + q * share, self.step) if way != "X" else first
        q = {"X": 0, "Y": at.y, "Z": at.z % 2, "S": at.seq % 4}[way]
        if way == "S":
            qy, qz, qd = q + 1 - 2 * (q % 2), (q + 2) % 4, 3 - q
        else:
            qy = qz = qd = 1 - q
        half = -(-share // (2 * self.step)) * self.step
        core, y, z = {"grp": at.core}, {"seq": at.sy}, {"seq": at.sz}
        if kind == "core":
            src, dst, device = self.own(first, size), self.slot(at.grp, first, size), core
        elif kind == "x":
            src, dst, device = self.own(part(q), share), self.slot(at.grp, part(q), share), {"grp": at.gx}
        else:
            start, count, device = {
                "y": (part(q), share, y),
                "z": (part(q), share, z),
                "dy": (part(qz), half, y),
                "dz": (part(qy) + half, share - half, z),
                "cx": (part(q), share, core),
                "cy": (part(qy), share, core),
                "cz": (part(qz), share, core),
                "cd": (part(qd), share, core),
            }[kind]
            if kind == "dz":
                start = pl.multiple_of(start, self.step)
            src = dst = self.slot(at.gx, start, count)
        n = len(self.KINDS) * p + self.KINDS.index(kind)
        return pltpu.make_async_remote_copy(
            src_ref=src, dst_ref=dst, send_sem=self.send_sems.at[n], recv_sem=self.recv_sems.at[n],
            device_id=device, device_id_type=MESH,
        )

    def steps(self, p):
        return len(self.WAYS[self.ways[p]])

    def leg(self, number, p):
        waits, starts = self.WAYS[self.ways[p]][number]
        for kind in waits:
            self.copy(kind, p).wait_recv()
        for kind in starts:
            self.copy(kind, p).start()

    def sent(self, p):
        for _, starts in self.WAYS[self.ways[p]]:
            for kind in starts:
                self.copy(kind, p).wait_send()


def adapter_mask(adapter_ref, seqs, length):
    column = lax.broadcasted_iota(jnp.int32, (length, 128), 1) // RANK
    return jnp.concatenate([jnp.where(column == adapter_ref[s], 1.0, 0.0) for s in range(seqs)], axis=0)


def fill_shuffle(perm_ref):
    diff = lax.broadcasted_iota(jnp.int32, (128, 1024), 1) - 8 * lax.broadcasted_iota(jnp.int32, (128, 1024), 0)
    for c in range(8):
        perm_ref[128 * c : 128 * c + 128, :] = jnp.where(diff == c, 1.0, 0.0).astype(bf16)


def build_own(na, grp, st_ref, tb_ref, lhs_ref, perm_ref):
    own = lambda a: pl.ds(pl.multiple_of((grp * na + a) * RANK, RANK), RANK)
    fill_shuffle(perm_ref)
    for n, (first, count) in enumerate(A_CHUNKS):
        for a in range(na):
            packed = st_ref[pl.ds(na * (first // 8) + a, 128, stride=na), :]
            turned = packed.T.astype(bf16)
            row = (n * na + a) * RANK
            for c in range(8):
                lhs_ref[row : row + RANK, 128 * c : 128 * c + 128] = turned[RANK * c : RANK * c + RANK, :]
    full = dot(lhs_ref[...], perm_ref[...]).astype(bf16)
    for n, (first, count) in enumerate(A_CHUNKS):
        for a in range(na):
            row = (n * na + a) * RANK
            for k, col, size in a_pieces(first, count):
                tb_ref[own(a), col : col + size] = full[row : row + RANK, k : k + size]
    for first, breadth in B_PARTS:
        blocks = breadth // 128
        for a in range(na):
            for c in range(blocks):
                part = st_ref[pl.ds(na * (first // 8 + c) + a, RANK, stride=na * blocks), :]
                col = wire(first, 128 * c)
                tb_ref[own(a), col : col + 128] = part.astype(bf16)


SPREAD_PIECES = ((W_A_IN, 1024), (W_B_B, 2048), (W_B_C, 1024), (W_A_OUT, 5120), (W_FFN, SPREAD_BLOCKS * W_BLOCK))


class Sums:
    CORE, X, Y, Z, BACK_Z, BACK_Y = range(6)
    COPIES = 10

    def __init__(self, at, g_ref, cr_ref, xr_ref, yr_ref, zr_ref, sum_ref, send_sems, recv_sems):
        self.at, self.g, self.cr, self.xr, self.yr, self.zr, self.sum = at, g_ref, cr_ref, xr_ref, yr_ref, zr_ref, sum_ref
        self.send_sems, self.recv_sems = send_sems, recv_sems

    def unit(self, z, start, size):
        rows = pl.ds(pl.multiple_of(RANK * (z // 2), RANK), RANK)
        quarter = size // 4
        return rows, pl.ds(pl.multiple_of(start + self.at.y * (size // 2) + (z % 2) * quarter, 128), quarter)

    def half(self, y, start, size):
        return pl.ds(pl.multiple_of(start + y * (size // 2), 128), size // 2)

    def slot(self, start, size, share):
        return pl.ds(pl.multiple_of(start // share, 128), size // share)

    def copies(self, stage, group):
        index, start, size = group
        at = self.at
        cols = pl.ds(start, size)
        if stage == self.CORE:
            parts = [(self.g.at[:, 1 - at.c, :, cols], self.cr.at[:, :, cols], {"grp": at.core})]
        elif stage == self.X:
            parts = [(self.g.at[1 - at.x, at.c, :, cols], self.xr.at[:, cols], {"grp": at.gx})]
        elif stage == self.Y:
            away = self.half(1 - at.y, start, size)
            parts = [(self.g.at[at.x, at.c, :, away], self.yr.at[:, self.slot(start, size, 2)], {"seq": at.sy})]
        elif stage == self.BACK_Y:
            part = self.sum.at[:, self.half(at.y, start, size)]
            parts = [(part, part, {"seq": at.sy})]
        else:
            parts = []
            for d in range(1, 4):
                if stage == self.Z:
                    rows, span = self.unit((at.z + d) % 4, start, size)
                    parts.append((
                        self.g.at[at.x, at.c, rows, span], self.zr.at[d - 1, :, self.slot(start, size, 4)],
                        {"seq": at.along_z(d)},
                    ))
                else:
                    rows, span = self.unit(at.z, start, size)
                    part = self.sum.at[rows, span]
                    parts.append((part, part, {"seq": at.along_z(d)}))
        first = self.COPIES * index + {self.CORE: 0, self.X: 1, self.Y: 2, self.Z: 3, self.BACK_Z: 6, self.BACK_Y: 9}[stage]
        return [
            pltpu.make_async_remote_copy(
                src_ref=src, dst_ref=dst, send_sem=self.send_sems.at[first + n], recv_sem=self.recv_sems.at[first + n],
                device_id=device, device_id_type=MESH,
            )
            for n, (src, dst, device) in enumerate(parts)
        ]

    def send(self, stage, group):
        for copy in self.copies(stage, group):
            copy.start()

    def take(self, stage, group):
        for copy in self.copies(stage, group):
            copy.wait()
        _, start, size = group
        at = self.at
        cols = pl.ds(start, size)
        wide = lambda value: value.astype(f32)
        if stage == self.CORE:
            for x in range(2):
                self.g[x, at.c, :, cols] = (wide(self.g[x, at.c, :, cols]) + wide(self.cr[x, :, cols])).astype(bf16)
        elif stage == self.X:
            self.g[at.x, at.c, :, cols] = (wide(self.g[at.x, at.c, :, cols]) + wide(self.xr[:, cols])).astype(bf16)
        elif stage == self.Y:
            mine = self.half(at.y, start, size)
            came = self.yr[:, self.slot(start, size, 2)]
            self.g[at.x, at.c, :, mine] = (wide(self.g[at.x, at.c, :, mine]) + wide(came)).astype(bf16)
        elif stage == self.Z:
            rows, span = self.unit(at.z, start, size)
            total = wide(self.g[at.x, at.c, rows, span])
            for d in range(3):
                total = total + wide(self.zr[d, :, self.slot(start, size, 4)])
            self.sum[rows, span] = total.astype(bf16)


def sums_scratch(cols):
    return [
        pltpu.VMEM((2, 2, 32, cols), bf16),
        pltpu.VMEM((2, 32, cols), bf16),
        pltpu.VMEM((32, cols), bf16),
        pltpu.VMEM((32, cols // 2), bf16),
        pltpu.VMEM((3, 16, cols // 4), bf16),
        pltpu.VMEM((32, cols), bf16),
    ]


def put_grad(g_ref, cols, value):
    for x in range(2):
        for c in range(2):
            first = 64 * x + 32 * c
            g_ref[x, c, :, cols] = value[first : first + 32, :].astype(bf16)


UPDATES = (
    (B_GATE, FF), (B_UP, FF), (A_DOWN, FF), (A_GATE, D), (A_UP, D), (B_DOWN, D), (A_OUT, 2 * D), (B_IN, 3 * D),
    (A_IN, D),
)
MOST = 2 * FF // 8
NATIVE = tuple((2 * first // 8, 2 * count // 8) for first, count in UPDATES)


def update_grad(na, part, sum_ref, lhs_ref, perm_ref, gn_ref):
    first, count = UPDATES[part]
    begin = na * first // 8
    inside = lambda start: first <= start < first + count
    chunks = [chunk for chunk in A_CHUNKS if inside(chunk[0])]
    for n, (start, size) in enumerate(chunks):
        for a in range(na):
            row = (n * na + a) * RANK
            if size < 1024:
                lhs_ref[row : row + RANK, size:] = jnp.zeros((RANK, 1024 - size), bf16)
            for k, col, breadth in a_pieces(start, size):
                lhs_ref[row : row + RANK, k : k + breadth] = sum_ref[a * RANK : (a + 1) * RANK, col : col + breadth]
    if chunks:
        height = len(chunks) * na * RANK
        full = dot_nt(lhs_ref[:height, :], perm_ref[...])
    for n, (start, size) in enumerate(chunks):
        for a in range(na):
            row = (n * na + a) * RANK
            turned = jnp.concatenate([full[row : row + RANK, 128 * c : 128 * c + 128] for c in range(8)], axis=0)
            gn_ref[pl.ds(na * (start // 8) + a - begin, size // 8, stride=na), :] = turned.T[: size // 8]
    for start, breadth in B_PARTS:
        if inside(start):
            blocks = breadth // 128
            for a in range(na):
                for c in range(blocks):
                    col = wire(start, 128 * c)
                    gn_ref[pl.ds(na * (start // 8 + c) + a - begin, RANK, stride=na * blocks), :] = sum_ref[
                        a * RANK : (a + 1) * RANK, col : col + 128
                    ].astype(f32)


def group_of(j):
    start = W_FFN + j * W_BLOCK
    return j, start if isinstance(j, int) else pl.multiple_of(start, 128), W_BLOCK


GROUPS = {
    "ends": (BLOCKS, W_ENDS, W_FFN - W_ENDS),
    "out": (BLOCKS + 1, W_B_C, W_ENDS - W_B_C),
    "in1": (BLOCKS + 2, W_B_B, W_B_C - W_B_B),
    "in2": (BLOCKS + 3, W_A_IN, W_B_B),
}
GROUPS.update({j: group_of(j) for j in range(BLOCKS)})


WAYS = "ZZYXXXYXX"
BACKWARD_ORDER = (
    (8, 7, 6, 5, 4, 3, 2, 8), 0, ("ends", 6, 7, 3, 5), 1, ("ends", 4, 8, 7, 6, 5), 2, (4, 8), 3, ("ends", 7, 5, 6), 4,
    ("out", 8), 5, ("out", "ends", 7, 6, 8), 6, ("in1",), 7, ("in1", "in2", 7, 8), 8, ("in2", "out", "ends"), 9,
    ("in1", "in2"), 10,
)
TAIL_ORDER = (
    ("sum", "out"), ("update", 0), ("sum", "in1"), ("sum", "in2"), ("sum", "ends"), ("update", 1), ("update", 2),
    ("out", 0), ("sum", "out"), ("sum", "ends"), ("update", 3), ("sum", "in1"), ("update", 4), ("sum", "in2"),
    ("update", 5), ("pass", 0), ("out", 1), ("pass", 1), ("out", 2), ("sum", "out"), ("out", 3), ("sum", "in1"),
    ("out", 4), ("sum", "in2"), ("pass", 2), ("out", 5), ("sum", "out"), ("update", 6), ("pass", 3), ("sum", "in1"),
    ("update", 7), ("sum", "in2"), ("update", 8), ("pass", 0), ("pass", 3), ("pass", 4), ("pass", 5), ("out", 6),
    ("pass", 0), ("pass", 1), ("pass", 4), ("pass", 2), ("pass", 5), ("pass", 6), ("out", 7), ("pass", 1), ("pass", 2),
    ("out", 8), ("pass", 7), ("pass", 6), ("pass", 8), ("pass", 7), ("pass", 6), ("pass", 8),
)


def rest_kernel(
    seqs, length, count, na,
    adapter_ref, rate_ref, step_ref, cot_ref, ids_ref, cw_ref, n1_ref, n2_ref,
    tok_hbm, wi_hbm, wo_hbm, wg_hbm, wu_hbm, wd_hbm, st_hbm, m_hbm, v_hbm,
    out_ref, ig_ref, new_hbm, all_hbm, hid_hbm, gated_hbm, b_hbm, c_hbm, x_hbm, conv_hbm, same_hbm, u1_hbm,
    u_ref, mg_ref, mu_ref, mo_ref, mi_ref, ahead_out_ref, ahead_in_ref, tb_ref, h1_ref, gn_ref, gh_ref, gb_ref, dmid_ref, gmg_ref, gmu_ref, gd_ref,
    edge_out_ref, edge_in_ref, g_ref, cr_ref, xr_ref, yr_ref, zr_ref, sum_ref, tab_ref,
    open_sems, store_sems, open_send, open_recv, load_sems, weight_sems, hid_sems, tab_send, tab_recv, send_sems, recv_sems,
    halo_sems, old_sems, new_sems, own_sems, spread_send, spread_recv,
):
    rows_all = seqs * length
    at = Place()
    seq = at.seq
    met = announce(seq, count, [{"grp": at.core}, {"grp": at.gx}] + [{"seq": at.along_z(d)} for d in range(1, 4)])
    sums = Sums(at, g_ref, cr_ref, xr_ref, yr_ref, zr_ref, sum_ref, send_sems, recv_sems)
    rows32 = lambda owner: pl.ds(pl.multiple_of(owner * 32, 32), 32)
    twice = 2.0 * adapter_mask(adapter_ref, seqs, length)
    block = lambda owner, first, size: tb_ref.at[rows32(owner), pl.ds(first, size)]
    table_spread = Spread(
        at, functools.partial(block, at.grp), block, SPREAD_PIECES, "XXXSS", 128, open_send, open_recv
    )

    def opening(
        st_ref, lhs_ref, perm_ref, wi_ref, wo_ref, tok_ref, u1_ref, b_ref, c_ref, x_ref, conv_ref, same_ref, gated_ref, ext_ref
    ):
        load_in = pltpu.make_async_copy(wi_hbm, wi_ref, open_sems.at[0])
        load_out = pltpu.make_async_copy(wo_hbm, wo_ref, open_sems.at[1])
        load_st = pltpu.make_async_copy(st_hbm, st_ref, open_sems.at[2])
        load_tok = pltpu.make_async_copy(tok_hbm, tok_ref, open_sems.at[3])
        for copy in (load_st, load_tok, load_in, load_out):
            copy.start()
        load_st.wait()
        build_own(na, at.grp, st_ref, tb_ref, lhs_ref, perm_ref)
        leg = table_spread.leg

        def keep(n, src, dst):
            return pltpu.make_async_copy(src, dst, store_sems.at[n])

        met()
        leg(0, 0)
        load_tok.wait()
        tokens = tok_ref[...].astype(f32)
        u1 = norm(tokens, n1_ref[...])[0].astype(bf16)
        u1_ref[...] = u1
        leg(0, 1)
        keep(0, u1_ref, u1_hbm).start()
        load_in.wait()
        for k in range(2):
            b_ref[:, 512 * k : 512 * k + 512] = dot(u1, wi_ref[:, 512 * k : 512 * k + 512])
        leg(0, 2)
        leg(1, 0)
        for k in range(2):
            x_ref[:, 512 * k : 512 * k + 512] = dot(u1, wi_ref[:, 2 * D + 512 * k : 2 * D + 512 * k + 512])
        leg(0, 3)
        leg(0, 4)
        for k in range(2):
            c_ref[:, 512 * k : 512 * k + 512] = dot(u1, wi_ref[:, D + 512 * k : D + 512 * k + 512])
        leg(1, 1)
        leg(2, 0)
        mid = (dot_nt(u1, tb_ref[:, W_A_IN : W_A_IN + D]).astype(bf16).astype(f32) * twice).astype(bf16)
        mi_ref[...] = mid
        leg(1, 2)
        leg(2, 1)
        for first, to_ref in ((W_B_B, b_ref), (W_B_X, x_ref)):
            for k in range(2):
                col = first + 512 * k
                to_ref[:, 512 * k : 512 * k + 512] += dot(mid, tb_ref[:, col : col + 512])
        leg(1, 3)
        leg(1, 4)
        keep(1, b_ref, b_hbm).start()
        keep(2, x_ref, x_hbm).start()
        width = D + 128
        for s in range(seqs):
            rows = pl.ds(s * length, length)
            ext_ref[s, 0:8, :] = jnp.zeros((8, width), f32)
            ext_ref[s, 8:, :D] = b_ref[rows, :] * x_ref[rows, :]
            ext_ref[s, 8:, D:] = jnp.broadcast_to(ids_ref[s : s + 1, :].astype(f32), (length, 128)).T
            ahead_out_ref[2 * s : 2 * s + 2, :] = ext_ref[s, length + 6 : length + 8, :]
        along = pltpu.make_async_remote_copy(
            src_ref=ahead_out_ref, dst_ref=ahead_in_ref, send_sem=halo_sems.at[2], recv_sem=halo_sems.at[3],
            device_id={"seq": seq + 1}, device_id_type=MESH,
        )

        @pl.when(seq < count - 1)
        def _():
            along.start()

        leg(2, 2)
        leg(2, 3)
        leg(3, 3)
        for k in range(2):
            col = W_B_C + 512 * k
            c_ref[:, 512 * k : 512 * k + 512] += dot(mid, tb_ref[:, col : col + 512])
        leg(2, 4)
        leg(3, 4)
        keep(3, c_ref, c_hbm).start()

        @pl.when(seq < count - 1)
        def _():
            along.wait_send()

        @pl.when(seq > 0)
        def _():
            along.wait_recv()
            for s in range(seqs):
                ext_ref[s, 6:8, :] = ahead_in_ref[2 * s : 2 * s + 2, :]

        for s in range(seqs):
            rows = pl.ds(s * length, length)
            now_ids = ext_ref[s, 8:, D:]
            same1 = jnp.where(ext_ref[s, pl.ds(7, length), D:] == now_ids, 1.0, 0.0)
            same2 = jnp.where(ext_ref[s, pl.ds(6, length), D:] == now_ids, 1.0, 0.0)
            same_ref[0, s] = same1
            same_ref[1, s] = same2
            conv = (
                cw_ref[2:3, :] * ext_ref[s, 8:, :D]
                + cw_ref[1:2, :] * same1[:, :1] * ext_ref[s, pl.ds(7, length), :D]
                + cw_ref[0:1, :] * same2[:, :1] * ext_ref[s, pl.ds(6, length), :D]
            )
            conv_ref[rows, :] = conv
            gated_ref[rows, :] = (c_ref[rows, :] * conv).astype(bf16)
        keep(4, conv_ref, conv_hbm).start()
        keep(5, same_ref, same_hbm).start()
        leg(4, 3)
        leg(4, 4)
        keep(6, gated_ref, gated_hbm).start()
        gated = gated_ref[...]
        load_out.wait()
        for k in range(2):
            cols = slice(512 * k, 512 * k + 512)
            h1_ref[:, cols] = tok_ref[:, cols].astype(f32) + dot(gated, wo_ref[:, cols])
        leg(5, 3)
        mid_out = (dot_nt(gated, tb_ref[:, W_A_OUT : W_A_OUT + D]).astype(bf16).astype(f32) * twice).astype(bf16)
        mo_ref[...] = mid_out
        for k in range(2):
            cols = slice(512 * k, 512 * k + 512)
            h1_ref[:, cols] += dot(mid_out, tb_ref[:, W_B_OUT + 512 * k : W_B_OUT + 512 * k + 512])
        u2 = norm(h1_ref[...], n2_ref[...])[0].astype(bf16)
        u_ref[...] = u2
        mg_ref[...] = (dot_nt(u2, tb_ref[:, W_A_GATE : W_A_GATE + D]).astype(bf16).astype(f32) * twice).astype(bf16)
        mu_ref[...] = (dot_nt(u2, tb_ref[:, W_A_UP : W_A_UP + D]).astype(bf16).astype(f32) * twice).astype(bf16)
        for n, (src, dst) in enumerate((
            (u1_ref, u1_hbm), (b_ref, b_hbm), (x_ref, x_hbm), (c_ref, c_hbm), (conv_ref, conv_hbm), (same_ref, same_hbm),
            (gated_ref, gated_hbm),
        )):
            keep(n, src, dst).wait()

    wide = pltpu.VMEM((rows_all, D), f32)
    half = pltpu.VMEM((rows_all, D), bf16)
    pl.run_scoped(
        opening,
        pltpu.VMEM((na * PACKROWS, 128), f32), pltpu.VMEM((len(A_CHUNKS) * na * RANK, 1024), bf16),
        pltpu.VMEM((1024, 1024), bf16), pltpu.VMEM((D, 3 * D), bf16), pltpu.VMEM((D, D), bf16),
        half, half, wide, wide, wide, wide, pltpu.VMEM((2, seqs, length, 128), f32), half,
        pltpu.VMEM((seqs, length + 8, D + 128), f32),
    )

    def table_copy(kind, j):
        _, start, size = group_of(j)
        owner, device = {
            "core": (at.grp, {"grp": at.core}), "x": (at.grp, {"grp": at.gx}), "far": (at.gx, {"grp": at.core})
        }[kind]
        part = tb_ref.at[rows32(owner), pl.ds(start, size)]
        n = 3 * j + ("core", "x", "far").index(kind)
        return pltpu.make_async_remote_copy(
            src_ref=part, dst_ref=part, send_sem=tab_send.at[n], recv_sem=tab_recv.at[n], device_id=device, device_id_type=MESH
        )

    def when(first, j, last, run):
        @pl.when((j >= first) & (j <= last))
        def _():
            run()

    def feed_forward(wg_ref, wu_ref, wd_ref, hid_ref):
        def fetch(j, slot):
            cols = pl.ds(j * FB if isinstance(j, int) else pl.multiple_of(j * FB, FB), FB)
            return [
                pltpu.make_async_copy(wg_hbm.at[:, cols], wg_ref.at[slot], weight_sems.at[slot, 0]),
                pltpu.make_async_copy(wu_hbm.at[:, cols], wu_ref.at[slot], weight_sems.at[slot, 1]),
                pltpu.make_async_copy(wd_hbm.at[cols, :], wd_ref.at[slot], weight_sems.at[slot, 2]),
            ]

        def keep(j, slot):
            cols = pl.ds(j * FB if isinstance(j, int) else pl.multiple_of(j * FB, FB), FB)
            return pltpu.make_async_copy(hid_ref.at[slot], hid_hbm.at[:, cols], hid_sems.at[slot])

        for copy in fetch(0, 0):
            copy.start()
        for ref in (gn_ref, dmid_ref, gmg_ref, gmu_ref):
            ref[...] = jnp.zeros_like(ref)
        gd_ref[...] = (dot_nt(cot_ref[...], tb_ref[:, W_B_DOWN : W_B_DOWN + D]) * twice).astype(bf16)
        table_spread.leg(5, 4)

        def block(j, carry):
            slot = j % 2
            for copy in fetch(j, slot):
                copy.wait()

            def more():
                for copy in fetch(j + 1, 1 - slot):
                    copy.start()

            when(0, j, BLOCKS - 2, more)
            when(2, j, BLOCKS - 1, lambda: keep(j - 2, slot).wait())
            lead = SPREAD_BLOCKS

            def leave():
                table_copy("x", j + lead).start()
                table_copy("core", j + lead).start()

            def go_on():
                table_copy("x", j + lead - 1).wait()
                table_copy("far", j + lead - 1).start()

            def there():
                table_copy("core", j).wait()
                table_copy("far", j).wait()

            when(0, j, BLOCKS - 1 - lead, leave)
            when(1, j, BLOCKS - lead, go_on)
            when(lead, j, BLOCKS - 1, there)
            for stage in range(6):

                def advance(stage=stage):
                    if stage > 0:
                        sums.take(stage - 1, group_of(j - 1 - stage))
                    sums.send(stage, group_of(j - 1 - stage))

                when(1 + stage, j, BLOCKS - 1, advance)
            when(7, j, BLOCKS - 1, lambda: sums.take(5, group_of(j - 7)))

            base = W_FFN + j * W_BLOCK
            part = lambda place: pl.ds(pl.multiple_of(base + place * FB, 128), FB)
            tab_gate, tab_up, tab_down = (tb_ref.at[:, part(place)] for place in range(3))
            u = u_ref[...]
            gate = dot(u, wg_ref[slot]) + dot(mg_ref[...], tab_gate[...])
            up = dot(u, wu_ref[slot]) + dot(mu_ref[...], tab_up[...])
            back = dot_nt(cot_ref[...], wd_ref[slot]) + dot(gd_ref[...], tab_down[...])
            sig = jax.nn.sigmoid(gate)
            silu = gate * sig
            hidden = (silu * up).astype(bf16)
            hid_ref[slot] = hidden
            keep(j, slot).start()
            grad_gate = (back * up * sig * (1.0 + gate * (1.0 - sig))).astype(bf16)
            grad_up = (back * silu).astype(bf16)
            gn_ref[...] += dot_nt(grad_gate, wg_ref[slot]) + dot_nt(grad_up, wu_ref[slot])
            dmid_ref[...] += dot_nt(hidden, tab_down[...])
            gmg_ref[...] += dot_nt(grad_gate, tab_gate[...])
            gmu_ref[...] += dot_nt(grad_up, tab_up[...])
            put_grad(g_ref, part(0), dot_tn(mg_ref[...], grad_gate))
            put_grad(g_ref, part(1), dot_tn(mu_ref[...], grad_up))
            put_grad(g_ref, part(2), dot_tn(gd_ref[...], hidden))
            return carry

        lax.fori_loop(0, BLOCKS, block, 0)
        for j in range(BLOCKS - 2, BLOCKS):
            keep(j, j % 2).wait()
        for p in range(len(SPREAD_PIECES)):
            table_spread.sent(p)

    pl.run_scoped(
        feed_forward,
        pltpu.VMEM((2, D, FB), bf16), pltpu.VMEM((2, D, FB), bf16), pltpu.VMEM((2, FB, D), bf16),
        pltpu.VMEM((2, rows_all, FB), bf16),
    )

    sent = {BLOCKS - 2 - stage: stage for stage in range(6)}

    def advance(*names):
        for name in names:
            stage = sent.get(name, -1)
            if stage >= 0:
                sums.take(stage, GROUPS[name])
            if stage < 5:
                sums.send(stage + 1, GROUPS[name])
            sent[name] = stage + 1

    dmid = (dmid_ref[...].astype(bf16).astype(f32) * twice).astype(bf16)

    def backward(gated_ref, one_ref, two_ref, same_ref, u1_ref, tok_ref, wi_ref, wo_ref, gg_ref, gp_ref):
        pairs = (
            (wo_hbm, wo_ref), (c_hbm, one_ref), (conv_hbm, two_ref), (same_hbm, same_ref.at[:, :, :length, :]),
            (gated_hbm, gated_ref), (wi_hbm, wi_ref), (u1_hbm, u1_ref), (tok_hbm, tok_ref), (x_hbm, one_ref), (b_hbm, two_ref),
        )
        copies = [pltpu.make_async_copy(*pair, load_sems.at[n]) for n, pair in enumerate(pairs)]
        get_wo, get_c, get_conv, get_same, get_gated, get_wi, get_u1, get_tok, get_x, get_b = copies
        for copy in (get_wo, get_c, get_conv, get_same):
            copy.start()
        held = {}

        def part0():
            held["gm_gate"] = (gmg_ref[...] * twice).astype(bf16)
            held["gm_up"] = (gmu_ref[...] * twice).astype(bf16)
            put_grad(g_ref, slice(W_A_GATE, W_A_GATE + D), dot_tn(held["gm_gate"], u_ref[...]))
            put_grad(g_ref, slice(W_A_UP, W_A_UP + D), dot_tn(held["gm_up"], u_ref[...]))
            put_grad(g_ref, slice(W_B_DOWN, W_B_DOWN + D), dot_tn(dmid, cot_ref[...]))

        def part1():
            for k in range(2):
                cols = slice(512 * k, 512 * k + 512)
                gn_ref[:, cols] += dot(held["gm_gate"], tb_ref[:, W_A_GATE + 512 * k : W_A_GATE + 512 * k + 512]) + dot(
                    held["gm_up"], tb_ref[:, W_A_UP + 512 * k : W_A_UP + 512 * k + 512]
                )
            for s in range(seqs):
                rows = pl.ds(s * length, length)
                h1 = h1_ref[rows, :]
                inv2 = norm(h1, n2_ref[...])[1]
                e2 = gn_ref[rows, :] * n2_ref[...]
                gh = cot_ref[rows, :].astype(f32) + inv2 * e2
                gh = gh - h1 * (inv2 * inv2 * inv2 * jnp.mean(h1 * e2, axis=-1, keepdims=True))
                gh_ref[rows, :] = gh
                gb_ref[rows, :] = gh.astype(bf16)
            for copy in (get_gated, get_wi, get_u1, get_tok):
                copy.start()

        def part2():
            get_wo.wait()
            held["gb"] = gb_ref[...]
            held["gm_out"] = (dot_nt(held["gb"], tb_ref[:, W_B_OUT : W_B_OUT + D]) * twice).astype(bf16)
            for k in range(2):
                cols = slice(512 * k, 512 * k + 512)
                part = dot_nt(held["gb"], wo_ref[cols, :]) + dot(held["gm_out"], tb_ref[:, W_A_OUT + 512 * k : W_A_OUT + 512 * k + 512])
                for s in range(seqs):
                    gg_ref[s, :length, cols] = part[s * length : (s + 1) * length, :]

        def part3():
            for copy in (get_c, get_conv, get_same):
                copy.wait()
            for s in range(seqs):
                rows = pl.ds(s * length, length)
                gg = gg_ref[s, :length, :]
                gp_ref[rows, D : 2 * D] = (gg * two_ref[rows, :]).astype(bf16)
                gg_ref[s, :length, :] = gg * one_ref[rows, :]
                gg_ref[s, length:, :] = jnp.zeros((8, D), f32)
                for k in range(2):
                    same_ref[k, s, length:, :] = jnp.zeros((8, 128), f32)
                edge_out_ref[2 * s : 2 * s + 1, :] = cw_ref[0:1, :] * same_ref[1, s, 0:1, 0:1] * gg_ref[s, 0:1, :]
                edge_out_ref[2 * s + 1 : 2 * s + 2, :] = (
                    cw_ref[0:1, :] * same_ref[1, s, 1:2, 0:1] * gg_ref[s, 1:2, :]
                    + cw_ref[1:2, :] * same_ref[0, s, 0:1, 0:1] * gg_ref[s, 0:1, :]
                )
            get_x.start()
            get_b.start()
            held["along"] = pltpu.make_async_remote_copy(
                src_ref=edge_out_ref, dst_ref=edge_in_ref, send_sem=halo_sems.at[0], recv_sem=halo_sems.at[1],
                device_id={"seq": seq - 1}, device_id_type=MESH,
            )

            @pl.when(seq > 0)
            def _():
                held["along"].start()

        def part4():
            get_gated.wait()
            put_grad(g_ref, slice(W_A_OUT, W_A_OUT + D), dot_tn(held["gm_out"], gated_ref[...]))
            put_grad(g_ref, slice(W_B_OUT, W_B_OUT + D), dot_tn(mo_ref[...], held["gb"]))
            put_grad(g_ref, slice(W_B_C, W_B_C + D), dot_tn(mi_ref[...], gp_ref[:, D : 2 * D]))

        def part5():

            @pl.when(seq > 0)
            def _():
                held["along"].wait_send()

            @pl.when(seq < count - 1)
            def _():
                held["along"].wait_recv()

            get_x.wait()
            get_b.wait()
            for s in range(seqs):
                one, two = pl.ds(1, length), pl.ds(2, length)
                gg_ref[s, :length, :] = (
                    cw_ref[2:3, :] * gg_ref[s, :length, :]
                    + cw_ref[1:2, :] * same_ref[0, s, one, 0:1] * gg_ref[s, one, :]
                    + cw_ref[0:1, :] * same_ref[1, s, two, 0:1] * gg_ref[s, two, :]
                )

            @pl.when(seq < count - 1)
            def _():
                for s in range(seqs):
                    gg_ref[s, length - 2 : length, :] += edge_in_ref[2 * s : 2 * s + 2, :]

            for s in range(seqs):
                rows = pl.ds(s * length, length)
                gmix = gg_ref[s, :length, :]
                gp_ref[rows, 0:D] = (gmix * one_ref[rows, :]).astype(bf16)
                gp_ref[rows, 2 * D :] = (gmix * two_ref[rows, :]).astype(bf16)

        def part6():
            put_grad(g_ref, slice(W_B_B, W_B_B + D), dot_tn(mi_ref[...], gp_ref[:, :D]))
            put_grad(g_ref, slice(W_B_X, W_B_X + D), dot_tn(mi_ref[...], gp_ref[:, 2 * D :]))

        def part7():
            gm_part = dot_nt(gp_ref[:, :D], tb_ref[:, W_B_B : W_B_B + D])
            gm_part += dot_nt(gp_ref[:, D : 2 * D], tb_ref[:, W_B_C : W_B_C + D])
            gm_part += dot_nt(gp_ref[:, 2 * D :], tb_ref[:, W_B_X : W_B_X + D])
            held["gm_in"] = (gm_part * twice).astype(bf16)
            get_u1.wait()
            put_grad(g_ref, slice(W_A_IN, W_A_IN + D), dot_tn(held["gm_in"], u1_ref[...]))

        def part8():
            get_wi.wait()
            for k in range(2):
                cols = slice(256 * k, 256 * k + 256)
                gn_ref[:, cols] = dot_nt(gp_ref[...], wi_ref[cols, :]) + dot(
                    held["gm_in"], tb_ref[:, W_A_IN + 256 * k : W_A_IN + 256 * k + 256]
                )

        def part9():
            for k in range(2, 4):
                cols = slice(256 * k, 256 * k + 256)
                gn_ref[:, cols] = dot_nt(gp_ref[...], wi_ref[cols, :]) + dot(
                    held["gm_in"], tb_ref[:, W_A_IN + 256 * k : W_A_IN + 256 * k + 256]
                )

        def part10():
            get_tok.wait()
            for s in range(seqs):
                rows = pl.ds(s * length, length)
                tokens = tok_ref[rows, :].astype(f32)
                inv1 = norm(tokens, n1_ref[...])[1]
                e1 = gn_ref[rows, :] * n1_ref[...]
                ig = gh_ref[rows, :] + inv1 * e1
                ig_ref[rows, :] = (
                    ig - tokens * (inv1 * inv1 * inv1 * jnp.mean(tokens * e1, axis=-1, keepdims=True))
                ).astype(bf16)

        parts = (part0, part1, part2, part3, part4, part5, part6, part7, part8, part9, part10)
        for what in BACKWARD_ORDER:
            if isinstance(what, tuple):
                advance(*what)
            else:
                parts[what]()

    pl.run_scoped(
        backward,
        half, wide, wide, pltpu.VMEM((2, seqs, length + 8, 128), f32), half, half,
        pltpu.VMEM((D, 3 * D), bf16), pltpu.VMEM((D, D), bf16), pltpu.VMEM((seqs, length + 8, D), f32),
        pltpu.VMEM((rows_all, 3 * D), bf16),
    )

    def updates(lhs_ref, perm_ref, old_ref, grad_ref, new_ref, wd_ref, hid_ref):
        own = lambda first, size: tab_ref.at[pl.ds(first, size), :]
        slot_of = lambda owner, first, size: all_hbm.at[owner, pl.ds(first, size), :]
        spread = Spread(at, own, slot_of, NATIVE, WAYS, 16, spread_send, spread_recv)
        going = {}

        def pass_on(*parts):
            for part in parts:
                spread.leg(going[part], part)
                going[part] += 1

        power = jnp.float32(1.0)
        for bit in range(8):
            power = power * jnp.where((step_ref[0] >> bit) % 2 == 1, jnp.float32(0.5 ** (2**bit)), jnp.float32(1.0))
        rate = rate_ref[0]
        correction = 1.0 - jnp.full((8, 128), power, f32)
        inv = (1.0 / correction)[0:1, :]

        def old(part):
            first, size = NATIVE[part]
            slot = part % 2
            return [
                pltpu.make_async_copy(ref.at[first : first + size], old_ref.at[slot, n, :size], old_sems.at[slot, n])
                for n, ref in enumerate((st_hbm, m_hbm, v_hbm))
            ]

        def new_copy(part):
            first, size = NATIVE[part]
            return pltpu.make_async_copy(new_ref.at[part % 2, :size], new_hbm.at[first : first + size], new_sems.at[part % 2])

        def own_copy(part):
            first, size = NATIVE[part]
            return pltpu.make_async_copy(
                tab_ref.at[first : first + size], all_hbm.at[at.grp, first : first + size], own_sems.at[part]
            )

        def update(part):
            first, size = NATIVE[part]
            slot = part % 2
            update_grad(na, part, sum_ref, lhs_ref, perm_ref, grad_ref)
            for copy in old(part):
                copy.wait()
            if part >= 2:
                new_copy(part - 2).wait()
            grad = grad_ref[:size]
            one = 0.5 * old_ref[slot, 1, :size] + 0.5 * grad
            two = 0.5 * old_ref[slot, 2, :size] + 0.5 * grad * grad
            new = old_ref[slot, 0, :size] - rate * (one * inv) / (jnp.sqrt(two * inv) + 1e-08)
            new_ref[slot, :size] = new
            tab_ref[first : first + size] = new.astype(bf16)
            new_copy(part).start()
            own_copy(part).start()
            if part + 2 < len(NATIVE):
                for copy in old(part + 2):
                    copy.start()
            going[part] = 0
            pass_on(part)

        def fetch(j):
            slot = j % 2
            return [
                pltpu.make_async_copy(wd_hbm.at[j * FB : (j + 1) * FB, :], wd_ref.at[slot], weight_sems.at[slot, 0]),
                pltpu.make_async_copy(hid_hbm.at[:, j * FB : (j + 1) * FB], hid_ref.at[slot], weight_sems.at[slot, 1]),
            ]

        def outputs(*blocks):
            for j in blocks:
                for copy in fetch(j):
                    copy.wait()
                h1_ref[...] += dot(hid_ref[j % 2], wd_ref[j % 2])
                if j + 2 < BLOCKS:
                    for copy in fetch(j + 2):
                        copy.start()

        for part in range(2):
            for copy in old(part):
                copy.start()
        for j in range(2):
            for copy in fetch(j):
                copy.start()
        fill_shuffle(perm_ref)
        for k in range(2):
            cols = slice(512 * k, 512 * k + 512)
            h1_ref[:, cols] += dot(dmid, tb_ref[:, W_B_DOWN + 512 * k : W_B_DOWN + 512 * k + 512])
        for what, *which in TAIL_ORDER:
            {"sum": advance, "update": update, "pass": pass_on, "out": outputs}[what](*which)
        out_ref[...] = h1_ref[...].astype(bf16)
        for part in range(len(NATIVE)):
            spread.sent(part)
            own_copy(part).wait()
        for part in range(len(NATIVE) - 2, len(NATIVE)):
            new_copy(part).wait()

    pl.run_scoped(
        updates,
        pltpu.VMEM((5 * na * RANK, 1024), bf16), pltpu.VMEM((1024, 1024), bf16),
        pltpu.VMEM((2, 3, MOST, 128), f32), pltpu.VMEM((MOST, 128), f32), pltpu.VMEM((2, MOST, 128), f32),
        pltpu.VMEM((2, FB, D), bf16), pltpu.VMEM((2, rows_all, FB), bf16),
    )


def rest(seqs, length, count, na, *args):
    rows = seqs * length
    sd = jax.ShapeDtypeStruct
    sm = pl.BlockSpec(memory_space=pltpu.SMEM)
    vm = pl.BlockSpec(memory_space=pltpu.VMEM)
    hbm = pl.BlockSpec(memory_space=pl.ANY)
    wide = pltpu.VMEM((rows, D), f32)
    thin = pltpu.VMEM((rows, 128), f32)
    half, full = sd((rows, D), bf16), sd((rows, D), f32)
    mids = [pltpu.VMEM((rows, 128), bf16)] * 4
    ahead = pltpu.VMEM((2 * seqs, D + 128), f32)
    parts = len(NATIVE)
    dma = lambda *shape: pltpu.SemaphoreType.DMA(shape)
    return pl.pallas_call(
        functools.partial(rest_kernel, seqs, length, count, na),
        in_specs=[sm] * 3 + [vm] * 5 + [hbm] * 9,
        out_specs=[vm, vm] + [hbm] * 10,
        out_shape=[
            sd((rows, D), bf16), sd((rows, D), bf16), sd((na * PACKROWS, 128), f32), sd((4, na * PACKROWS, 128), bf16),
            sd((rows, FF), bf16), half, full, full, full, full, sd((2, seqs, length, 128), f32), half,
        ],
        scratch_shapes=[
            pltpu.VMEM((rows, D), bf16), *mids, ahead, ahead,
            pltpu.VMEM((128, WIRE), bf16), wide, wide, wide, pltpu.VMEM((rows, D), bf16), thin, thin, thin,
            pltpu.VMEM((rows, 128), bf16),
            pltpu.VMEM((2 * seqs, D), f32), pltpu.VMEM((2 * seqs, D), f32),
            *sums_scratch(WIRE),
            pltpu.VMEM((na * PACKROWS, 128), bf16),
            dma(4), dma(7), dma(len(Spread.KINDS) * len(SPREAD_PIECES)), dma(len(Spread.KINDS) * len(SPREAD_PIECES)),
            dma(10), dma(2, 3), dma(2), dma(3 * BLOCKS), dma(3 * BLOCKS),
            dma(Sums.COPIES * len(GROUPS)), dma(Sums.COPIES * len(GROUPS)),
            dma(4), dma(2, 3), dma(2), dma(parts), dma(len(Spread.KINDS) * parts), dma(len(Spread.KINDS) * parts),
        ],
        compiler_params=pltpu.CompilerParams(vmem_limit_bytes=63 * MIB, collective_id=3, has_side_effects=True),
    )(*args)


def lay_kernel(all_hbm, new_hbm, out_hbm, ig_hbm, to_ref, new_to, out_to, ig_to, all_ref, new_ref, out_ref, ig_ref, load_sems, store_sems):
    cuts = 4
    share = PACKROWS // cuts
    moves = []
    for k in range(cuts):
        rows = pl.ds(k * share, share)
        moves += [(all_hbm.at[g, rows], all_ref.at[g, rows], to_ref.at[rows, g]) for g in range(4)]
    for k in range(2):
        rows = pl.ds(k * PACKROWS, PACKROWS)
        moves.append((new_hbm.at[rows], new_ref.at[rows], new_to.at[rows]))
    moves += [(out_hbm, out_ref, out_to), (ig_hbm, ig_ref, ig_to)]
    loads = [pltpu.make_async_copy(src, mid, load_sems.at[n]) for n, (src, mid, _) in enumerate(moves)]
    stores = [pltpu.make_async_copy(mid, dst, store_sems.at[n]) for n, (_, mid, dst) in enumerate(moves)]
    for copy in loads:
        copy.start()
    for came, goes in zip(loads, stores):
        came.wait()
        goes.start()
    for copy in stores:
        copy.wait()


def lay_out(every, new, out, ig, na):
    hbm = pl.BlockSpec(memory_space=pl.ANY)
    scratch = lambda x: pltpu.VMEM(x.shape, x.dtype)
    like = lambda x: jax.ShapeDtypeStruct(x.shape, x.dtype)
    every = every.reshape(4, PACKROWS, na, 128)
    return pl.pallas_call(
        lay_kernel,
        in_specs=[hbm] * 4,
        out_specs=[hbm] * 4,
        out_shape=[jax.ShapeDtypeStruct((PACKROWS, 4, na, 128), bf16), like(new), like(out), like(ig)],
        scratch_shapes=[
            *(scratch(x) for x in (every, new, out, ig)), pltpu.SemaphoreType.DMA((20,)), pltpu.SemaphoreType.DMA((20,)),
        ],
        compiler_params=pltpu.CompilerParams(vmem_limit_bytes=60 * MIB),
    )(every, new, out, ig)


def fast_device(
    tokens, segment_ids, adapter_ids, input_weight, conv_weight, output_weight, gate_weight, up_weight, down_weight,
    norm_one, norm_two, cotangent, adapter_state, first_moment, second_moment, rate, step,
):
    seqs, length, _ = tokens.shape
    na = adapter_state.shape[0]
    adapters, count = na * lax.axis_size("grp"), lax.axis_size("seq")
    native = lambda x: x.reshape(na, PACKROWS, 128).swapaxes(0, 1).reshape(na * PACKROWS, 128)
    st, m, v = native(adapter_state), native(first_moment), native(second_moment)
    rows = seqs * length
    tok2, cot2 = tokens.reshape(rows, D), cotangent.reshape(rows, D)
    n1, n2 = norm_one.reshape(1, D), norm_two.reshape(1, D)
    out, ig, new, every, *_ = rest(
        seqs, length, count, na, adapter_ids, rate, step, cot2, segment_ids, conv_weight, n1, n2,
        tok2, input_weight, output_weight, gate_weight, up_weight, down_weight, st, m, v,
    )
    every, new, out, ig = lay_out(every, new, out, ig, na)
    every = every.reshape(PACKROWS, adapters, 128).swapaxes(0, 1).reshape(adapters, PACKROWS * 128)
    new = new.reshape(PACKROWS, na, 128).swapaxes(0, 1).reshape(na, PACKROWS * 128)
    return out.reshape(tokens.shape), ig.reshape(tokens.shape), new, every


def solution(mesh):
    rows = P("grp", "seq", None)
    own = P("grp", None)
    return jax.shard_map(
        fast_device if tuple(mesh.shape[axis] for axis in ("seq", "grp")) == (8, 4) else general_device,
        mesh=mesh,
        in_specs=(rows, P("grp", "seq"), P("grp")) + (P(),) * 8 + (rows, own, own, own, P(), P()),
        out_specs=(rows, rows, own, P()),
        check_vma=False,
    )
```

```python
import functools

import jax
import jax.numpy as jnp
from jax import lax
from jax.experimental import pallas as pl
from jax.experimental.pallas import tpu as pltpu
from jax.sharding import PartitionSpec as P

D = 1024
FF = 4608
RANK = 16
EPS = 1e-05
FB = 512
MIB = 2**20

f32 = jnp.float32
bf16 = jnp.bfloat16
MESH = pl.DeviceIdType.MESH

WIRE = RANK * 0 + 23040
PACKROWS = 2880
A_IN, B_IN, A_OUT, B_OUT, A_GATE, B_GATE, A_UP, B_UP, A_DOWN, B_DOWN = (
    0, 1024, 4096, 5120, 6144, 7168, 11776, 12800, 17408, 22016,
)
B_PARTS = ((B_IN, 3 * D), (B_OUT, D), (B_GATE, FF), (B_UP, FF), (B_DOWN, D))
A_PARTS = ((A_IN, D), (A_OUT, D), (A_GATE, D), (A_UP, D), (A_DOWN, FF))
A_CHUNKS = tuple(
    (first + start, min(1024, height - start))
    for first, height in A_PARTS
    for start in range(0, height, 1024)
)


def dot(a, b):
    return jnp.dot(a, b, preferred_element_type=f32)


def dot_nt(a, b):
    return lax.dot_general(a, b, (((1,), (1,)), ((), ())), preferred_element_type=f32)


def dot_tn(a, b):
    return lax.dot_general(a, b, (((0,), (0,)), ((), ())), preferred_element_type=f32)


def shuffle_matrix():
    row = lax.broadcasted_iota(jnp.int32, (1024, 1024), 0)
    col = lax.broadcasted_iota(jnp.int32, (1024, 1024), 1)
    return jnp.where(col == 8 * (row % 128) + row // 128, 1.0, 0.0).astype(bf16)


def table_kernel(na, st_ref, out_ref, lhs_ref):
    for n, (first, count) in enumerate(A_CHUNKS):
        for a in range(na):
            packed = st_ref[pl.ds(na * (first // 8) + a, 128, stride=na), :]
            turned = packed.T.astype(bf16)
            row = (n * na + a) * RANK
            for c in range(8):
                lhs_ref[row : row + RANK, 128 * c : 128 * c + 128] = turned[RANK * c : RANK * c + RANK, :]
    full = dot(lhs_ref[...], shuffle_matrix()).astype(bf16)
    for n, (first, count) in enumerate(A_CHUNKS):
        for a in range(na):
            row = (n * na + a) * RANK
            out_ref[a * RANK : (a + 1) * RANK, first : first + count] = full[row : row + RANK, :count]
    for first, breadth in B_PARTS:
        blocks = breadth // 128
        for a in range(na):
            for c in range(blocks):
                part = st_ref[pl.ds(na * (first // 8 + c) + a, RANK, stride=na * blocks), :]
                out_ref[a * RANK : (a + 1) * RANK, first + 128 * c : first + 128 * c + 128] = part.astype(bf16)


def build_table(state_native, na):
    return pl.pallas_call(
        functools.partial(table_kernel, na),
        out_shape=jax.ShapeDtypeStruct((na * RANK, WIRE), bf16),
        scratch_shapes=[pltpu.VMEM((len(A_CHUNKS) * na * RANK, 1024), bf16)],
        compiler_params=pltpu.CompilerParams(vmem_limit_bytes=40 * MIB),
    )(state_native)


def adam_kernel(na, scal_ref, gw_ref, st_ref, m_ref, v_ref, new_ref, tab_ref, lhs_ref, gn_ref):
    for n, (first, count) in enumerate(A_CHUNKS):
        for a in range(na):
            row = (n * na + a) * RANK
            lhs_ref[row : row + RANK, :] = gw_ref[a * RANK : (a + 1) * RANK, first : first + 1024].astype(bf16)
    full = dot_nt(lhs_ref[...], shuffle_matrix())
    for n, (first, count) in enumerate(A_CHUNKS):
        for a in range(na):
            row = (n * na + a) * RANK
            turned = jnp.concatenate(
                [full[row : row + RANK, 128 * c : 128 * c + 128] for c in range(8)], axis=0
            )
            gn_ref[pl.ds(na * (first // 8) + a, count // 8, stride=na), :] = turned.T[: count // 8]
    for first, breadth in B_PARTS:
        blocks = breadth // 128
        for a in range(na):
            for c in range(blocks):
                gn_ref[pl.ds(na * (first // 8 + c) + a, RANK, stride=na * blocks), :] = gw_ref[
                    a * RANK : (a + 1) * RANK, first + 128 * c : first + 128 * c + 128
                ].astype(f32)
    rate = scal_ref[0]
    inv = scal_ref[1]
    grad = gn_ref[...]
    one = 0.5 * m_ref[...] + 0.5 * grad
    two = 0.5 * v_ref[...] + 0.5 * grad * grad
    new = st_ref[...] - rate * (one * inv) / (jnp.sqrt(two * inv) + 1e-08)
    new_ref[...] = new
    tab_ref[...] = new.astype(bf16)


def adam(scal, gw, st, m, v, na):
    rows = na * PACKROWS
    vm = pl.BlockSpec(memory_space=pltpu.VMEM)
    return pl.pallas_call(
        functools.partial(adam_kernel, na),
        in_specs=[pl.BlockSpec(memory_space=pltpu.SMEM)] + [vm] * 4,
        out_shape=(jax.ShapeDtypeStruct((rows, 128), f32), jax.ShapeDtypeStruct((rows, 128), bf16)),
        scratch_shapes=[
            pltpu.VMEM((len(A_CHUNKS) * na * RANK, 1024), bf16),
            pltpu.VMEM((rows, 128), f32),
        ],
        compiler_params=pltpu.CompilerParams(vmem_limit_bytes=56 * MIB),
    )(scal, gw, st, m, v)


def greet(seq, count):
    barrier = pltpu.get_barrier_semaphore()

    @pl.when(seq > 0)
    def _():
        pl.semaphore_signal(barrier, inc=1, device_id={"seq": seq - 1}, device_id_type=MESH)

    @pl.when(seq < count - 1)
    def _():
        pl.semaphore_signal(barrier, inc=1, device_id={"seq": seq + 1}, device_id_type=MESH)

    before = (seq + count - 1) // count
    after = (2 * count - 2 - seq) // count
    pl.semaphore_wait(barrier, before + after)


def row_mask(mask_ref, seqs, length):
    return jnp.concatenate(
        [jnp.broadcast_to(mask_ref[s : s + 1, :], (length, 128)) for s in range(seqs)], axis=0
    )


def norm(values, gain):
    inverse = lax.rsqrt(jnp.mean(values * values, axis=-1, keepdims=True) + EPS)
    return values * inverse * gain, inverse


def pre_kernel(
    seqs, length, count,
    tok_ref, ids_ref, mask_ref, tb_ref, wi_ref, cw_ref, wo_ref, n1_ref, n2_ref, cot_ref,
    u1_ref, mi_ref, b_ref, c_ref, x_ref, conv_ref, same_ref, gated_ref, mo_ref, h1_ref, u2_ref, mg_ref, mu_ref, gd_ref,
    ext_ref, out_ref, in_ref, send_sem, recv_sem,
):
    seq = lax.axis_index("seq")
    greet(seq, count)
    mask = row_mask(mask_ref, seqs, length)
    twice = 2.0 * mask
    tokens = tok_ref[...].astype(f32)
    u1 = norm(tokens, n1_ref[...])[0].astype(bf16)
    u1_ref[...] = u1
    mid = (dot_nt(u1, tb_ref[:, A_IN : A_IN + D]).astype(bf16).astype(f32) * twice).astype(bf16)
    mi_ref[...] = mid
    for third, to_ref in ((0, b_ref), (2, x_ref)):
        for k in range(2):
            col = third * D + 512 * k
            to_ref[:, 512 * k : 512 * k + 512] = dot(u1, wi_ref[:, col : col + 512]) + dot(
                mid, tb_ref[:, B_IN + col : B_IN + col + 512]
            )
    width = D + 128
    for s in range(seqs):
        rows = pl.ds(s * length, length)
        ext_ref[s, 0:8, :] = jnp.zeros((8, width), f32)
        ext_ref[s, 8:, :D] = b_ref[rows, :] * x_ref[rows, :]
        ext_ref[s, 8:, D:] = jnp.broadcast_to(ids_ref[s : s + 1, :], (length, 128)).T
        out_ref[2 * s : 2 * s + 2, :] = ext_ref[s, length + 6 : length + 8, :]
    along = pltpu.make_async_remote_copy(
        src_ref=out_ref, dst_ref=in_ref, send_sem=send_sem, recv_sem=recv_sem,
        device_id={"seq": seq + 1}, device_id_type=MESH,
    )

    @pl.when(seq < count - 1)
    def _():
        along.start()

    for k in range(2):
        col = D + 512 * k
        c_ref[:, 512 * k : 512 * k + 512] = dot(u1, wi_ref[:, col : col + 512]) + dot(
            mid, tb_ref[:, B_IN + col : B_IN + col + 512]
        )
    gd_ref[...] = (dot_nt(cot_ref[...], tb_ref[:, B_DOWN : B_DOWN + D]) * twice).astype(bf16)

    @pl.when(seq < count - 1)
    def _():
        along.wait_send()

    @pl.when(seq > 0)
    def _():
        along.wait_recv()
        for s in range(seqs):
            ext_ref[s, 6:8, :] = in_ref[2 * s : 2 * s + 2, :]

    for s in range(seqs):
        rows = pl.ds(s * length, length)
        now_ids = ext_ref[s, 8:, D:]
        same1 = jnp.where(ext_ref[s, pl.ds(7, length), D:] == now_ids, 1.0, 0.0)
        same2 = jnp.where(ext_ref[s, pl.ds(6, length), D:] == now_ids, 1.0, 0.0)
        same_ref[0, rows, :] = same1
        same_ref[1, rows, :] = same2
        conv = (
            cw_ref[2:3, :] * ext_ref[s, 8:, :D]
            + cw_ref[1:2, :] * same1[:, :1] * ext_ref[s, pl.ds(7, length), :D]
            + cw_ref[0:1, :] * same2[:, :1] * ext_ref[s, pl.ds(6, length), :D]
        )
        conv_ref[rows, :] = conv
        gated_ref[rows, :] = (c_ref[rows, :] * conv).astype(bf16)
    gated = gated_ref[...]
    mid_out = (dot_nt(gated, tb_ref[:, A_OUT : A_OUT + D]).astype(bf16).astype(f32) * twice).astype(bf16)
    mo_ref[...] = mid_out
    for k in range(2):
        cols = slice(512 * k, 512 * k + 512)
        h1_ref[:, cols] = (
            tok_ref[:, cols].astype(f32)
            + dot(gated, wo_ref[:, cols])
            + dot(mid_out, tb_ref[:, B_OUT + 512 * k : B_OUT + 512 * k + 512])
        )
    u2 = norm(h1_ref[...], n2_ref[...])[0].astype(bf16)
    u2_ref[...] = u2
    mg_ref[...] = (dot_nt(u2, tb_ref[:, A_GATE : A_GATE + D]).astype(bf16).astype(f32) * twice).astype(bf16)
    mu_ref[...] = (dot_nt(u2, tb_ref[:, A_UP : A_UP + D]).astype(bf16).astype(f32) * twice).astype(bf16)


def pre(seqs, length, count, *args):
    rows = seqs * length
    sd = jax.ShapeDtypeStruct
    width = D + 128
    vm = pl.BlockSpec(memory_space=pltpu.VMEM)
    wide = sd((rows, D), f32)
    half = sd((rows, D), bf16)
    thin = sd((rows, 128), bf16)
    return pl.pallas_call(
        functools.partial(pre_kernel, seqs, length, count),
        in_specs=[vm] * 10,
        out_specs=[vm] * 14,
        out_shape=[half, thin, wide, wide, wide, wide, sd((2, rows, 128), f32), half, thin, wide, half, thin, thin, thin],
        scratch_shapes=[
            pltpu.VMEM((seqs, length + 8, width), f32),
            pltpu.VMEM((2 * seqs, width), f32),
            pltpu.VMEM((2 * seqs, width), f32),
            pltpu.SemaphoreType.DMA,
            pltpu.SemaphoreType.DMA,
        ],
        compiler_params=pltpu.CompilerParams(vmem_limit_bytes=60 * MIB, collective_id=0, has_side_effects=True),
    )(*args)


def ffn_kernel(
    seqs, length,
    u_ref, cot_ref, mg_ref, mu_ref, gd_ref, mask_ref, h1_ref, wg_ref, wu_ref, wd_ref, bg_ref, bu_ref, ad_ref, ag_ref, au_ref, bd_ref,
    out_ref, gn_ref, dbg_ref, dbu_ref, dad_ref, dag_ref, dau_ref, dbd_ref,
    acc_ref, dmid_ref, gmg_ref, gmu_ref,
):
    j = pl.program_id(0)

    @pl.when(j == 0)
    def _():
        for ref in (acc_ref, gn_ref, dmid_ref, gmg_ref, gmu_ref):
            ref[...] = jnp.zeros_like(ref)

    u = u_ref[...]
    gate = dot(u, wg_ref[...]) + dot(mg_ref[...], bg_ref[...])
    up = dot(u, wu_ref[...]) + dot(mu_ref[...], bu_ref[...])
    back = dot_nt(cot_ref[...], wd_ref[...]) + dot(gd_ref[...], ad_ref[...])
    sig = jax.nn.sigmoid(gate)
    silu = gate * sig
    hidden = (silu * up).astype(bf16)
    grad_gate = (back * up * sig * (1.0 + gate * (1.0 - sig))).astype(bf16)
    grad_up = (back * silu).astype(bf16)
    acc_ref[...] += dot(hidden, wd_ref[...])
    gn_ref[...] += dot_nt(grad_gate, wg_ref[...]) + dot_nt(grad_up, wu_ref[...])
    dmid_ref[...] += dot_nt(hidden, ad_ref[...])
    gmg_ref[...] += dot_nt(grad_gate, bg_ref[...])
    gmu_ref[...] += dot_nt(grad_up, bu_ref[...])
    dbg_ref[...] = dot_tn(mg_ref[...], grad_gate).astype(bf16)
    dbu_ref[...] = dot_tn(mu_ref[...], grad_up).astype(bf16)
    dad_ref[...] = dot_tn(gd_ref[...], hidden).astype(bf16)

    @pl.when(j == pl.num_programs(0) - 1)
    def _():
        twice = 2.0 * row_mask(mask_ref, seqs, length)
        dmid = (dmid_ref[...].astype(bf16).astype(f32) * twice).astype(bf16)
        out_ref[...] = (h1_ref[...] + acc_ref[...] + dot(dmid, bd_ref[...])).astype(bf16)
        dbd_ref[...] = dot_tn(dmid, cot_ref[...]).astype(bf16)
        gm_gate = (gmg_ref[...] * twice).astype(bf16)
        gm_up = (gmu_ref[...] * twice).astype(bf16)
        gn_ref[...] += dot(gm_gate, ag_ref[...]) + dot(gm_up, au_ref[...])
        dag_ref[...] = dot_tn(gm_gate, u_ref[...]).astype(bf16)
        dau_ref[...] = dot_tn(gm_up, u_ref[...]).astype(bf16)


def ffn(seqs, length, u2, cot, mg, mu, gd, mask, h1, wg, wu, wd, table):
    rows = seqs * length
    sd = jax.ShapeDtypeStruct
    whole = lambda s: pl.BlockSpec(s, lambda j: (0, 0))
    col = lambda h: pl.BlockSpec((h, FB), lambda j: (0, j))
    tab = lambda first: pl.BlockSpec((128, FB), lambda j: (0, first // FB + j))
    fixed = lambda first: pl.BlockSpec((128, D), lambda j: (0, 0))
    cut = lambda first: lax.slice_in_dim(table, first, first + D, axis=1)
    return pl.pallas_call(
        functools.partial(ffn_kernel, seqs, length),
        grid=(FF // FB,),
        in_specs=[whole((rows, D)), whole((rows, D)), whole((rows, 128)), whole((rows, 128)), whole((rows, 128)),
                  whole(mask.shape), whole((rows, D)),
                  col(D), col(D), pl.BlockSpec((FB, D), lambda j: (j, 0)),
                  tab(B_GATE), tab(B_UP), tab(A_DOWN), whole((128, D)), whole((128, D)), whole((128, D))],
        out_specs=[whole((rows, D)), whole((rows, D)), col(128), col(128), col(128),
                   whole((128, D)), whole((128, D)), whole((128, D))],
        out_shape=[sd((rows, D), bf16), sd((rows, D), f32)] + [sd((128, FF), bf16)] * 3 + [sd((128, D), bf16)] * 3,
        scratch_shapes=[pltpu.VMEM((rows, D), f32)] + [pltpu.VMEM((rows, 128), f32)] * 3,
        compiler_params=pltpu.CompilerParams(vmem_limit_bytes=60 * MIB),
    )(u2, cot, mg, mu, gd, mask, h1, wg, wu, wd, table, table, table, cut(A_GATE), cut(A_UP), cut(B_DOWN))


def post_kernel(
    seqs, length, count,
    tok_ref, cot_ref, mask_ref, h1_ref, gn_ref, gated_ref, mo_ref, b_ref, c_ref, x_ref, conv_ref, same_ref, u1_ref, mi_ref,
    tb_ref, wi_ref, cw_ref, wo_ref, n1_ref, n2_ref,
    ig_ref, dai_ref, dbi_ref, dao_ref, dbo_ref,
    gh_ref, gb_ref, gg_ref, gc_ref, gp_ref, one_ref, two_ref, out_ref, in_ref, send_sem, recv_sem,
):
    seq = lax.axis_index("seq")
    greet(seq, count)
    twice = 2.0 * row_mask(mask_ref, seqs, length)
    h1 = h1_ref[...]
    inv2 = norm(h1, n2_ref[...])[1]
    e2 = gn_ref[...] * n2_ref[...]
    gh = cot_ref[...].astype(f32) + inv2 * e2 - h1 * (inv2 * inv2 * inv2 * jnp.mean(h1 * e2, axis=-1, keepdims=True))
    gh_ref[...] = gh
    gb = gh.astype(bf16)
    gb_ref[...] = gb
    gm_out = (dot_nt(gb, tb_ref[:, B_OUT : B_OUT + D]) * twice).astype(bf16)
    for k in range(2):
        cols = slice(512 * k, 512 * k + 512)
        gg_ref[:, cols] = dot_nt(gb, wo_ref[cols, :]) + dot(gm_out, tb_ref[:, A_OUT + 512 * k : A_OUT + 512 * k + 512])
    for s in range(seqs):
        rows = pl.ds(s * length, length)
        gg = gg_ref[rows, :]
        gp_ref[rows, D : 2 * D] = (gg * conv_ref[rows, :]).astype(bf16)
        gconv = gg * c_ref[rows, :]
        gc_ref[rows, :] = gconv
        one_ref[s, 0:length, :] = cw_ref[1:2, :] * same_ref[0, rows, 0:1] * gconv
        two_ref[s, 0:length, :] = cw_ref[0:1, :] * same_ref[1, rows, 0:1] * gconv
        one_ref[s, length:, :] = jnp.zeros((8, D), f32)
        two_ref[s, length:, :] = jnp.zeros((8, D), f32)
        out_ref[2 * s : 2 * s + 1, :] = two_ref[s, 0:1, :]
        out_ref[2 * s + 1 : 2 * s + 2, :] = two_ref[s, 1:2, :] + one_ref[s, 0:1, :]
    along = pltpu.make_async_remote_copy(
        src_ref=out_ref, dst_ref=in_ref, send_sem=send_sem, recv_sem=recv_sem,
        device_id={"seq": seq - 1}, device_id_type=MESH,
    )

    @pl.when(seq > 0)
    def _():
        along.start()

    dbo_ref[...] = dot_tn(mo_ref[...], gb).astype(bf16)
    dao_ref[...] = dot_tn(gm_out, gated_ref[...]).astype(bf16)

    @pl.when(seq > 0)
    def _():
        along.wait_send()

    @pl.when(seq < count - 1)
    def _():
        along.wait_recv()
        for s in range(seqs):
            two_ref[s, length : length + 2, :] = in_ref[2 * s : 2 * s + 2, :]

    for s in range(seqs):
        rows = pl.ds(s * length, length)
        gmix = (
            cw_ref[2:3, :] * gc_ref[rows, :]
            + one_ref[s, pl.ds(1, length), :]
            + two_ref[s, pl.ds(2, length), :]
        )
        gp_ref[rows, 0:D] = (gmix * x_ref[rows, :]).astype(bf16)
        gp_ref[rows, 2 * D :] = (gmix * b_ref[rows, :]).astype(bf16)
    gm_in = (dot_nt(gp_ref[...], tb_ref[:, B_IN : B_IN + 3 * D]) * twice).astype(bf16)
    for k in range(2):
        cols = slice(512 * k, 512 * k + 512)
        gg_ref[:, cols] = dot_nt(gp_ref[...], wi_ref[cols, :]) + dot(gm_in, tb_ref[:, A_IN + 512 * k : A_IN + 512 * k + 512])
    for k in range(6):
        cols = slice(512 * k, 512 * k + 512)
        dbi_ref[:, cols] = dot_tn(mi_ref[...], gp_ref[:, cols]).astype(bf16)
    dai_ref[...] = dot_tn(gm_in, u1_ref[...]).astype(bf16)
    tokens = tok_ref[...].astype(f32)
    inv1 = norm(tokens, n1_ref[...])[1]
    e1 = gg_ref[...] * n1_ref[...]
    ig_ref[...] = (
        gh_ref[...] + inv1 * e1 - tokens * (inv1 * inv1 * inv1 * jnp.mean(tokens * e1, axis=-1, keepdims=True))
    ).astype(bf16)


def post(seqs, length, count, *args):
    rows = seqs * length
    sd = jax.ShapeDtypeStruct
    vm = pl.BlockSpec(memory_space=pltpu.VMEM)
    return pl.pallas_call(
        functools.partial(post_kernel, seqs, length, count),
        in_specs=[vm] * 20,
        out_specs=[vm] * 5,
        out_shape=[sd((rows, D), bf16), sd((128, D), bf16), sd((128, 3 * D), bf16), sd((128, D), bf16), sd((128, D), bf16)],
        scratch_shapes=[
            pltpu.VMEM((rows, D), f32),
            pltpu.VMEM((rows, D), bf16),
            pltpu.VMEM((rows, D), f32),
            pltpu.VMEM((rows, D), f32),
            pltpu.VMEM((rows, 3 * D), bf16),
            pltpu.VMEM((seqs, length + 8, D), f32),
            pltpu.VMEM((seqs, length + 8, D), f32),
            pltpu.VMEM((2 * seqs, D), f32),
            pltpu.VMEM((2 * seqs, D), f32),
            pltpu.SemaphoreType.DMA,
            pltpu.SemaphoreType.DMA,
        ],
        compiler_params=pltpu.CompilerParams(vmem_limit_bytes=62 * MIB, collective_id=1, has_side_effects=True),
    )(*args)


def general_device(
    tokens, segment_ids, adapter_ids, input_weight, conv_weight, output_weight, gate_weight, up_weight, down_weight,
    norm_one, norm_two, cotangent, adapter_state, first_moment, second_moment, rate, step,
):
    seqs, length, _ = tokens.shape
    na = adapter_state.shape[0]
    groups = lax.axis_size("grp")
    count = lax.axis_size("seq")
    native = lambda x: x.reshape(na, PACKROWS, 128).swapaxes(0, 1).reshape(na * PACKROWS, 128)
    st, m, v = native(adapter_state), native(first_moment), native(second_moment)
    own = build_table(st, na)
    table = lax.all_gather(own, "grp", axis=0, tiled=True)
    adapters = na * groups
    mask = (adapter_ids[:, None] == jnp.arange(adapters * RANK, dtype=jnp.int32)[None, :] // RANK).astype(f32)
    ids = segment_ids.astype(f32)
    rows = seqs * length
    tok2, cot2 = tokens.reshape(rows, D), cotangent.reshape(rows, D)
    n1, n2 = norm_one.reshape(1, D), norm_two.reshape(1, D)
    u1, mi, b, c, x, conv, same, gated, mo, h1, u2, mg, mu, gd = pre(
        seqs, length, count, tok2, ids, mask, table, input_weight, conv_weight, output_weight, n1, n2, cot2
    )
    out, gn, dbg, dbu, dad, dag, dau, dbd = ffn(
        seqs, length, u2, cot2, mg, mu, gd, mask, h1, gate_weight, up_weight, down_weight, table
    )
    ig, dai, dbi, dao, dbo = post(
        seqs, length, count, tok2, cot2, mask, h1, gn, gated, mo, b, c, x, conv, same, u1, mi,
        table, input_weight, conv_weight, output_weight, n1, n2,
    )
    grads = jnp.concatenate([dai, dbi, dao, dbo, dag, dbg, dau, dbu, dad, dbd], axis=1).astype(f32)
    owned = lax.psum(lax.psum_scatter(grads, "grp", scatter_dimension=0, tiled=True), "seq")
    correction = 1.0 - jnp.power(jnp.float32(0.5), step[0].astype(f32))
    scal = jnp.stack([rate[0], 1.0 / correction])
    new, tab = adam(scal, owned, st, m, v, na)
    every = lax.all_gather(tab, "grp", axis=0, tiled=False)
    every = every.reshape(groups, PACKROWS, na, 128).transpose(1, 0, 2, 3).reshape(PACKROWS, adapters, 128)
    every = every.swapaxes(0, 1).reshape(adapters, PACKROWS * 128)
    new = new.reshape(PACKROWS, na, 128).swapaxes(0, 1).reshape(na, PACKROWS * 128)
    return out.reshape(tokens.shape), ig.reshape(tokens.shape), new, every


W_A_IN, W_B_B, W_B_X, W_B_C, W_A_OUT, W_B_OUT, W_A_GATE, W_A_UP, W_B_DOWN, W_FFN = (1024 * n for n in range(10))
W_ENDS = W_A_GATE
BLOCKS = FF // FB
W_BLOCK = 3 * FB
FFN_COLS = WIRE - W_ENDS
SPREAD_BLOCKS = 2


def wire(first, n):
    if first == B_IN:
        return (W_B_B, W_B_C, W_B_X)[n // D] + n % D
    for place, matrix in enumerate((B_GATE, B_UP, A_DOWN)):
        if first == matrix:
            return W_FFN + n // FB * W_BLOCK + place * FB + n % FB
    return {A_IN: W_A_IN, A_OUT: W_A_OUT, B_OUT: W_B_OUT, A_GATE: W_A_GATE, A_UP: W_A_UP, B_DOWN: W_B_DOWN}[first] + n


def a_pieces(first, count):
    for matrix, height in A_PARTS:
        if matrix <= first < matrix + height:
            return [(k, wire(matrix, first - matrix + k), FB) for k in range(0, count, FB)]


class Place:
    def __init__(self):
        seq, grp = lax.axis_index("seq"), lax.axis_index("grp")
        self.seq, self.grp = seq, grp
        self.c, self.x, self.y, self.z = grp % 2, grp // 2, seq % 2, seq // 2
        self.core = grp + 1 - 2 * self.c
        self.gx = (grp + 2) % 4
        self.sy = seq + 1 - 2 * self.y
        self.sz = seq + 2 - 4 * (self.z % 2)

    def along_z(self, d):
        return (self.seq + 2 * d) % 8


def announce(seq, count, devices, both=True):
    barrier = pltpu.get_barrier_semaphore()
    if both:

        @pl.when(seq > 0)
        def _():
            pl.semaphore_signal(barrier, inc=1, device_id={"seq": seq - 1}, device_id_type=MESH)

        @pl.when(seq < count - 1)
        def _():
            pl.semaphore_signal(barrier, inc=1, device_id={"seq": seq + 1}, device_id_type=MESH)

    for device in devices:
        pl.semaphore_signal(barrier, inc=1, device_id=device, device_id_type=MESH)
    ends = (seq + count - 1) // count + (2 * count - 2 - seq) // count if both else 0
    return lambda: pl.semaphore_wait(barrier, ends + len(devices))


class Spread:
    WAYS = {
        "X": (((), ("x", "core")), (("x",), ("cx",)), (("core", "cx"), ())),
        "Y": (((), ("x", "core")), (("x",), ("y", "cx")), (("y",), ("cy",)), (("core", "cx", "cy"), ())),
        "Z": (((), ("x", "core")), (("x",), ("z", "cx")), (("z",), ("cz",)), (("core", "cx", "cz"), ())),
        "S": (
            ((), ("x", "core")), (("x",), ("y", "z", "cx")), (("y",), ("dz", "cy")), (("z",), ("dy", "cz")), (("dy", "dz"), ("cd",)),
            (("core", "cx", "cy", "cz", "cd"), ()),
        ),
    }
    KINDS = ("core", "x", "y", "z", "dy", "dz", "cx", "cy", "cz", "cd")

    def __init__(self, at, own, slot, pieces, ways, step, send_sems, recv_sems):
        self.at, self.own, self.slot, self.pieces, self.ways, self.step = at, own, slot, pieces, ways, step
        self.send_sems, self.recv_sems = send_sems, recv_sems

    def copy(self, kind, p):
        at, way = self.at, self.ways[p]
        first, size = self.pieces[p]
        share = size // {"X": 1, "Y": 2, "Z": 2, "S": 4}[way]
        part = lambda q: pl.multiple_of(first + q * share, self.step) if way != "X" else first
        q = {"X": 0, "Y": at.y, "Z": at.z % 2, "S": at.seq % 4}[way]
        if way == "S":
            qy, qz, qd = q + 1 - 2 * (q % 2), (q + 2) % 4, 3 - q
        else:
            qy = qz = qd = 1 - q
        half = -(-share // (2 * self.step)) * self.step
        core, y, z = {"grp": at.core}, {"seq": at.sy}, {"seq": at.sz}
        if kind == "core":
            src, dst, device = self.own(first, size), self.slot(at.grp, first, size), core
        elif kind == "x":
            src, dst, device = self.own(part(q), share), self.slot(at.grp, part(q), share), {"grp": at.gx}
        else:
            start, count, device = {
                "y": (part(q), share, y),
                "z": (part(q), share, z),
                "dy": (part(qz), half, y),
                "dz": (part(qy) + half, share - half, z),
                "cx": (part(q), share, core),
                "cy": (part(qy), share, core),
                "cz": (part(qz), share, core),
                "cd": (part(qd), share, core),
            }[kind]
            if kind == "dz":
                start = pl.multiple_of(start, self.step)
            src = dst = self.slot(at.gx, start, count)
        n = len(self.KINDS) * p + self.KINDS.index(kind)
        return pltpu.make_async_remote_copy(
            src_ref=src, dst_ref=dst, send_sem=self.send_sems.at[n], recv_sem=self.recv_sems.at[n],
            device_id=device, device_id_type=MESH,
        )

    def steps(self, p):
        return len(self.WAYS[self.ways[p]])

    def leg(self, number, p):
        waits, starts = self.WAYS[self.ways[p]][number]
        for kind in waits:
            self.copy(kind, p).wait_recv()
        for kind in starts:
            self.copy(kind, p).start()

    def sent(self, p):
        for _, starts in self.WAYS[self.ways[p]]:
            for kind in starts:
                self.copy(kind, p).wait_send()


def adapter_mask(adapter_ref, seqs, length):
    column = lax.broadcasted_iota(jnp.int32, (length, 128), 1) // RANK
    return jnp.concatenate([jnp.where(column == adapter_ref[s], 1.0, 0.0) for s in range(seqs)], axis=0)


def fill_shuffle(perm_ref):
    diff = lax.broadcasted_iota(jnp.int32, (128, 1024), 1) - 8 * lax.broadcasted_iota(jnp.int32, (128, 1024), 0)
    for c in range(8):
        perm_ref[128 * c : 128 * c + 128, :] = jnp.where(diff == c, 1.0, 0.0).astype(bf16)


def build_own(na, grp, st_ref, tb_ref, lhs_ref, perm_ref):
    own = lambda a: pl.ds(pl.multiple_of((grp * na + a) * RANK, RANK), RANK)
    fill_shuffle(perm_ref)
    for n, (first, count) in enumerate(A_CHUNKS):
        for a in range(na):
            packed = st_ref[pl.ds(na * (first // 8) + a, 128, stride=na), :]
            turned = packed.T.astype(bf16)
            row = (n * na + a) * RANK
            for c in range(8):
                lhs_ref[row : row + RANK, 128 * c : 128 * c + 128] = turned[RANK * c : RANK * c + RANK, :]
    full = dot(lhs_ref[...], perm_ref[...]).astype(bf16)
    for n, (first, count) in enumerate(A_CHUNKS):
        for a in range(na):
            row = (n * na + a) * RANK
            for k, col, size in a_pieces(first, count):
                tb_ref[own(a), col : col + size] = full[row : row + RANK, k : k + size]
    for first, breadth in B_PARTS:
        blocks = breadth // 128
        for a in range(na):
            for c in range(blocks):
                part = st_ref[pl.ds(na * (first // 8 + c) + a, RANK, stride=na * blocks), :]
                col = wire(first, 128 * c)
                tb_ref[own(a), col : col + 128] = part.astype(bf16)


SPREAD_PIECES = ((W_A_IN, 1024), (W_B_B, 2048), (W_B_C, 1024), (W_A_OUT, 5120), (W_FFN, SPREAD_BLOCKS * W_BLOCK))


class Sums:
    CORE, X, Y, Z, BACK_Z, BACK_Y = range(6)
    COPIES = 10

    def __init__(self, at, g_ref, cr_ref, xr_ref, yr_ref, zr_ref, sum_ref, send_sems, recv_sems):
        self.at, self.g, self.cr, self.xr, self.yr, self.zr, self.sum = at, g_ref, cr_ref, xr_ref, yr_ref, zr_ref, sum_ref
        self.send_sems, self.recv_sems = send_sems, recv_sems

    def unit(self, z, start, size):
        rows = pl.ds(pl.multiple_of(RANK * (z // 2), RANK), RANK)
        quarter = size // 4
        return rows, pl.ds(pl.multiple_of(start + self.at.y * (size // 2) + (z % 2) * quarter, 128), quarter)

    def half(self, y, start, size):
        return pl.ds(pl.multiple_of(start + y * (size // 2), 128), size // 2)

    def slot(self, start, size, share):
        return pl.ds(pl.multiple_of(start // share, 128), size // share)

    def copies(self, stage, group):
        index, start, size = group
        at = self.at
        cols = pl.ds(start, size)
        if stage == self.CORE:
            parts = [(self.g.at[:, 1 - at.c, :, cols], self.cr.at[:, :, cols], {"grp": at.core})]
        elif stage == self.X:
            parts = [(self.g.at[1 - at.x, at.c, :, cols], self.xr.at[:, cols], {"grp": at.gx})]
        elif stage == self.Y:
            away = self.half(1 - at.y, start, size)
            parts = [(self.g.at[at.x, at.c, :, away], self.yr.at[:, self.slot(start, size, 2)], {"seq": at.sy})]
        elif stage == self.BACK_Y:
            part = self.sum.at[:, self.half(at.y, start, size)]
            parts = [(part, part, {"seq": at.sy})]
        else:
            parts = []
            for d in range(1, 4):
                if stage == self.Z:
                    rows, span = self.unit((at.z + d) % 4, start, size)
                    parts.append((
                        self.g.at[at.x, at.c, rows, span], self.zr.at[d - 1, :, self.slot(start, size, 4)],
                        {"seq": at.along_z(d)},
                    ))
                else:
                    rows, span = self.unit(at.z, start, size)
                    part = self.sum.at[rows, span]
                    parts.append((part, part, {"seq": at.along_z(d)}))
        first = self.COPIES * index + {self.CORE: 0, self.X: 1, self.Y: 2, self.Z: 3, self.BACK_Z: 6, self.BACK_Y: 9}[stage]
        return [
            pltpu.make_async_remote_copy(
                src_ref=src, dst_ref=dst, send_sem=self.send_sems.at[first + n], recv_sem=self.recv_sems.at[first + n],
                device_id=device, device_id_type=MESH,
            )
            for n, (src, dst, device) in enumerate(parts)
        ]

    def send(self, stage, group):
        for copy in self.copies(stage, group):
            copy.start()

    def take(self, stage, group):
        for copy in self.copies(stage, group):
            copy.wait()
        _, start, size = group
        at = self.at
        cols = pl.ds(start, size)
        wide = lambda value: value.astype(f32)
        if stage == self.CORE:
            for x in range(2):
                self.g[x, at.c, :, cols] = (wide(self.g[x, at.c, :, cols]) + wide(self.cr[x, :, cols])).astype(bf16)
        elif stage == self.X:
            self.g[at.x, at.c, :, cols] = (wide(self.g[at.x, at.c, :, cols]) + wide(self.xr[:, cols])).astype(bf16)
        elif stage == self.Y:
            mine = self.half(at.y, start, size)
            came = self.yr[:, self.slot(start, size, 2)]
            self.g[at.x, at.c, :, mine] = (wide(self.g[at.x, at.c, :, mine]) + wide(came)).astype(bf16)
        elif stage == self.Z:
            rows, span = self.unit(at.z, start, size)
            total = wide(self.g[at.x, at.c, rows, span])
            for d in range(3):
                total = total + wide(self.zr[d, :, self.slot(start, size, 4)])
            self.sum[rows, span] = total.astype(bf16)


def sums_scratch(cols):
    return [
        pltpu.VMEM((2, 2, 32, cols), bf16),
        pltpu.VMEM((2, 32, cols), bf16),
        pltpu.VMEM((32, cols), bf16),
        pltpu.VMEM((32, cols // 2), bf16),
        pltpu.VMEM((3, 16, cols // 4), bf16),
        pltpu.VMEM((32, cols), bf16),
    ]


def put_grad(g_ref, cols, value):
    for x in range(2):
        for c in range(2):
            first = 64 * x + 32 * c
            g_ref[x, c, :, cols] = value[first : first + 32, :].astype(bf16)


UPDATES = (
    (B_GATE, FF), (B_UP, FF), (A_DOWN, FF), (A_GATE, D), (A_UP, D), (B_DOWN, D), (A_OUT, 2 * D), (B_IN, 3 * D),
    (A_IN, D),
)
MOST = 2 * FF // 8
NATIVE = tuple((2 * first // 8, 2 * count // 8) for first, count in UPDATES)


def update_grad(na, part, sum_ref, lhs_ref, perm_ref, gn_ref):
    first, count = UPDATES[part]
    begin = na * first // 8
    inside = lambda start: first <= start < first + count
    chunks = [chunk for chunk in A_CHUNKS if inside(chunk[0])]
    for n, (start, size) in enumerate(chunks):
        for a in range(na):
            row = (n * na + a) * RANK
            if size < 1024:
                lhs_ref[row : row + RANK, size:] = jnp.zeros((RANK, 1024 - size), bf16)
            for k, col, breadth in a_pieces(start, size):
                lhs_ref[row : row + RANK, k : k + breadth] = sum_ref[a * RANK : (a + 1) * RANK, col : col + breadth]
    if chunks:
        height = len(chunks) * na * RANK
        full = dot_nt(lhs_ref[:height, :], perm_ref[...])
    for n, (start, size) in enumerate(chunks):
        for a in range(na):
            row = (n * na + a) * RANK
            turned = jnp.concatenate([full[row : row + RANK, 128 * c : 128 * c + 128] for c in range(8)], axis=0)
            gn_ref[pl.ds(na * (start // 8) + a - begin, size // 8, stride=na), :] = turned.T[: size // 8]
    for start, breadth in B_PARTS:
        if inside(start):
            blocks = breadth // 128
            for a in range(na):
                for c in range(blocks):
                    col = wire(start, 128 * c)
                    gn_ref[pl.ds(na * (start // 8 + c) + a - begin, RANK, stride=na * blocks), :] = sum_ref[
                        a * RANK : (a + 1) * RANK, col : col + 128
                    ].astype(f32)


def group_of(j):
    start = W_FFN + j * W_BLOCK
    return j, start if isinstance(j, int) else pl.multiple_of(start, 128), W_BLOCK


GROUPS = {
    "ends": (BLOCKS, W_ENDS, W_FFN - W_ENDS),
    "out": (BLOCKS + 1, W_B_C, W_ENDS - W_B_C),
    "in1": (BLOCKS + 2, W_B_B, W_B_C - W_B_B),
    "in2": (BLOCKS + 3, W_A_IN, W_B_B),
}
GROUPS.update({j: group_of(j) for j in range(BLOCKS)})


WAYS = "ZZYXXXYXX"
BACKWARD_ORDER = (
    (8, 7, 6, 5, 4, 3, 2, 8), 0, ("ends", 6, 7, 3, 5), 1, ("ends", 4, 8, 7, 6, 5), 2, (4, 8), 3, ("ends", 7, 5, 6), 4,
    ("out", 8), 5, ("out", "ends", 7, 6, 8), 6, ("in1",), 7, ("in1", "in2", 7, 8), 8, ("in2", "out", "ends"), 9,
    ("in1", "in2"), 10,
)
TAIL_ORDER = (
    ("sum", "out"), ("update", 0), ("sum", "in1"), ("sum", "in2"), ("sum", "ends"), ("update", 1), ("update", 2),
    ("out", 0), ("sum", "out"), ("sum", "ends"), ("update", 3), ("sum", "in1"), ("update", 4), ("sum", "in2"),
    ("update", 5), ("pass", 0), ("out", 1), ("pass", 1), ("out", 2), ("sum", "out"), ("out", 3), ("sum", "in1"),
    ("out", 4), ("sum", "in2"), ("pass", 2), ("out", 5), ("sum", "out"), ("update", 6), ("pass", 3), ("sum", "in1"),
    ("update", 7), ("sum", "in2"), ("update", 8), ("pass", 0), ("pass", 3), ("pass", 4), ("pass", 5), ("out", 6),
    ("pass", 0), ("pass", 1), ("pass", 4), ("pass", 2), ("pass", 5), ("pass", 6), ("out", 7), ("pass", 1), ("pass", 2),
    ("out", 8), ("pass", 7), ("pass", 6), ("pass", 8), ("pass", 7), ("pass", 6), ("pass", 8),
)


def rest_kernel(
    seqs, length, count, na,
    adapter_ref, rate_ref, step_ref, ids_ref, cw_ref, n1_ref, n2_ref,
    cot_hbm, tok_hbm, wi_hbm, wo_hbm, wg_hbm, wu_hbm, wd_hbm, st_hbm, m_hbm, v_hbm,
    out_hbm, ig_hbm, new_hbm, all_hbm, hid_hbm, gated_hbm, b_hbm, c_hbm, x_hbm, conv_hbm, same_hbm, u1_hbm,
    cot_ref, u_ref, mg_ref, mu_ref, mo_ref, mi_ref, ahead_out_ref, ahead_in_ref, tb_ref, h1_ref, gn_ref, gh_ref, gb_ref, dmid_ref, gmg_ref, gmu_ref, gd_ref,
    edge_out_ref, edge_in_ref, g_ref, cr_ref, xr_ref, yr_ref, zr_ref, sum_ref, tab_ref,
    result_sems, open_sems, store_sems, open_send, open_recv, load_sems, weight_sems, hid_sems, tab_send, tab_recv, send_sems, recv_sems,
    halo_sems, old_sems, new_sems, own_sems, spread_send, spread_recv,
):
    rows_all = seqs * length
    at = Place()
    seq = at.seq
    met = announce(seq, count, [{"grp": at.core}, {"grp": at.gx}] + [{"seq": at.along_z(d)} for d in range(1, 4)])
    sums = Sums(at, g_ref, cr_ref, xr_ref, yr_ref, zr_ref, sum_ref, send_sems, recv_sems)
    rows32 = lambda owner: pl.ds(pl.multiple_of(owner * 32, 32), 32)
    twice = 2.0 * adapter_mask(adapter_ref, seqs, length)
    block = lambda owner, first, size: tb_ref.at[rows32(owner), pl.ds(first, size)]
    table_spread = Spread(
        at, functools.partial(block, at.grp), block, SPREAD_PIECES, "XXXSS", 128, open_send, open_recv
    )

    load_cot = pltpu.make_async_copy(cot_hbm, cot_ref, result_sems.at[2])
    keep_grad = pltpu.make_async_copy(gb_ref, ig_hbm, result_sems.at[0])
    keep_out = pltpu.make_async_copy(u_ref, out_hbm, result_sems.at[1])

    def opening(
        st_ref, lhs_ref, perm_ref, wi_ref, wo_ref, tok_ref, u1_ref, b_ref, c_ref, x_ref, conv_ref, same_ref, gated_ref, ext_ref
    ):
        load_in = pltpu.make_async_copy(wi_hbm, wi_ref, open_sems.at[0])
        load_out = pltpu.make_async_copy(wo_hbm, wo_ref, open_sems.at[1])
        load_st = pltpu.make_async_copy(st_hbm, st_ref, open_sems.at[2])
        load_tok = pltpu.make_async_copy(tok_hbm, tok_ref, open_sems.at[3])
        for copy in (load_st, load_tok, load_in, load_out, load_cot):
            copy.start()
        load_st.wait()
        build_own(na, at.grp, st_ref, tb_ref, lhs_ref, perm_ref)
        leg = table_spread.leg

        def keep(n, src, dst):
            return pltpu.make_async_copy(src, dst, store_sems.at[n])

        met()
        leg(0, 0)
        load_tok.wait()
        tokens = tok_ref[...].astype(f32)
        u1 = norm(tokens, n1_ref[...])[0].astype(bf16)
        u1_ref[...] = u1
        leg(0, 1)
        keep(0, u1_ref, u1_hbm).start()
        load_in.wait()
        for k in range(2):
            b_ref[:, 512 * k : 512 * k + 512] = dot(u1, wi_ref[:, 512 * k : 512 * k + 512])
        leg(0, 2)
        leg(1, 0)
        for k in range(2):
            x_ref[:, 512 * k : 512 * k + 512] = dot(u1, wi_ref[:, 2 * D + 512 * k : 2 * D + 512 * k + 512])
        leg(0, 3)
        leg(0, 4)
        for k in range(2):
            c_ref[:, 512 * k : 512 * k + 512] = dot(u1, wi_ref[:, D + 512 * k : D + 512 * k + 512])
        leg(1, 1)
        leg(2, 0)
        mid = (dot_nt(u1, tb_ref[:, W_A_IN : W_A_IN + D]).astype(bf16).astype(f32) * twice).astype(bf16)
        mi_ref[...] = mid
        leg(1, 2)
        leg(2, 1)
        for first, to_ref in ((W_B_B, b_ref), (W_B_X, x_ref)):
            for k in range(2):
                col = first + 512 * k
                to_ref[:, 512 * k : 512 * k + 512] += dot(mid, tb_ref[:, col : col + 512])
        leg(1, 3)
        leg(1, 4)
        keep(1, b_ref, b_hbm).start()
        keep(2, x_ref, x_hbm).start()
        width = D + 128
        for s in range(seqs):
            rows = pl.ds(s * length, length)
            ext_ref[s, 0:8, :] = jnp.zeros((8, width), f32)
            ext_ref[s, 8:, :D] = b_ref[rows, :] * x_ref[rows, :]
            ext_ref[s, 8:, D:] = jnp.broadcast_to(ids_ref[s : s + 1, :].astype(f32), (length, 128)).T
            ahead_out_ref[2 * s : 2 * s + 2, :] = ext_ref[s, length + 6 : length + 8, :]
        along = pltpu.make_async_remote_copy(
            src_ref=ahead_out_ref, dst_ref=ahead_in_ref, send_sem=halo_sems.at[2], recv_sem=halo_sems.at[3],
            device_id={"seq": seq + 1}, device_id_type=MESH,
        )

        @pl.when(seq < count - 1)
        def _():
            along.start()

        leg(2, 2)
        leg(2, 3)
        leg(3, 3)
        for k in range(2):
            col = W_B_C + 512 * k
            c_ref[:, 512 * k : 512 * k + 512] += dot(mid, tb_ref[:, col : col + 512])
        leg(2, 4)
        leg(3, 4)
        keep(3, c_ref, c_hbm).start()

        @pl.when(seq < count - 1)
        def _():
            along.wait_send()

        @pl.when(seq > 0)
        def _():
            along.wait_recv()
            for s in range(seqs):
                ext_ref[s, 6:8, :] = ahead_in_ref[2 * s : 2 * s + 2, :]

        for s in range(seqs):
            rows = pl.ds(s * length, length)
            now_ids = ext_ref[s, 8:, D:]
            same1 = jnp.where(ext_ref[s, pl.ds(7, length), D:] == now_ids, 1.0, 0.0)
            same2 = jnp.where(ext_ref[s, pl.ds(6, length), D:] == now_ids, 1.0, 0.0)
            same_ref[0, s] = same1
            same_ref[1, s] = same2
            conv = (
                cw_ref[2:3, :] * ext_ref[s, 8:, :D]
                + cw_ref[1:2, :] * same1[:, :1] * ext_ref[s, pl.ds(7, length), :D]
                + cw_ref[0:1, :] * same2[:, :1] * ext_ref[s, pl.ds(6, length), :D]
            )
            conv_ref[rows, :] = conv
            gated_ref[rows, :] = (c_ref[rows, :] * conv).astype(bf16)
        keep(4, conv_ref, conv_hbm).start()
        keep(5, same_ref, same_hbm).start()
        leg(4, 3)
        leg(4, 4)
        keep(6, gated_ref, gated_hbm).start()
        gated = gated_ref[...]
        load_out.wait()
        for k in range(2):
            cols = slice(512 * k, 512 * k + 512)
            h1_ref[:, cols] = tok_ref[:, cols].astype(f32) + dot(gated, wo_ref[:, cols])
        leg(5, 3)
        mid_out = (dot_nt(gated, tb_ref[:, W_A_OUT : W_A_OUT + D]).astype(bf16).astype(f32) * twice).astype(bf16)
        mo_ref[...] = mid_out
        for k in range(2):
            cols = slice(512 * k, 512 * k + 512)
            h1_ref[:, cols] += dot(mid_out, tb_ref[:, W_B_OUT + 512 * k : W_B_OUT + 512 * k + 512])
        u2 = norm(h1_ref[...], n2_ref[...])[0].astype(bf16)
        u_ref[...] = u2
        mg_ref[...] = (dot_nt(u2, tb_ref[:, W_A_GATE : W_A_GATE + D]).astype(bf16).astype(f32) * twice).astype(bf16)
        mu_ref[...] = (dot_nt(u2, tb_ref[:, W_A_UP : W_A_UP + D]).astype(bf16).astype(f32) * twice).astype(bf16)
        for n, (src, dst) in enumerate((
            (u1_ref, u1_hbm), (b_ref, b_hbm), (x_ref, x_hbm), (c_ref, c_hbm), (conv_ref, conv_hbm), (same_ref, same_hbm),
            (gated_ref, gated_hbm),
        )):
            keep(n, src, dst).wait()

    wide = pltpu.VMEM((rows_all, D), f32)
    half = pltpu.VMEM((rows_all, D), bf16)
    pl.run_scoped(
        opening,
        pltpu.VMEM((na * PACKROWS, 128), f32), pltpu.VMEM((len(A_CHUNKS) * na * RANK, 1024), bf16),
        pltpu.VMEM((1024, 1024), bf16), pltpu.VMEM((D, 3 * D), bf16), pltpu.VMEM((D, D), bf16),
        half, half, wide, wide, wide, wide, pltpu.VMEM((2, seqs, length, 128), f32), half,
        pltpu.VMEM((seqs, length + 8, D + 128), f32),
    )

    def table_copy(kind, j):
        _, start, size = group_of(j)
        owner, device = {
            "core": (at.grp, {"grp": at.core}), "x": (at.grp, {"grp": at.gx}), "far": (at.gx, {"grp": at.core})
        }[kind]
        part = tb_ref.at[rows32(owner), pl.ds(start, size)]
        n = 3 * j + ("core", "x", "far").index(kind)
        return pltpu.make_async_remote_copy(
            src_ref=part, dst_ref=part, send_sem=tab_send.at[n], recv_sem=tab_recv.at[n], device_id=device, device_id_type=MESH
        )

    def when(first, j, last, run):
        @pl.when((j >= first) & (j <= last))
        def _():
            run()

    def feed_forward(wg_ref, wu_ref, wd_ref, hid_ref):
        def fetch(j, slot):
            cols = pl.ds(j * FB if isinstance(j, int) else pl.multiple_of(j * FB, FB), FB)
            return [
                pltpu.make_async_copy(wg_hbm.at[:, cols], wg_ref.at[slot], weight_sems.at[slot, 0]),
                pltpu.make_async_copy(wu_hbm.at[:, cols], wu_ref.at[slot], weight_sems.at[slot, 1]),
                pltpu.make_async_copy(wd_hbm.at[cols, :], wd_ref.at[slot], weight_sems.at[slot, 2]),
            ]

        def keep(j, slot):
            cols = pl.ds(j * FB if isinstance(j, int) else pl.multiple_of(j * FB, FB), FB)
            return pltpu.make_async_copy(hid_ref.at[slot], hid_hbm.at[:, cols], hid_sems.at[slot])

        for copy in fetch(0, 0):
            copy.start()
        for ref in (gn_ref, dmid_ref, gmg_ref, gmu_ref):
            ref[...] = jnp.zeros_like(ref)
        load_cot.wait()
        gd_ref[...] = (dot_nt(cot_ref[...], tb_ref[:, W_B_DOWN : W_B_DOWN + D]) * twice).astype(bf16)
        table_spread.leg(5, 4)

        def block(j, carry):
            slot = j % 2
            for copy in fetch(j, slot):
                copy.wait()

            def more():
                for copy in fetch(j + 1, 1 - slot):
                    copy.start()

            when(0, j, BLOCKS - 2, more)
            when(2, j, BLOCKS - 1, lambda: keep(j - 2, slot).wait())
            lead = SPREAD_BLOCKS

            def leave():
                table_copy("x", j + lead).start()
                table_copy("core", j + lead).start()

            def go_on():
                table_copy("x", j + lead - 1).wait()
                table_copy("far", j + lead - 1).start()

            def there():
                table_copy("core", j).wait()
                table_copy("far", j).wait()

            when(0, j, BLOCKS - 1 - lead, leave)
            when(1, j, BLOCKS - lead, go_on)
            when(lead, j, BLOCKS - 1, there)
            for stage in range(6):

                def advance(stage=stage):
                    if stage > 0:
                        sums.take(stage - 1, group_of(j - 1 - stage))
                    sums.send(stage, group_of(j - 1 - stage))

                when(1 + stage, j, BLOCKS - 1, advance)
            when(7, j, BLOCKS - 1, lambda: sums.take(5, group_of(j - 7)))

            base = W_FFN + j * W_BLOCK
            part = lambda place: pl.ds(pl.multiple_of(base + place * FB, 128), FB)
            tab_gate, tab_up, tab_down = (tb_ref.at[:, part(place)] for place in range(3))
            u = u_ref[...]
            gate = dot(u, wg_ref[slot]) + dot(mg_ref[...], tab_gate[...])
            up = dot(u, wu_ref[slot]) + dot(mu_ref[...], tab_up[...])
            back = dot_nt(cot_ref[...], wd_ref[slot]) + dot(gd_ref[...], tab_down[...])
            sig = jax.nn.sigmoid(gate)
            silu = gate * sig
            hidden = (silu * up).astype(bf16)
            hid_ref[slot] = hidden
            keep(j, slot).start()
            grad_gate = (back * up * sig * (1.0 + gate * (1.0 - sig))).astype(bf16)
            grad_up = (back * silu).astype(bf16)
            gn_ref[...] += dot_nt(grad_gate, wg_ref[slot]) + dot_nt(grad_up, wu_ref[slot])
            dmid_ref[...] += dot_nt(hidden, tab_down[...])
            gmg_ref[...] += dot_nt(grad_gate, tab_gate[...])
            gmu_ref[...] += dot_nt(grad_up, tab_up[...])
            put_grad(g_ref, part(0), dot_tn(mg_ref[...], grad_gate))
            put_grad(g_ref, part(1), dot_tn(mu_ref[...], grad_up))
            put_grad(g_ref, part(2), dot_tn(gd_ref[...], hidden))
            return carry

        lax.fori_loop(0, BLOCKS, block, 0)
        for j in range(BLOCKS - 2, BLOCKS):
            keep(j, j % 2).wait()
        for p in range(len(SPREAD_PIECES)):
            table_spread.sent(p)

    pl.run_scoped(
        feed_forward,
        pltpu.VMEM((2, D, FB), bf16), pltpu.VMEM((2, D, FB), bf16), pltpu.VMEM((2, FB, D), bf16),
        pltpu.VMEM((2, rows_all, FB), bf16),
    )

    sent = {BLOCKS - 2 - stage: stage for stage in range(6)}

    def advance(*names):
        for name in names:
            stage = sent.get(name, -1)
            if stage >= 0:
                sums.take(stage, GROUPS[name])
            if stage < 5:
                sums.send(stage + 1, GROUPS[name])
            sent[name] = stage + 1

    dmid = (dmid_ref[...].astype(bf16).astype(f32) * twice).astype(bf16)

    def backward(gated_ref, one_ref, two_ref, same_ref, u1_ref, tok_ref, wi_ref, wo_ref, gg_ref, gp_ref):
        pairs = (
            (wo_hbm, wo_ref), (c_hbm, one_ref), (conv_hbm, two_ref), (same_hbm, same_ref.at[:, :, :length, :]),
            (gated_hbm, gated_ref), (wi_hbm, wi_ref), (u1_hbm, u1_ref), (tok_hbm, tok_ref), (x_hbm, one_ref), (b_hbm, two_ref),
        )
        copies = [pltpu.make_async_copy(*pair, load_sems.at[n]) for n, pair in enumerate(pairs)]
        get_wo, get_c, get_conv, get_same, get_gated, get_wi, get_u1, get_tok, get_x, get_b = copies
        for copy in (get_wo, get_c, get_conv, get_same):
            copy.start()
        held = {}

        def part0():
            held["gm_gate"] = (gmg_ref[...] * twice).astype(bf16)
            held["gm_up"] = (gmu_ref[...] * twice).astype(bf16)
            put_grad(g_ref, slice(W_A_GATE, W_A_GATE + D), dot_tn(held["gm_gate"], u_ref[...]))
            put_grad(g_ref, slice(W_A_UP, W_A_UP + D), dot_tn(held["gm_up"], u_ref[...]))
            put_grad(g_ref, slice(W_B_DOWN, W_B_DOWN + D), dot_tn(dmid, cot_ref[...]))

        def part1():
            for k in range(2):
                cols = slice(512 * k, 512 * k + 512)
                gn_ref[:, cols] += dot(held["gm_gate"], tb_ref[:, W_A_GATE + 512 * k : W_A_GATE + 512 * k + 512]) + dot(
                    held["gm_up"], tb_ref[:, W_A_UP + 512 * k : W_A_UP + 512 * k + 512]
                )
            for s in range(seqs):
                rows = pl.ds(s * length, length)
                h1 = h1_ref[rows, :]
                inv2 = norm(h1, n2_ref[...])[1]
                e2 = gn_ref[rows, :] * n2_ref[...]
                gh = cot_ref[rows, :].astype(f32) + inv2 * e2
                gh = gh - h1 * (inv2 * inv2 * inv2 * jnp.mean(h1 * e2, axis=-1, keepdims=True))
                gh_ref[rows, :] = gh
                gb_ref[rows, :] = gh.astype(bf16)
            for copy in (get_gated, get_wi, get_u1, get_tok):
                copy.start()

        def part2():
            get_wo.wait()
            held["gb"] = gb_ref[...]
            held["gm_out"] = (dot_nt(held["gb"], tb_ref[:, W_B_OUT : W_B_OUT + D]) * twice).astype(bf16)
            for k in range(2):
                cols = slice(512 * k, 512 * k + 512)
                part = dot_nt(held["gb"], wo_ref[cols, :]) + dot(held["gm_out"], tb_ref[:, W_A_OUT + 512 * k : W_A_OUT + 512 * k + 512])
                for s in range(seqs):
                    gg_ref[s, :length, cols] = part[s * length : (s + 1) * length, :]

        def part3():
            for copy in (get_c, get_conv, get_same):
                copy.wait()
            for s in range(seqs):
                rows = pl.ds(s * length, length)
                gg = gg_ref[s, :length, :]
                gp_ref[rows, D : 2 * D] = (gg * two_ref[rows, :]).astype(bf16)
                gg_ref[s, :length, :] = gg * one_ref[rows, :]
                gg_ref[s, length:, :] = jnp.zeros((8, D), f32)
                for k in range(2):
                    same_ref[k, s, length:, :] = jnp.zeros((8, 128), f32)
                edge_out_ref[2 * s : 2 * s + 1, :] = cw_ref[0:1, :] * same_ref[1, s, 0:1, 0:1] * gg_ref[s, 0:1, :]
                edge_out_ref[2 * s + 1 : 2 * s + 2, :] = (
                    cw_ref[0:1, :] * same_ref[1, s, 1:2, 0:1] * gg_ref[s, 1:2, :]
                    + cw_ref[1:2, :] * same_ref[0, s, 0:1, 0:1] * gg_ref[s, 0:1, :]
                )
            get_x.start()
            get_b.start()
            held["along"] = pltpu.make_async_remote_copy(
                src_ref=edge_out_ref, dst_ref=edge_in_ref, send_sem=halo_sems.at[0], recv_sem=halo_sems.at[1],
                device_id={"seq": seq - 1}, device_id_type=MESH,
            )

            @pl.when(seq > 0)
            def _():
                held["along"].start()

        def part4():
            get_gated.wait()
            put_grad(g_ref, slice(W_A_OUT, W_A_OUT + D), dot_tn(held["gm_out"], gated_ref[...]))
            put_grad(g_ref, slice(W_B_OUT, W_B_OUT + D), dot_tn(mo_ref[...], held["gb"]))
            put_grad(g_ref, slice(W_B_C, W_B_C + D), dot_tn(mi_ref[...], gp_ref[:, D : 2 * D]))

        def part5():

            @pl.when(seq > 0)
            def _():
                held["along"].wait_send()

            @pl.when(seq < count - 1)
            def _():
                held["along"].wait_recv()

            get_x.wait()
            get_b.wait()
            for s in range(seqs):
                one, two = pl.ds(1, length), pl.ds(2, length)
                gg_ref[s, :length, :] = (
                    cw_ref[2:3, :] * gg_ref[s, :length, :]
                    + cw_ref[1:2, :] * same_ref[0, s, one, 0:1] * gg_ref[s, one, :]
                    + cw_ref[0:1, :] * same_ref[1, s, two, 0:1] * gg_ref[s, two, :]
                )

            @pl.when(seq < count - 1)
            def _():
                for s in range(seqs):
                    gg_ref[s, length - 2 : length, :] += edge_in_ref[2 * s : 2 * s + 2, :]

            for s in range(seqs):
                rows = pl.ds(s * length, length)
                gmix = gg_ref[s, :length, :]
                gp_ref[rows, 0:D] = (gmix * one_ref[rows, :]).astype(bf16)
                gp_ref[rows, 2 * D :] = (gmix * two_ref[rows, :]).astype(bf16)

        def part6():
            put_grad(g_ref, slice(W_B_B, W_B_B + D), dot_tn(mi_ref[...], gp_ref[:, :D]))
            put_grad(g_ref, slice(W_B_X, W_B_X + D), dot_tn(mi_ref[...], gp_ref[:, 2 * D :]))

        def part7():
            gm_part = dot_nt(gp_ref[:, :D], tb_ref[:, W_B_B : W_B_B + D])
            gm_part += dot_nt(gp_ref[:, D : 2 * D], tb_ref[:, W_B_C : W_B_C + D])
            gm_part += dot_nt(gp_ref[:, 2 * D :], tb_ref[:, W_B_X : W_B_X + D])
            held["gm_in"] = (gm_part * twice).astype(bf16)
            get_u1.wait()
            put_grad(g_ref, slice(W_A_IN, W_A_IN + D), dot_tn(held["gm_in"], u1_ref[...]))

        def part8():
            get_wi.wait()
            for k in range(2):
                cols = slice(256 * k, 256 * k + 256)
                gn_ref[:, cols] = dot_nt(gp_ref[...], wi_ref[cols, :]) + dot(
                    held["gm_in"], tb_ref[:, W_A_IN + 256 * k : W_A_IN + 256 * k + 256]
                )

        def part9():
            for k in range(2, 4):
                cols = slice(256 * k, 256 * k + 256)
                gn_ref[:, cols] = dot_nt(gp_ref[...], wi_ref[cols, :]) + dot(
                    held["gm_in"], tb_ref[:, W_A_IN + 256 * k : W_A_IN + 256 * k + 256]
                )

        def part10():
            get_tok.wait()
            for s in range(seqs):
                rows = pl.ds(s * length, length)
                tokens = tok_ref[rows, :].astype(f32)
                inv1 = norm(tokens, n1_ref[...])[1]
                e1 = gn_ref[rows, :] * n1_ref[...]
                ig = gh_ref[rows, :] + inv1 * e1
                gb_ref[rows, :] = (
                    ig - tokens * (inv1 * inv1 * inv1 * jnp.mean(tokens * e1, axis=-1, keepdims=True))
                ).astype(bf16)
            keep_grad.start()

        parts = (part0, part1, part2, part3, part4, part5, part6, part7, part8, part9, part10)
        for what in BACKWARD_ORDER:
            if isinstance(what, tuple):
                advance(*what)
            else:
                parts[what]()

    pl.run_scoped(
        backward,
        half, wide, wide, pltpu.VMEM((2, seqs, length + 8, 128), f32), half, half,
        pltpu.VMEM((D, 3 * D), bf16), pltpu.VMEM((D, D), bf16), pltpu.VMEM((seqs, length + 8, D), f32),
        pltpu.VMEM((rows_all, 3 * D), bf16),
    )

    def updates(lhs_ref, perm_ref, old_ref, grad_ref, new_ref, wd_ref, hid_ref):
        own = lambda first, size: tab_ref.at[pl.ds(first, size), :]
        slot_of = lambda owner, first, size: all_hbm.at[owner, pl.ds(first, size), :]
        spread = Spread(at, own, slot_of, NATIVE, WAYS, 16, spread_send, spread_recv)
        going = {}

        def pass_on(*parts):
            for part in parts:
                spread.leg(going[part], part)
                going[part] += 1

        power = jnp.float32(1.0)
        for bit in range(8):
            power = power * jnp.where((step_ref[0] >> bit) % 2 == 1, jnp.float32(0.5 ** (2**bit)), jnp.float32(1.0))
        rate = rate_ref[0]
        correction = 1.0 - jnp.full((8, 128), power, f32)
        inv = (1.0 / correction)[0:1, :]

        def old(part):
            first, size = NATIVE[part]
            slot = part % 2
            return [
                pltpu.make_async_copy(ref.at[first : first + size], old_ref.at[slot, n, :size], old_sems.at[slot, n])
                for n, ref in enumerate((st_hbm, m_hbm, v_hbm))
            ]

        def new_copy(part):
            first, size = NATIVE[part]
            return pltpu.make_async_copy(new_ref.at[part % 2, :size], new_hbm.at[first : first + size], new_sems.at[part % 2])

        def own_copy(part):
            first, size = NATIVE[part]
            return pltpu.make_async_copy(
                tab_ref.at[first : first + size], all_hbm.at[at.grp, first : first + size], own_sems.at[part]
            )

        def update(part):
            first, size = NATIVE[part]
            slot = part % 2
            update_grad(na, part, sum_ref, lhs_ref, perm_ref, grad_ref)
            for copy in old(part):
                copy.wait()
            if part >= 2:
                new_copy(part - 2).wait()
            grad = grad_ref[:size]
            one = 0.5 * old_ref[slot, 1, :size] + 0.5 * grad
            two = 0.5 * old_ref[slot, 2, :size] + 0.5 * grad * grad
            new = old_ref[slot, 0, :size] - rate * (one * inv) / (jnp.sqrt(two * inv) + 1e-08)
            new_ref[slot, :size] = new
            tab_ref[first : first + size] = new.astype(bf16)
            new_copy(part).start()
            own_copy(part).start()
            if part + 2 < len(NATIVE):
                for copy in old(part + 2):
                    copy.start()
            going[part] = 0
            pass_on(part)

        def fetch(j):
            slot = j % 2
            return [
                pltpu.make_async_copy(wd_hbm.at[j * FB : (j + 1) * FB, :], wd_ref.at[slot], weight_sems.at[slot, 0]),
                pltpu.make_async_copy(hid_hbm.at[:, j * FB : (j + 1) * FB], hid_ref.at[slot], weight_sems.at[slot, 1]),
            ]

        def outputs(*blocks):
            for j in blocks:
                for copy in fetch(j):
                    copy.wait()
                h1_ref[...] += dot(hid_ref[j % 2], wd_ref[j % 2])
                if j + 2 < BLOCKS:
                    for copy in fetch(j + 2):
                        copy.start()
                if j == BLOCKS - 1:
                    u_ref[...] = h1_ref[...].astype(bf16)
                    keep_out.start()

        for part in range(2):
            for copy in old(part):
                copy.start()
        for j in range(2):
            for copy in fetch(j):
                copy.start()
        fill_shuffle(perm_ref)
        for k in range(2):
            cols = slice(512 * k, 512 * k + 512)
            h1_ref[:, cols] += dot(dmid, tb_ref[:, W_B_DOWN + 512 * k : W_B_DOWN + 512 * k + 512])
        for what, *which in TAIL_ORDER:
            {"sum": advance, "update": update, "pass": pass_on, "out": outputs}[what](*which)
        keep_grad.wait()
        keep_out.wait()
        for part in range(len(NATIVE)):
            spread.sent(part)
            own_copy(part).wait()
        for part in range(len(NATIVE) - 2, len(NATIVE)):
            new_copy(part).wait()

    pl.run_scoped(
        updates,
        pltpu.VMEM((5 * na * RANK, 1024), bf16), pltpu.VMEM((1024, 1024), bf16),
        pltpu.VMEM((2, 3, MOST, 128), f32), pltpu.VMEM((MOST, 128), f32), pltpu.VMEM((2, MOST, 128), f32),
        pltpu.VMEM((2, FB, D), bf16), pltpu.VMEM((2, rows_all, FB), bf16),
    )


def rest(seqs, length, count, na, *args):
    rows = seqs * length
    sd = jax.ShapeDtypeStruct
    sm = pl.BlockSpec(memory_space=pltpu.SMEM)
    vm = pl.BlockSpec(memory_space=pltpu.VMEM)
    hbm = pl.BlockSpec(memory_space=pl.ANY)
    wide = pltpu.VMEM((rows, D), f32)
    thin = pltpu.VMEM((rows, 128), f32)
    half, full = sd((rows, D), bf16), sd((rows, D), f32)
    mids = [pltpu.VMEM((rows, 128), bf16)] * 4
    ahead = pltpu.VMEM((2 * seqs, D + 128), f32)
    parts = len(NATIVE)
    dma = lambda *shape: pltpu.SemaphoreType.DMA(shape)
    return pl.pallas_call(
        functools.partial(rest_kernel, seqs, length, count, na),
        in_specs=[sm] * 3 + [vm] * 4 + [hbm] * 10,
        out_specs=[hbm] * 12,
        out_shape=[
            sd((rows, D), bf16), sd((rows, D), bf16), sd((na * PACKROWS, 128), f32), sd((4, na * PACKROWS, 128), bf16),
            sd((rows, FF), bf16), half, full, full, full, full, sd((2, seqs, length, 128), f32), half,
        ],
        scratch_shapes=[
            pltpu.VMEM((rows, D), bf16), pltpu.VMEM((rows, D), bf16), *mids, ahead, ahead,
            pltpu.VMEM((128, WIRE), bf16), wide, wide, wide, pltpu.VMEM((rows, D), bf16), thin, thin, thin,
            pltpu.VMEM((rows, 128), bf16),
            pltpu.VMEM((2 * seqs, D), f32), pltpu.VMEM((2 * seqs, D), f32),
            *sums_scratch(WIRE),
            pltpu.VMEM((na * PACKROWS, 128), bf16),
            dma(3), dma(4), dma(7), dma(len(Spread.KINDS) * len(SPREAD_PIECES)), dma(len(Spread.KINDS) * len(SPREAD_PIECES)),
            dma(10), dma(2, 3), dma(2), dma(3 * BLOCKS), dma(3 * BLOCKS),
            dma(Sums.COPIES * len(GROUPS)), dma(Sums.COPIES * len(GROUPS)),
            dma(4), dma(2, 3), dma(2), dma(parts), dma(len(Spread.KINDS) * parts), dma(len(Spread.KINDS) * parts),
        ],
        compiler_params=pltpu.CompilerParams(vmem_limit_bytes=63 * MIB, collective_id=3, has_side_effects=True),
    )(*args)


def lay_kernel(all_hbm, new_hbm, out_hbm, ig_hbm, to_ref, new_to, out_to, ig_to, all_ref, new_ref, out_ref, ig_ref, load_sems, store_sems):
    cuts = 4
    share = PACKROWS // cuts
    moves = []
    for k in range(cuts):
        rows = pl.ds(k * share, share)
        moves += [(all_hbm.at[g, rows], all_ref.at[g, rows], to_ref.at[rows, g]) for g in range(4)]
    for k in range(2):
        rows = pl.ds(k * PACKROWS, PACKROWS)
        moves.append((new_hbm.at[rows], new_ref.at[rows], new_to.at[rows]))
    moves += [(out_hbm, out_ref, out_to), (ig_hbm, ig_ref, ig_to)]
    loads = [pltpu.make_async_copy(src, mid, load_sems.at[n]) for n, (src, mid, _) in enumerate(moves)]
    stores = [pltpu.make_async_copy(mid, dst, store_sems.at[n]) for n, (_, mid, dst) in enumerate(moves)]
    for copy in loads:
        copy.start()
    for came, goes in zip(loads, stores):
        came.wait()
        goes.start()
    for copy in stores:
        copy.wait()


def lay_out(every, new, out, ig, na):
    hbm = pl.BlockSpec(memory_space=pl.ANY)
    scratch = lambda x: pltpu.VMEM(x.shape, x.dtype)
    like = lambda x: jax.ShapeDtypeStruct(x.shape, x.dtype)
    every = every.reshape(4, PACKROWS, na, 128)
    return pl.pallas_call(
        lay_kernel,
        in_specs=[hbm] * 4,
        out_specs=[hbm] * 4,
        out_shape=[jax.ShapeDtypeStruct((PACKROWS, 4, na, 128), bf16), like(new), like(out), like(ig)],
        scratch_shapes=[
            *(scratch(x) for x in (every, new, out, ig)), pltpu.SemaphoreType.DMA((20,)), pltpu.SemaphoreType.DMA((20,)),
        ],
        compiler_params=pltpu.CompilerParams(vmem_limit_bytes=60 * MIB),
    )(every, new, out, ig)


def fast_device(
    tokens, segment_ids, adapter_ids, input_weight, conv_weight, output_weight, gate_weight, up_weight, down_weight,
    norm_one, norm_two, cotangent, adapter_state, first_moment, second_moment, rate, step,
):
    seqs, length, _ = tokens.shape
    na = adapter_state.shape[0]
    adapters, count = na * lax.axis_size("grp"), lax.axis_size("seq")
    native = lambda x: x.reshape(na, PACKROWS, 128).swapaxes(0, 1).reshape(na * PACKROWS, 128)
    st, m, v = native(adapter_state), native(first_moment), native(second_moment)
    rows = seqs * length
    tok2, cot2 = tokens.reshape(rows, D), cotangent.reshape(rows, D)
    n1, n2 = norm_one.reshape(1, D), norm_two.reshape(1, D)
    out, ig, new, every, *_ = rest(
        seqs, length, count, na, adapter_ids, rate, step, segment_ids, conv_weight, n1, n2,
        cot2, tok2, input_weight, output_weight, gate_weight, up_weight, down_weight, st, m, v,
    )
    every, new, out, ig = lay_out(every, new, out, ig, na)
    every = every.reshape(PACKROWS, adapters, 128).swapaxes(0, 1).reshape(adapters, PACKROWS * 128)
    new = new.reshape(PACKROWS, na, 128).swapaxes(0, 1).reshape(na, PACKROWS * 128)
    return out.reshape(tokens.shape), ig.reshape(tokens.shape), new, every


def solution(mesh):
    rows = P("grp", "seq", None)
    own = P("grp", None)
    return jax.shard_map(
        fast_device if tuple(mesh.shape[axis] for axis in ("seq", "grp")) == (8, 4) else general_device,
        mesh=mesh,
        in_specs=(rows, P("grp", "seq"), P("grp")) + (P(),) * 8 + (rows, own, own, own, P(), P()),
        out_specs=(rows, rows, own, P()),
        check_vma=False,
    )
```

```python
import functools

import jax
import jax.numpy as jnp
from jax import lax
from jax.experimental import pallas as pl
from jax.experimental.pallas import tpu as pltpu
from jax.sharding import PartitionSpec as P

D = 1024
FF = 4608
RANK = 16
EPS = 1e-05
FB = 512
MIB = 2**20

f32 = jnp.float32
bf16 = jnp.bfloat16
MESH = pl.DeviceIdType.MESH

WIRE = RANK * 0 + 23040
PACKROWS = 2880
A_IN, B_IN, A_OUT, B_OUT, A_GATE, B_GATE, A_UP, B_UP, A_DOWN, B_DOWN = (
    0, 1024, 4096, 5120, 6144, 7168, 11776, 12800, 17408, 22016,
)
B_PARTS = ((B_IN, 3 * D), (B_OUT, D), (B_GATE, FF), (B_UP, FF), (B_DOWN, D))
A_PARTS = ((A_IN, D), (A_OUT, D), (A_GATE, D), (A_UP, D), (A_DOWN, FF))
A_CHUNKS = tuple(
    (first + start, min(1024, height - start))
    for first, height in A_PARTS
    for start in range(0, height, 1024)
)


def dot(a, b):
    return jnp.dot(a, b, preferred_element_type=f32)


def dot_nt(a, b):
    return lax.dot_general(a, b, (((1,), (1,)), ((), ())), preferred_element_type=f32)


def dot_tn(a, b):
    return lax.dot_general(a, b, (((0,), (0,)), ((), ())), preferred_element_type=f32)


def shuffle_matrix():
    row = lax.broadcasted_iota(jnp.int32, (1024, 1024), 0)
    col = lax.broadcasted_iota(jnp.int32, (1024, 1024), 1)
    return jnp.where(col == 8 * (row % 128) + row // 128, 1.0, 0.0).astype(bf16)


def table_kernel(na, st_ref, out_ref, lhs_ref):
    for n, (first, count) in enumerate(A_CHUNKS):
        for a in range(na):
            packed = st_ref[pl.ds(na * (first // 8) + a, 128, stride=na), :]
            turned = packed.T.astype(bf16)
            row = (n * na + a) * RANK
            for c in range(8):
                lhs_ref[row : row + RANK, 128 * c : 128 * c + 128] = turned[RANK * c : RANK * c + RANK, :]
    full = dot(lhs_ref[...], shuffle_matrix()).astype(bf16)
    for n, (first, count) in enumerate(A_CHUNKS):
        for a in range(na):
            row = (n * na + a) * RANK
            out_ref[a * RANK : (a + 1) * RANK, first : first + count] = full[row : row + RANK, :count]
    for first, breadth in B_PARTS:
        blocks = breadth // 128
        for a in range(na):
            for c in range(blocks):
                part = st_ref[pl.ds(na * (first // 8 + c) + a, RANK, stride=na * blocks), :]
                out_ref[a * RANK : (a + 1) * RANK, first + 128 * c : first + 128 * c + 128] = part.astype(bf16)


def build_table(state_native, na):
    return pl.pallas_call(
        functools.partial(table_kernel, na),
        out_shape=jax.ShapeDtypeStruct((na * RANK, WIRE), bf16),
        scratch_shapes=[pltpu.VMEM((len(A_CHUNKS) * na * RANK, 1024), bf16)],
        compiler_params=pltpu.CompilerParams(vmem_limit_bytes=40 * MIB),
    )(state_native)


def adam_kernel(na, scal_ref, gw_ref, st_ref, m_ref, v_ref, new_ref, tab_ref, lhs_ref, gn_ref):
    for n, (first, count) in enumerate(A_CHUNKS):
        for a in range(na):
            row = (n * na + a) * RANK
            lhs_ref[row : row + RANK, :] = gw_ref[a * RANK : (a + 1) * RANK, first : first + 1024].astype(bf16)
    full = dot_nt(lhs_ref[...], shuffle_matrix())
    for n, (first, count) in enumerate(A_CHUNKS):
        for a in range(na):
            row = (n * na + a) * RANK
            turned = jnp.concatenate(
                [full[row : row + RANK, 128 * c : 128 * c + 128] for c in range(8)], axis=0
            )
            gn_ref[pl.ds(na * (first // 8) + a, count // 8, stride=na), :] = turned.T[: count // 8]
    for first, breadth in B_PARTS:
        blocks = breadth // 128
        for a in range(na):
            for c in range(blocks):
                gn_ref[pl.ds(na * (first // 8 + c) + a, RANK, stride=na * blocks), :] = gw_ref[
                    a * RANK : (a + 1) * RANK, first + 128 * c : first + 128 * c + 128
                ].astype(f32)
    rate = scal_ref[0]
    inv = scal_ref[1]
    grad = gn_ref[...]
    one = 0.5 * m_ref[...] + 0.5 * grad
    two = 0.5 * v_ref[...] + 0.5 * grad * grad
    new = st_ref[...] - rate * (one * inv) / (jnp.sqrt(two * inv) + 1e-08)
    new_ref[...] = new
    tab_ref[...] = new.astype(bf16)


def adam(scal, gw, st, m, v, na):
    rows = na * PACKROWS
    vm = pl.BlockSpec(memory_space=pltpu.VMEM)
    return pl.pallas_call(
        functools.partial(adam_kernel, na),
        in_specs=[pl.BlockSpec(memory_space=pltpu.SMEM)] + [vm] * 4,
        out_shape=(jax.ShapeDtypeStruct((rows, 128), f32), jax.ShapeDtypeStruct((rows, 128), bf16)),
        scratch_shapes=[
            pltpu.VMEM((len(A_CHUNKS) * na * RANK, 1024), bf16),
            pltpu.VMEM((rows, 128), f32),
        ],
        compiler_params=pltpu.CompilerParams(vmem_limit_bytes=56 * MIB),
    )(scal, gw, st, m, v)


def greet(seq, count):
    barrier = pltpu.get_barrier_semaphore()

    @pl.when(seq > 0)
    def _():
        pl.semaphore_signal(barrier, inc=1, device_id={"seq": seq - 1}, device_id_type=MESH)

    @pl.when(seq < count - 1)
    def _():
        pl.semaphore_signal(barrier, inc=1, device_id={"seq": seq + 1}, device_id_type=MESH)

    before = (seq + count - 1) // count
    after = (2 * count - 2 - seq) // count
    pl.semaphore_wait(barrier, before + after)


def row_mask(mask_ref, seqs, length):
    return jnp.concatenate(
        [jnp.broadcast_to(mask_ref[s : s + 1, :], (length, 128)) for s in range(seqs)], axis=0
    )


def norm(values, gain):
    inverse = lax.rsqrt(jnp.mean(values * values, axis=-1, keepdims=True) + EPS)
    return values * inverse * gain, inverse


def pre_kernel(
    seqs, length, count,
    tok_ref, ids_ref, mask_ref, tb_ref, wi_ref, cw_ref, wo_ref, n1_ref, n2_ref, cot_ref,
    u1_ref, mi_ref, b_ref, c_ref, x_ref, conv_ref, same_ref, gated_ref, mo_ref, h1_ref, u2_ref, mg_ref, mu_ref, gd_ref,
    ext_ref, out_ref, in_ref, send_sem, recv_sem,
):
    seq = lax.axis_index("seq")
    greet(seq, count)
    mask = row_mask(mask_ref, seqs, length)
    twice = 2.0 * mask
    tokens = tok_ref[...].astype(f32)
    u1 = norm(tokens, n1_ref[...])[0].astype(bf16)
    u1_ref[...] = u1
    mid = (dot_nt(u1, tb_ref[:, A_IN : A_IN + D]).astype(bf16).astype(f32) * twice).astype(bf16)
    mi_ref[...] = mid
    for third, to_ref in ((0, b_ref), (2, x_ref)):
        for k in range(2):
            col = third * D + 512 * k
            to_ref[:, 512 * k : 512 * k + 512] = dot(u1, wi_ref[:, col : col + 512]) + dot(
                mid, tb_ref[:, B_IN + col : B_IN + col + 512]
            )
    width = D + 128
    for s in range(seqs):
        rows = pl.ds(s * length, length)
        ext_ref[s, 0:8, :] = jnp.zeros((8, width), f32)
        ext_ref[s, 8:, :D] = b_ref[rows, :] * x_ref[rows, :]
        ext_ref[s, 8:, D:] = jnp.broadcast_to(ids_ref[s : s + 1, :], (length, 128)).T
        out_ref[2 * s : 2 * s + 2, :] = ext_ref[s, length + 6 : length + 8, :]
    along = pltpu.make_async_remote_copy(
        src_ref=out_ref, dst_ref=in_ref, send_sem=send_sem, recv_sem=recv_sem,
        device_id={"seq": seq + 1}, device_id_type=MESH,
    )

    @pl.when(seq < count - 1)
    def _():
        along.start()

    for k in range(2):
        col = D + 512 * k
        c_ref[:, 512 * k : 512 * k + 512] = dot(u1, wi_ref[:, col : col + 512]) + dot(
            mid, tb_ref[:, B_IN + col : B_IN + col + 512]
        )
    gd_ref[...] = (dot_nt(cot_ref[...], tb_ref[:, B_DOWN : B_DOWN + D]) * twice).astype(bf16)

    @pl.when(seq < count - 1)
    def _():
        along.wait_send()

    @pl.when(seq > 0)
    def _():
        along.wait_recv()
        for s in range(seqs):
            ext_ref[s, 6:8, :] = in_ref[2 * s : 2 * s + 2, :]

    for s in range(seqs):
        rows = pl.ds(s * length, length)
        now_ids = ext_ref[s, 8:, D:]
        same1 = jnp.where(ext_ref[s, pl.ds(7, length), D:] == now_ids, 1.0, 0.0)
        same2 = jnp.where(ext_ref[s, pl.ds(6, length), D:] == now_ids, 1.0, 0.0)
        same_ref[0, rows, :] = same1
        same_ref[1, rows, :] = same2
        conv = (
            cw_ref[2:3, :] * ext_ref[s, 8:, :D]
            + cw_ref[1:2, :] * same1[:, :1] * ext_ref[s, pl.ds(7, length), :D]
            + cw_ref[0:1, :] * same2[:, :1] * ext_ref[s, pl.ds(6, length), :D]
        )
        conv_ref[rows, :] = conv
        gated_ref[rows, :] = (c_ref[rows, :] * conv).astype(bf16)
    gated = gated_ref[...]
    mid_out = (dot_nt(gated, tb_ref[:, A_OUT : A_OUT + D]).astype(bf16).astype(f32) * twice).astype(bf16)
    mo_ref[...] = mid_out
    for k in range(2):
        cols = slice(512 * k, 512 * k + 512)
        h1_ref[:, cols] = (
            tok_ref[:, cols].astype(f32)
            + dot(gated, wo_ref[:, cols])
            + dot(mid_out, tb_ref[:, B_OUT + 512 * k : B_OUT + 512 * k + 512])
        )
    u2 = norm(h1_ref[...], n2_ref[...])[0].astype(bf16)
    u2_ref[...] = u2
    mg_ref[...] = (dot_nt(u2, tb_ref[:, A_GATE : A_GATE + D]).astype(bf16).astype(f32) * twice).astype(bf16)
    mu_ref[...] = (dot_nt(u2, tb_ref[:, A_UP : A_UP + D]).astype(bf16).astype(f32) * twice).astype(bf16)


def pre(seqs, length, count, *args):
    rows = seqs * length
    sd = jax.ShapeDtypeStruct
    width = D + 128
    vm = pl.BlockSpec(memory_space=pltpu.VMEM)
    wide = sd((rows, D), f32)
    half = sd((rows, D), bf16)
    thin = sd((rows, 128), bf16)
    return pl.pallas_call(
        functools.partial(pre_kernel, seqs, length, count),
        in_specs=[vm] * 10,
        out_specs=[vm] * 14,
        out_shape=[half, thin, wide, wide, wide, wide, sd((2, rows, 128), f32), half, thin, wide, half, thin, thin, thin],
        scratch_shapes=[
            pltpu.VMEM((seqs, length + 8, width), f32),
            pltpu.VMEM((2 * seqs, width), f32),
            pltpu.VMEM((2 * seqs, width), f32),
            pltpu.SemaphoreType.DMA,
            pltpu.SemaphoreType.DMA,
        ],
        compiler_params=pltpu.CompilerParams(vmem_limit_bytes=60 * MIB, collective_id=0, has_side_effects=True),
    )(*args)


def ffn_kernel(
    seqs, length,
    u_ref, cot_ref, mg_ref, mu_ref, gd_ref, mask_ref, h1_ref, wg_ref, wu_ref, wd_ref, bg_ref, bu_ref, ad_ref, ag_ref, au_ref, bd_ref,
    out_ref, gn_ref, dbg_ref, dbu_ref, dad_ref, dag_ref, dau_ref, dbd_ref,
    acc_ref, dmid_ref, gmg_ref, gmu_ref,
):
    j = pl.program_id(0)

    @pl.when(j == 0)
    def _():
        for ref in (acc_ref, gn_ref, dmid_ref, gmg_ref, gmu_ref):
            ref[...] = jnp.zeros_like(ref)

    u = u_ref[...]
    gate = dot(u, wg_ref[...]) + dot(mg_ref[...], bg_ref[...])
    up = dot(u, wu_ref[...]) + dot(mu_ref[...], bu_ref[...])
    back = dot_nt(cot_ref[...], wd_ref[...]) + dot(gd_ref[...], ad_ref[...])
    sig = jax.nn.sigmoid(gate)
    silu = gate * sig
    hidden = (silu * up).astype(bf16)
    grad_gate = (back * up * sig * (1.0 + gate * (1.0 - sig))).astype(bf16)
    grad_up = (back * silu).astype(bf16)
    acc_ref[...] += dot(hidden, wd_ref[...])
    gn_ref[...] += dot_nt(grad_gate, wg_ref[...]) + dot_nt(grad_up, wu_ref[...])
    dmid_ref[...] += dot_nt(hidden, ad_ref[...])
    gmg_ref[...] += dot_nt(grad_gate, bg_ref[...])
    gmu_ref[...] += dot_nt(grad_up, bu_ref[...])
    dbg_ref[...] = dot_tn(mg_ref[...], grad_gate).astype(bf16)
    dbu_ref[...] = dot_tn(mu_ref[...], grad_up).astype(bf16)
    dad_ref[...] = dot_tn(gd_ref[...], hidden).astype(bf16)

    @pl.when(j == pl.num_programs(0) - 1)
    def _():
        twice = 2.0 * row_mask(mask_ref, seqs, length)
        dmid = (dmid_ref[...].astype(bf16).astype(f32) * twice).astype(bf16)
        out_ref[...] = (h1_ref[...] + acc_ref[...] + dot(dmid, bd_ref[...])).astype(bf16)
        dbd_ref[...] = dot_tn(dmid, cot_ref[...]).astype(bf16)
        gm_gate = (gmg_ref[...] * twice).astype(bf16)
        gm_up = (gmu_ref[...] * twice).astype(bf16)
        gn_ref[...] += dot(gm_gate, ag_ref[...]) + dot(gm_up, au_ref[...])
        dag_ref[...] = dot_tn(gm_gate, u_ref[...]).astype(bf16)
        dau_ref[...] = dot_tn(gm_up, u_ref[...]).astype(bf16)


def ffn(seqs, length, u2, cot, mg, mu, gd, mask, h1, wg, wu, wd, table):
    rows = seqs * length
    sd = jax.ShapeDtypeStruct
    whole = lambda s: pl.BlockSpec(s, lambda j: (0, 0))
    col = lambda h: pl.BlockSpec((h, FB), lambda j: (0, j))
    tab = lambda first: pl.BlockSpec((128, FB), lambda j: (0, first // FB + j))
    fixed = lambda first: pl.BlockSpec((128, D), lambda j: (0, 0))
    cut = lambda first: lax.slice_in_dim(table, first, first + D, axis=1)
    return pl.pallas_call(
        functools.partial(ffn_kernel, seqs, length),
        grid=(FF // FB,),
        in_specs=[whole((rows, D)), whole((rows, D)), whole((rows, 128)), whole((rows, 128)), whole((rows, 128)),
                  whole(mask.shape), whole((rows, D)),
                  col(D), col(D), pl.BlockSpec((FB, D), lambda j: (j, 0)),
                  tab(B_GATE), tab(B_UP), tab(A_DOWN), whole((128, D)), whole((128, D)), whole((128, D))],
        out_specs=[whole((rows, D)), whole((rows, D)), col(128), col(128), col(128),
                   whole((128, D)), whole((128, D)), whole((128, D))],
        out_shape=[sd((rows, D), bf16), sd((rows, D), f32)] + [sd((128, FF), bf16)] * 3 + [sd((128, D), bf16)] * 3,
        scratch_shapes=[pltpu.VMEM((rows, D), f32)] + [pltpu.VMEM((rows, 128), f32)] * 3,
        compiler_params=pltpu.CompilerParams(vmem_limit_bytes=60 * MIB),
    )(u2, cot, mg, mu, gd, mask, h1, wg, wu, wd, table, table, table, cut(A_GATE), cut(A_UP), cut(B_DOWN))


def post_kernel(
    seqs, length, count,
    tok_ref, cot_ref, mask_ref, h1_ref, gn_ref, gated_ref, mo_ref, b_ref, c_ref, x_ref, conv_ref, same_ref, u1_ref, mi_ref,
    tb_ref, wi_ref, cw_ref, wo_ref, n1_ref, n2_ref,
    ig_ref, dai_ref, dbi_ref, dao_ref, dbo_ref,
    gh_ref, gb_ref, gg_ref, gc_ref, gp_ref, one_ref, two_ref, out_ref, in_ref, send_sem, recv_sem,
):
    seq = lax.axis_index("seq")
    greet(seq, count)
    twice = 2.0 * row_mask(mask_ref, seqs, length)
    h1 = h1_ref[...]
    inv2 = norm(h1, n2_ref[...])[1]
    e2 = gn_ref[...] * n2_ref[...]
    gh = cot_ref[...].astype(f32) + inv2 * e2 - h1 * (inv2 * inv2 * inv2 * jnp.mean(h1 * e2, axis=-1, keepdims=True))
    gh_ref[...] = gh
    gb = gh.astype(bf16)
    gb_ref[...] = gb
    gm_out = (dot_nt(gb, tb_ref[:, B_OUT : B_OUT + D]) * twice).astype(bf16)
    for k in range(2):
        cols = slice(512 * k, 512 * k + 512)
        gg_ref[:, cols] = dot_nt(gb, wo_ref[cols, :]) + dot(gm_out, tb_ref[:, A_OUT + 512 * k : A_OUT + 512 * k + 512])
    for s in range(seqs):
        rows = pl.ds(s * length, length)
        gg = gg_ref[rows, :]
        gp_ref[rows, D : 2 * D] = (gg * conv_ref[rows, :]).astype(bf16)
        gconv = gg * c_ref[rows, :]
        gc_ref[rows, :] = gconv
        one_ref[s, 0:length, :] = cw_ref[1:2, :] * same_ref[0, rows, 0:1] * gconv
        two_ref[s, 0:length, :] = cw_ref[0:1, :] * same_ref[1, rows, 0:1] * gconv
        one_ref[s, length:, :] = jnp.zeros((8, D), f32)
        two_ref[s, length:, :] = jnp.zeros((8, D), f32)
        out_ref[2 * s : 2 * s + 1, :] = two_ref[s, 0:1, :]
        out_ref[2 * s + 1 : 2 * s + 2, :] = two_ref[s, 1:2, :] + one_ref[s, 0:1, :]
    along = pltpu.make_async_remote_copy(
        src_ref=out_ref, dst_ref=in_ref, send_sem=send_sem, recv_sem=recv_sem,
        device_id={"seq": seq - 1}, device_id_type=MESH,
    )

    @pl.when(seq > 0)
    def _():
        along.start()

    dbo_ref[...] = dot_tn(mo_ref[...], gb).astype(bf16)
    dao_ref[...] = dot_tn(gm_out, gated_ref[...]).astype(bf16)

    @pl.when(seq > 0)
    def _():
        along.wait_send()

    @pl.when(seq < count - 1)
    def _():
        along.wait_recv()
        for s in range(seqs):
            two_ref[s, length : length + 2, :] = in_ref[2 * s : 2 * s + 2, :]

    for s in range(seqs):
        rows = pl.ds(s * length, length)
        gmix = (
            cw_ref[2:3, :] * gc_ref[rows, :]
            + one_ref[s, pl.ds(1, length), :]
            + two_ref[s, pl.ds(2, length), :]
        )
        gp_ref[rows, 0:D] = (gmix * x_ref[rows, :]).astype(bf16)
        gp_ref[rows, 2 * D :] = (gmix * b_ref[rows, :]).astype(bf16)
    gm_in = (dot_nt(gp_ref[...], tb_ref[:, B_IN : B_IN + 3 * D]) * twice).astype(bf16)
    for k in range(2):
        cols = slice(512 * k, 512 * k + 512)
        gg_ref[:, cols] = dot_nt(gp_ref[...], wi_ref[cols, :]) + dot(gm_in, tb_ref[:, A_IN + 512 * k : A_IN + 512 * k + 512])
    for k in range(6):
        cols = slice(512 * k, 512 * k + 512)
        dbi_ref[:, cols] = dot_tn(mi_ref[...], gp_ref[:, cols]).astype(bf16)
    dai_ref[...] = dot_tn(gm_in, u1_ref[...]).astype(bf16)
    tokens = tok_ref[...].astype(f32)
    inv1 = norm(tokens, n1_ref[...])[1]
    e1 = gg_ref[...] * n1_ref[...]
    ig_ref[...] = (
        gh_ref[...] + inv1 * e1 - tokens * (inv1 * inv1 * inv1 * jnp.mean(tokens * e1, axis=-1, keepdims=True))
    ).astype(bf16)


def post(seqs, length, count, *args):
    rows = seqs * length
    sd = jax.ShapeDtypeStruct
    vm = pl.BlockSpec(memory_space=pltpu.VMEM)
    return pl.pallas_call(
        functools.partial(post_kernel, seqs, length, count),
        in_specs=[vm] * 20,
        out_specs=[vm] * 5,
        out_shape=[sd((rows, D), bf16), sd((128, D), bf16), sd((128, 3 * D), bf16), sd((128, D), bf16), sd((128, D), bf16)],
        scratch_shapes=[
            pltpu.VMEM((rows, D), f32),
            pltpu.VMEM((rows, D), bf16),
            pltpu.VMEM((rows, D), f32),
            pltpu.VMEM((rows, D), f32),
            pltpu.VMEM((rows, 3 * D), bf16),
            pltpu.VMEM((seqs, length + 8, D), f32),
            pltpu.VMEM((seqs, length + 8, D), f32),
            pltpu.VMEM((2 * seqs, D), f32),
            pltpu.VMEM((2 * seqs, D), f32),
            pltpu.SemaphoreType.DMA,
            pltpu.SemaphoreType.DMA,
        ],
        compiler_params=pltpu.CompilerParams(vmem_limit_bytes=62 * MIB, collective_id=1, has_side_effects=True),
    )(*args)


def general_device(
    tokens, segment_ids, adapter_ids, input_weight, conv_weight, output_weight, gate_weight, up_weight, down_weight,
    norm_one, norm_two, cotangent, adapter_state, first_moment, second_moment, rate, step,
):
    seqs, length, _ = tokens.shape
    na = adapter_state.shape[0]
    groups = lax.axis_size("grp")
    count = lax.axis_size("seq")
    native = lambda x: x.reshape(na, PACKROWS, 128).swapaxes(0, 1).reshape(na * PACKROWS, 128)
    st, m, v = native(adapter_state), native(first_moment), native(second_moment)
    own = build_table(st, na)
    table = lax.all_gather(own, "grp", axis=0, tiled=True)
    adapters = na * groups
    mask = (adapter_ids[:, None] == jnp.arange(adapters * RANK, dtype=jnp.int32)[None, :] // RANK).astype(f32)
    ids = segment_ids.astype(f32)
    rows = seqs * length
    tok2, cot2 = tokens.reshape(rows, D), cotangent.reshape(rows, D)
    n1, n2 = norm_one.reshape(1, D), norm_two.reshape(1, D)
    u1, mi, b, c, x, conv, same, gated, mo, h1, u2, mg, mu, gd = pre(
        seqs, length, count, tok2, ids, mask, table, input_weight, conv_weight, output_weight, n1, n2, cot2
    )
    out, gn, dbg, dbu, dad, dag, dau, dbd = ffn(
        seqs, length, u2, cot2, mg, mu, gd, mask, h1, gate_weight, up_weight, down_weight, table
    )
    ig, dai, dbi, dao, dbo = post(
        seqs, length, count, tok2, cot2, mask, h1, gn, gated, mo, b, c, x, conv, same, u1, mi,
        table, input_weight, conv_weight, output_weight, n1, n2,
    )
    grads = jnp.concatenate([dai, dbi, dao, dbo, dag, dbg, dau, dbu, dad, dbd], axis=1).astype(f32)
    owned = lax.psum(lax.psum_scatter(grads, "grp", scatter_dimension=0, tiled=True), "seq")
    correction = 1.0 - jnp.power(jnp.float32(0.5), step[0].astype(f32))
    scal = jnp.stack([rate[0], 1.0 / correction])
    new, tab = adam(scal, owned, st, m, v, na)
    every = lax.all_gather(tab, "grp", axis=0, tiled=False)
    every = every.reshape(groups, PACKROWS, na, 128).transpose(1, 0, 2, 3).reshape(PACKROWS, adapters, 128)
    every = every.swapaxes(0, 1).reshape(adapters, PACKROWS * 128)
    new = new.reshape(PACKROWS, na, 128).swapaxes(0, 1).reshape(na, PACKROWS * 128)
    return out.reshape(tokens.shape), ig.reshape(tokens.shape), new, every


W_A_IN, W_B_B, W_B_X, W_B_C, W_A_OUT, W_B_OUT, W_A_GATE, W_A_UP, W_B_DOWN, W_FFN = (1024 * n for n in range(10))
W_ENDS = W_A_GATE
BLOCKS = FF // FB
W_BLOCK = 3 * FB
FFN_COLS = WIRE - W_ENDS
SPREAD_BLOCKS = 2


def wire(first, n):
    if first == B_IN:
        return (W_B_B, W_B_C, W_B_X)[n // D] + n % D
    for place, matrix in enumerate((B_GATE, B_UP, A_DOWN)):
        if first == matrix:
            return W_FFN + n // FB * W_BLOCK + place * FB + n % FB
    return {A_IN: W_A_IN, A_OUT: W_A_OUT, B_OUT: W_B_OUT, A_GATE: W_A_GATE, A_UP: W_A_UP, B_DOWN: W_B_DOWN}[first] + n


def a_pieces(first, count):
    for matrix, height in A_PARTS:
        if matrix <= first < matrix + height:
            return [(k, wire(matrix, first - matrix + k), FB) for k in range(0, count, FB)]


class Place:
    def __init__(self):
        seq, grp = lax.axis_index("seq"), lax.axis_index("grp")
        self.seq, self.grp = seq, grp
        self.c, self.x, self.y, self.z = grp % 2, grp // 2, seq % 2, seq // 2
        self.core = grp + 1 - 2 * self.c
        self.gx = (grp + 2) % 4
        self.sy = seq + 1 - 2 * self.y
        self.sz = seq + 2 - 4 * (self.z % 2)

    def along_z(self, d):
        return (self.seq + 2 * d) % 8


def announce(seq, count, devices, both=True):
    barrier = pltpu.get_barrier_semaphore()
    if both:

        @pl.when(seq > 0)
        def _():
            pl.semaphore_signal(barrier, inc=1, device_id={"seq": seq - 1}, device_id_type=MESH)

        @pl.when(seq < count - 1)
        def _():
            pl.semaphore_signal(barrier, inc=1, device_id={"seq": seq + 1}, device_id_type=MESH)

    for device in devices:
        pl.semaphore_signal(barrier, inc=1, device_id=device, device_id_type=MESH)
    ends = (seq + count - 1) // count + (2 * count - 2 - seq) // count if both else 0
    return lambda: pl.semaphore_wait(barrier, ends + len(devices))


class Spread:
    WAYS = {
        "X": (((), ("x", "core")), (("x",), ("cx",)), (("core", "cx"), ())),
        "Y": (((), ("x", "core")), (("x",), ("y", "cx")), (("y",), ("cy",)), (("core", "cx", "cy"), ())),
        "Z": (((), ("x", "core")), (("x",), ("z", "cx")), (("z",), ("cz",)), (("core", "cx", "cz"), ())),
        "S": (
            ((), ("x", "core")), (("x",), ("y", "z", "cx")), (("y",), ("dz", "cy")), (("z",), ("dy", "cz")), (("dy", "dz"), ("cd",)),
            (("core", "cx", "cy", "cz", "cd"), ()),
        ),
    }
    KINDS = ("core", "x", "y", "z", "dy", "dz", "cx", "cy", "cz", "cd")

    def __init__(self, at, own, slot, pieces, ways, step, send_sems, recv_sems):
        self.at, self.own, self.slot, self.pieces, self.ways, self.step = at, own, slot, pieces, ways, step
        self.send_sems, self.recv_sems = send_sems, recv_sems

    def copy(self, kind, p):
        at, way = self.at, self.ways[p]
        first, size = self.pieces[p]
        share = size // {"X": 1, "Y": 2, "Z": 2, "S": 4}[way]
        part = lambda q: pl.multiple_of(first + q * share, self.step) if way != "X" else first
        q = {"X": 0, "Y": at.y, "Z": at.z % 2, "S": at.seq % 4}[way]
        if way == "S":
            qy, qz, qd = q + 1 - 2 * (q % 2), (q + 2) % 4, 3 - q
        else:
            qy = qz = qd = 1 - q
        half = -(-share // (2 * self.step)) * self.step
        core, y, z = {"grp": at.core}, {"seq": at.sy}, {"seq": at.sz}
        if kind == "core":
            src, dst, device = self.own(first, size), self.slot(at.grp, first, size), core
        elif kind == "x":
            src, dst, device = self.own(part(q), share), self.slot(at.grp, part(q), share), {"grp": at.gx}
        else:
            start, count, device = {
                "y": (part(q), share, y),
                "z": (part(q), share, z),
                "dy": (part(qz), half, y),
                "dz": (part(qy) + half, share - half, z),
                "cx": (part(q), share, core),
                "cy": (part(qy), share, core),
                "cz": (part(qz), share, core),
                "cd": (part(qd), share, core),
            }[kind]
            if kind == "dz":
                start = pl.multiple_of(start, self.step)
            src = dst = self.slot(at.gx, start, count)
        n = len(self.KINDS) * p + self.KINDS.index(kind)
        return pltpu.make_async_remote_copy(
            src_ref=src, dst_ref=dst, send_sem=self.send_sems.at[n], recv_sem=self.recv_sems.at[n],
            device_id=device, device_id_type=MESH,
        )

    def steps(self, p):
        return len(self.WAYS[self.ways[p]])

    def leg(self, number, p):
        waits, starts = self.WAYS[self.ways[p]][number]
        for kind in waits:
            self.copy(kind, p).wait_recv()
        for kind in starts:
            self.copy(kind, p).start()

    def sent(self, p):
        for _, starts in self.WAYS[self.ways[p]]:
            for kind in starts:
                self.copy(kind, p).wait_send()


def adapter_mask(adapter_ref, seqs, length):
    column = lax.broadcasted_iota(jnp.int32, (length, 128), 1) // RANK
    return jnp.concatenate([jnp.where(column == adapter_ref[s], 1.0, 0.0) for s in range(seqs)], axis=0)


def fill_shuffle(perm_ref):
    diff = lax.broadcasted_iota(jnp.int32, (128, 1024), 1) - 8 * lax.broadcasted_iota(jnp.int32, (128, 1024), 0)
    for c in range(8):
        perm_ref[128 * c : 128 * c + 128, :] = jnp.where(diff == c, 1.0, 0.0).astype(bf16)


def build_own(na, grp, st_ref, tb_ref, lhs_ref, perm_ref, chunks, matrices):
    own = lambda a: pl.ds(pl.multiple_of((grp * na + a) * RANK, RANK), RANK)
    for n, (first, count) in enumerate(chunks):
        for a in range(na):
            packed = st_ref[pl.ds(na * (first // 8) + a, 128, stride=na), :]
            turned = packed.T.astype(bf16)
            row = (n * na + a) * RANK
            for c in range(8):
                lhs_ref[row : row + RANK, 128 * c : 128 * c + 128] = turned[RANK * c : RANK * c + RANK, :]
    full = dot(lhs_ref[: len(chunks) * na * RANK, :], perm_ref[...]).astype(bf16)
    for n, (first, count) in enumerate(chunks):
        for a in range(na):
            row = (n * na + a) * RANK
            for k, col, size in a_pieces(first, count):
                tb_ref[own(a), col : col + size] = full[row : row + RANK, k : k + size]
    for first, breadth in matrices:
        blocks = breadth // 128
        for a in range(na):
            for c in range(blocks):
                part = st_ref[pl.ds(na * (first // 8 + c) + a, RANK, stride=na * blocks), :]
                col = wire(first, 128 * c)
                tb_ref[own(a), col : col + 128] = part.astype(bf16)


SPREAD_PIECES = ((W_A_IN, 1024), (W_B_B, 2048), (W_B_C, 1024), (W_A_OUT, 5120), (W_FFN, SPREAD_BLOCKS * W_BLOCK))


class Sums:
    CORE, X, Y, Z, BACK_Z, BACK_Y = range(6)
    COPIES = 10

    def __init__(self, at, g_ref, cr_ref, xr_ref, yr_ref, zr_ref, sum_ref, send_sems, recv_sems):
        self.at, self.g, self.cr, self.xr, self.yr, self.zr, self.sum = at, g_ref, cr_ref, xr_ref, yr_ref, zr_ref, sum_ref
        self.send_sems, self.recv_sems = send_sems, recv_sems

    def unit(self, z, start, size):
        rows = pl.ds(pl.multiple_of(RANK * (z // 2), RANK), RANK)
        quarter = size // 4
        return rows, pl.ds(pl.multiple_of(start + self.at.y * (size // 2) + (z % 2) * quarter, 128), quarter)

    def half(self, y, start, size):
        return pl.ds(pl.multiple_of(start + y * (size // 2), 128), size // 2)

    def slot(self, start, size, share):
        return pl.ds(pl.multiple_of(start // share, 128), size // share)

    def copies(self, stage, group):
        index, start, size = group
        at = self.at
        cols = pl.ds(start, size)
        if stage == self.CORE:
            parts = [(self.g.at[:, 1 - at.c, :, cols], self.cr.at[:, :, cols], {"grp": at.core})]
        elif stage == self.X:
            parts = [(self.g.at[1 - at.x, at.c, :, cols], self.xr.at[:, cols], {"grp": at.gx})]
        elif stage == self.Y:
            away = self.half(1 - at.y, start, size)
            parts = [(self.g.at[at.x, at.c, :, away], self.yr.at[:, self.slot(start, size, 2)], {"seq": at.sy})]
        elif stage == self.BACK_Y:
            part = self.sum.at[:, self.half(at.y, start, size)]
            parts = [(part, part, {"seq": at.sy})]
        else:
            parts = []
            for d in range(1, 4):
                if stage == self.Z:
                    rows, span = self.unit((at.z + d) % 4, start, size)
                    parts.append((
                        self.g.at[at.x, at.c, rows, span], self.zr.at[d - 1, :, self.slot(start, size, 4)],
                        {"seq": at.along_z(d)},
                    ))
                else:
                    rows, span = self.unit(at.z, start, size)
                    part = self.sum.at[rows, span]
                    parts.append((part, part, {"seq": at.along_z(d)}))
        first = self.COPIES * index + {self.CORE: 0, self.X: 1, self.Y: 2, self.Z: 3, self.BACK_Z: 6, self.BACK_Y: 9}[stage]
        return [
            pltpu.make_async_remote_copy(
                src_ref=src, dst_ref=dst, send_sem=self.send_sems.at[first + n], recv_sem=self.recv_sems.at[first + n],
                device_id=device, device_id_type=MESH,
            )
            for n, (src, dst, device) in enumerate(parts)
        ]

    def send(self, stage, group):
        for copy in self.copies(stage, group):
            copy.start()

    def take(self, stage, group):
        for copy in self.copies(stage, group):
            copy.wait()
        _, start, size = group
        at = self.at
        cols = pl.ds(start, size)
        wide = lambda value: value.astype(f32)
        if stage == self.CORE:
            for x in range(2):
                self.g[x, at.c, :, cols] = (wide(self.g[x, at.c, :, cols]) + wide(self.cr[x, :, cols])).astype(bf16)
        elif stage == self.X:
            self.g[at.x, at.c, :, cols] = (wide(self.g[at.x, at.c, :, cols]) + wide(self.xr[:, cols])).astype(bf16)
        elif stage == self.Y:
            mine = self.half(at.y, start, size)
            came = self.yr[:, self.slot(start, size, 2)]
            self.g[at.x, at.c, :, mine] = (wide(self.g[at.x, at.c, :, mine]) + wide(came)).astype(bf16)
        elif stage == self.Z:
            rows, span = self.unit(at.z, start, size)
            total = wide(self.g[at.x, at.c, rows, span])
            for d in range(3):
                total = total + wide(self.zr[d, :, self.slot(start, size, 4)])
            self.sum[rows, span] = total.astype(bf16)


def sums_scratch(cols):
    return [
        pltpu.VMEM((2, 2, 32, cols), bf16),
        pltpu.VMEM((2, 32, cols), bf16),
        pltpu.VMEM((32, cols), bf16),
        pltpu.VMEM((32, cols // 2), bf16),
        pltpu.VMEM((3, 16, cols // 4), bf16),
        pltpu.VMEM((32, cols), bf16),
    ]


def put_grad(g_ref, cols, value):
    for x in range(2):
        for c in range(2):
            first = 64 * x + 32 * c
            g_ref[x, c, :, cols] = value[first : first + 32, :].astype(bf16)


UPDATES = (
    (B_GATE, FF), (B_UP, FF), (A_DOWN, FF), (A_GATE, D), (A_UP, D), (B_DOWN, D), (A_OUT, 2 * D), (B_IN, 3 * D),
    (A_IN, D),
)
MOST = 2 * FF // 8
NATIVE = tuple((2 * first // 8, 2 * count // 8) for first, count in UPDATES)


def update_grad(na, part, sum_ref, lhs_ref, perm_ref, gn_ref):
    first, count = UPDATES[part]
    begin = na * first // 8
    inside = lambda start: first <= start < first + count
    chunks = [chunk for chunk in A_CHUNKS if inside(chunk[0])]
    for n, (start, size) in enumerate(chunks):
        for a in range(na):
            row = (n * na + a) * RANK
            if size < 1024:
                lhs_ref[row : row + RANK, size:] = jnp.zeros((RANK, 1024 - size), bf16)
            for k, col, breadth in a_pieces(start, size):
                lhs_ref[row : row + RANK, k : k + breadth] = sum_ref[a * RANK : (a + 1) * RANK, col : col + breadth]
    if chunks:
        height = len(chunks) * na * RANK
        full = dot_nt(lhs_ref[:height, :], perm_ref[...])
    for n, (start, size) in enumerate(chunks):
        for a in range(na):
            row = (n * na + a) * RANK
            turned = jnp.concatenate([full[row : row + RANK, 128 * c : 128 * c + 128] for c in range(8)], axis=0)
            gn_ref[pl.ds(na * (start // 8) + a - begin, size // 8, stride=na), :] = turned.T[: size // 8]
    for start, breadth in B_PARTS:
        if inside(start):
            blocks = breadth // 128
            for a in range(na):
                for c in range(blocks):
                    col = wire(start, 128 * c)
                    gn_ref[pl.ds(na * (start // 8 + c) + a - begin, RANK, stride=na * blocks), :] = sum_ref[
                        a * RANK : (a + 1) * RANK, col : col + 128
                    ].astype(f32)


def group_of(j):
    start = W_FFN + j * W_BLOCK
    return j, start if isinstance(j, int) else pl.multiple_of(start, 128), W_BLOCK


GROUPS = {
    "ends": (BLOCKS, W_ENDS, W_FFN - W_ENDS),
    "out": (BLOCKS + 1, W_B_C, W_ENDS - W_B_C),
    "in1": (BLOCKS + 2, W_B_B, W_B_C - W_B_B),
    "in2": (BLOCKS + 3, W_A_IN, W_B_B),
}
GROUPS.update({j: group_of(j) for j in range(BLOCKS)})


WAYS = "ZZYXXXYXX"
BACKWARD_ORDER = (
    (8, 7, 6, 5, 4, 3, 2, 8), 0, ("ends", 6, 7, 3, 5), 1, ("ends", 4, 8, 7, 6, 5), 2, (4, 8), 3, ("ends", 7, 5, 6), 4,
    ("out", 8), 5, ("out", "ends", 7, 6, 8), 6, ("in1",), 7, ("in1", "in2", 7, 8), 8, ("in2", "out", "ends"), 9,
    ("in1", "in2"), 10,
)
TAIL_ORDER = (
    ("sum", "out"), ("update", 0), ("sum", "in1"), ("sum", "in2"), ("sum", "ends"), ("update", 1), ("update", 2),
    ("out", 0), ("sum", "out"), ("sum", "ends"), ("update", 3), ("sum", "in1"), ("update", 4), ("sum", "in2"),
    ("update", 5), ("pass", 0), ("out", 1), ("pass", 1), ("out", 2), ("sum", "out"), ("out", 3), ("sum", "in1"),
    ("out", 4), ("sum", "in2"), ("pass", 2), ("out", 5), ("sum", "out"), ("update", 6), ("pass", 3), ("sum", "in1"),
    ("update", 7), ("sum", "in2"), ("update", 8), ("pass", 0), ("pass", 3), ("pass", 4), ("pass", 5), ("out", 6),
    ("pass", 0), ("pass", 1), ("pass", 4), ("pass", 2), ("pass", 5), ("pass", 6), ("out", 7), ("pass", 1), ("pass", 2),
    ("out", 8), ("pass", 7), ("pass", 6), ("pass", 8), ("pass", 7), ("pass", 6), ("pass", 8),
)


def rest_kernel(
    seqs, length, count, na,
    adapter_ref, rate_ref, step_ref, ids_ref, cw_ref, n1_ref, n2_ref,
    cot_hbm, tok_hbm, wi_hbm, wo_hbm, wg_hbm, wu_hbm, wd_hbm, st_hbm, m_hbm, v_hbm,
    out_hbm, ig_hbm, new_hbm, all_hbm, hid_hbm, gated_hbm, b_hbm, c_hbm, x_hbm, conv_hbm, same_hbm, u1_hbm,
    cot_ref, u_ref, mg_ref, mu_ref, mo_ref, mi_ref, ahead_out_ref, ahead_in_ref, tb_ref, h1_ref, gn_ref, gh_ref, gb_ref, dmid_ref, gmg_ref, gmu_ref, gd_ref,
    edge_out_ref, edge_in_ref, g_ref, cr_ref, xr_ref, yr_ref, zr_ref, sum_ref, tab_ref,
    result_sems, open_sems, store_sems, open_send, open_recv, load_sems, weight_sems, hid_sems, tab_send, tab_recv, send_sems, recv_sems,
    halo_sems, old_sems, new_sems, own_sems, spread_send, spread_recv,
):
    rows_all = seqs * length
    at = Place()
    seq = at.seq
    met = announce(seq, count, [{"grp": at.core}, {"grp": at.gx}] + [{"seq": at.along_z(d)} for d in range(1, 4)])
    sums = Sums(at, g_ref, cr_ref, xr_ref, yr_ref, zr_ref, sum_ref, send_sems, recv_sems)
    rows32 = lambda owner: pl.ds(pl.multiple_of(owner * 32, 32), 32)
    twice = 2.0 * adapter_mask(adapter_ref, seqs, length)
    block = lambda owner, first, size: tb_ref.at[rows32(owner), pl.ds(first, size)]
    table_spread = Spread(
        at, functools.partial(block, at.grp), block, SPREAD_PIECES, "XXXSS", 128, open_send, open_recv
    )

    load_cot = pltpu.make_async_copy(cot_hbm, cot_ref, result_sems.at[2])
    keep_grad = pltpu.make_async_copy(gb_ref, ig_hbm, result_sems.at[0])
    keep_out = pltpu.make_async_copy(u_ref, out_hbm, result_sems.at[1])

    def opening(
        st_ref, lhs_ref, perm_ref, wi_ref, wo_ref, tok_ref, u1_ref, b_ref, c_ref, x_ref, conv_ref, same_ref, gated_ref, ext_ref
    ):
        load_in = pltpu.make_async_copy(wi_hbm, wi_ref, open_sems.at[0])
        load_out = pltpu.make_async_copy(wo_hbm, wo_ref, open_sems.at[1])
        load_st = pltpu.make_async_copy(st_hbm, st_ref, open_sems.at[2])
        load_tok = pltpu.make_async_copy(tok_hbm, tok_ref, open_sems.at[3])
        for copy in (load_st, load_tok, load_in, load_out, load_cot):
            copy.start()
        load_st.wait()
        build = functools.partial(build_own, na, at.grp, st_ref, tb_ref, lhs_ref, perm_ref)
        fill_shuffle(perm_ref)
        build(A_CHUNKS[:1], B_PARTS[:1])
        leg = table_spread.leg

        def keep(n, src, dst):
            return pltpu.make_async_copy(src, dst, store_sems.at[n])

        met()
        leg(0, 0)
        build(A_CHUNKS[1:], B_PARTS[1:])
        load_tok.wait()
        tokens = tok_ref[...].astype(f32)
        u1 = norm(tokens, n1_ref[...])[0].astype(bf16)
        u1_ref[...] = u1
        leg(0, 1)
        keep(0, u1_ref, u1_hbm).start()
        load_in.wait()
        for k in range(2):
            b_ref[:, 512 * k : 512 * k + 512] = dot(u1, wi_ref[:, 512 * k : 512 * k + 512])
        leg(0, 2)
        leg(1, 0)
        for k in range(2):
            x_ref[:, 512 * k : 512 * k + 512] = dot(u1, wi_ref[:, 2 * D + 512 * k : 2 * D + 512 * k + 512])
        leg(0, 3)
        leg(0, 4)
        for k in range(2):
            c_ref[:, 512 * k : 512 * k + 512] = dot(u1, wi_ref[:, D + 512 * k : D + 512 * k + 512])
        leg(1, 1)
        leg(2, 0)
        mid = (dot_nt(u1, tb_ref[:, W_A_IN : W_A_IN + D]).astype(bf16).astype(f32) * twice).astype(bf16)
        mi_ref[...] = mid
        leg(1, 2)
        leg(2, 1)
        for first, to_ref in ((W_B_B, b_ref), (W_B_X, x_ref)):
            for k in range(2):
                col = first + 512 * k
                to_ref[:, 512 * k : 512 * k + 512] += dot(mid, tb_ref[:, col : col + 512])
        leg(1, 3)
        leg(1, 4)
        keep(1, b_ref, b_hbm).start()
        keep(2, x_ref, x_hbm).start()
        width = D + 128
        for s in range(seqs):
            rows = pl.ds(s * length, length)
            ext_ref[s, 0:8, :] = jnp.zeros((8, width), f32)
            ext_ref[s, 8:, :D] = b_ref[rows, :] * x_ref[rows, :]
            ext_ref[s, 8:, D:] = jnp.broadcast_to(ids_ref[s : s + 1, :].astype(f32), (length, 128)).T
            ahead_out_ref[2 * s : 2 * s + 2, :] = ext_ref[s, length + 6 : length + 8, :]
        along = pltpu.make_async_remote_copy(
            src_ref=ahead_out_ref, dst_ref=ahead_in_ref, send_sem=halo_sems.at[2], recv_sem=halo_sems.at[3],
            device_id={"seq": seq + 1}, device_id_type=MESH,
        )

        @pl.when(seq < count - 1)
        def _():
            along.start()

        leg(2, 2)
        leg(2, 3)
        leg(3, 3)
        for k in range(2):
            col = W_B_C + 512 * k
            c_ref[:, 512 * k : 512 * k + 512] += dot(mid, tb_ref[:, col : col + 512])
        leg(2, 4)
        leg(3, 4)
        keep(3, c_ref, c_hbm).start()

        @pl.when(seq < count - 1)
        def _():
            along.wait_send()

        @pl.when(seq > 0)
        def _():
            along.wait_recv()
            for s in range(seqs):
                ext_ref[s, 6:8, :] = ahead_in_ref[2 * s : 2 * s + 2, :]

        for s in range(seqs):
            rows = pl.ds(s * length, length)
            now_ids = ext_ref[s, 8:, D:]
            same1 = jnp.where(ext_ref[s, pl.ds(7, length), D:] == now_ids, 1.0, 0.0)
            same2 = jnp.where(ext_ref[s, pl.ds(6, length), D:] == now_ids, 1.0, 0.0)
            same_ref[0, s] = same1
            same_ref[1, s] = same2
            conv = (
                cw_ref[2:3, :] * ext_ref[s, 8:, :D]
                + cw_ref[1:2, :] * same1[:, :1] * ext_ref[s, pl.ds(7, length), :D]
                + cw_ref[0:1, :] * same2[:, :1] * ext_ref[s, pl.ds(6, length), :D]
            )
            conv_ref[rows, :] = conv
            gated_ref[rows, :] = (c_ref[rows, :] * conv).astype(bf16)
        keep(4, conv_ref, conv_hbm).start()
        keep(5, same_ref, same_hbm).start()
        leg(4, 3)
        leg(4, 4)
        keep(6, gated_ref, gated_hbm).start()
        gated = gated_ref[...]
        load_out.wait()
        for k in range(2):
            cols = slice(512 * k, 512 * k + 512)
            h1_ref[:, cols] = tok_ref[:, cols].astype(f32) + dot(gated, wo_ref[:, cols])
        leg(5, 3)
        mid_out = (dot_nt(gated, tb_ref[:, W_A_OUT : W_A_OUT + D]).astype(bf16).astype(f32) * twice).astype(bf16)
        mo_ref[...] = mid_out
        for k in range(2):
            cols = slice(512 * k, 512 * k + 512)
            h1_ref[:, cols] += dot(mid_out, tb_ref[:, W_B_OUT + 512 * k : W_B_OUT + 512 * k + 512])
        u2 = norm(h1_ref[...], n2_ref[...])[0].astype(bf16)
        u_ref[...] = u2
        mg_ref[...] = (dot_nt(u2, tb_ref[:, W_A_GATE : W_A_GATE + D]).astype(bf16).astype(f32) * twice).astype(bf16)
        mu_ref[...] = (dot_nt(u2, tb_ref[:, W_A_UP : W_A_UP + D]).astype(bf16).astype(f32) * twice).astype(bf16)
        for n, (src, dst) in enumerate((
            (u1_ref, u1_hbm), (b_ref, b_hbm), (x_ref, x_hbm), (c_ref, c_hbm), (conv_ref, conv_hbm), (same_ref, same_hbm),
            (gated_ref, gated_hbm),
        )):
            keep(n, src, dst).wait()

    wide = pltpu.VMEM((rows_all, D), f32)
    half = pltpu.VMEM((rows_all, D), bf16)
    pl.run_scoped(
        opening,
        pltpu.VMEM((na * PACKROWS, 128), f32), pltpu.VMEM((len(A_CHUNKS) * na * RANK, 1024), bf16),
        pltpu.VMEM((1024, 1024), bf16), pltpu.VMEM((D, 3 * D), bf16), pltpu.VMEM((D, D), bf16),
        half, half, wide, wide, wide, wide, pltpu.VMEM((2, seqs, length, 128), f32), half,
        pltpu.VMEM((seqs, length + 8, D + 128), f32),
    )

    def table_copy(kind, j):
        _, start, size = group_of(j)
        owner, device = {
            "core": (at.grp, {"grp": at.core}), "x": (at.grp, {"grp": at.gx}), "far": (at.gx, {"grp": at.core})
        }[kind]
        part = tb_ref.at[rows32(owner), pl.ds(start, size)]
        n = 3 * j + ("core", "x", "far").index(kind)
        return pltpu.make_async_remote_copy(
            src_ref=part, dst_ref=part, send_sem=tab_send.at[n], recv_sem=tab_recv.at[n], device_id=device, device_id_type=MESH
        )

    def when(first, j, last, run):
        @pl.when((j >= first) & (j <= last))
        def _():
            run()

    def feed_forward(wg_ref, wu_ref, wd_ref, hid_ref):
        def fetch(j, slot):
            cols = pl.ds(j * FB if isinstance(j, int) else pl.multiple_of(j * FB, FB), FB)
            return [
                pltpu.make_async_copy(wg_hbm.at[:, cols], wg_ref.at[slot], weight_sems.at[slot, 0]),
                pltpu.make_async_copy(wu_hbm.at[:, cols], wu_ref.at[slot], weight_sems.at[slot, 1]),
                pltpu.make_async_copy(wd_hbm.at[cols, :], wd_ref.at[slot], weight_sems.at[slot, 2]),
            ]

        def keep(j, slot):
            cols = pl.ds(j * FB if isinstance(j, int) else pl.multiple_of(j * FB, FB), FB)
            return pltpu.make_async_copy(hid_ref.at[slot], hid_hbm.at[:, cols], hid_sems.at[slot])

        for copy in fetch(0, 0):
            copy.start()
        for ref in (gn_ref, dmid_ref, gmg_ref, gmu_ref):
            ref[...] = jnp.zeros_like(ref)
        load_cot.wait()
        gd_ref[...] = (dot_nt(cot_ref[...], tb_ref[:, W_B_DOWN : W_B_DOWN + D]) * twice).astype(bf16)
        table_spread.leg(5, 4)

        def block(j, carry):
            slot = j % 2
            for copy in fetch(j, slot):
                copy.wait()

            def more():
                for copy in fetch(j + 1, 1 - slot):
                    copy.start()

            when(0, j, BLOCKS - 2, more)
            when(2, j, BLOCKS - 1, lambda: keep(j - 2, slot).wait())
            lead = SPREAD_BLOCKS

            def leave():
                table_copy("x", j + lead).start()
                table_copy("core", j + lead).start()

            def go_on():
                table_copy("x", j + lead - 1).wait()
                table_copy("far", j + lead - 1).start()

            def there():
                table_copy("core", j).wait()
                table_copy("far", j).wait()

            when(0, j, BLOCKS - 1 - lead, leave)
            when(1, j, BLOCKS - lead, go_on)
            when(lead, j, BLOCKS - 1, there)
            for stage in range(6):

                def advance(stage=stage):
                    if stage > 0:
                        sums.take(stage - 1, group_of(j - 1 - stage))
                    sums.send(stage, group_of(j - 1 - stage))

                when(1 + stage, j, BLOCKS - 1, advance)
            when(7, j, BLOCKS - 1, lambda: sums.take(5, group_of(j - 7)))

            base = W_FFN + j * W_BLOCK
            part = lambda place: pl.ds(pl.multiple_of(base + place * FB, 128), FB)
            tab_gate, tab_up, tab_down = (tb_ref.at[:, part(place)] for place in range(3))
            u = u_ref[...]
            gate = dot(u, wg_ref[slot]) + dot(mg_ref[...], tab_gate[...])
            up = dot(u, wu_ref[slot]) + dot(mu_ref[...], tab_up[...])
            back = dot_nt(cot_ref[...], wd_ref[slot]) + dot(gd_ref[...], tab_down[...])
            sig = jax.nn.sigmoid(gate)
            silu = gate * sig
            hidden = (silu * up).astype(bf16)
            hid_ref[slot] = hidden
            keep(j, slot).start()
            grad_gate = (back * up * sig * (1.0 + gate * (1.0 - sig))).astype(bf16)
            grad_up = (back * silu).astype(bf16)
            gn_ref[...] += dot_nt(grad_gate, wg_ref[slot]) + dot_nt(grad_up, wu_ref[slot])
            dmid_ref[...] += dot_nt(hidden, tab_down[...])
            gmg_ref[...] += dot_nt(grad_gate, tab_gate[...])
            gmu_ref[...] += dot_nt(grad_up, tab_up[...])
            put_grad(g_ref, part(0), dot_tn(mg_ref[...], grad_gate))
            put_grad(g_ref, part(1), dot_tn(mu_ref[...], grad_up))
            put_grad(g_ref, part(2), dot_tn(gd_ref[...], hidden))
            return carry

        lax.fori_loop(0, BLOCKS, block, 0)
        for j in range(BLOCKS - 2, BLOCKS):
            keep(j, j % 2).wait()
        for p in range(len(SPREAD_PIECES)):
            table_spread.sent(p)

    pl.run_scoped(
        feed_forward,
        pltpu.VMEM((2, D, FB), bf16), pltpu.VMEM((2, D, FB), bf16), pltpu.VMEM((2, FB, D), bf16),
        pltpu.VMEM((2, rows_all, FB), bf16),
    )

    sent = {BLOCKS - 2 - stage: stage for stage in range(6)}

    def advance(*names):
        for name in names:
            stage = sent.get(name, -1)
            if stage >= 0:
                sums.take(stage, GROUPS[name])
            if stage < 5:
                sums.send(stage + 1, GROUPS[name])
            sent[name] = stage + 1

    dmid = (dmid_ref[...].astype(bf16).astype(f32) * twice).astype(bf16)

    def backward(gated_ref, one_ref, two_ref, same_ref, u1_ref, tok_ref, wi_ref, wo_ref, gg_ref, gp_ref):
        pairs = (
            (wo_hbm, wo_ref), (c_hbm, one_ref), (conv_hbm, two_ref), (same_hbm, same_ref.at[:, :, :length, :]),
            (gated_hbm, gated_ref), (wi_hbm, wi_ref), (u1_hbm, u1_ref), (tok_hbm, tok_ref), (x_hbm, one_ref), (b_hbm, two_ref),
        )
        copies = [pltpu.make_async_copy(*pair, load_sems.at[n]) for n, pair in enumerate(pairs)]
        get_wo, get_c, get_conv, get_same, get_gated, get_wi, get_u1, get_tok, get_x, get_b = copies
        for copy in (get_wo, get_c, get_conv, get_same):
            copy.start()
        held = {}

        def part0():
            held["gm_gate"] = (gmg_ref[...] * twice).astype(bf16)
            held["gm_up"] = (gmu_ref[...] * twice).astype(bf16)
            put_grad(g_ref, slice(W_A_GATE, W_A_GATE + D), dot_tn(held["gm_gate"], u_ref[...]))
            put_grad(g_ref, slice(W_A_UP, W_A_UP + D), dot_tn(held["gm_up"], u_ref[...]))
            put_grad(g_ref, slice(W_B_DOWN, W_B_DOWN + D), dot_tn(dmid, cot_ref[...]))

        def part1():
            for k in range(2):
                cols = slice(512 * k, 512 * k + 512)
                gn_ref[:, cols] += dot(held["gm_gate"], tb_ref[:, W_A_GATE + 512 * k : W_A_GATE + 512 * k + 512]) + dot(
                    held["gm_up"], tb_ref[:, W_A_UP + 512 * k : W_A_UP + 512 * k + 512]
                )
            for s in range(seqs):
                rows = pl.ds(s * length, length)
                h1 = h1_ref[rows, :]
                inv2 = norm(h1, n2_ref[...])[1]
                e2 = gn_ref[rows, :] * n2_ref[...]
                gh = cot_ref[rows, :].astype(f32) + inv2 * e2
                gh = gh - h1 * (inv2 * inv2 * inv2 * jnp.mean(h1 * e2, axis=-1, keepdims=True))
                gh_ref[rows, :] = gh
                gb_ref[rows, :] = gh.astype(bf16)
            for copy in (get_gated, get_wi, get_u1, get_tok):
                copy.start()

        def part2():
            get_wo.wait()
            held["gb"] = gb_ref[...]
            held["gm_out"] = (dot_nt(held["gb"], tb_ref[:, W_B_OUT : W_B_OUT + D]) * twice).astype(bf16)
            for k in range(2):
                cols = slice(512 * k, 512 * k + 512)
                part = dot_nt(held["gb"], wo_ref[cols, :]) + dot(held["gm_out"], tb_ref[:, W_A_OUT + 512 * k : W_A_OUT + 512 * k + 512])
                for s in range(seqs):
                    gg_ref[s, :length, cols] = part[s * length : (s + 1) * length, :]

        def part3():
            for copy in (get_c, get_conv, get_same):
                copy.wait()
            for s in range(seqs):
                rows = pl.ds(s * length, length)
                gg = gg_ref[s, :length, :]
                gp_ref[rows, D : 2 * D] = (gg * two_ref[rows, :]).astype(bf16)
                gg_ref[s, :length, :] = gg * one_ref[rows, :]
                gg_ref[s, length:, :] = jnp.zeros((8, D), f32)
                for k in range(2):
                    same_ref[k, s, length:, :] = jnp.zeros((8, 128), f32)
                edge_out_ref[2 * s : 2 * s + 1, :] = cw_ref[0:1, :] * same_ref[1, s, 0:1, 0:1] * gg_ref[s, 0:1, :]
                edge_out_ref[2 * s + 1 : 2 * s + 2, :] = (
                    cw_ref[0:1, :] * same_ref[1, s, 1:2, 0:1] * gg_ref[s, 1:2, :]
                    + cw_ref[1:2, :] * same_ref[0, s, 0:1, 0:1] * gg_ref[s, 0:1, :]
                )
            get_x.start()
            get_b.start()
            held["along"] = pltpu.make_async_remote_copy(
                src_ref=edge_out_ref, dst_ref=edge_in_ref, send_sem=halo_sems.at[0], recv_sem=halo_sems.at[1],
                device_id={"seq": seq - 1}, device_id_type=MESH,
            )

            @pl.when(seq > 0)
            def _():
                held["along"].start()

        def part4():
            get_gated.wait()
            put_grad(g_ref, slice(W_A_OUT, W_A_OUT + D), dot_tn(held["gm_out"], gated_ref[...]))
            put_grad(g_ref, slice(W_B_OUT, W_B_OUT + D), dot_tn(mo_ref[...], held["gb"]))
            put_grad(g_ref, slice(W_B_C, W_B_C + D), dot_tn(mi_ref[...], gp_ref[:, D : 2 * D]))

        def part5():

            @pl.when(seq > 0)
            def _():
                held["along"].wait_send()

            @pl.when(seq < count - 1)
            def _():
                held["along"].wait_recv()

            get_x.wait()
            get_b.wait()
            for s in range(seqs):
                one, two = pl.ds(1, length), pl.ds(2, length)
                gg_ref[s, :length, :] = (
                    cw_ref[2:3, :] * gg_ref[s, :length, :]
                    + cw_ref[1:2, :] * same_ref[0, s, one, 0:1] * gg_ref[s, one, :]
                    + cw_ref[0:1, :] * same_ref[1, s, two, 0:1] * gg_ref[s, two, :]
                )

            @pl.when(seq < count - 1)
            def _():
                for s in range(seqs):
                    gg_ref[s, length - 2 : length, :] += edge_in_ref[2 * s : 2 * s + 2, :]

            for s in range(seqs):
                rows = pl.ds(s * length, length)
                gmix = gg_ref[s, :length, :]
                gp_ref[rows, 0:D] = (gmix * one_ref[rows, :]).astype(bf16)
                gp_ref[rows, 2 * D :] = (gmix * two_ref[rows, :]).astype(bf16)

        def part6():
            put_grad(g_ref, slice(W_B_B, W_B_B + D), dot_tn(mi_ref[...], gp_ref[:, :D]))
            put_grad(g_ref, slice(W_B_X, W_B_X + D), dot_tn(mi_ref[...], gp_ref[:, 2 * D :]))

        def part7():
            gm_part = dot_nt(gp_ref[:, :D], tb_ref[:, W_B_B : W_B_B + D])
            gm_part += dot_nt(gp_ref[:, D : 2 * D], tb_ref[:, W_B_C : W_B_C + D])
            gm_part += dot_nt(gp_ref[:, 2 * D :], tb_ref[:, W_B_X : W_B_X + D])
            held["gm_in"] = (gm_part * twice).astype(bf16)
            get_u1.wait()
            put_grad(g_ref, slice(W_A_IN, W_A_IN + D), dot_tn(held["gm_in"], u1_ref[...]))

        def part8():
            get_wi.wait()
            for k in range(2):
                cols = slice(256 * k, 256 * k + 256)
                gn_ref[:, cols] = dot_nt(gp_ref[...], wi_ref[cols, :]) + dot(
                    held["gm_in"], tb_ref[:, W_A_IN + 256 * k : W_A_IN + 256 * k + 256]
                )

        def part9():
            for k in range(2, 4):
                cols = slice(256 * k, 256 * k + 256)
                gn_ref[:, cols] = dot_nt(gp_ref[...], wi_ref[cols, :]) + dot(
                    held["gm_in"], tb_ref[:, W_A_IN + 256 * k : W_A_IN + 256 * k + 256]
                )

        def part10():
            get_tok.wait()
            for s in range(seqs):
                rows = pl.ds(s * length, length)
                tokens = tok_ref[rows, :].astype(f32)
                inv1 = norm(tokens, n1_ref[...])[1]
                e1 = gn_ref[rows, :] * n1_ref[...]
                ig = gh_ref[rows, :] + inv1 * e1
                gb_ref[rows, :] = (
                    ig - tokens * (inv1 * inv1 * inv1 * jnp.mean(tokens * e1, axis=-1, keepdims=True))
                ).astype(bf16)
            keep_grad.start()

        parts = (part0, part1, part2, part3, part4, part5, part6, part7, part8, part9, part10)
        for what in BACKWARD_ORDER:
            if isinstance(what, tuple):
                advance(*what)
            else:
                parts[what]()

    pl.run_scoped(
        backward,
        half, wide, wide, pltpu.VMEM((2, seqs, length + 8, 128), f32), half, half,
        pltpu.VMEM((D, 3 * D), bf16), pltpu.VMEM((D, D), bf16), pltpu.VMEM((seqs, length + 8, D), f32),
        pltpu.VMEM((rows_all, 3 * D), bf16),
    )

    def updates(lhs_ref, perm_ref, old_ref, grad_ref, new_ref, wd_ref, hid_ref):
        own = lambda first, size: tab_ref.at[pl.ds(first, size), :]
        slot_of = lambda owner, first, size: all_hbm.at[owner, pl.ds(first, size), :]
        spread = Spread(at, own, slot_of, NATIVE, WAYS, 16, spread_send, spread_recv)
        going = {}

        def pass_on(*parts):
            for part in parts:
                spread.leg(going[part], part)
                going[part] += 1

        power = jnp.float32(1.0)
        for bit in range(8):
            power = power * jnp.where((step_ref[0] >> bit) % 2 == 1, jnp.float32(0.5 ** (2**bit)), jnp.float32(1.0))
        rate = rate_ref[0]
        correction = 1.0 - jnp.full((8, 128), power, f32)
        inv = (1.0 / correction)[0:1, :]

        def old(part):
            first, size = NATIVE[part]
            slot = part % 2
            return [
                pltpu.make_async_copy(ref.at[first : first + size], old_ref.at[slot, n, :size], old_sems.at[slot, n])
                for n, ref in enumerate((st_hbm, m_hbm, v_hbm))
            ]

        def new_copy(part):
            first, size = NATIVE[part]
            return pltpu.make_async_copy(new_ref.at[part % 2, :size], new_hbm.at[first : first + size], new_sems.at[part % 2])

        def own_copy(part):
            first, size = NATIVE[part]
            return pltpu.make_async_copy(
                tab_ref.at[first : first + size], all_hbm.at[at.grp, first : first + size], own_sems.at[part]
            )

        def update(part):
            first, size = NATIVE[part]
            slot = part % 2
            update_grad(na, part, sum_ref, lhs_ref, perm_ref, grad_ref)
            for copy in old(part):
                copy.wait()
            if part >= 2:
                new_copy(part - 2).wait()
            grad = grad_ref[:size]
            one = 0.5 * old_ref[slot, 1, :size] + 0.5 * grad
            two = 0.5 * old_ref[slot, 2, :size] + 0.5 * grad * grad
            new = old_ref[slot, 0, :size] - rate * (one * inv) / (jnp.sqrt(two * inv) + 1e-08)
            new_ref[slot, :size] = new
            tab_ref[first : first + size] = new.astype(bf16)
            new_copy(part).start()
            own_copy(part).start()
            if part + 2 < len(NATIVE):
                for copy in old(part + 2):
                    copy.start()
            going[part] = 0
            pass_on(part)

        def fetch(j):
            slot = j % 2
            return [
                pltpu.make_async_copy(wd_hbm.at[j * FB : (j + 1) * FB, :], wd_ref.at[slot], weight_sems.at[slot, 0]),
                pltpu.make_async_copy(hid_hbm.at[:, j * FB : (j + 1) * FB], hid_ref.at[slot], weight_sems.at[slot, 1]),
            ]

        def outputs(*blocks):
            for j in blocks:
                for copy in fetch(j):
                    copy.wait()
                h1_ref[...] += dot(hid_ref[j % 2], wd_ref[j % 2])
                if j + 2 < BLOCKS:
                    for copy in fetch(j + 2):
                        copy.start()
                if j == BLOCKS - 1:
                    u_ref[...] = h1_ref[...].astype(bf16)
                    keep_out.start()

        for part in range(2):
            for copy in old(part):
                copy.start()
        for j in range(2):
            for copy in fetch(j):
                copy.start()
        fill_shuffle(perm_ref)
        for k in range(2):
            cols = slice(512 * k, 512 * k + 512)
            h1_ref[:, cols] += dot(dmid, tb_ref[:, W_B_DOWN + 512 * k : W_B_DOWN + 512 * k + 512])
        for what, *which in TAIL_ORDER:
            {"sum": advance, "update": update, "pass": pass_on, "out": outputs}[what](*which)
        keep_grad.wait()
        keep_out.wait()
        for part in range(len(NATIVE)):
            spread.sent(part)
            own_copy(part).wait()
        for part in range(len(NATIVE) - 2, len(NATIVE)):
            new_copy(part).wait()

    pl.run_scoped(
        updates,
        pltpu.VMEM((5 * na * RANK, 1024), bf16), pltpu.VMEM((1024, 1024), bf16),
        pltpu.VMEM((2, 3, MOST, 128), f32), pltpu.VMEM((MOST, 128), f32), pltpu.VMEM((2, MOST, 128), f32),
        pltpu.VMEM((2, FB, D), bf16), pltpu.VMEM((2, rows_all, FB), bf16),
    )


def rest(seqs, length, count, na, *args):
    rows = seqs * length
    sd = jax.ShapeDtypeStruct
    sm = pl.BlockSpec(memory_space=pltpu.SMEM)
    vm = pl.BlockSpec(memory_space=pltpu.VMEM)
    hbm = pl.BlockSpec(memory_space=pl.ANY)
    wide = pltpu.VMEM((rows, D), f32)
    thin = pltpu.VMEM((rows, 128), f32)
    half, full = sd((rows, D), bf16), sd((rows, D), f32)
    mids = [pltpu.VMEM((rows, 128), bf16)] * 4
    ahead = pltpu.VMEM((2 * seqs, D + 128), f32)
    parts = len(NATIVE)
    dma = lambda *shape: pltpu.SemaphoreType.DMA(shape)
    return pl.pallas_call(
        functools.partial(rest_kernel, seqs, length, count, na),
        in_specs=[sm] * 3 + [vm] * 4 + [hbm] * 10,
        out_specs=[hbm] * 12,
        out_shape=[
            sd((rows, D), bf16), sd((rows, D), bf16), sd((na * PACKROWS, 128), f32), sd((4, na * PACKROWS, 128), bf16),
            sd((rows, FF), bf16), half, full, full, full, full, sd((2, seqs, length, 128), f32), half,
        ],
        scratch_shapes=[
            pltpu.VMEM((rows, D), bf16), pltpu.VMEM((rows, D), bf16), *mids, ahead, ahead,
            pltpu.VMEM((128, WIRE), bf16), wide, wide, wide, pltpu.VMEM((rows, D), bf16), thin, thin, thin,
            pltpu.VMEM((rows, 128), bf16),
            pltpu.VMEM((2 * seqs, D), f32), pltpu.VMEM((2 * seqs, D), f32),
            *sums_scratch(WIRE),
            pltpu.VMEM((na * PACKROWS, 128), bf16),
            dma(3), dma(4), dma(7), dma(len(Spread.KINDS) * len(SPREAD_PIECES)), dma(len(Spread.KINDS) * len(SPREAD_PIECES)),
            dma(10), dma(2, 3), dma(2), dma(3 * BLOCKS), dma(3 * BLOCKS),
            dma(Sums.COPIES * len(GROUPS)), dma(Sums.COPIES * len(GROUPS)),
            dma(4), dma(2, 3), dma(2), dma(parts), dma(len(Spread.KINDS) * parts), dma(len(Spread.KINDS) * parts),
        ],
        compiler_params=pltpu.CompilerParams(vmem_limit_bytes=63 * MIB, collective_id=3, has_side_effects=True),
    )(*args)


def lay_kernel(all_hbm, new_hbm, out_hbm, ig_hbm, to_ref, new_to, out_to, ig_to, all_ref, new_ref, out_ref, ig_ref, load_sems, store_sems):
    cuts = 4
    share = PACKROWS // cuts
    moves = []
    for k in range(cuts):
        rows = pl.ds(k * share, share)
        moves += [(all_hbm.at[g, rows], all_ref.at[g, rows], to_ref.at[rows, g]) for g in range(4)]
    for k in range(2):
        rows = pl.ds(k * PACKROWS, PACKROWS)
        moves.append((new_hbm.at[rows], new_ref.at[rows], new_to.at[rows]))
    moves += [(out_hbm, out_ref, out_to), (ig_hbm, ig_ref, ig_to)]
    loads = [pltpu.make_async_copy(src, mid, load_sems.at[n]) for n, (src, mid, _) in enumerate(moves)]
    stores = [pltpu.make_async_copy(mid, dst, store_sems.at[n]) for n, (_, mid, dst) in enumerate(moves)]
    for copy in loads:
        copy.start()
    for came, goes in zip(loads, stores):
        came.wait()
        goes.start()
    for copy in stores:
        copy.wait()


def lay_out(every, new, out, ig, na):
    hbm = pl.BlockSpec(memory_space=pl.ANY)
    scratch = lambda x: pltpu.VMEM(x.shape, x.dtype)
    like = lambda x: jax.ShapeDtypeStruct(x.shape, x.dtype)
    every = every.reshape(4, PACKROWS, na, 128)
    return pl.pallas_call(
        lay_kernel,
        in_specs=[hbm] * 4,
        out_specs=[hbm] * 4,
        out_shape=[jax.ShapeDtypeStruct((PACKROWS, 4, na, 128), bf16), like(new), like(out), like(ig)],
        scratch_shapes=[
            *(scratch(x) for x in (every, new, out, ig)), pltpu.SemaphoreType.DMA((20,)), pltpu.SemaphoreType.DMA((20,)),
        ],
        compiler_params=pltpu.CompilerParams(vmem_limit_bytes=60 * MIB),
    )(every, new, out, ig)


def fast_device(
    tokens, segment_ids, adapter_ids, input_weight, conv_weight, output_weight, gate_weight, up_weight, down_weight,
    norm_one, norm_two, cotangent, adapter_state, first_moment, second_moment, rate, step,
):
    seqs, length, _ = tokens.shape
    na = adapter_state.shape[0]
    adapters, count = na * lax.axis_size("grp"), lax.axis_size("seq")
    native = lambda x: x.reshape(na, PACKROWS, 128).swapaxes(0, 1).reshape(na * PACKROWS, 128)
    st, m, v = native(adapter_state), native(first_moment), native(second_moment)
    rows = seqs * length
    tok2, cot2 = tokens.reshape(rows, D), cotangent.reshape(rows, D)
    n1, n2 = norm_one.reshape(1, D), norm_two.reshape(1, D)
    out, ig, new, every, *_ = rest(
        seqs, length, count, na, adapter_ids, rate, step, segment_ids, conv_weight, n1, n2,
        cot2, tok2, input_weight, output_weight, gate_weight, up_weight, down_weight, st, m, v,
    )
    every, new, out, ig = lay_out(every, new, out, ig, na)
    every = every.reshape(PACKROWS, adapters, 128).swapaxes(0, 1).reshape(adapters, PACKROWS * 128)
    new = new.reshape(PACKROWS, na, 128).swapaxes(0, 1).reshape(na, PACKROWS * 128)
    return out.reshape(tokens.shape), ig.reshape(tokens.shape), new, every


def solution(mesh):
    rows = P("grp", "seq", None)
    own = P("grp", None)
    return jax.shard_map(
        fast_device if tuple(mesh.shape[axis] for axis in ("seq", "grp")) == (8, 4) else general_device,
        mesh=mesh,
        in_specs=(rows, P("grp", "seq"), P("grp")) + (P(),) * 8 + (rows, own, own, own, P(), P()),
        out_specs=(rows, rows, own, P()),
        check_vma=False,
    )
```
